32 devices in a mesh: dp: 16 (over z, y, core), tp: 2 (over x).
Axes of the slice: x: 2, y: 2, z: 4, core: 2. Of those that a mesh axis runs over, the one named last changes fastest.
Arguments:
- tokens: bfloat16 [16, 512, 1024], P('dp', 'tp'), may hold values from -6 to 6
- doc_starts: int32 [16, 4], P('dp'), may hold values from 0 to 511, as said below
- attn_gain: float32 [1024], replicated, may hold values from 0.5 to 1.5
- w_query: bfloat16 [1024, 1024], P('dp', 'tp'), may hold values from -0.1875 to 0.1875
- w_key: bfloat16 [1024, 512], P('dp', 'tp'), may hold values from -0.1875 to 0.1875
- w_value: bfloat16 [1024, 512], P('dp', 'tp'), may hold values from -0.1875 to 0.1875
- q_gain: float32 [64], replicated, may hold values from 0.5 to 1.5
- k_gain: float32 [64], replicated, may hold values from 0.5 to 1.5
- w_out: bfloat16 [1024, 1024], P('dp', 'tp'), may hold values from -1.5 to 1.5
- mlp_gain: float32 [1024], replicated, may hold values from 0.5 to 1.5
- w_gate: bfloat16 [1024, 4608], P('dp', 'tp'), may hold values from -0.1875 to 0.1875
- w_up: bfloat16 [1024, 4608], P('dp', 'tp'), may hold values from -0.1875 to 0.1875
- w_down: bfloat16 [1024, 4608], P('dp', 'tp'), may hold values from -0.09375 to 0.09375
- out_grad: bfloat16 [16, 512, 1024], P('dp', 'tp'), may hold values from -6 to 6
Outputs:
- output: bfloat16 [16, 512, 1024], P('dp', 'tp')
- tokens_grad: bfloat16 [16, 512, 1024], P('dp', 'tp')
- attn_gain_grad: float32 [1024], replicated
- w_query_grad: float32 [1024, 1024], P('dp', 'tp')
- w_key_grad: float32 [1024, 512], P('dp', 'tp')
- w_value_grad: float32 [1024, 512], P('dp', 'tp')
- q_gain_grad: float32 [64], replicated
- k_gain_grad: float32 [64], replicated
- w_out_grad: float32 [1024, 1024], P('dp', 'tp')
- mlp_gain_grad: float32 [1024], replicated
- w_gate_grad: float32 [1024, 4608], P('dp', 'tp')
- w_up_grad: float32 [1024, 4608], P('dp', 'tp')
- w_down_grad: float32 [1024, 4608], P('dp', 'tp')
The draws below stay inside these ranges and needn't reach their ends.
Inputs may be any that keep to these rules, and one draw needn't show every extreme that they name: In each packed row the entries start at 0 and rise strictly; document k covers tokens doc_starts[k] up to the next start (the last up to 512). In every row one document begins within the first 256 tokens and ends within the last 256.
All inputs are finite; a program needn't handle non-finite values.
Results may differ from the reference program's by a relative error of at most 0.02.
Values may be sent and summed in bfloat16 or wider, within the bound.
No kernel may reach another device: no remote copies, remote signals or barrier semaphores. Data moves between devices by JAX's collectives and lax.ppermute only.
A program may use at most 128 MiB of HBM per device.

```python
import jax
import jax.numpy as jnp
from jax import lax

D = 1024
H = 16
KV = 8
HD = 64
FF = 4608
TOK_DEV = 256
DOCS = 4
ROW = 512
ROWS = 16


def draw_doc_starts(key, part):
    key = jax.random.fold_in(key, 11)
    key_short, key_long = jax.random.split(key)
    short_lengths = jax.random.randint(key_short, (ROWS, DOCS), 1, TOK_DEV // 4 + 1)
    long_index = jax.random.randint(key_long, (ROWS, 1), 0, DOCS - 1)
    columns = jnp.arange(DOCS, dtype=jnp.int32)[None, :]
    row_ids = jnp.arange(ROWS, dtype=jnp.int32)[:, None]
    short_lengths = jnp.where((row_ids == 0) & (columns == DOCS - 1), 1, short_lengths)
    is_long = columns == long_index
    short_part = jnp.where(is_long, 0, short_lengths)
    long_length = ROW - jnp.sum(short_part, axis=1, keepdims=True)
    lengths = jnp.where(is_long, long_length, short_part)
    return (jnp.cumsum(lengths, axis=1) - lengths).astype(jnp.int32)


def block_scale(own_key, extent, pieces, smallest, high):
    loudness, own = 1.0, jax.random.fold_in(own_key, 6)
    for dim, parts in pieces:
        steps = jnp.exp(jax.random.uniform(jax.random.fold_in(own, dim), (parts,), jnp.float32, smallest / len(pieces), high / len(pieces)))
        loudness = loudness * jnp.repeat(steps, extent[dim] // parts).reshape([-1 if axis == dim else 1 for axis in range(len(extent))])
    return loudness


def scatter_about(key, dims, spread, limit, shards=(), kind=jnp.bfloat16):
    values = jax.random.normal(key, dims, jnp.float32) * spread
    if len(shards) > 0:
        values = block_scale(key, dims, shards, -0.22, 0.18) * values
    return jnp.clip(values, min=-limit, max=limit).astype(kind)


def setup_inputs(seed: int = 0) -> dict:
    key_of = jax.random.split(jax.random.key(seed), 15)
    return {
        "tokens": scatter_about(key_of[0], (ROWS, ROW, D), 1.0, 6.0, ((0, 16), (1, 2))),
        "doc_starts": draw_doc_starts(jax.random.fold_in(key_of[14], 71), 0),
        "attn_gain": jnp.clip(1.0 + 0.1 * jax.random.normal(key_of[2], (D,), jnp.float32), 0.5, 1.5),
        "w_query": scatter_about(key_of[3], (D, H * HD), D ** -0.5, 0.1875, ((0, 16), (1, 2))),
        "w_key": scatter_about(key_of[4], (D, KV * HD), D ** -0.5, 0.1875, ((0, 16), (1, 2))),
        "w_value": scatter_about(key_of[5], (D, KV * HD), D ** -0.5, 0.1875, ((0, 16), (1, 2))),
        "q_gain": jnp.clip(1.0 + 0.1 * jax.random.normal(key_of[6], (HD,), jnp.float32), 0.5, 1.5),
        "k_gain": jnp.clip(1.0 + 0.1 * jax.random.normal(key_of[7], (HD,), jnp.float32), 0.5, 1.5),
        "w_out": scatter_about(key_of[8], (D, H * HD), 16 ** -0.5, 1.5, ((0, 16), (1, 2))),
        "mlp_gain": jnp.clip(1.0 + 0.1 * jax.random.normal(key_of[9], (D,), jnp.float32), 0.5, 1.5),
        "w_gate": scatter_about(key_of[10], (D, FF), D ** -0.5, 0.1875, ((0, 16), (1, 2))),
        "w_up": scatter_about(key_of[11], (D, FF), D ** -0.5, 0.1875, ((0, 16), (1, 2))),
        "w_down": scatter_about(key_of[12], (D, FF), FF ** -0.5, 0.09375, ((0, 16), (1, 2))),
        "out_grad": scatter_about(key_of[13], (ROWS, ROW, D), 1.0, 6.0, ((0, 16), (1, 2))),
    }


EPSILON = 1e-05
THETA = 1000000.0
HIGHEST = lax.Precision.HIGHEST

@jax.custom_vjp
def low(v):
    return lax.optimization_barrier(v.astype(jnp.bfloat16)).astype(jnp.float32)

@jax.custom_vjp
def low_back(v):
    return v

def low_keep(v):
    return (low(v), None)

def low_pass(kept, grad):
    return (grad,)

def back_keep(v):
    return (v, None)

def back_low(kept, grad):
    return (low(grad),)
low.defvjp(low_keep, low_pass)
low_back.defvjp(back_keep, back_low)

def rms_norm(values, gain):
    return values * lax.rsqrt(lax.optimization_barrier(jnp.mean(values * values, axis=-1, keepdims=True)) + EPSILON) * gain

def documents(starts, length):
    places = jnp.arange(length, dtype=jnp.int32)
    inside = places[:, None] >= starts[None, :]
    segment = lax.optimization_barrier(jnp.sum(inside.astype(jnp.int32), axis=1)) - 1
    firsts = lax.optimization_barrier(jnp.max(jnp.where(inside, starts[None, :], 0), axis=1))
    return (segment, places - firsts)

def rope_tables(position, width):
    half_width = width // 2
    freqs = THETA ** (-(jnp.arange(half_width, dtype=jnp.float32) * 2.0 / width))
    angles = position.astype(jnp.float32)[:, None] * freqs[None, :]
    return (jnp.cos(angles), jnp.sin(angles))

def rotate(values, cosine, sine):
    half_width = values.shape[-1] // 2
    first_half = values[..., :half_width]
    second_half = values[..., half_width:]
    tile_shape = (values.shape[0],) + (1,) * (values.ndim - 2) + (half_width,)
    cos_tile = cosine.reshape(tile_shape)
    sin_tile = sine.reshape(tile_shape)
    return jnp.concatenate([first_half * cos_tile - second_half * sin_tile, second_half * cos_tile + first_half * sin_tile], axis=-1)

def attention(queries, keys, values, segment):
    block_rows = min(512, ROW)
    blocks = ROW // block_rows
    places = jnp.arange(ROW, dtype=jnp.int32)
    score_scale = HD ** (-0.5)

    def block_out(block_item):
        query_block, block_segment, block_places = block_item
        scores = low_back(jnp.einsum('qgrd,kgd->grqk', query_block, keys, precision=HIGHEST) * score_scale)
        allowed = (places[None, :] <= block_places[:, None]) & (segment[None, :] == block_segment[:, None])
        scores = jnp.where(allowed, scores, -1e+30)
        shifted = jnp.exp(scores - lax.optimization_barrier(jnp.max(scores, axis=-1, keepdims=True)))
        attn_probs = shifted / lax.optimization_barrier(jnp.sum(shifted, axis=-1, keepdims=True))
        return jnp.einsum('grqk,kgd->qgrd', low(attn_probs), values, precision=HIGHEST)
    outputs = lax.map(jax.checkpoint(block_out), (queries.reshape((blocks, block_rows) + queries.shape[1:]), segment.reshape(blocks, block_rows), places.reshape(blocks, block_rows)))
    return outputs.reshape(ROW, H * HD)

def layer_forward(inputs, starts, attn_gain, w_query, w_key, w_value, q_gain, k_gain, w_out, mlp_gain, w_gate, w_up, w_down):
    segment, position = documents(starts, ROW)
    normed_first = low(rms_norm(inputs, attn_gain))
    query_raw = low_back(jnp.dot(normed_first, w_query, precision=HIGHEST)).reshape(ROW, KV, H // KV, HD)
    key_raw = low_back(jnp.dot(normed_first, w_key, precision=HIGHEST)).reshape(ROW, KV, HD)
    value_rows = low(low_back(jnp.dot(normed_first, w_value, precision=HIGHEST))).reshape(ROW, KV, HD)
    cosine, sine = rope_tables(position, HD)
    query_rows = low(rotate(rms_norm(query_raw, q_gain), cosine, sine))
    key_rows = low(rotate(rms_norm(key_raw, k_gain), cosine, sine))
    attended = low(low_back(attention(query_rows, key_rows, value_rows, segment)))
    hidden = inputs + low_back(jnp.dot(attended, w_out.T, precision=HIGHEST))
    normed_second = low(rms_norm(hidden, mlp_gain))
    gate_pre = low_back(jnp.dot(normed_second, w_gate, precision=HIGHEST))
    up_pre = low_back(jnp.dot(normed_second, w_up, precision=HIGHEST))
    activated = low(jax.nn.silu(gate_pre) * up_pre)
    return hidden + low_back(jnp.dot(activated, w_down.T, precision=HIGHEST))

def reference(tokens, doc_starts, attn_gain, w_query, w_key, w_value, q_gain, k_gain, w_out, mlp_gain, w_gate, w_up, w_down, out_grad):
    params = tuple((param.astype(jnp.float32) for param in (attn_gain, w_query, w_key, w_value, q_gain, k_gain, w_out, mlp_gain, w_gate, w_up, w_down)))

    def one_row(totals, row_item):
        row_tokens, row_starts, row_cot = row_item

        def forward(row_input, *weights):
            return layer_forward(row_input, row_starts, *weights)
        result, pullback = jax.vjp(forward, row_tokens, *params)
        gradients = pullback(row_cot)
        return (tuple((running + gradient for running, gradient in zip(totals, gradients[1:]))), (result, gradients[0]))
    initial = tuple((jnp.zeros_like(param) for param in params))
    totals, (results, input_grads) = lax.scan(one_row, initial, (tokens.astype(jnp.float32), doc_starts, out_grad.astype(jnp.float32)))
    return (results.astype(jnp.bfloat16), input_grads.astype(jnp.bfloat16), totals[0], totals[1], totals[2], totals[3], totals[4], totals[5], totals[6], totals[7], totals[8], totals[9], totals[10])
```

```python
import jax
import jax.numpy as jnp
from jax import lax
from jax.sharding import PartitionSpec as P

HD = 64


EPSILON = 1e-05
THETA = 1000000.0


def documents(starts, places):
    inside = places[:, None] >= starts[None, :]
    segment = jnp.sum(inside.astype(jnp.int32), axis=1) - 1
    firsts = jnp.max(jnp.where(inside, starts[None, :], 0), axis=1)
    return (segment, places - firsts)


def rope_tables(position, width):
    half_width = width // 2
    freqs = THETA ** (-(jnp.arange(half_width, dtype=jnp.float32) * 2.0 / width))
    angles = position.astype(jnp.float32)[:, None] * freqs[None, :]
    return (jnp.cos(angles), jnp.sin(angles))


def rotate(values, cosine, sine):
    half_width = values.shape[-1] // 2
    first_half = values[..., :half_width]
    second_half = values[..., half_width:]
    tile_shape = (values.shape[0],) + (1,) * (values.ndim - 2) + (half_width,)
    cos_tile = cosine.reshape(tile_shape)
    sin_tile = sine.reshape(tile_shape)
    return jnp.concatenate(
        [
            first_half * cos_tile - second_half * sin_tile,
            second_half * cos_tile + first_half * sin_tile,
        ],
        axis=-1,
    )


def norm_forward(values, gain):
    inverse = lax.rsqrt(jnp.mean(values * values, axis=-1, keepdims=True) + EPSILON)
    normed_hat = values * inverse
    return (normed_hat * gain, normed_hat, inverse)


def norm_backward(grad_normed, normed_hat, inverse, gain):
    grad_hat = grad_normed * gain
    grad_values = inverse * (
        grad_hat - normed_hat * jnp.mean(grad_hat * normed_hat, axis=-1, keepdims=True)
    )
    gain_part = jnp.sum((grad_normed * normed_hat).reshape(-1, normed_hat.shape[-1]), axis=0)
    return (grad_values, gain_part)


def partners(size, mask):
    return [(own, own ^ mask) for own in range(size)]


def swap(values, axis_name, mask):
    return lax.ppermute(values, axis_name, partners(lax.axis_size(axis_name), mask))


def layout_masks():
    size = lax.axis_size("dp")
    masks = []
    mask = 1
    while mask < size:
        masks.append(mask)
        mask *= 2
    return masks


def gather_weight(shard, order):
    held = []
    for mask in order:
        other = swap(shard, "dp", mask)
        held = sorted(held + [mask])
        shard = jnp.stack([shard, other], axis=held.index(mask))
    return shard.reshape((-1, shard.shape[-1]))


def scatter_weight(summed, order):
    held = sorted(order)
    summed = summed.reshape((2,) * len(held) + (-1, summed.shape[-1]))
    for mask in order:
        axis = held.index(mask)
        held.remove(mask)
        sent = lax.index_in_dim(summed, 1, axis, keepdims=False).astype(jnp.bfloat16)
        kept = lax.index_in_dim(summed, 0, axis, keepdims=False)
        summed = kept + swap(sent, "dp", mask).astype(jnp.float32)
    return summed


def weight_grad(left, right, order):
    half = left.shape[1] // 2
    sent = jnp.einsum(
        "rd,rf->df", left[:, half:], right, preferred_element_type=jnp.float32
    ).astype(jnp.bfloat16)
    kept = jnp.einsum("rd,rf->df", left[:, :half], right, preferred_element_type=jnp.float32)
    kept = kept + swap(sent, "dp", 1).astype(jnp.float32)
    return scatter_weight(kept, order)


def reversed_bits(block):
    masks = layout_masks()
    flipped = jnp.zeros_like(block)
    for rank, mask in enumerate(masks):
        flipped = flipped + ((block >> (len(masks) - 1 - rank)) & 1) * mask
    return flipped


def order_index(place, width):
    chunk = width // lax.axis_size("dp")
    return (lax.axis_index("dp") ^ reversed_bits(place // chunk)) * chunk + place % chunk


def order_back(entry, width):
    chunk = width // lax.axis_size("dp")
    return reversed_bits(lax.axis_index("dp") ^ (entry // chunk)) * chunk + entry % chunk


def order_matrix(width, dtype):
    place = lax.broadcasted_iota(jnp.int32, (width, width), 1)
    source = lax.broadcasted_iota(jnp.int32, (width, width), 0)
    return (source == order_index(place, width)).astype(dtype)


def reorder(values, matrix):
    return jnp.dot(values, matrix, preferred_element_type=jnp.float32).astype(values.dtype)


def restore(values, matrix):
    return lax.dot_general(
        values, matrix, (((1,), (1,)), ((), ())), preferred_element_type=jnp.float32
    ).astype(values.dtype)


def gather_rows(values):
    if lax.axis_size("tp") == 2:
        return jnp.concatenate([values, swap(values, "tp", 1)], axis=0)
    return lax.all_gather(values, "tp", axis=0, tiled=True)


def row_places(own_rows):
    if lax.axis_size("tp") == 2:
        own = jnp.arange(own_rows, dtype=jnp.int32)
        index = lax.axis_index("tp")
        return jnp.concatenate([own + index * own_rows, own + (1 - index) * own_rows])
    return jnp.arange(own_rows * lax.axis_size("tp"), dtype=jnp.int32)


def project_back(left_rows, right_weight):
    return jnp.dot(left_rows, right_weight.T, preferred_element_type=jnp.float32)


def sum_rows(left_rows, right_weight):
    if lax.axis_size("tp") == 2:
        half = left_rows.shape[0] // 2
        sent = project_back(left_rows[half:], right_weight).astype(jnp.bfloat16)
        other = swap(sent, "tp", 1)
        return project_back(left_rows[:half], right_weight) + other.astype(jnp.float32)
    return lax.psum_scatter(
        project_back(left_rows, right_weight).astype(jnp.bfloat16),
        "tp",
        scatter_dimension=0,
        tiled=True,
    ).astype(jnp.float32)


def sum_rows_two(left_one, weight_one, left_two, weight_two):
    if lax.axis_size("tp") == 2:
        half = left_one.shape[0] // 2
        sent = project_back(left_one[half:], weight_one) + project_back(left_two[half:], weight_two)
        other = swap(sent.astype(jnp.bfloat16), "tp", 1)
        kept = project_back(left_one[:half], weight_one) + project_back(left_two[:half], weight_two)
        return kept + other.astype(jnp.float32)
    both = project_back(left_one, weight_one) + project_back(left_two, weight_two)
    return lax.psum_scatter(
        both.astype(jnp.bfloat16), "tp", scatter_dimension=0, tiled=True
    ).astype(jnp.float32)


def masked_scores(query_block, key_rows, block_segment, block_places, segment, places, score_scale):
    scores = (
        jnp.einsum("qgrd,kgd->grqk", query_block, key_rows, preferred_element_type=jnp.float32)
        * score_scale
    )
    allowed = (places[None, :] <= block_places[:, None]) & (
        segment[None, :] == block_segment[:, None]
    )
    return jnp.where(allowed, scores, -1e30)


def attend(query_rows, key_rows, value_rows, segment, places, block_rows):
    row_len = query_rows.shape[0]
    blocks = row_len // block_rows
    score_scale = query_rows.shape[-1] ** (-0.5)

    def block_out(block_item):
        query_block, block_segment, block_places = block_item
        scores = masked_scores(
            query_block, key_rows, block_segment, block_places, segment, places, score_scale
        )
        peaks = jnp.max(scores, axis=-1, keepdims=True)
        shifted = jnp.exp(scores - peaks)
        totals = jnp.sum(shifted, axis=-1, keepdims=True)
        attn_probs = (shifted / totals).astype(jnp.bfloat16)
        outputs = jnp.einsum(
            "grqk,kgd->qgrd", attn_probs, value_rows, preferred_element_type=jnp.float32
        )
        return (outputs, (peaks + jnp.log(totals))[..., 0])

    outputs, log_totals = lax.map(
        block_out,
        (
            query_rows.reshape((blocks, block_rows) + query_rows.shape[1:]),
            segment.reshape(blocks, block_rows),
            places.reshape(blocks, block_rows),
        ),
    )
    return (outputs.reshape(query_rows.shape), log_totals)


def attend_back(
    query_rows, key_rows, value_rows, grad_out, log_totals, segment, places, block_rows
):
    row_len = query_rows.shape[0]
    blocks = row_len // block_rows
    score_scale = query_rows.shape[-1] ** (-0.5)

    def block_back(carry, block_item):
        grad_keys, grad_values = carry
        query_block, grad_block, total_block, block_segment, block_places = block_item
        scores = masked_scores(
            query_block, key_rows, block_segment, block_places, segment, places, score_scale
        )
        attn_probs = jnp.exp(scores - total_block[..., None])
        grad_probs = jnp.einsum(
            "qgrd,kgd->grqk", grad_block, value_rows, preferred_element_type=jnp.float32
        )
        inner = jnp.sum(attn_probs * grad_probs, axis=-1, keepdims=True)
        grad_scores = (attn_probs * (grad_probs - inner)).astype(jnp.bfloat16)
        grad_query = (
            jnp.einsum("grqk,kgd->qgrd", grad_scores, key_rows, preferred_element_type=jnp.float32)
            * score_scale
        )
        grad_keys = (
            grad_keys
            + jnp.einsum(
                "grqk,qgrd->kgd", grad_scores, query_block, preferred_element_type=jnp.float32
            )
            * score_scale
        )
        grad_values = grad_values + jnp.einsum(
            "grqk,qgrd->kgd",
            attn_probs.astype(jnp.bfloat16),
            grad_block,
            preferred_element_type=jnp.float32,
        )
        return ((grad_keys, grad_values), grad_query)

    zeros_kv = jnp.zeros(key_rows.shape, jnp.float32)
    block_shape = (blocks, block_rows) + query_rows.shape[1:]
    (grad_keys, grad_values), grad_queries = lax.scan(
        block_back,
        (zeros_kv, zeros_kv),
        (
            query_rows.reshape(block_shape),
            grad_out.reshape(block_shape),
            log_totals,
            segment.reshape(blocks, block_rows),
            places.reshape(blocks, block_rows),
        ),
    )
    return (grad_queries.reshape(query_rows.shape), grad_keys, grad_values)


def local(
    tokens,
    doc_starts,
    attn_gain,
    w_query,
    w_key,
    w_value,
    q_gain,
    k_gain,
    w_out,
    mlp_gain,
    w_gate,
    w_up,
    w_down,
    out_grad,
):
    masks = layout_masks()
    late = masks[::-1]
    early = masks[1:2] + masks[:1:-1] + masks[:1]
    qkv_weight = gather_weight(jnp.concatenate([w_query, w_key, w_value], axis=1), early)
    out_w = gather_weight(w_out, early)
    gate_w = gather_weight(w_gate, late)
    up_w = gather_weight(w_up, late)
    down_w = gather_weight(w_down, late)
    matrix = order_matrix(tokens.shape[-1], jnp.bfloat16)
    entries = jnp.arange(tokens.shape[-1], dtype=jnp.int32)
    index = order_index(entries, tokens.shape[-1])
    attn_gain = attn_gain[index]
    mlp_gain = mlp_gain[index]
    inputs = reorder(tokens[0], matrix).astype(jnp.float32)
    cotangent = reorder(out_grad[0], matrix)
    own_rows = inputs.shape[0]
    row_len = own_rows * lax.axis_size("tp")
    head_dim = HD
    groups = w_key.shape[1] // head_dim
    repeat = w_query.shape[1] // w_key.shape[1]
    query_cols = w_query.shape[1]
    key_cols = w_key.shape[1]
    ff_cols = w_gate.shape[1]
    block_rows = min(512, row_len)
    places = row_places(own_rows)
    segment, position = documents(doc_starts[0], places)
    cosine, sine = rope_tables(position, head_dim)
    normed_first, hat_first, inv_first = norm_forward(inputs, attn_gain)
    rows_first = gather_rows(normed_first.astype(jnp.bfloat16))
    projected = jnp.dot(rows_first, qkv_weight, preferred_element_type=jnp.float32)
    query_raw = projected[:, :query_cols].reshape(row_len, groups, repeat, head_dim)
    key_raw = projected[:, query_cols : query_cols + key_cols].reshape(row_len, groups, head_dim)
    value_rows = (
        projected[:, query_cols + key_cols :]
        .astype(jnp.bfloat16)
        .reshape(row_len, groups, head_dim)
    )
    query_normed, query_hat, query_inv = norm_forward(query_raw, q_gain)
    key_normed, key_hat, key_inv = norm_forward(key_raw, k_gain)
    query_rows = rotate(query_normed, cosine, sine).astype(jnp.bfloat16)
    key_rows = rotate(key_normed, cosine, sine).astype(jnp.bfloat16)
    attended, log_totals = attend(query_rows, key_rows, value_rows, segment, places, block_rows)
    attended = attended.reshape(row_len, query_cols).astype(jnp.bfloat16)
    branch_out = sum_rows(attended, out_w)
    hidden = inputs + branch_out
    normed_second, hat_second, inv_second = norm_forward(hidden, mlp_gain)
    rows_second = gather_rows(normed_second.astype(jnp.bfloat16))
    gate_pre = jnp.dot(rows_second, gate_w, preferred_element_type=jnp.float32)
    up_pre = jnp.dot(rows_second, up_w, preferred_element_type=jnp.float32)
    sigmoid_gate = jax.nn.sigmoid(gate_pre)
    activated = (gate_pre * sigmoid_gate * up_pre).astype(jnp.bfloat16)
    result = hidden + sum_rows(activated, down_w)
    cot_rows = gather_rows(cotangent)
    grad_act = jnp.dot(cot_rows, down_w, preferred_element_type=jnp.float32)
    grad_gate = grad_act * up_pre * sigmoid_gate * (1.0 + gate_pre * (1.0 - sigmoid_gate))
    grad_up = grad_act * gate_pre * sigmoid_gate
    grad_gate = grad_gate.astype(jnp.bfloat16)
    grad_up = grad_up.astype(jnp.bfloat16)
    grad_normed_second = sum_rows_two(grad_gate, gate_w, grad_up, up_w)
    grad_hidden_norm, mlp_gain_part = norm_backward(
        grad_normed_second, hat_second, inv_second, mlp_gain
    )
    grad_hidden = cotangent.astype(jnp.float32) + grad_hidden_norm
    grad_branch = grad_hidden.astype(jnp.bfloat16)
    branch_rows = gather_rows(grad_branch)
    grad_attended = jnp.dot(branch_rows, out_w, preferred_element_type=jnp.float32).astype(
        jnp.bfloat16
    )
    grad_query_rot, grad_key_rot, grad_value = attend_back(
        query_rows,
        key_rows,
        value_rows,
        grad_attended.reshape(row_len, groups, repeat, head_dim),
        log_totals,
        segment,
        places,
        block_rows,
    )
    grad_query_norm = rotate(grad_query_rot, cosine, -sine)
    grad_key_norm = rotate(grad_key_rot, cosine, -sine)
    grad_query_raw, q_gain_part = norm_backward(grad_query_norm, query_hat, query_inv, q_gain)
    grad_key_raw, k_gain_part = norm_backward(grad_key_norm, key_hat, key_inv, k_gain)
    grad_projected = jnp.concatenate(
        [
            grad_query_raw.reshape(row_len, query_cols),
            grad_key_raw.reshape(row_len, key_cols),
            grad_value.reshape(row_len, key_cols),
        ],
        axis=1,
    ).astype(jnp.bfloat16)
    grad_normed_first = sum_rows(grad_projected, qkv_weight)
    grad_input_norm, attn_gain_part = norm_backward(
        grad_normed_first, hat_first, inv_first, attn_gain
    )
    grad_inputs = grad_hidden + grad_input_norm
    late_back = late[-2::-1]
    early_back = early[-2::-1]
    down_grad = weight_grad(cot_rows, activated, late_back)
    gate_grad = weight_grad(rows_second, grad_gate, late_back)
    up_grad = weight_grad(rows_second, grad_up, late_back)
    out_w_grad = weight_grad(branch_rows, attended, early_back)
    qkv_grad = weight_grad(rows_first, grad_projected, early_back)
    summed = (
        qkv_grad[:, :query_cols],
        qkv_grad[:, query_cols : query_cols + key_cols],
        qkv_grad[:, query_cols + key_cols :],
        out_w_grad,
        gate_grad,
        up_grad,
        down_grad,
    )
    back = order_back(entries, tokens.shape[-1])
    attn_gain_part = attn_gain_part[back]
    mlp_gain_part = mlp_gain_part[back]
    gains = lax.psum((attn_gain_part, q_gain_part, k_gain_part, mlp_gain_part), ("dp", "tp"))
    return (
        restore(result.astype(jnp.bfloat16), matrix)[None],
        restore(grad_inputs.astype(jnp.bfloat16), matrix)[None],
        gains[0],
        summed[0],
        summed[1],
        summed[2],
        gains[1],
        gains[2],
        summed[3],
        gains[3],
        summed[4],
        summed[5],
        summed[6],
    )


def solution(mesh):
    in_specs = (
        P("dp", "tp", None),
        P("dp", None),
        P(),
        P("dp", "tp"),
        P("dp", "tp"),
        P("dp", "tp"),
        P(),
        P(),
        P("dp", "tp"),
        P(),
        P("dp", "tp"),
        P("dp", "tp"),
        P("dp", "tp"),
        P("dp", "tp", None),
    )
    out_specs = (
        P("dp", "tp", None),
        P("dp", "tp", None),
        P(),
        P("dp", "tp"),
        P("dp", "tp"),
        P("dp", "tp"),
        P(),
        P(),
        P("dp", "tp"),
        P(),
        P("dp", "tp"),
        P("dp", "tp"),
        P("dp", "tp"),
    )
    return jax.shard_map(local, mesh=mesh, in_specs=in_specs, out_specs=out_specs, check_vma=False)
```

```python
import functools

import jax
import jax.numpy as jnp
from jax import lax
from jax.experimental import pallas as pl
from jax.experimental.pallas import tpu as pltpu
from jax.sharding import PartitionSpec as P

HD = 64


EPSILON = 1e-05
THETA = 1000000.0


def documents(starts, places):
    inside = places[:, None] >= starts[None, :]
    segment = jnp.sum(inside.astype(jnp.int32), axis=1) - 1
    firsts = jnp.max(jnp.where(inside, starts[None, :], 0), axis=1)
    return (segment, places - firsts)


def rope_tables(position, width):
    half_width = width // 2
    freqs = THETA ** (-(jnp.arange(half_width, dtype=jnp.float32) * 2.0 / width))
    angles = position.astype(jnp.float32)[:, None] * freqs[None, :]
    return (jnp.cos(angles), jnp.sin(angles))


def rotate(values, cosine, sine):
    half_width = values.shape[-1] // 2
    first_half = values[..., :half_width]
    second_half = values[..., half_width:]
    tile_shape = (values.shape[0],) + (1,) * (values.ndim - 2) + (half_width,)
    cos_tile = cosine.reshape(tile_shape)
    sin_tile = sine.reshape(tile_shape)
    return jnp.concatenate(
        [
            first_half * cos_tile - second_half * sin_tile,
            second_half * cos_tile + first_half * sin_tile,
        ],
        axis=-1,
    )


def norm_forward(values, gain):
    inverse = lax.rsqrt(jnp.mean(values * values, axis=-1, keepdims=True) + EPSILON)
    normed_hat = values * inverse
    return (normed_hat * gain, normed_hat, inverse)


def norm_backward(grad_normed, normed_hat, inverse, gain):
    grad_hat = grad_normed * gain
    grad_values = inverse * (
        grad_hat - normed_hat * jnp.mean(grad_hat * normed_hat, axis=-1, keepdims=True)
    )
    gain_part = jnp.sum((grad_normed * normed_hat).reshape(-1, normed_hat.shape[-1]), axis=0)
    return (grad_values, gain_part)


F32 = jnp.float32
BF16 = jnp.bfloat16
VMEM_BYTES = 50 * 1024 * 1024


def partners(size, mask):
    return [(own, own ^ mask) for own in range(size)]


def swap(values, axis_name, mask):
    return lax.ppermute(values, axis_name, partners(lax.axis_size(axis_name), mask))


def layout_masks():
    size = lax.axis_size("dp")
    masks = []
    mask = 1
    while mask < size:
        masks.append(mask)
        mask *= 2
    return masks


def gather_weight(shard):
    for mask in layout_masks()[:1:-1]:
        shard = jnp.concatenate([shard, swap(shard, "dp", mask)], axis=0)
    beside = swap(shard, "dp", 2)
    return [shard, beside, swap(shard, "dp", 1), swap(beside, "dp", 1)]


def product(left, right, flipped):
    return lax.dot_general(
        left, right, (((0,), (1 if flipped else 0,)), ((), ())), preferred_element_type=F32
    )


def weight_grad(left, right, flipped=False):
    half = left.shape[1] // 2
    quarter = half // 2
    sent = product(left[:, half:], right, flipped).astype(BF16)
    core = swap(sent, "dp", 1)
    sent = product(left[:, quarter:half], right, flipped) + core[quarter:].astype(F32)
    beside = swap(sent.astype(BF16), "dp", 2)
    kept = product(left[:, :quarter], right, flipped) + core[:quarter].astype(F32)
    kept = kept + beside.astype(F32)
    for mask in layout_masks()[2:]:
        half = kept.shape[0] // 2
        other = swap(kept[half:].astype(BF16), "dp", mask)
        kept = kept[:half] + other.astype(F32)
    return kept


def reversed_bits(block):
    masks = layout_masks()
    flipped = jnp.zeros_like(block)
    for rank, mask in enumerate(masks):
        flipped = flipped + ((block >> (len(masks) - 1 - rank)) & 1) * mask
    return flipped


def order_matrix(width, dtype):
    chunk = width // lax.axis_size("dp")
    place = lax.broadcasted_iota(jnp.int32, (width, width), 1)
    source = lax.broadcasted_iota(jnp.int32, (width, width), 0)
    entry = (lax.axis_index("dp") ^ reversed_bits(place // chunk)) * chunk + place % chunk
    return (source == entry).astype(dtype)


def reorder(values, matrix, precision=None):
    return jnp.dot(
        values, matrix.astype(values.dtype), precision=precision, preferred_element_type=F32
    ).astype(values.dtype)


def restore(values, matrix, precision=None):
    return lax.dot_general(
        values,
        matrix.astype(values.dtype),
        (((1,), (1,)), ((), ())),
        precision=precision,
        preferred_element_type=F32,
    ).astype(values.dtype)


def total(values):
    for mask in layout_masks()[::-1]:
        values = values + swap(values, "dp", mask)
    if lax.axis_size("tp") == 2:
        return values + swap(values, "tp", 1)
    return lax.psum(values, "tp")


def gather_rows(values):
    if lax.axis_size("tp") == 2:
        return jnp.concatenate([values, swap(values, "tp", 1)], axis=0)
    return lax.all_gather(values, "tp", axis=0, tiled=True)


def row_places(own_rows):
    if lax.axis_size("tp") == 2:
        own = jnp.arange(own_rows, dtype=jnp.int32)
        index = lax.axis_index("tp")
        return jnp.concatenate([own + index * own_rows, own + (1 - index) * own_rows])
    return jnp.arange(own_rows * lax.axis_size("tp"), dtype=jnp.int32)


def back_kernel(count, flipped, *refs):
    lefts = refs[:count]
    weights = refs[count : 5 * count]
    out_ref, total_ref = refs[5 * count :]
    step = pl.program_id(0)
    width = weights[0].shape[0]
    for part in range(4):
        value = None
        for one in range(count):
            term = lax.dot_general(
                lefts[one][...],
                weights[4 * one + part][...],
                (((0 if flipped else 1,), (1,)), ((), ())),
                preferred_element_type=F32,
            )
            value = term if value is None else value + term
        columns = slice(part * width, (part + 1) * width)

        @pl.when(step == 0)
        def _():
            total_ref[:, columns] = value

        @pl.when(step > 0)
        def _():
            total_ref[:, columns] += value

    @pl.when(step == pl.num_programs(0) - 1)
    def _():
        out_ref[...] = total_ref[...].astype(out_ref.dtype)


def project_back(lefts, weights, half, halves, out_dtype, flipped=False):
    inner = weights[0][0].shape[1]
    rows = lefts[0].shape[1 if flipped else 0] // halves
    width = weights[0][0].shape[0]
    steps = 3 if inner % 384 == 0 else 1
    block = inner // steps
    if flipped:
        left_spec = pl.BlockSpec((block, rows), lambda k: (k, half))
    else:
        left_spec = pl.BlockSpec((rows, block), lambda k: (half, k))
    flat = [quarter for quarters in weights for quarter in quarters]
    return pl.pallas_call(
        functools.partial(back_kernel, len(lefts), flipped),
        grid=(steps,),
        in_specs=[left_spec] * len(lefts)
        + [pl.BlockSpec((width, block), lambda k: (0, k))] * len(flat),
        out_specs=pl.BlockSpec((rows, 4 * width), lambda k: (0, 0)),
        out_shape=jax.ShapeDtypeStruct((rows, 4 * width), out_dtype),
        scratch_shapes=[pltpu.VMEM((rows, 4 * width), F32)],
        compiler_params=pltpu.CompilerParams(vmem_limit_bytes=VMEM_BYTES),
        cost_estimate=pl.CostEstimate(
            flops=8 * rows * width * inner * len(lefts),
            bytes_accessed=8 * width * inner * len(lefts),
            transcendentals=0,
        ),
    )(*lefts, *flat)


def sum_rows(lefts, weights, flipped=False):
    if lax.axis_size("tp") == 2:
        sent = project_back(lefts, weights, 1, 2, BF16, flipped)
        other = swap(sent, "tp", 1)
        return project_back(lefts, weights, 0, 2, F32, flipped) + other.astype(F32)
    both = 0.0
    for left, quarters in zip(lefts, weights):
        both = both + lax.dot_general(
            left,
            jnp.concatenate(quarters, axis=0),
            (((0 if flipped else 1,), (1,)), ((), ())),
            preferred_element_type=F32,
        )
    return lax.psum_scatter(both.astype(BF16), "tp", scatter_dimension=0, tiled=True).astype(F32)


def head_normed(raw, gain, cosine, sine):
    inverse = lax.rsqrt(jnp.mean(raw * raw, axis=0, keepdims=True) + EPSILON)
    normed = raw * inverse * gain
    half = raw.shape[0] // 2
    first, second = normed[:half], normed[half:]
    return jnp.concatenate(
        [first * cosine - second * sine, second * cosine + first * sine], axis=0
    )


def weighted_columns(weights, rows_ref, target_ref):
    width = weights[0].shape[0]
    value = None
    for part in range(4):
        term = lax.dot_general(
            weights[part][...],
            rows_ref[:, part * width : (part + 1) * width],
            (((0,), (1,)), ((), ())),
            preferred_element_type=F32,
        )
        value = term if value is None else value + term
    target_ref[...] = value.astype(target_ref.dtype)


def attend_kernel(
    groups,
    repeat,
    w0,
    w1,
    w2,
    w3,
    rows_ref,
    cos_ref,
    sin_ref,
    q_gain_ref,
    k_gain_ref,
    place_ref,
    first_ref,
    place_col_ref,
    raw_ref,
    q_ref,
    k_ref,
    v_ref,
    log_ref,
    out_ref,
    bias_ref,
):
    weighted_columns((w0, w1, w2, w3), rows_ref, raw_ref)
    places = place_col_ref[...]
    allowed = (places <= place_ref[...]) & (places >= first_ref[...])
    bias_ref[...] = jnp.where(allowed, 0.0, -1e30)
    cosine, sine = cos_ref[...], sin_ref[...]
    heads = groups * repeat

    def group_step(group, carry):
        k_row = pl.multiple_of(group * HD, HD)
        keys = head_normed(
            raw_ref[pl.ds(heads * HD + k_row, HD), :], k_gain_ref[...], cosine, sine
        ).astype(BF16)
        values = raw_ref[pl.ds((heads + groups) * HD + k_row, HD), :].astype(BF16)
        k_ref[pl.ds(k_row, HD), :] = keys
        v_ref[pl.ds(k_row, HD), :] = values
        for one in range(repeat):
            q_row = pl.multiple_of((group * repeat + one) * HD, HD)
            queries = head_normed(
                raw_ref[pl.ds(q_row, HD), :], q_gain_ref[...], cosine, sine
            ).astype(BF16)
            queries = queries * jnp.asarray(HD ** (-0.5), BF16)
            q_ref[pl.ds(q_row, HD), :] = queries
            scores = (
                lax.dot_general(
                    keys, queries, (((0,), (0,)), ((), ())), preferred_element_type=F32
                )
                + bias_ref[...]
            )
            peaks = jnp.max(scores, axis=0, keepdims=True)
            shifted = jnp.exp(scores - peaks)
            totals = jnp.sum(shifted, axis=0, keepdims=True)
            outputs = jnp.dot(values, shifted.astype(BF16), preferred_element_type=F32)
            out_ref[pl.ds(q_row, HD), :] = (outputs / totals).astype(BF16)
            log_ref[group * repeat + one] = peaks + jnp.log(totals)
        return carry

    lax.fori_loop(0, groups, group_step, 0)


def attend_rows(weights, rows, tables, groups, repeat):
    row_len = rows.shape[0]
    heads = groups * repeat
    columns = weights[0].shape[1]
    shapes = [
        jax.ShapeDtypeStruct((columns, row_len), F32),
        jax.ShapeDtypeStruct((heads * HD, row_len), BF16),
        jax.ShapeDtypeStruct((groups * HD, row_len), BF16),
        jax.ShapeDtypeStruct((groups * HD, row_len), BF16),
        jax.ShapeDtypeStruct((heads, 1, row_len), F32),
        jax.ShapeDtypeStruct((heads * HD, row_len), BF16),
    ]
    return pl.pallas_call(
        functools.partial(attend_kernel, groups, repeat),
        out_shape=shapes,
        scratch_shapes=[pltpu.VMEM((row_len, row_len), F32)],
        compiler_params=pltpu.CompilerParams(vmem_limit_bytes=VMEM_BYTES),
        cost_estimate=pl.CostEstimate(
            flops=12_000_000_000, bytes_accessed=4_000_000, transcendentals=2_000_000
        ),
    )(*weights, rows, *tables)


def head_back(raw, gain, grad_rot, cosine, sine):
    half = raw.shape[0] // 2
    first, second = grad_rot[:half], grad_rot[half:]
    grad = jnp.concatenate(
        [first * cosine + second * sine, second * cosine - first * sine], axis=0
    )
    inverse = lax.rsqrt(jnp.mean(raw * raw, axis=0, keepdims=True) + EPSILON)
    hat = raw * inverse
    terms = grad * hat
    grad_hat = grad * gain
    inner = jnp.mean(terms * gain, axis=0, keepdims=True)
    return inverse * (grad_hat - hat * inner), terms


def attend_back_kernel(
    groups,
    repeat,
    w0,
    w1,
    w2,
    w3,
    rows_ref,
    cos_ref,
    sin_ref,
    q_gain_ref,
    k_gain_ref,
    place_ref,
    first_ref,
    place_col_ref,
    raw_ref,
    q_ref,
    k_ref,
    v_ref,
    log_ref,
    grad_ref,
    q_part_ref,
    k_part_ref,
    bias_ref,
    outer_ref,
    q_terms_ref,
    k_terms_ref,
):
    weighted_columns((w0, w1, w2, w3), rows_ref, outer_ref)
    places = place_col_ref[...]
    allowed = (places <= place_ref[...]) & (places >= first_ref[...])
    bias_ref[...] = jnp.where(allowed, 0.0, -1e30)
    cosine, sine = cos_ref[...], sin_ref[...]
    heads = groups * repeat
    q_terms_ref[...] = jnp.zeros_like(q_terms_ref)
    k_terms_ref[...] = jnp.zeros_like(k_terms_ref)

    def group_step(group, carry):
        k_row = pl.multiple_of(group * HD, HD)
        keys = k_ref[pl.ds(k_row, HD), :]
        values = v_ref[pl.ds(k_row, HD), :]
        grad_keys = None
        for one in range(repeat):
            q_row = pl.multiple_of((group * repeat + one) * HD, HD)
            queries = q_ref[pl.ds(q_row, HD), :]
            outer = outer_ref[pl.ds(q_row, HD), :]
            scores = (
                lax.dot_general(
                    keys, queries, (((0,), (0,)), ((), ())), preferred_element_type=F32
                )
                + bias_ref[...]
            )
            attn_probs = jnp.exp(scores - log_ref[group * repeat + one])
            grad_probs = lax.dot_general(
                values, outer, (((0,), (0,)), ((), ())), preferred_element_type=F32
            )
            inner = jnp.sum(attn_probs * grad_probs, axis=0, keepdims=True)
            grad_scores = (attn_probs * (grad_probs - inner)).astype(BF16)
            grad_query = jnp.dot(keys, grad_scores, preferred_element_type=F32) * (HD ** (-0.5))
            grad_key = lax.dot_general(
                queries, grad_scores, (((1,), (1,)), ((), ())), preferred_element_type=F32
            )
            grad_value = lax.dot_general(
                outer,
                attn_probs.astype(BF16),
                (((1,), (1,)), ((), ())),
                preferred_element_type=F32,
            )
            grad_raw, terms = head_back(
                raw_ref[pl.ds(q_row, HD), :], q_gain_ref[...], grad_query, cosine, sine
            )
            grad_ref[pl.ds(q_row, HD), :] = grad_raw.astype(BF16)
            q_terms_ref[...] += terms
            if grad_keys is None:
                grad_keys, grad_values = grad_key, grad_value
            else:
                grad_keys, grad_values = grad_keys + grad_key, grad_values + grad_value
        grad_raw, terms = head_back(
            raw_ref[pl.ds(heads * HD + k_row, HD), :], k_gain_ref[...], grad_keys, cosine, sine
        )
        k_terms_ref[...] += terms
        grad_ref[pl.ds(heads * HD + k_row, HD), :] = grad_raw.astype(BF16)
        grad_ref[pl.ds((heads + groups) * HD + k_row, HD), :] = grad_values.astype(BF16)
        return carry

    lax.fori_loop(0, groups, group_step, 0)
    q_part_ref[...] = jnp.sum(q_terms_ref[...], axis=1, keepdims=True)
    k_part_ref[...] = jnp.sum(k_terms_ref[...], axis=1, keepdims=True)


def attend_rows_back(weights, rows, tables, kept, groups, repeat):
    row_len = rows.shape[0]
    heads = groups * repeat
    columns = (heads + 2 * groups) * HD
    shapes = [
        jax.ShapeDtypeStruct((columns, row_len), BF16),
        jax.ShapeDtypeStruct((HD, 1), F32),
        jax.ShapeDtypeStruct((HD, 1), F32),
    ]
    return pl.pallas_call(
        functools.partial(attend_back_kernel, groups, repeat),
        out_shape=shapes,
        scratch_shapes=[
            pltpu.VMEM((row_len, row_len), F32),
            pltpu.VMEM((heads * HD, row_len), BF16),
            pltpu.VMEM((HD, row_len), F32),
            pltpu.VMEM((HD, row_len), F32),
        ],
        compiler_params=pltpu.CompilerParams(vmem_limit_bytes=VMEM_BYTES),
        cost_estimate=pl.CostEstimate(
            flops=15_000_000_000, bytes_accessed=4_000_000, transcendentals=2_000_000
        ),
    )(*weights, rows, *tables, *kept)


def hidden_kernel(*refs):
    weights = refs[:12]
    rows_ref, cot_ref, act_ref, gate_grad_ref, up_grad_ref = refs[12:]
    width = weights[0].shape[0]

    def summed(source_ref, quarters):
        value = None
        for part in range(4):
            term = jnp.dot(
                source_ref[:, part * width : (part + 1) * width],
                quarters[part][...],
                preferred_element_type=F32,
            )
            value = term if value is None else value + term
        return value

    gate = summed(rows_ref, weights[0:4])
    up = summed(rows_ref, weights[4:8])
    grad_act = summed(cot_ref, weights[8:12])
    sigmoid_gate = jax.nn.sigmoid(gate)
    silu = gate * sigmoid_gate
    act_ref[...] = (silu * up).astype(BF16)
    up_grad_ref[...] = (grad_act * silu).astype(BF16)
    gate_grad_ref[...] = (
        grad_act * up * sigmoid_gate * (1.0 + gate * (1.0 - sigmoid_gate))
    ).astype(BF16)


def hidden_rows(gate_w, up_w, down_w, rows, cot_rows):
    row_len, width = rows.shape
    columns = gate_w[0].shape[1]
    block = 256 if columns % 256 == 0 else columns
    whole = pl.BlockSpec((row_len, width), lambda k: (0, 0))
    return pl.pallas_call(
        hidden_kernel,
        grid=(columns // block,),
        in_specs=[pl.BlockSpec((width // 4, block), lambda k: (0, k))] * 12 + [whole] * 2,
        out_specs=[pl.BlockSpec((row_len, block), lambda k: (0, k))] * 3,
        out_shape=[jax.ShapeDtypeStruct((row_len, columns), BF16)] * 3,
        compiler_params=pltpu.CompilerParams(vmem_limit_bytes=VMEM_BYTES),
        cost_estimate=pl.CostEstimate(
            flops=6 * row_len * width * columns,
            bytes_accessed=6 * width * columns + 6 * row_len * columns,
            transcendentals=row_len * columns,
        ),
    )(*gate_w, *up_w, *down_w, rows, cot_rows)


def masked_scores(query_block, key_rows, block_segment, block_places, segment, places, score_scale):
    scores = (
        jnp.einsum("qgrd,kgd->grqk", query_block, key_rows, preferred_element_type=jnp.float32)
        * score_scale
    )
    allowed = (places[None, :] <= block_places[:, None]) & (
        segment[None, :] == block_segment[:, None]
    )
    return jnp.where(allowed, scores, -1e30)


def attend(query_rows, key_rows, value_rows, segment, places, block_rows):
    row_len = query_rows.shape[0]
    blocks = row_len // block_rows
    score_scale = query_rows.shape[-1] ** (-0.5)

    def block_out(block_item):
        query_block, block_segment, block_places = block_item
        scores = masked_scores(
            query_block, key_rows, block_segment, block_places, segment, places, score_scale
        )
        peaks = jnp.max(scores, axis=-1, keepdims=True)
        shifted = jnp.exp(scores - peaks)
        totals = jnp.sum(shifted, axis=-1, keepdims=True)
        attn_probs = (shifted / totals).astype(jnp.bfloat16)
        outputs = jnp.einsum(
            "grqk,kgd->qgrd", attn_probs, value_rows, preferred_element_type=jnp.float32
        )
        return (outputs, (peaks + jnp.log(totals))[..., 0])

    outputs, log_totals = lax.map(
        block_out,
        (
            query_rows.reshape((blocks, block_rows) + query_rows.shape[1:]),
            segment.reshape(blocks, block_rows),
            places.reshape(blocks, block_rows),
        ),
    )
    return (outputs.reshape(query_rows.shape), log_totals)


def attend_back(
    query_rows, key_rows, value_rows, grad_out, log_totals, segment, places, block_rows
):
    row_len = query_rows.shape[0]
    blocks = row_len // block_rows
    score_scale = query_rows.shape[-1] ** (-0.5)

    def block_back(carry, block_item):
        grad_keys, grad_values = carry
        query_block, grad_block, total_block, block_segment, block_places = block_item
        scores = masked_scores(
            query_block, key_rows, block_segment, block_places, segment, places, score_scale
        )
        attn_probs = jnp.exp(scores - total_block[..., None])
        grad_probs = jnp.einsum(
            "qgrd,kgd->grqk", grad_block, value_rows, preferred_element_type=jnp.float32
        )
        inner = jnp.sum(attn_probs * grad_probs, axis=-1, keepdims=True)
        grad_scores = (attn_probs * (grad_probs - inner)).astype(jnp.bfloat16)
        grad_query = (
            jnp.einsum("grqk,kgd->qgrd", grad_scores, key_rows, preferred_element_type=jnp.float32)
            * score_scale
        )
        grad_keys = (
            grad_keys
            + jnp.einsum(
                "grqk,qgrd->kgd", grad_scores, query_block, preferred_element_type=jnp.float32
            )
            * score_scale
        )
        grad_values = grad_values + jnp.einsum(
            "grqk,qgrd->kgd",
            attn_probs.astype(jnp.bfloat16),
            grad_block,
            preferred_element_type=jnp.float32,
        )
        return ((grad_keys, grad_values), grad_query)

    zeros_kv = jnp.zeros(key_rows.shape, jnp.float32)
    block_shape = (blocks, block_rows) + query_rows.shape[1:]
    (grad_keys, grad_values), grad_queries = lax.scan(
        block_back,
        (zeros_kv, zeros_kv),
        (
            query_rows.reshape(block_shape),
            grad_out.reshape(block_shape),
            log_totals,
            segment.reshape(blocks, block_rows),
            places.reshape(blocks, block_rows),
        ),
    )
    return (grad_queries.reshape(query_rows.shape), grad_keys, grad_values)


def attention_small(qkv_w, rows_first, tables, groups, repeat):
    raw, queries, keys, values, logs, attended = attend_rows(
        qkv_w, rows_first, tables, groups, repeat
    )

    def back(out_w, branch_rows):
        grads, q_part, k_part = attend_rows_back(
            out_w, branch_rows, tables, (raw, queries, keys, values, logs), groups, repeat
        )
        return grads, q_part[:, 0], k_part[:, 0]

    return attended, back


def attention_large(qkv_w, rows_first, doc_tables, q_gain, k_gain, groups, repeat):
    segment, places, cosine, sine = doc_tables
    row_len = rows_first.shape[0]
    query_cols, key_cols = groups * repeat * HD, groups * HD
    block_rows = min(512, row_len)
    projected = jnp.dot(rows_first, jnp.concatenate(qkv_w, axis=0), preferred_element_type=F32)
    query_raw = projected[:, :query_cols].reshape(row_len, groups, repeat, HD)
    key_raw = projected[:, query_cols : query_cols + key_cols].reshape(row_len, groups, HD)
    value_rows = projected[:, query_cols + key_cols :].astype(BF16).reshape(row_len, groups, HD)
    query_normed, query_hat, query_inv = norm_forward(query_raw, q_gain)
    key_normed, key_hat, key_inv = norm_forward(key_raw, k_gain)
    query_rows = rotate(query_normed, cosine, sine).astype(BF16)
    key_rows = rotate(key_normed, cosine, sine).astype(BF16)
    attended, log_totals = attend(query_rows, key_rows, value_rows, segment, places, block_rows)

    def back(out_w, branch_rows):
        grad_attended = jnp.dot(
            branch_rows, jnp.concatenate(out_w, axis=0), preferred_element_type=F32
        ).astype(BF16)
        grad_query_rot, grad_key_rot, grad_value = attend_back(
            query_rows,
            key_rows,
            value_rows,
            grad_attended.reshape(row_len, groups, repeat, HD),
            log_totals,
            segment,
            places,
            block_rows,
        )
        grad_query_norm = rotate(grad_query_rot, cosine, -sine)
        grad_key_norm = rotate(grad_key_rot, cosine, -sine)
        grad_query_raw, q_part = norm_backward(grad_query_norm, query_hat, query_inv, q_gain)
        grad_key_raw, k_part = norm_backward(grad_key_norm, key_hat, key_inv, k_gain)
        grads = jnp.concatenate(
            [
                grad_query_raw.reshape(row_len, query_cols),
                grad_key_raw.reshape(row_len, key_cols),
                grad_value.reshape(row_len, key_cols),
            ],
            axis=1,
        )
        return grads.astype(BF16).T, q_part, k_part

    return attended.reshape(row_len, query_cols).astype(BF16).T, back


def hidden_large(gate_w, up_w, down_w, rows, cot_rows):
    gate = jnp.dot(rows, jnp.concatenate(gate_w, axis=0), preferred_element_type=F32)
    up = jnp.dot(rows, jnp.concatenate(up_w, axis=0), preferred_element_type=F32)
    grad_act = jnp.dot(cot_rows, jnp.concatenate(down_w, axis=0), preferred_element_type=F32)
    sigmoid_gate = jax.nn.sigmoid(gate)
    silu = gate * sigmoid_gate
    grad_gate = grad_act * up * sigmoid_gate * (1.0 + gate * (1.0 - sigmoid_gate))
    return (silu * up).astype(BF16), grad_gate.astype(BF16), (grad_act * silu).astype(BF16)


def local(
    tokens,
    doc_starts,
    attn_gain,
    w_query,
    w_key,
    w_value,
    q_gain,
    k_gain,
    w_out,
    mlp_gain,
    w_gate,
    w_up,
    w_down,
    out_grad,
):
    width = tokens.shape[-1]
    own_rows = tokens.shape[1]
    row_len = own_rows * lax.axis_size("tp")
    small = lax.axis_size("tp") == 2 and row_len <= 512
    groups = w_key.shape[1] // HD
    repeat = w_query.shape[1] // w_key.shape[1]
    query_cols = w_query.shape[1]
    key_cols = w_key.shape[1]
    highest = lax.Precision.HIGHEST

    qkv_w = gather_weight(jnp.concatenate([w_query, w_key, w_value], axis=1))
    out_w = gather_weight(w_out)
    gate_w = gather_weight(w_gate)
    up_w = gather_weight(w_up)
    down_w = gather_weight(w_down)

    matrix = order_matrix(width, BF16)
    gains = reorder(jnp.stack([attn_gain, mlp_gain]), matrix, highest)
    attn_gain, mlp_gain = gains[0], gains[1]
    inputs = reorder(tokens[0], matrix).astype(F32)
    cotangent = reorder(out_grad[0], matrix)
    places = row_places(own_rows)
    segment, position = documents(doc_starts[0], places)
    cosine, sine = rope_tables(position, HD)

    normed_first, hat_first, inv_first = norm_forward(inputs, attn_gain)
    rows_first = gather_rows(normed_first.astype(BF16))
    if small:
        tables = (
            cosine.T,
            sine.T,
            q_gain[:, None],
            k_gain[:, None],
            places[None, :],
            (places - position)[None, :],
            places[:, None],
        )
        attended, attention_back = attention_small(qkv_w, rows_first, tables, groups, repeat)
    else:
        doc_tables = (segment, places, cosine, sine)
        attended, attention_back = attention_large(
            qkv_w, rows_first, doc_tables, q_gain, k_gain, groups, repeat
        )
    hidden = inputs + sum_rows([attended], [out_w], flipped=True)
    normed_second, hat_second, inv_second = norm_forward(hidden, mlp_gain)
    rows_second = gather_rows(normed_second.astype(BF16))
    cot_rows = gather_rows(cotangent)
    hidden_step = hidden_rows if small else hidden_large
    activated, grad_gate, grad_up = hidden_step(gate_w, up_w, down_w, rows_second, cot_rows)
    grad_normed_second = sum_rows([grad_gate, grad_up], [gate_w, up_w])
    down_grad = weight_grad(cot_rows, activated)
    gate_grad = weight_grad(rows_second, grad_gate)
    up_grad = weight_grad(rows_second, grad_up)
    result = hidden + sum_rows([activated], [down_w])
    grad_hidden_norm, mlp_gain_part = norm_backward(
        grad_normed_second, hat_second, inv_second, mlp_gain
    )
    grad_hidden = cotangent.astype(F32) + grad_hidden_norm
    branch_rows = gather_rows(grad_hidden.astype(BF16))
    grad_projected, q_gain_part, k_gain_part = attention_back(out_w, branch_rows)
    grad_normed_first = sum_rows([grad_projected], [qkv_w], flipped=True)
    out_w_grad = weight_grad(branch_rows, attended, flipped=True)
    qkv_grad = weight_grad(rows_first, grad_projected, flipped=True)
    grad_input_norm, attn_gain_part = norm_backward(
        grad_normed_first, hat_first, inv_first, attn_gain
    )
    grad_inputs = grad_hidden + grad_input_norm
    parts = restore(jnp.stack([attn_gain_part, mlp_gain_part]), matrix, highest)
    parts = total(jnp.concatenate([parts[0], parts[1], q_gain_part, k_gain_part]))
    return (
        restore(result.astype(BF16), matrix)[None],
        restore(grad_inputs.astype(BF16), matrix)[None],
        parts[:width],
        qkv_grad[:, :query_cols],
        qkv_grad[:, query_cols : query_cols + key_cols],
        qkv_grad[:, query_cols + key_cols :],
        parts[2 * width : 2 * width + HD],
        parts[2 * width + HD :],
        out_w_grad,
        parts[width : 2 * width],
        gate_grad,
        up_grad,
        down_grad,
    )


def solution(mesh):
    in_specs = (
        P("dp", "tp", None),
        P("dp", None),
        P(),
        P("dp", "tp"),
        P("dp", "tp"),
        P("dp", "tp"),
        P(),
        P(),
        P("dp", "tp"),
        P(),
        P("dp", "tp"),
        P("dp", "tp"),
        P("dp", "tp"),
        P("dp", "tp", None),
    )
    out_specs = (
        P("dp", "tp", None),
        P("dp", "tp", None),
        P(),
        P("dp", "tp"),
        P("dp", "tp"),
        P("dp", "tp"),
        P(),
        P(),
        P("dp", "tp"),
        P(),
        P("dp", "tp"),
        P("dp", "tp"),
        P("dp", "tp"),
    )
    return jax.shard_map(local, mesh=mesh, in_specs=in_specs, out_specs=out_specs, check_vma=False)
```

```python
import functools

import jax
import jax.numpy as jnp
from jax import lax
from jax.experimental import pallas as pl
from jax.experimental.pallas import tpu as pltpu
from jax.sharding import PartitionSpec as P

HD = 64


EPSILON = 1e-05
THETA = 1000000.0


def documents(starts, places):
    inside = places[:, None] >= starts[None, :]
    segment = jnp.sum(inside.astype(jnp.int32), axis=1) - 1
    firsts = jnp.max(jnp.where(inside, starts[None, :], 0), axis=1)
    return (segment, places - firsts)


def rope_tables(position, width):
    half_width = width // 2
    freqs = THETA ** (-(jnp.arange(half_width, dtype=jnp.float32) * 2.0 / width))
    angles = position.astype(jnp.float32)[:, None] * freqs[None, :]
    return (jnp.cos(angles), jnp.sin(angles))


def rotate(values, cosine, sine):
    half_width = values.shape[-1] // 2
    first_half = values[..., :half_width]
    second_half = values[..., half_width:]
    tile_shape = (values.shape[0],) + (1,) * (values.ndim - 2) + (half_width,)
    cos_tile = cosine.reshape(tile_shape)
    sin_tile = sine.reshape(tile_shape)
    return jnp.concatenate(
        [
            first_half * cos_tile - second_half * sin_tile,
            second_half * cos_tile + first_half * sin_tile,
        ],
        axis=-1,
    )


def norm_forward(values, gain):
    inverse = lax.rsqrt(jnp.mean(values * values, axis=-1, keepdims=True) + EPSILON)
    normed_hat = values * inverse
    return (normed_hat * gain, normed_hat, inverse)


def norm_backward(grad_normed, normed_hat, inverse, gain):
    grad_hat = grad_normed * gain
    grad_values = inverse * (
        grad_hat - normed_hat * jnp.mean(grad_hat * normed_hat, axis=-1, keepdims=True)
    )
    gain_part = jnp.sum((grad_normed * normed_hat).reshape(-1, normed_hat.shape[-1]), axis=0)
    return (grad_values, gain_part)


F32 = jnp.float32
BF16 = jnp.bfloat16
VMEM_BYTES = 40 * 1024 * 1024
LIGHT = pl.CostEstimate(flops=1000, bytes_accessed=1000, transcendentals=0)
CHUNKS = 3


def partners(size, mask):
    return [(own, own ^ mask) for own in range(size)]


def swap(values, axis_name, mask):
    return lax.ppermute(values, axis_name, partners(lax.axis_size(axis_name), mask))


def layout_masks():
    size = lax.axis_size("dp")
    masks = []
    mask = 1
    while mask < size:
        masks.append(mask)
        mask *= 2
    return masks


def tied(values, *others):
    return lax.optimization_barrier((values, *others))[0]


def pack_kernel(counts, *refs):
    ins = refs[: counts[0]]
    outs = refs[counts[0] :]
    for out_ref, spans in zip(outs, counts[1]):
        place = 0
        for source, start, stop in spans:
            out_ref[:, place : place + stop - start] = ins[source][:, start:stop]
            place += stop - start


def pack(shards, plans):
    if any(stop % 128 or start % 128 for plan in plans for _, start, stop in plan):
        return [
            jnp.concatenate([shards[source][:, start:stop] for source, start, stop in plan], axis=1)
            for plan in plans
        ]
    rows = shards[0].shape[0]
    return pl.pallas_call(
        functools.partial(pack_kernel, (len(shards), plans)),
        out_shape=[
            jax.ShapeDtypeStruct((rows, sum(stop - start for _, start, stop in plan)), BF16)
            for plan in plans
        ],
        compiler_params=pltpu.CompilerParams(vmem_limit_bytes=VMEM_BYTES),
        cost_estimate=LIGHT,
    )(*shards)


class Lane:
    def __init__(self, window, arrivals):
        self.window = window
        self.arrivals = arrivals
        self.arrived = []

    def swap(self, values, axis_name, mask, after=()):
        waits = list(after)
        if len(self.arrived) >= self.window:
            waits.append(self.arrived[-self.window])
        if waits:
            values = tied(values, *waits)
        other = swap(values, axis_name, mask)
        self.arrived.append(other)
        if self.arrivals:
            other = tied(other, self.arrivals[-1])
        self.arrivals.append(other)
        return other


class Order:
    def __init__(self):
        self.last = None

    def extra(self):
        return [] if self.last is None else [self.last]

    def __call__(self, *values):
        out = lax.optimization_barrier((*values, *self.extra()))[: len(values)]
        return out if len(out) > 1 else out[0]

    def done(self, value):
        self.last = value
        return value


class Gather:
    def __init__(self, shard, lanes):
        self.near = shard
        self.lanes = lanes

    def far(self, mask, after=()):
        other = self.lanes["z"].swap(self.near, "dp", mask, after)
        self.near = jnp.concatenate([self.near, other], axis=0)

    def last_far(self, mask, after=()):
        self.next = self.lanes["z"].swap(self.near, "dp", mask, after)

    def beside(self):
        self.across = self.lanes["y"].swap(self.near, "dp", 2)

    def beside_next(self, after=()):
        self.last = self.lanes["y"].swap(self.next, "dp", 2, after)

    def join(self, after=()):
        last = tied(self.last, *after) if after else self.last
        self.own = jnp.concatenate([self.near, self.next, self.across, last], axis=0)

    def core(self, after=()):
        self.halves = [self.own, self.lanes["core"].swap(self.own, "dp", 1, after)]


class Scatter:
    def __init__(self, pairs, lanes, order, flipped=False):
        self.pairs, self.flipped = pairs, flipped
        self.lanes, self.order = lanes, order

    def inputs(self):
        flat = self.order(*[one for pair in self.pairs for one in pair])
        return [(flat[2 * k], flat[2 * k + 1]) for k in range(len(self.pairs))]

    def core(self):
        sent = self.order.done(grad_half(self.inputs(), 1, None, self.flipped)[0])
        self.other = self.lanes["core"].swap(sent, "dp", 1)

    def beside(self):
        self.own, near = grad_half(self.inputs(), 0, self.other, self.flipped)
        self.order.done(near)
        self.across = self.lanes["y"].swap(near, "dp", 2)

    def meet(self):
        self.kept = self.own + self.order(self.across).astype(F32)

    def far(self, mask):
        half = self.kept.shape[0] // 2
        sent = self.order.done(self.order(self.kept[half:]).astype(BF16))
        self.kept = self.kept[:half]
        self.next = self.lanes["z"].swap(sent, "dp", mask)

    def far_meet(self):
        self.kept = self.kept + self.order(self.next).astype(F32)


def grad_kernel(count, flipped, added, *refs):
    lefts, rights = refs[:count], refs[count : 2 * count]
    outs = refs[2 * count + (1 if added else 0) :]
    step = pl.program_id(0)
    for one in range(count):

        @pl.when(step == one)
        def _(one=one):
            value = lax.dot_general(
                lefts[one][...],
                rights[one][...],
                (((0,), (1 if flipped else 0,)), ((), ())),
                preferred_element_type=F32,
            )
            if added:
                value = value + refs[2 * count][...].astype(F32)
            rows = value.shape[0] // len(outs)
            for place, out_ref in enumerate(outs):
                out_ref[...] = value[place * rows : (place + 1) * rows].astype(out_ref.dtype)


def grad_half(pairs, side, added, flipped):
    count = len(pairs)
    row_len, width = pairs[0][0].shape
    half = width // 2
    columns = pairs[0][1].shape[0 if flipped else 1]
    arrays = [left for left, _ in pairs] + [right for _, right in pairs]
    specs = [pl.BlockSpec((row_len, half), lambda k: (0, side))] * count
    specs += [pl.BlockSpec(right.shape, lambda k: (0, 0)) for _, right in pairs]
    if columns % 128:
        values = []
        for left, right in pairs:
            dims = (((0,), (1 if flipped else 0,)), ((), ()))
            left = left[:, side * half : (side + 1) * half]
            values.append(lax.dot_general(left, right, dims, preferred_element_type=F32))
        value = jnp.concatenate(values, axis=1)
        if added is None:
            return [value.astype(BF16)]
        value = value + added.astype(F32)
        return [value[: half // 2], value[half // 2 :].astype(BF16)]
    if added is None:
        types = [BF16]
    else:
        arrays.append(added)
        specs.append(pl.BlockSpec((half, columns), lambda k: (0, k)))
        types = [F32, BF16]
    rows = half // len(types)
    return pl.pallas_call(
        functools.partial(grad_kernel, count, flipped, added is not None),
        grid=(count,),
        in_specs=specs,
        out_specs=[pl.BlockSpec((rows, columns), lambda k: (0, k))] * len(types),
        out_shape=[jax.ShapeDtypeStruct((rows, count * columns), kind) for kind in types],
        compiler_params=pltpu.CompilerParams(vmem_limit_bytes=VMEM_BYTES),
        cost_estimate=LIGHT,
    )(*arrays)


def reversed_bits(block):
    masks = layout_masks()
    flipped = jnp.zeros_like(block)
    for rank, mask in enumerate(masks):
        flipped = flipped + ((block >> (len(masks) - 1 - rank)) & 1) * mask
    return flipped


def order_matrix(width, dtype):
    chunk = width // lax.axis_size("dp")
    place = lax.broadcasted_iota(jnp.int32, (width, width), 1)
    source = lax.broadcasted_iota(jnp.int32, (width, width), 0)
    entry = (lax.axis_index("dp") ^ reversed_bits(place // chunk)) * chunk + place % chunk
    return (source == entry).astype(dtype)


def thirds(values):
    high = values.astype(BF16)
    rest = values - high.astype(F32)
    middle = rest.astype(BF16)
    return jnp.concatenate([high, middle, (rest - middle.astype(F32)).astype(BF16)], axis=0)


def reorder(values, matrix):
    if values.dtype == F32:
        rows = values.shape[0]
        value = jnp.dot(thirds(values), matrix, preferred_element_type=F32)
        return value[:rows] + value[rows : 2 * rows] + value[2 * rows :]
    return jnp.dot(values, matrix, preferred_element_type=F32).astype(values.dtype)


def restore(values, matrix):
    dims = (((1,), (1,)), ((), ()))
    if values.dtype == F32:
        rows = values.shape[0]
        value = lax.dot_general(thirds(values), matrix, dims, preferred_element_type=F32)
        return value[:rows] + value[rows : 2 * rows] + value[2 * rows :]
    return lax.dot_general(values, matrix, dims, preferred_element_type=F32).astype(values.dtype)


def total(values):
    for mask in layout_masks()[::-1]:
        values = values + swap(values, "dp", mask)
    if lax.axis_size("tp") == 2:
        return values + swap(values, "tp", 1)
    return lax.psum(values, "tp")


def gather_rows(values, lane):
    if lax.axis_size("tp") == 2:
        return jnp.concatenate([values, lane.swap(values, "tp", 1)], axis=0)
    return lax.all_gather(values, "tp", axis=0, tiled=True)


def row_places(own_rows):
    if lax.axis_size("tp") == 2:
        own = jnp.arange(own_rows, dtype=jnp.int32)
        index = lax.axis_index("tp")
        return jnp.concatenate([own + index * own_rows, own + (1 - index) * own_rows])
    return jnp.arange(own_rows * lax.axis_size("tp"), dtype=jnp.int32)


def back_kernel(count, flipped, *refs):
    lefts, weights = refs[:count], refs[count : 3 * count]
    kept_ref, sent_ref = refs[3 * count :]
    rows = kept_ref.shape[0]
    block = weights[0].shape[0]
    step = pl.program_id(0)
    for side in range(2):
        value = None
        for one in range(count):
            term = lax.dot_general(
                lefts[one][...],
                weights[2 * one + side][...],
                (((0 if flipped else 1,), (1,)), ((), ())),
                preferred_element_type=F32,
            )
            value = term if value is None else value + term
        start = pl.multiple_of((side * pl.num_programs(0) + step) * block, block)
        kept_ref[:, pl.ds(start, block)] = value[:rows]
        sent_ref[:, pl.ds(start, block)] = value[rows:].astype(BF16)


def project_back(lefts, weights, parts, flipped=False):
    count = len(lefts)
    half = weights[0][0].shape[0]
    block = half // 2
    row_len, inner = lefts[0].shape[::-1] if flipped else lefts[0].shape
    specs = [pl.BlockSpec(left.shape, lambda k: (0, 0)) for left in lefts]
    for part in parts:
        specs += [pl.BlockSpec((block, inner), lambda k, part=part: (k, part))] * 2
    flat = [side for halves in weights for side in halves]
    whole = pl.BlockSpec((row_len // 2, 2 * half), lambda k: (0, 0))
    return pl.pallas_call(
        functools.partial(back_kernel, count, flipped),
        grid=(2,),
        in_specs=specs,
        out_specs=[whole, whole],
        out_shape=[
            jax.ShapeDtypeStruct((row_len // 2, 2 * half), F32),
            jax.ShapeDtypeStruct((row_len // 2, 2 * half), BF16),
        ],
        compiler_params=pltpu.CompilerParams(vmem_limit_bytes=VMEM_BYTES),
        cost_estimate=LIGHT,
    )(*lefts, *flat)


def scatter_rows(lefts, weights, parts, flipped):
    both = 0.0
    for left, halves, part in zip(lefts, weights, parts):
        inner = left.shape[0 if flipped else 1]
        whole = jnp.concatenate(halves, axis=0)[:, part * inner : (part + 1) * inner]
        dims = (((0 if flipped else 1,), (1,)), ((), ()))
        both = both + lax.dot_general(left, whole, dims, preferred_element_type=F32)
    return lax.psum_scatter(both.astype(BF16), "tp", scatter_dimension=0, tiled=True).astype(F32)


def head_normed(raw, gain, cosine, sine):
    inverse = lax.rsqrt(jnp.mean(raw * raw, axis=0, keepdims=True) + EPSILON)
    normed = raw * inverse * gain
    half = raw.shape[0] // 2
    first, second = normed[:half], normed[half:]
    return jnp.concatenate(
        [first * cosine - second * sine, second * cosine + first * sine], axis=0
    )


def weighted_columns(weights, rows_ref, target_ref):
    width = weights[0].shape[0]
    value = None
    for part in range(len(weights)):
        term = lax.dot_general(
            weights[part][...],
            rows_ref[:, part * width : (part + 1) * width],
            (((0,), (1,)), ((), ())),
            preferred_element_type=F32,
        )
        value = term if value is None else value + term
    target_ref[...] = value.astype(target_ref.dtype)


def attend_kernel(
    groups,
    repeat,
    w0,
    w1,
    rows_ref,
    cos_ref,
    sin_ref,
    q_gain_ref,
    k_gain_ref,
    place_ref,
    first_ref,
    place_col_ref,
    raw_ref,
    q_ref,
    k_ref,
    v_ref,
    log_ref,
    out_ref,
    bias_ref,
):
    weighted_columns((w0, w1), rows_ref, raw_ref)
    places = place_col_ref[...]
    allowed = (places <= place_ref[...]) & (places >= first_ref[...])
    bias_ref[...] = jnp.where(allowed, 0.0, -1e30)
    cosine, sine = cos_ref[...], sin_ref[...]
    heads = groups * repeat

    def group_step(group, carry):
        k_row = pl.multiple_of(group * HD, HD)
        keys = head_normed(
            raw_ref[pl.ds(heads * HD + k_row, HD), :], k_gain_ref[...], cosine, sine
        ).astype(BF16)
        values = raw_ref[pl.ds((heads + groups) * HD + k_row, HD), :].astype(BF16)
        k_ref[pl.ds(k_row, HD), :] = keys
        v_ref[pl.ds(k_row, HD), :] = values
        for one in range(repeat):
            q_row = pl.multiple_of((group * repeat + one) * HD, HD)
            queries = head_normed(
                raw_ref[pl.ds(q_row, HD), :], q_gain_ref[...], cosine, sine
            ).astype(BF16)
            queries = queries * jnp.asarray(HD ** (-0.5), BF16)
            q_ref[pl.ds(q_row, HD), :] = queries
            scores = (
                lax.dot_general(
                    keys, queries, (((0,), (0,)), ((), ())), preferred_element_type=F32
                )
                + bias_ref[...]
            )
            peaks = jnp.max(scores, axis=0, keepdims=True)
            shifted = jnp.exp(scores - peaks)
            totals = jnp.sum(shifted, axis=0, keepdims=True)
            outputs = jnp.dot(values, shifted.astype(BF16), preferred_element_type=F32)
            out_ref[pl.ds(q_row, HD), :] = (outputs / totals).astype(BF16)
            log_ref[group * repeat + one] = peaks + jnp.log(totals)
        return carry

    lax.fori_loop(0, groups, group_step, 0)


def whole_block(value):
    return pl.BlockSpec(value.shape, lambda k: (0,) * len(value.shape))


def attend_rows(weights, rows, tables, groups, repeat):
    row_len = rows.shape[0]
    heads = groups * repeat
    columns = (heads + 2 * groups) * HD
    shapes = [
        jax.ShapeDtypeStruct((columns, row_len), F32),
        jax.ShapeDtypeStruct((heads * HD, row_len), BF16),
        jax.ShapeDtypeStruct((groups * HD, row_len), BF16),
        jax.ShapeDtypeStruct((groups * HD, row_len), BF16),
        jax.ShapeDtypeStruct((heads, 1, row_len), F32),
        jax.ShapeDtypeStruct((heads * HD, row_len), BF16),
    ]
    return pl.pallas_call(
        functools.partial(attend_kernel, groups, repeat),
        grid=(1,),
        in_specs=[pl.BlockSpec((weights[0].shape[0], columns), lambda k: (0, 0))] * 2
        + [whole_block(one) for one in (rows, *tables)],
        out_specs=[whole_block(one) for one in shapes],
        out_shape=shapes,
        scratch_shapes=[pltpu.VMEM((row_len, row_len), F32)],
        compiler_params=pltpu.CompilerParams(vmem_limit_bytes=VMEM_BYTES),
        cost_estimate=LIGHT,
    )(*weights, rows, *tables)


def head_back(raw, gain, grad_rot, cosine, sine):
    half = raw.shape[0] // 2
    first, second = grad_rot[:half], grad_rot[half:]
    grad = jnp.concatenate(
        [first * cosine + second * sine, second * cosine - first * sine], axis=0
    )
    inverse = lax.rsqrt(jnp.mean(raw * raw, axis=0, keepdims=True) + EPSILON)
    hat = raw * inverse
    terms = grad * hat
    grad_hat = grad * gain
    inner = jnp.mean(terms * gain, axis=0, keepdims=True)
    return inverse * (grad_hat - hat * inner), terms


def attend_back_kernel(
    groups,
    repeat,
    w0,
    w1,
    rows_ref,
    cos_ref,
    sin_ref,
    q_gain_ref,
    k_gain_ref,
    place_ref,
    first_ref,
    place_col_ref,
    raw_ref,
    q_ref,
    k_ref,
    v_ref,
    log_ref,
    grad_ref,
    q_part_ref,
    k_part_ref,
    bias_ref,
    outer_ref,
    q_terms_ref,
    k_terms_ref,
):
    weighted_columns((w0, w1), rows_ref, outer_ref)
    places = place_col_ref[...]
    allowed = (places <= place_ref[...]) & (places >= first_ref[...])
    bias_ref[...] = jnp.where(allowed, 0.0, -1e30)
    cosine, sine = cos_ref[...], sin_ref[...]
    heads = groups * repeat
    q_terms_ref[...] = jnp.zeros_like(q_terms_ref)
    k_terms_ref[...] = jnp.zeros_like(k_terms_ref)

    def group_step(group, carry):
        k_row = pl.multiple_of(group * HD, HD)
        keys = k_ref[pl.ds(k_row, HD), :]
        values = v_ref[pl.ds(k_row, HD), :]
        grad_keys = None
        for one in range(repeat):
            q_row = pl.multiple_of((group * repeat + one) * HD, HD)
            queries = q_ref[pl.ds(q_row, HD), :]
            outer = outer_ref[pl.ds(q_row, HD), :]
            scores = (
                lax.dot_general(
                    keys, queries, (((0,), (0,)), ((), ())), preferred_element_type=F32
                )
                + bias_ref[...]
            )
            attn_probs = jnp.exp(scores - log_ref[group * repeat + one])
            grad_probs = lax.dot_general(
                values, outer, (((0,), (0,)), ((), ())), preferred_element_type=F32
            )
            inner = jnp.sum(attn_probs * grad_probs, axis=0, keepdims=True)
            grad_scores = (attn_probs * (grad_probs - inner)).astype(BF16)
            grad_query = jnp.dot(keys, grad_scores, preferred_element_type=F32) * (HD ** (-0.5))
            grad_key = lax.dot_general(
                queries, grad_scores, (((1,), (1,)), ((), ())), preferred_element_type=F32
            )
            grad_value = lax.dot_general(
                outer,
                attn_probs.astype(BF16),
                (((1,), (1,)), ((), ())),
                preferred_element_type=F32,
            )
            grad_raw, terms = head_back(
                raw_ref[pl.ds(q_row, HD), :], q_gain_ref[...], grad_query, cosine, sine
            )
            grad_ref[pl.ds(q_row, HD), :] = grad_raw.astype(BF16)
            q_terms_ref[...] += terms
            if grad_keys is None:
                grad_keys, grad_values = grad_key, grad_value
            else:
                grad_keys, grad_values = grad_keys + grad_key, grad_values + grad_value
        grad_raw, terms = head_back(
            raw_ref[pl.ds(heads * HD + k_row, HD), :], k_gain_ref[...], grad_keys, cosine, sine
        )
        k_terms_ref[...] += terms
        grad_ref[pl.ds(heads * HD + k_row, HD), :] = grad_raw.astype(BF16)
        grad_ref[pl.ds((heads + groups) * HD + k_row, HD), :] = grad_values.astype(BF16)
        return carry

    lax.fori_loop(0, groups, group_step, 0)
    q_part_ref[...] = jnp.sum(q_terms_ref[...], axis=1, keepdims=True)
    k_part_ref[...] = jnp.sum(k_terms_ref[...], axis=1, keepdims=True)


def attend_rows_back(weights, rows, tables, kept, groups, repeat):
    row_len = rows.shape[0]
    heads = groups * repeat
    columns = (heads + 2 * groups) * HD
    shapes = [
        jax.ShapeDtypeStruct((columns, row_len), BF16),
        jax.ShapeDtypeStruct((HD, 1), F32),
        jax.ShapeDtypeStruct((HD, 1), F32),
    ]
    return pl.pallas_call(
        functools.partial(attend_back_kernel, groups, repeat),
        grid=(1,),
        in_specs=[
            pl.BlockSpec(
                (weights[0].shape[0], heads * HD), lambda k: (0, columns // (heads * HD))
            )
        ]
        * 2
        + [whole_block(one) for one in (rows, *tables, *kept)],
        out_specs=[whole_block(one) for one in shapes],
        out_shape=shapes,
        scratch_shapes=[
            pltpu.VMEM((row_len, row_len), F32),
            pltpu.VMEM((heads * HD, row_len), BF16),
            pltpu.VMEM((HD, row_len), F32),
            pltpu.VMEM((HD, row_len), F32),
        ],
        compiler_params=pltpu.CompilerParams(vmem_limit_bytes=VMEM_BYTES),
        cost_estimate=LIGHT,
    )(*weights, rows, *tables, *kept)


def hidden_kernel(
    gate_own, gate_other, up_own, up_other, down_own, down_other, rows_ref, cot_ref, *outs
):
    gate_grad_ref, up_grad_ref, act_ref = outs
    width = gate_own.shape[0]

    def summed(source_ref, own_ref, other_ref):
        return jnp.dot(
            source_ref[:, :width], own_ref[...], preferred_element_type=F32
        ) + jnp.dot(source_ref[:, width:], other_ref[...], preferred_element_type=F32)

    gate = summed(rows_ref, gate_own, gate_other)
    up = summed(rows_ref, up_own, up_other)
    grad_act = summed(cot_ref, down_own, down_other)
    sigmoid_gate = jax.nn.sigmoid(gate)
    silu = gate * sigmoid_gate
    act_ref[...] = (silu * up).astype(BF16)
    up_grad_ref[...] = (grad_act * silu).astype(BF16)
    gate_grad_ref[...] = (
        grad_act * up * (sigmoid_gate + silu * (1.0 - sigmoid_gate))
    ).astype(BF16)


def hidden_small(weights, rows, cot_rows):
    row_len, width = rows.shape
    columns = weights[0].shape[1] // 3
    block = 256 if columns % 256 == 0 else columns
    steps = columns // block
    specs = []
    for part in range(3):
        specs += [
            pl.BlockSpec((width // 2, block), lambda k, part=part: (0, part * steps + k))
        ] * 2
    whole = pl.BlockSpec((row_len, width), lambda k: (0, 0))
    return pl.pallas_call(
        hidden_kernel,
        grid=(steps,),
        in_specs=specs + [whole, whole],
        out_specs=[pl.BlockSpec((row_len, block), lambda k: (0, k))] * 3,
        out_shape=[jax.ShapeDtypeStruct((row_len, columns), BF16)] * 3,
        compiler_params=pltpu.CompilerParams(vmem_limit_bytes=VMEM_BYTES),
        cost_estimate=LIGHT,
    )(*weights, *weights, *weights, rows, cot_rows)


def masked_scores(query_block, key_rows, block_segment, block_places, segment, places, score_scale):
    scores = (
        jnp.einsum("qgrd,kgd->grqk", query_block, key_rows, preferred_element_type=jnp.float32)
        * score_scale
    )
    allowed = (places[None, :] <= block_places[:, None]) & (
        segment[None, :] == block_segment[:, None]
    )
    return jnp.where(allowed, scores, -1e30)


def attend(query_rows, key_rows, value_rows, segment, places, block_rows):
    row_len = query_rows.shape[0]
    blocks = row_len // block_rows
    score_scale = query_rows.shape[-1] ** (-0.5)

    def block_out(block_item):
        query_block, block_segment, block_places = block_item
        scores = masked_scores(
            query_block, key_rows, block_segment, block_places, segment, places, score_scale
        )
        peaks = jnp.max(scores, axis=-1, keepdims=True)
        shifted = jnp.exp(scores - peaks)
        totals = jnp.sum(shifted, axis=-1, keepdims=True)
        attn_probs = (shifted / totals).astype(jnp.bfloat16)
        outputs = jnp.einsum(
            "grqk,kgd->qgrd", attn_probs, value_rows, preferred_element_type=jnp.float32
        )
        return (outputs, (peaks + jnp.log(totals))[..., 0])

    outputs, log_totals = lax.map(
        block_out,
        (
            query_rows.reshape((blocks, block_rows) + query_rows.shape[1:]),
            segment.reshape(blocks, block_rows),
            places.reshape(blocks, block_rows),
        ),
    )
    return (outputs.reshape(query_rows.shape), log_totals)


def attend_back(
    query_rows, key_rows, value_rows, grad_out, log_totals, segment, places, block_rows
):
    row_len = query_rows.shape[0]
    blocks = row_len // block_rows
    score_scale = query_rows.shape[-1] ** (-0.5)

    def block_back(carry, block_item):
        grad_keys, grad_values = carry
        query_block, grad_block, total_block, block_segment, block_places = block_item
        scores = masked_scores(
            query_block, key_rows, block_segment, block_places, segment, places, score_scale
        )
        attn_probs = jnp.exp(scores - total_block[..., None])
        grad_probs = jnp.einsum(
            "qgrd,kgd->grqk", grad_block, value_rows, preferred_element_type=jnp.float32
        )
        inner = jnp.sum(attn_probs * grad_probs, axis=-1, keepdims=True)
        grad_scores = (attn_probs * (grad_probs - inner)).astype(jnp.bfloat16)
        grad_query = (
            jnp.einsum("grqk,kgd->qgrd", grad_scores, key_rows, preferred_element_type=jnp.float32)
            * score_scale
        )
        grad_keys = (
            grad_keys
            + jnp.einsum(
                "grqk,qgrd->kgd", grad_scores, query_block, preferred_element_type=jnp.float32
            )
            * score_scale
        )
        grad_values = grad_values + jnp.einsum(
            "grqk,qgrd->kgd",
            attn_probs.astype(jnp.bfloat16),
            grad_block,
            preferred_element_type=jnp.float32,
        )
        return ((grad_keys, grad_values), grad_query)

    zeros_kv = jnp.zeros(key_rows.shape, jnp.float32)
    block_shape = (blocks, block_rows) + query_rows.shape[1:]
    (grad_keys, grad_values), grad_queries = lax.scan(
        block_back,
        (zeros_kv, zeros_kv),
        (
            query_rows.reshape(block_shape),
            grad_out.reshape(block_shape),
            log_totals,
            segment.reshape(blocks, block_rows),
            places.reshape(blocks, block_rows),
        ),
    )
    return (grad_queries.reshape(query_rows.shape), grad_keys, grad_values)


def attention_small(qkv_w, rows_first, tables, groups, repeat):
    raw, queries, keys, values, logs, attended = attend_rows(
        qkv_w, rows_first, tables, groups, repeat
    )

    def back(out_w, branch_rows):
        grads, q_part, k_part = attend_rows_back(
            out_w, branch_rows, tables, (raw, queries, keys, values, logs), groups, repeat
        )
        return grads, q_part[:, 0], k_part[:, 0]

    return attended, back


def attention_large(qkv_w, rows_first, doc_tables, q_gain, k_gain, groups, repeat):
    segment, places, cosine, sine = doc_tables
    row_len = rows_first.shape[0]
    query_cols, key_cols = groups * repeat * HD, groups * HD
    block_rows = min(512, row_len)
    projected = jnp.dot(rows_first, jnp.concatenate(qkv_w, axis=0), preferred_element_type=F32)
    query_raw = projected[:, :query_cols].reshape(row_len, groups, repeat, HD)
    key_raw = projected[:, query_cols : query_cols + key_cols].reshape(row_len, groups, HD)
    value_rows = projected[:, query_cols + key_cols :].astype(BF16).reshape(row_len, groups, HD)
    query_normed, query_hat, query_inv = norm_forward(query_raw, q_gain)
    key_normed, key_hat, key_inv = norm_forward(key_raw, k_gain)
    query_rows = rotate(query_normed, cosine, sine).astype(BF16)
    key_rows = rotate(key_normed, cosine, sine).astype(BF16)
    attended, log_totals = attend(query_rows, key_rows, value_rows, segment, places, block_rows)

    def back(out_w, branch_rows):
        out_w = [half[:, query_cols + 2 * key_cols :] for half in out_w]
        grad_attended = jnp.dot(
            branch_rows, jnp.concatenate(out_w, axis=0), preferred_element_type=F32
        ).astype(BF16)
        grad_query_rot, grad_key_rot, grad_value = attend_back(
            query_rows,
            key_rows,
            value_rows,
            grad_attended.reshape(row_len, groups, repeat, HD),
            log_totals,
            segment,
            places,
            block_rows,
        )
        grad_query_norm = rotate(grad_query_rot, cosine, -sine)
        grad_key_norm = rotate(grad_key_rot, cosine, -sine)
        grad_query_raw, q_part = norm_backward(grad_query_norm, query_hat, query_inv, q_gain)
        grad_key_raw, k_part = norm_backward(grad_key_norm, key_hat, key_inv, k_gain)
        grads = jnp.concatenate(
            [
                grad_query_raw.reshape(row_len, query_cols),
                grad_key_raw.reshape(row_len, key_cols),
                grad_value.reshape(row_len, key_cols),
            ],
            axis=1,
        )
        return grads.astype(BF16).T, q_part, k_part

    return attended.reshape(row_len, query_cols).astype(BF16).T, back


def hidden_large(weights, rows, cot_rows):
    columns = weights[0].shape[1] // 3
    whole = jnp.concatenate(weights, axis=0)
    gate = jnp.dot(rows, whole[:, :columns], preferred_element_type=F32)
    up = jnp.dot(rows, whole[:, columns : 2 * columns], preferred_element_type=F32)
    grad_act = jnp.dot(cot_rows, whole[:, 2 * columns :], preferred_element_type=F32)
    sigmoid_gate = jax.nn.sigmoid(gate)
    silu = gate * sigmoid_gate
    grad_gate = grad_act * up * sigmoid_gate * (1.0 + gate * (1.0 - sigmoid_gate))
    return grad_gate.astype(BF16), (grad_act * silu).astype(BF16), (silu * up).astype(BF16)


def local(
    tokens,
    doc_starts,
    attn_gain,
    w_query,
    w_key,
    w_value,
    q_gain,
    k_gain,
    w_out,
    mlp_gain,
    w_gate,
    w_up,
    w_down,
    out_grad,
):
    width = tokens.shape[-1]
    own_rows = tokens.shape[1]
    row_len = own_rows * lax.axis_size("tp")
    small = lax.axis_size("tp") == 2 and row_len <= 512
    groups = w_key.shape[1] // HD
    repeat = w_query.shape[1] // w_key.shape[1]
    query_cols = w_query.shape[1]
    key_cols = w_key.shape[1]

    arrivals = []
    lanes = {name: Lane(2, arrivals) for name in ("x", "y", "z", "core")}
    far = layout_masks()[:1:-1]
    ff_cols = w_gate.shape[1]
    cut = ff_cols // CHUNKS if ff_cols % (CHUNKS * 128) == 0 else ff_cols
    shards = [w_query, w_key, w_value, w_out, w_gate, w_up, w_down]
    plans = [[(one, 0, shards[one].shape[1]) for one in range(4)]]
    plans += [
        [(one, start, start + cut) for one in (4, 5, 6)] for start in range(0, ff_cols, cut)
    ]
    attn, *chunks = (Gather(packed, lanes) for packed in pack(shards, plans))
    first, second, third = chunks if len(chunks) == 3 else (None, None, None)

    def start_far(one, after=()):
        for mask in far[:-1]:
            one.far(mask, after)

    def gather_all(one):
        one.last_far(far[-1])
        one.beside()
        one.beside_next()
        one.join()
        one.core()

    start_far(attn)
    for one in chunks if first is None else [first]:
        start_far(one)
    matrix = order_matrix(width, BF16)
    gains = reorder(jnp.stack([attn_gain, mlp_gain]), matrix)
    attn_gain, mlp_gain = gains[0], gains[1]
    attn.last_far(far[-1])
    attn.beside()
    inputs = reorder(tied(tokens[0], attn.near), matrix).astype(F32)
    places = row_places(own_rows)
    segment, position = documents(doc_starts[0], places)
    cosine, sine = rope_tables(position, HD)
    normed_first, hat_first, inv_first = norm_forward(inputs, attn_gain)
    rows_first = gather_rows(normed_first.astype(BF16), lanes["x"])
    cotangent = reorder(tied(out_grad[0], attn.near), matrix)
    if first is not None:
        first.last_far(far[-1])
        first.beside()
    attn.beside_next()
    cot_rows = gather_rows(cotangent, lanes["x"])
    if second is not None:
        start_far(second)
    attn.join()
    attn.core()
    key_cols = w_key.shape[1]
    columns = query_cols + 2 * key_cols
    if small:
        tables = (
            cosine.T,
            sine.T,
            q_gain[:, None],
            k_gain[:, None],
            places[None, :],
            (places - position)[None, :],
            places[:, None],
        )
        attended, attention_back = attention_small(attn.halves, rows_first, tables, groups, repeat)
    else:
        doc_tables = (segment, places, cosine, sine)
        attended, attention_back = attention_large(
            [half[:, :columns] for half in attn.halves], rows_first, doc_tables, q_gain, k_gain, groups, repeat
        )
    order = Order()
    order.done(attended)

    def sum_rows(lefts, weights, parts, flipped=False):
        if lax.axis_size("tp") != 2:
            order.sent = cot_rows
            return scatter_rows(lefts, weights, parts, flipped)
        lefts = order(*lefts)
        lefts = lefts if isinstance(lefts, tuple) else (lefts,)
        kept, sent = project_back(lefts, weights, parts, flipped)
        order.sent = order.done(sent)
        return kept + lanes["x"].swap(sent, "tp", 1).astype(F32)

    out_part = columns // query_cols
    if first is not None:
        first.beside_next([attended])
        second.last_far(far[-1], [attended])
        second.beside()
    branch = sum_rows([attended], [attn.halves], [out_part], True)
    if first is not None:
        start_far(third, [order.sent])
        first.join([order.sent])
        first.core()
    hidden = inputs + branch
    normed_second, hat_second, inv_second = norm_forward(hidden, mlp_gain)
    rows_second = gather_rows(order.done(normed_second.astype(BF16)), lanes["x"])
    if first is None:
        for one in chunks:
            gather_all(one)
    else:
        second.beside_next()
        third.last_far(far[-1])
        third.beside()
        second.join([normed_second])
        second.core()
        third.beside_next()
    hidden_step = hidden_small if small else hidden_large
    acts, grads, sums = [], [], []

    def hidden_chunk(place):
        rows, cots = order(rows_second, cot_rows)
        gate_part, up_part, act_part = hidden_step(chunks[place].halves, rows, cots)
        acts.append(order.done(act_part))
        grads.extend([gate_part, up_part])
        pairs = [(rows_second, gate_part), (rows_second, up_part), (cot_rows, act_part)]
        sums.append(Scatter(pairs, lanes, order))

    back = far[::-1]
    def hidden_back():
        return sum_rows(
            grads, [one.halves for one in chunks for _ in range(2)], [0, 1] * len(chunks)
        )

    if first is None:
        for place in range(len(chunks)):
            hidden_chunk(place)
            sums[place].core()
            sums[place].beside()
        grad_normed_second = hidden_back()
    if first is not None:
        hidden_chunk(0)
        sums[0].core()
        hidden_chunk(1)
        third.join([acts[1]])
        third.core()
        sums[0].beside()
        sums[1].core()
        hidden_chunk(2)
        grad_normed_second = hidden_back()
        sum_one, sum_two, sum_three = sums
        sum_three.core()
        grad_hidden_norm, mlp_gain_part = norm_backward(
            order(grad_normed_second), hat_second, inv_second, mlp_gain
        )
        grad_hidden = cotangent.astype(F32) + grad_hidden_norm
        branch_rows = gather_rows(order.done(grad_hidden.astype(BF16)), lanes["x"])
        sum_two.beside()
        out_sum = Scatter([(branch_rows, attended)], lanes, order, True)
        qkv_sum = Scatter([(rows_first, None)], lanes, order, True)
        sum_one.meet()
        sum_one.far(back[0])
        grad_projected, q_gain_part, k_gain_part = attention_back(attn.halves, order(branch_rows))
        qkv_sum.pairs = [(rows_first, order.done(grad_projected))]
        grad_normed_first = sum_rows([grad_projected], [attn.halves], [0], True)
        qkv_sum.core()
        out_sum.core()
        sum_three.beside()
        sum_one.far_meet()
        sum_one.far(back[1])
        sum_two.meet()
        sum_two.far(back[0])
        qkv_sum.beside()
        out_sum.beside()
        grad_input_norm, attn_gain_part = norm_backward(
            order(grad_normed_first), hat_first, inv_first, attn_gain
        )
        order.done(attn_gain_part)
        sum_one.far_meet()
        result = hidden + sum_rows(acts, [one.halves for one in chunks], [2] * len(chunks))
        sum_two.far_meet()
        sum_two.far(back[1])
        for one in (sum_three, qkv_sum, out_sum):
            one.meet()
            one.far(back[0])
        sum_two.far_meet()
        for one in (sum_three, qkv_sum, out_sum):
            one.far_meet()
            one.far(back[1])
        for one in (sum_three, qkv_sum, out_sum):
            one.far_meet()
    else:
        grad_hidden_norm, mlp_gain_part = norm_backward(
            order(grad_normed_second), hat_second, inv_second, mlp_gain
        )
        grad_hidden = cotangent.astype(F32) + grad_hidden_norm
        branch_rows = gather_rows(order.done(grad_hidden.astype(BF16)), lanes["x"])
        result = hidden + sum_rows(acts, [one.halves for one in chunks], [2] * len(chunks))
        grad_projected, q_gain_part, k_gain_part = attention_back(attn.halves, order(branch_rows))
        order.done(grad_projected)
        grad_normed_first = sum_rows([grad_projected], [attn.halves], [0], True)
        out_sum = Scatter([(branch_rows, attended)], lanes, order, True)
        qkv_sum = Scatter([(rows_first, grad_projected)], lanes, order, True)
        for one in (qkv_sum, out_sum):
            one.core()
            one.beside()
        grad_input_norm, attn_gain_part = norm_backward(
            order(grad_normed_first), hat_first, inv_first, attn_gain
        )
        for one in (*sums, qkv_sum, out_sum):
            one.meet()
            for mask in back:
                one.far(mask)
                one.far_meet()
    grad_inputs = grad_hidden + grad_input_norm
    qkv_grad, out_w_grad = qkv_sum.kept, out_sum.kept
    gate_grad, up_grad, down_grad = (
        jnp.concatenate([one.kept[:, part * cut : (part + 1) * cut] for one in sums], axis=1)
        for part in range(3)
    )
    parts = restore(jnp.stack([attn_gain_part, mlp_gain_part]), matrix)
    parts = total(jnp.concatenate([parts[0], parts[1], q_gain_part, k_gain_part]))
    return (
        restore(result.astype(BF16), matrix)[None],
        restore(grad_inputs.astype(BF16), matrix)[None],
        parts[:width],
        qkv_grad[:, :query_cols],
        qkv_grad[:, query_cols : query_cols + key_cols],
        qkv_grad[:, query_cols + key_cols :],
        parts[2 * width : 2 * width + HD],
        parts[2 * width + HD :],
        out_w_grad,
        parts[width : 2 * width],
        gate_grad,
        up_grad,
        down_grad,
    )


def solution(mesh):
    in_specs = (
        P("dp", "tp", None),
        P("dp", None),
        P(),
        P("dp", "tp"),
        P("dp", "tp"),
        P("dp", "tp"),
        P(),
        P(),
        P("dp", "tp"),
        P(),
        P("dp", "tp"),
        P("dp", "tp"),
        P("dp", "tp"),
        P("dp", "tp", None),
    )
    out_specs = (
        P("dp", "tp", None),
        P("dp", "tp", None),
        P(),
        P("dp", "tp"),
        P("dp", "tp"),
        P("dp", "tp"),
        P(),
        P(),
        P("dp", "tp"),
        P(),
        P("dp", "tp"),
        P("dp", "tp"),
        P("dp", "tp"),
    )
    return jax.shard_map(local, mesh=mesh, in_specs=in_specs, out_specs=out_specs, check_vma=False)
```

```python
import functools

import jax
import jax.numpy as jnp
from jax import lax
from jax.experimental import pallas as pl
from jax.experimental.pallas import tpu as pltpu
from jax.sharding import PartitionSpec as P

HD = 64


EPSILON = 1e-05
THETA = 1000000.0


def documents(starts, length):
    places = jnp.arange(length, dtype=jnp.int32)
    inside = places[:, None] >= starts[None, :]
    segment = jnp.sum(inside.astype(jnp.int32), axis=1) - 1
    firsts = jnp.max(jnp.where(inside, starts[None, :], 0), axis=1)
    return (segment, places - firsts)


def rope_tables(position, width):
    half_width = width // 2
    freqs = THETA ** (-(jnp.arange(half_width, dtype=jnp.float32) * 2.0 / width))
    angles = position.astype(jnp.float32)[:, None] * freqs[None, :]
    return (jnp.cos(angles), jnp.sin(angles))


def rotate(values, cosine, sine):
    half_width = values.shape[-1] // 2
    first_half = values[..., :half_width]
    second_half = values[..., half_width:]
    tile_shape = (values.shape[0],) + (1,) * (values.ndim - 2) + (half_width,)
    cos_tile = cosine.reshape(tile_shape)
    sin_tile = sine.reshape(tile_shape)
    return jnp.concatenate(
        [
            first_half * cos_tile - second_half * sin_tile,
            second_half * cos_tile + first_half * sin_tile,
        ],
        axis=-1,
    )


def norm_forward(values, gain):
    inverse = lax.rsqrt(jnp.mean(values * values, axis=-1, keepdims=True) + EPSILON)
    normed_hat = values * inverse
    return (normed_hat * gain, normed_hat, inverse)


def norm_backward(grad_normed, normed_hat, inverse, gain):
    grad_hat = grad_normed * gain
    grad_values = inverse * (
        grad_hat - normed_hat * jnp.mean(grad_hat * normed_hat, axis=-1, keepdims=True)
    )
    gain_part = jnp.sum((grad_normed * normed_hat).reshape(-1, normed_hat.shape[-1]), axis=0)
    return (grad_values, gain_part)


def gather_rows(values):
    return lax.all_gather(values, "tp", axis=0, tiled=True)


def sum_rows(left_rows, right_weight):
    return lax.psum_scatter(
        jnp.dot(left_rows, right_weight.T, preferred_element_type=jnp.float32).astype(jnp.bfloat16),
        "tp",
        scatter_dimension=0,
        tiled=True,
    ).astype(jnp.float32)


def masked_scores(query_block, key_rows, block_segment, block_places, segment, places, score_scale):
    scores = (
        jnp.einsum("qgrd,kgd->grqk", query_block, key_rows, preferred_element_type=jnp.float32)
        * score_scale
    )
    allowed = (places[None, :] <= block_places[:, None]) & (
        segment[None, :] == block_segment[:, None]
    )
    return jnp.where(allowed, scores, -1e30)


def attend(query_rows, key_rows, value_rows, segment, block_rows):
    row_len = query_rows.shape[0]
    blocks = row_len // block_rows
    places = jnp.arange(row_len, dtype=jnp.int32)
    score_scale = query_rows.shape[-1] ** (-0.5)

    def block_out(block_item):
        query_block, block_segment, block_places = block_item
        scores = masked_scores(
            query_block, key_rows, block_segment, block_places, segment, places, score_scale
        )
        peaks = jnp.max(scores, axis=-1, keepdims=True)
        shifted = jnp.exp(scores - peaks)
        totals = jnp.sum(shifted, axis=-1, keepdims=True)
        attn_probs = (shifted / totals).astype(jnp.bfloat16)
        outputs = jnp.einsum(
            "grqk,kgd->qgrd", attn_probs, value_rows, preferred_element_type=jnp.float32
        )
        return (outputs, (peaks + jnp.log(totals))[..., 0])

    outputs, log_totals = lax.map(
        block_out,
        (
            query_rows.reshape((blocks, block_rows) + query_rows.shape[1:]),
            segment.reshape(blocks, block_rows),
            places.reshape(blocks, block_rows),
        ),
    )
    return (outputs.reshape(query_rows.shape), log_totals)


def attend_back(query_rows, key_rows, value_rows, grad_out, log_totals, segment, block_rows):
    row_len = query_rows.shape[0]
    blocks = row_len // block_rows
    places = jnp.arange(row_len, dtype=jnp.int32)
    score_scale = query_rows.shape[-1] ** (-0.5)

    def block_back(carry, block_item):
        grad_keys, grad_values = carry
        query_block, grad_block, total_block, block_segment, block_places = block_item
        scores = masked_scores(
            query_block, key_rows, block_segment, block_places, segment, places, score_scale
        )
        attn_probs = jnp.exp(scores - total_block[..., None])
        grad_probs = jnp.einsum(
            "qgrd,kgd->grqk", grad_block, value_rows, preferred_element_type=jnp.float32
        )
        inner = jnp.sum(attn_probs * grad_probs, axis=-1, keepdims=True)
        grad_scores = (attn_probs * (grad_probs - inner)).astype(jnp.bfloat16)
        grad_query = (
            jnp.einsum("grqk,kgd->qgrd", grad_scores, key_rows, preferred_element_type=jnp.float32)
            * score_scale
        )
        grad_keys = (
            grad_keys
            + jnp.einsum(
                "grqk,qgrd->kgd", grad_scores, query_block, preferred_element_type=jnp.float32
            )
            * score_scale
        )
        grad_values = grad_values + jnp.einsum(
            "grqk,qgrd->kgd",
            attn_probs.astype(jnp.bfloat16),
            grad_block,
            preferred_element_type=jnp.float32,
        )
        return ((grad_keys, grad_values), grad_query)

    zeros_kv = jnp.zeros(key_rows.shape, jnp.float32)
    block_shape = (blocks, block_rows) + query_rows.shape[1:]
    (grad_keys, grad_values), grad_queries = lax.scan(
        block_back,
        (zeros_kv, zeros_kv),
        (
            query_rows.reshape(block_shape),
            grad_out.reshape(block_shape),
            log_totals,
            segment.reshape(blocks, block_rows),
            places.reshape(blocks, block_rows),
        ),
    )
    return (grad_queries.reshape(query_rows.shape), grad_keys, grad_values)


def local_large(
    tokens,
    doc_starts,
    attn_gain,
    w_query,
    w_key,
    w_value,
    q_gain,
    k_gain,
    w_out,
    mlp_gain,
    w_gate,
    w_up,
    w_down,
    out_grad,
):
    query_w, key_w, value_w, out_w, gate_w, up_w, down_w = (
        lax.all_gather(w_query, "dp", axis=0, tiled=True),
        lax.all_gather(w_key, "dp", axis=0, tiled=True),
        lax.all_gather(w_value, "dp", axis=0, tiled=True),
        lax.all_gather(w_out, "dp", axis=0, tiled=True),
        lax.all_gather(w_gate, "dp", axis=0, tiled=True),
        lax.all_gather(w_up, "dp", axis=0, tiled=True),
        lax.all_gather(w_down, "dp", axis=0, tiled=True),
    )
    inputs = tokens[0].astype(jnp.float32)
    cotangent = out_grad[0]
    own_rows = inputs.shape[0]
    row_len = own_rows * lax.axis_size("tp")
    head_dim = HD
    groups = key_w.shape[1] // head_dim
    repeat = query_w.shape[1] // key_w.shape[1]
    query_cols = query_w.shape[1]
    key_cols = key_w.shape[1]
    ff_cols = gate_w.shape[1]
    block_rows = min(512, row_len)
    segment, position = documents(doc_starts[0], row_len)
    cosine, sine = rope_tables(position, head_dim)
    qkv_weight = jnp.concatenate([query_w, key_w, value_w], axis=1)
    gate_up_weight = jnp.concatenate([gate_w, up_w], axis=1)
    normed_first, hat_first, inv_first = norm_forward(inputs, attn_gain)
    rows_first = gather_rows(normed_first.astype(jnp.bfloat16))
    projected = jnp.dot(rows_first, qkv_weight, preferred_element_type=jnp.float32)
    query_raw = projected[:, :query_cols].reshape(row_len, groups, repeat, head_dim)
    key_raw = projected[:, query_cols : query_cols + key_cols].reshape(row_len, groups, head_dim)
    value_rows = (
        projected[:, query_cols + key_cols :]
        .astype(jnp.bfloat16)
        .reshape(row_len, groups, head_dim)
    )
    query_normed, query_hat, query_inv = norm_forward(query_raw, q_gain)
    key_normed, key_hat, key_inv = norm_forward(key_raw, k_gain)
    query_rows = rotate(query_normed, cosine, sine).astype(jnp.bfloat16)
    key_rows = rotate(key_normed, cosine, sine).astype(jnp.bfloat16)
    attended, log_totals = attend(query_rows, key_rows, value_rows, segment, block_rows)
    attended = attended.reshape(row_len, query_cols).astype(jnp.bfloat16)
    branch_out = sum_rows(attended, out_w)
    hidden = inputs + branch_out
    normed_second, hat_second, inv_second = norm_forward(hidden, mlp_gain)
    rows_second = gather_rows(normed_second.astype(jnp.bfloat16))
    gate_up = jnp.dot(rows_second, gate_up_weight, preferred_element_type=jnp.float32)
    gate_pre = gate_up[:, :ff_cols]
    up_pre = gate_up[:, ff_cols:]
    sigmoid_gate = jax.nn.sigmoid(gate_pre)
    activated = (gate_pre * sigmoid_gate * up_pre).astype(jnp.bfloat16)
    result = hidden + sum_rows(activated, down_w)
    cot_rows = gather_rows(cotangent)
    grad_act = jnp.dot(cot_rows, down_w, preferred_element_type=jnp.float32)
    grad_down = jnp.einsum("rd,rf->df", cot_rows, activated, preferred_element_type=jnp.float32)
    grad_gate = grad_act * up_pre * sigmoid_gate * (1.0 + gate_pre * (1.0 - sigmoid_gate))
    grad_up = grad_act * gate_pre * sigmoid_gate
    grad_gate_up = jnp.concatenate([grad_gate, grad_up], axis=1).astype(jnp.bfloat16)
    grad_gate_up_w = jnp.einsum(
        "rd,rf->df", rows_second, grad_gate_up, preferred_element_type=jnp.float32
    )
    grad_normed_second = sum_rows(grad_gate_up, gate_up_weight)
    grad_hidden_norm, mlp_gain_part = norm_backward(
        grad_normed_second, hat_second, inv_second, mlp_gain
    )
    grad_hidden = cotangent.astype(jnp.float32) + grad_hidden_norm
    grad_branch = grad_hidden.astype(jnp.bfloat16)
    branch_rows = gather_rows(grad_branch)
    grad_out_w = jnp.einsum("rd,rq->dq", branch_rows, attended, preferred_element_type=jnp.float32)
    grad_attended = jnp.dot(branch_rows, out_w, preferred_element_type=jnp.float32).astype(
        jnp.bfloat16
    )
    grad_query_rot, grad_key_rot, grad_value = attend_back(
        query_rows,
        key_rows,
        value_rows,
        grad_attended.reshape(row_len, groups, repeat, head_dim),
        log_totals,
        segment,
        block_rows,
    )
    grad_query_norm = rotate(grad_query_rot, cosine, -sine)
    grad_key_norm = rotate(grad_key_rot, cosine, -sine)
    grad_query_raw, q_gain_part = norm_backward(grad_query_norm, query_hat, query_inv, q_gain)
    grad_key_raw, k_gain_part = norm_backward(grad_key_norm, key_hat, key_inv, k_gain)
    grad_projected = jnp.concatenate(
        [
            grad_query_raw.reshape(row_len, query_cols),
            grad_key_raw.reshape(row_len, key_cols),
            grad_value.reshape(row_len, key_cols),
        ],
        axis=1,
    ).astype(jnp.bfloat16)
    grad_qkv_w = jnp.einsum(
        "rd,rf->df", rows_first, grad_projected, preferred_element_type=jnp.float32
    )
    grad_normed_first = sum_rows(grad_projected, qkv_weight)
    grad_input_norm, attn_gain_part = norm_backward(
        grad_normed_first, hat_first, inv_first, attn_gain
    )
    grad_inputs = grad_hidden + grad_input_norm
    summed = (
        lax.psum_scatter(
            grad_qkv_w[:, :query_cols].astype(jnp.bfloat16), "dp", scatter_dimension=0, tiled=True
        ).astype(jnp.float32),
        lax.psum_scatter(
            grad_qkv_w[:, query_cols : query_cols + key_cols].astype(jnp.bfloat16),
            "dp",
            scatter_dimension=0,
            tiled=True,
        ).astype(jnp.float32),
        lax.psum_scatter(
            grad_qkv_w[:, query_cols + key_cols :].astype(jnp.bfloat16),
            "dp",
            scatter_dimension=0,
            tiled=True,
        ).astype(jnp.float32),
        lax.psum_scatter(
            grad_out_w.astype(jnp.bfloat16), "dp", scatter_dimension=0, tiled=True
        ).astype(jnp.float32),
        lax.psum_scatter(
            grad_gate_up_w[:, :ff_cols].astype(jnp.bfloat16), "dp", scatter_dimension=0, tiled=True
        ).astype(jnp.float32),
        lax.psum_scatter(
            grad_gate_up_w[:, ff_cols:].astype(jnp.bfloat16), "dp", scatter_dimension=0, tiled=True
        ).astype(jnp.float32),
        lax.psum_scatter(
            grad_down.astype(jnp.bfloat16), "dp", scatter_dimension=0, tiled=True
        ).astype(jnp.float32),
    )
    gains = lax.psum((attn_gain_part, q_gain_part, k_gain_part, mlp_gain_part), ("dp", "tp"))
    return (
        result.astype(jnp.bfloat16)[None],
        grad_inputs.astype(jnp.bfloat16)[None],
        gains[0],
        summed[0],
        summed[1],
        summed[2],
        gains[1],
        gains[2],
        summed[3],
        gains[3],
        summed[4],
        summed[5],
        summed[6],
    )


F32 = jnp.float32
BF16 = jnp.bfloat16
VMEM_BYTES = 26 * 1024 * 1024
LIGHT = pl.CostEstimate(flops=1000, bytes_accessed=1000, transcendentals=0)


DEVICES = 16
MASKS = (1, 2, 4, 8)


def tied(values, *others):
    return lax.optimization_barrier((values, *others))[0]


class Program:
    def __init__(self):
        self.arrival = None
        self.step = None

    def begun(self):
        return [one for one in (self.arrival, self.step) if one is not None]

    def ready(self, *values):
        out = lax.optimization_barrier((*values, *self.begun()))[: len(values)]
        return out if len(out) > 1 else out[0]

    def run(self, function, *values):
        flat, tree = jax.tree.flatten(values)
        flat = lax.optimization_barrier((*flat, *self.begun()))[: len(flat)]
        out = function(*jax.tree.unflatten(tree, flat))
        self.step = jax.tree.leaves(out)[0]
        return out

    def send(self, values, mask, across=0):
        pairs = []
        for own in range(DEVICES):
            for side in range(2):
                pairs.append((own * 2 + side, (own ^ mask) * 2 + (side ^ across)))
        return lax.ppermute(self.ready(values), ("dp", "tp"), pairs)

    def arrive(self, other):
        if self.arrival is not None:
            other = tied(other, self.arrival)
        self.arrival = other
        return other


def pack_kernel(counts, *refs):
    ins = refs[: counts[0]]
    outs = refs[counts[0] :]
    for out_ref, spans in zip(outs, counts[1]):
        place = 0
        for source, start, stop in spans:
            out_ref[:, place : place + stop - start] = ins[source][:, start:stop]
            place += stop - start


def pack(shards, plans):
    rows = shards[0].shape[0]
    return pl.pallas_call(
        functools.partial(pack_kernel, (len(shards), plans)),
        out_shape=[
            jax.ShapeDtypeStruct((rows, sum(stop - start for _, start, stop in plan)), BF16)
            for plan in plans
        ],
        compiler_params=pltpu.CompilerParams(vmem_limit_bytes=VMEM_BYTES),
        cost_estimate=LIGHT,
    )(*shards)


def grad_kernel(count, flipped, added, *refs):
    lefts, rights = refs[:count], refs[count : 2 * count]
    outs = refs[2 * count + (1 if added else 0) :]
    step = pl.program_id(0)
    for one in range(count):

        @pl.when(step == one)
        def _(one=one):
            value = lax.dot_general(
                lefts[one][...],
                rights[one][...],
                (((0,), (1 if flipped else 0,)), ((), ())),
                preferred_element_type=F32,
            )
            if added:
                value = value + refs[2 * count][...].astype(F32)
            rows = value.shape[0] // len(outs)
            for place, out_ref in enumerate(outs):
                out_ref[...] = value[place * rows : (place + 1) * rows].astype(out_ref.dtype)


def grad_half(pairs, side, added, flipped):
    count = len(pairs)
    row_len, width = pairs[0][0].shape
    half = width // 2
    blocks = [pair[2] if len(pair) > 2 else 0 for pair in pairs]
    pairs = [pair[:2] for pair in pairs]
    columns = pairs[-1][1].shape[0 if flipped else 1]
    arrays = [left for left, _ in pairs] + [right for _, right in pairs]
    specs = [pl.BlockSpec((row_len, half), lambda k: (0, side))] * count
    for block in blocks:
        shape = (columns, row_len) if flipped else (row_len, columns)
        specs.append(pl.BlockSpec(shape, lambda k, block=block: (block, 0)))
    if added is None:
        types = [BF16]
    else:
        arrays.append(added)
        specs.append(pl.BlockSpec((half, columns), lambda k: (0, k)))
        types = [F32, F32, BF16, BF16]
    rows = half // len(types)
    return pl.pallas_call(
        functools.partial(grad_kernel, count, flipped, added is not None),
        grid=(count,),
        in_specs=specs,
        out_specs=[pl.BlockSpec((rows, columns), lambda k: (0, k))] * len(types),
        out_shape=[jax.ShapeDtypeStruct((rows, count * columns), kind) for kind in types],
        compiler_params=pltpu.CompilerParams(vmem_limit_bytes=VMEM_BYTES),
        cost_estimate=LIGHT,
    )(*arrays)


def reversed_bits(block):
    masks = MASKS
    flipped = jnp.zeros_like(block)
    for rank, mask in enumerate(masks):
        flipped = flipped + ((block >> (len(masks) - 1 - rank)) & 1) * mask
    return flipped


def order_matrix(width, dtype):
    chunk = width // DEVICES
    place = lax.broadcasted_iota(jnp.int32, (width, width), 1)
    source = lax.broadcasted_iota(jnp.int32, (width, width), 0)
    entry = (lax.axis_index("dp") ^ reversed_bits(place // chunk)) * chunk + place % chunk
    return (source == entry).astype(dtype)


def thirds(values):
    high = values.astype(BF16)
    rest = values - high.astype(F32)
    middle = rest.astype(BF16)
    return jnp.concatenate([high, middle, (rest - middle.astype(F32)).astype(BF16)], axis=0)


def reorder(values, matrix):
    if values.dtype == F32:
        rows = values.shape[0]
        value = jnp.dot(thirds(values), matrix, preferred_element_type=F32)
        return value[:rows] + value[rows : 2 * rows] + value[2 * rows :]
    return jnp.dot(values, matrix, preferred_element_type=F32).astype(values.dtype)


def restore(values, matrix):
    dims = (((1,), (1,)), ((), ()))
    if values.dtype == F32:
        rows = values.shape[0]
        value = lax.dot_general(thirds(values), matrix, dims, preferred_element_type=F32)
        return value[:rows] + value[rows : 2 * rows] + value[2 * rows :]
    return lax.dot_general(values, matrix, dims, preferred_element_type=F32).astype(values.dtype)


def back_kernel(count, flipped, *refs):
    lefts, weights = refs[:count], refs[count : 3 * count]
    kept_ref, sent_ref = refs[3 * count :]
    rows = kept_ref.shape[0]
    block = weights[0].shape[0]
    step = pl.program_id(0)
    for side in range(2):
        value = None
        for one in range(count):
            term = lax.dot_general(
                lefts[one][...],
                weights[2 * one + side][...],
                (((0 if flipped else 1,), (1,)), ((), ())),
                preferred_element_type=F32,
            )
            value = term if value is None else value + term
        start = pl.multiple_of((side * pl.num_programs(0) + step) * block, block)
        kept_ref[:, pl.ds(start, block)] = value[:rows]
        sent_ref[:, pl.ds(start, block)] = value[rows:].astype(BF16)


def project_back(lefts, weights, parts, flipped=False):
    count = len(lefts)
    half = weights[0][0].shape[0]
    block = half // 2
    row_len, inner = lefts[0].shape[::-1] if flipped else lefts[0].shape
    specs = [pl.BlockSpec(left.shape, lambda k: (0, 0)) for left in lefts]
    for part in parts:
        specs += [pl.BlockSpec((block, inner), lambda k, part=part: (k, part))] * 2
    flat = [side for halves in weights for side in halves]
    whole = pl.BlockSpec((row_len // 2, 2 * half), lambda k: (0, 0))
    return pl.pallas_call(
        functools.partial(back_kernel, count, flipped),
        grid=(2,),
        in_specs=specs,
        out_specs=[whole, whole],
        out_shape=[
            jax.ShapeDtypeStruct((row_len // 2, 2 * half), F32),
            jax.ShapeDtypeStruct((row_len // 2, 2 * half), BF16),
        ],
        compiler_params=pltpu.CompilerParams(vmem_limit_bytes=VMEM_BYTES),
        cost_estimate=LIGHT,
    )(*lefts, *flat)


def head_normed(raw, gain, cosine, sine):
    inverse = lax.rsqrt(jnp.mean(raw * raw, axis=0, keepdims=True) + EPSILON)
    normed = raw * inverse * gain
    half = raw.shape[0] // 2
    first, second = normed[:half], normed[half:]
    return jnp.concatenate(
        [first * cosine - second * sine, second * cosine + first * sine], axis=0
    )


def weighted_columns(weights, rows_ref, target_ref):
    width = weights[0].shape[0]
    value = None
    for part in range(len(weights)):
        term = lax.dot_general(
            weights[part][...],
            rows_ref[:, part * width : (part + 1) * width],
            (((0,), (1,)), ((), ())),
            preferred_element_type=F32,
        )
        value = term if value is None else value + term
    target_ref[...] = value.astype(target_ref.dtype)


def attend_kernel(
    groups,
    repeat,
    w0,
    w1,
    rows_ref,
    cos_ref,
    sin_ref,
    q_gain_ref,
    k_gain_ref,
    place_ref,
    first_ref,
    place_col_ref,
    raw_ref,
    q_ref,
    k_ref,
    v_ref,
    log_ref,
    out_ref,
    bias_ref,
):
    weighted_columns((w0, w1), rows_ref, raw_ref)
    places = place_col_ref[...]
    allowed = (places <= place_ref[...]) & (places >= first_ref[...])
    bias_ref[...] = jnp.where(allowed, 0.0, -1e30)
    cosine, sine = cos_ref[...], sin_ref[...]
    heads = groups * repeat

    def group_step(group, carry):
        k_row = pl.multiple_of(group * HD, HD)
        keys = head_normed(
            raw_ref[pl.ds(heads * HD + k_row, HD), :], k_gain_ref[...], cosine, sine
        ).astype(BF16)
        values = raw_ref[pl.ds((heads + groups) * HD + k_row, HD), :].astype(BF16)
        k_ref[pl.ds(k_row, HD), :] = keys
        v_ref[pl.ds(k_row, HD), :] = values
        for one in range(repeat):
            q_row = pl.multiple_of((group * repeat + one) * HD, HD)
            queries = head_normed(
                raw_ref[pl.ds(q_row, HD), :], q_gain_ref[...], cosine, sine
            ).astype(BF16)
            queries = queries * jnp.asarray(HD ** (-0.5), BF16)
            q_ref[pl.ds(q_row, HD), :] = queries
            scores = (
                lax.dot_general(
                    keys, queries, (((0,), (0,)), ((), ())), preferred_element_type=F32
                )
                + bias_ref[...]
            )
            peaks = jnp.max(scores, axis=0, keepdims=True)
            shifted = jnp.exp(scores - peaks)
            totals = jnp.sum(shifted, axis=0, keepdims=True)
            outputs = jnp.dot(values, shifted.astype(BF16), preferred_element_type=F32)
            out_ref[pl.ds(q_row, HD), :] = (outputs / totals).astype(BF16)
            log_ref[group * repeat + one] = peaks + jnp.log(totals)
        return carry

    lax.fori_loop(0, groups, group_step, 0)


def whole_block(value):
    return pl.BlockSpec(value.shape, lambda k: (0,) * len(value.shape))


def attend_rows(weights, rows, tables, groups, repeat):
    row_len = rows.shape[0]
    heads = groups * repeat
    columns = (heads + 2 * groups) * HD
    shapes = [
        jax.ShapeDtypeStruct((columns, row_len), F32),
        jax.ShapeDtypeStruct((heads * HD, row_len), BF16),
        jax.ShapeDtypeStruct((groups * HD, row_len), BF16),
        jax.ShapeDtypeStruct((groups * HD, row_len), BF16),
        jax.ShapeDtypeStruct((heads, 1, row_len), F32),
        jax.ShapeDtypeStruct((heads * HD, row_len), BF16),
    ]
    return pl.pallas_call(
        functools.partial(attend_kernel, groups, repeat),
        grid=(1,),
        in_specs=[pl.BlockSpec((weights[0].shape[0], columns), lambda k: (0, 0))] * 2
        + [whole_block(one) for one in (rows, *tables)],
        out_specs=[whole_block(one) for one in shapes],
        out_shape=shapes,
        scratch_shapes=[pltpu.VMEM((row_len, row_len), F32)],
        compiler_params=pltpu.CompilerParams(vmem_limit_bytes=VMEM_BYTES),
        cost_estimate=LIGHT,
    )(*weights, rows, *tables)


def head_back(raw, gain, grad_rot, cosine, sine):
    half = raw.shape[0] // 2
    first, second = grad_rot[:half], grad_rot[half:]
    grad = jnp.concatenate(
        [first * cosine + second * sine, second * cosine - first * sine], axis=0
    )
    inverse = lax.rsqrt(jnp.mean(raw * raw, axis=0, keepdims=True) + EPSILON)
    hat = raw * inverse
    terms = grad * hat
    grad_hat = grad * gain
    inner = jnp.mean(terms * gain, axis=0, keepdims=True)
    return inverse * (grad_hat - hat * inner), terms


def attend_back_kernel(
    groups,
    repeat,
    w0,
    w1,
    rows_ref,
    cos_ref,
    sin_ref,
    q_gain_ref,
    k_gain_ref,
    place_ref,
    first_ref,
    place_col_ref,
    raw_ref,
    q_ref,
    k_ref,
    v_ref,
    log_ref,
    grad_ref,
    q_part_ref,
    k_part_ref,
    bias_ref,
    outer_ref,
    q_terms_ref,
    k_terms_ref,
):
    weighted_columns((w0, w1), rows_ref, outer_ref)
    places = place_col_ref[...]
    allowed = (places <= place_ref[...]) & (places >= first_ref[...])
    bias_ref[...] = jnp.where(allowed, 0.0, -1e30)
    cosine, sine = cos_ref[...], sin_ref[...]
    heads = groups * repeat
    q_terms_ref[...] = jnp.zeros_like(q_terms_ref)
    k_terms_ref[...] = jnp.zeros_like(k_terms_ref)

    def group_step(group, carry):
        k_row = pl.multiple_of(group * HD, HD)
        keys = k_ref[pl.ds(k_row, HD), :]
        values = v_ref[pl.ds(k_row, HD), :]
        grad_keys = None
        for one in range(repeat):
            q_row = pl.multiple_of((group * repeat + one) * HD, HD)
            queries = q_ref[pl.ds(q_row, HD), :]
            outer = outer_ref[pl.ds(q_row, HD), :]
            scores = (
                lax.dot_general(
                    keys, queries, (((0,), (0,)), ((), ())), preferred_element_type=F32
                )
                + bias_ref[...]
            )
            attn_probs = jnp.exp(scores - log_ref[group * repeat + one])
            grad_probs = lax.dot_general(
                values, outer, (((0,), (0,)), ((), ())), preferred_element_type=F32
            )
            inner = jnp.sum(attn_probs * grad_probs, axis=0, keepdims=True)
            grad_scores = (attn_probs * (grad_probs - inner)).astype(BF16)
            grad_query = jnp.dot(keys, grad_scores, preferred_element_type=F32) * (HD ** (-0.5))
            grad_key = lax.dot_general(
                queries, grad_scores, (((1,), (1,)), ((), ())), preferred_element_type=F32
            )
            grad_value = lax.dot_general(
                outer,
                attn_probs.astype(BF16),
                (((1,), (1,)), ((), ())),
                preferred_element_type=F32,
            )
            grad_raw, terms = head_back(
                raw_ref[pl.ds(q_row, HD), :], q_gain_ref[...], grad_query, cosine, sine
            )
            grad_ref[pl.ds(q_row, HD), :] = grad_raw.astype(BF16)
            q_terms_ref[...] += terms
            if grad_keys is None:
                grad_keys, grad_values = grad_key, grad_value
            else:
                grad_keys, grad_values = grad_keys + grad_key, grad_values + grad_value
        grad_raw, terms = head_back(
            raw_ref[pl.ds(heads * HD + k_row, HD), :], k_gain_ref[...], grad_keys, cosine, sine
        )
        k_terms_ref[...] += terms
        grad_ref[pl.ds(heads * HD + k_row, HD), :] = grad_raw.astype(BF16)
        grad_ref[pl.ds((heads + groups) * HD + k_row, HD), :] = grad_values.astype(BF16)
        return carry

    lax.fori_loop(0, groups, group_step, 0)
    q_part_ref[...] = jnp.sum(q_terms_ref[...], axis=1, keepdims=True)
    k_part_ref[...] = jnp.sum(k_terms_ref[...], axis=1, keepdims=True)


def attend_rows_back(weights, rows, tables, kept, groups, repeat):
    row_len = rows.shape[0]
    heads = groups * repeat
    columns = (heads + 2 * groups) * HD
    shapes = [
        jax.ShapeDtypeStruct((columns, row_len), BF16),
        jax.ShapeDtypeStruct((HD, 1), F32),
        jax.ShapeDtypeStruct((HD, 1), F32),
    ]
    return pl.pallas_call(
        functools.partial(attend_back_kernel, groups, repeat),
        grid=(1,),
        in_specs=[
            pl.BlockSpec(
                (weights[0].shape[0], heads * HD), lambda k: (0, columns // (heads * HD))
            )
        ]
        * 2
        + [whole_block(one) for one in (rows, *tables, *kept)],
        out_specs=[whole_block(one) for one in shapes],
        out_shape=shapes,
        scratch_shapes=[
            pltpu.VMEM((row_len, row_len), F32),
            pltpu.VMEM((heads * HD, row_len), BF16),
            pltpu.VMEM((HD, row_len), F32),
            pltpu.VMEM((HD, row_len), F32),
        ],
        compiler_params=pltpu.CompilerParams(vmem_limit_bytes=VMEM_BYTES),
        cost_estimate=LIGHT,
    )(*weights, rows, *tables, *kept)


def hidden_kernel(
    gate_own, gate_other, up_own, up_other, down_own, down_other, rows_ref, cot_ref, *outs
):
    gate_grad_ref, up_grad_ref, act_ref = outs
    width = gate_own.shape[0]

    def summed(source_ref, own_ref, other_ref):
        return jnp.dot(
            source_ref[:, :width], own_ref[...], preferred_element_type=F32
        ) + jnp.dot(source_ref[:, width:], other_ref[...], preferred_element_type=F32)

    gate = summed(rows_ref, gate_own, gate_other)
    up = summed(rows_ref, up_own, up_other)
    grad_act = summed(cot_ref, down_own, down_other)
    sigmoid_gate = jax.nn.sigmoid(gate)
    silu = gate * sigmoid_gate
    act_ref[...] = (silu * up).astype(BF16)
    up_grad_ref[...] = (grad_act * silu).astype(BF16)
    gate_grad_ref[...] = (
        grad_act * up * (sigmoid_gate + silu * (1.0 - sigmoid_gate))
    ).astype(BF16)


def hidden_small(weights, rows, cot_rows):
    row_len, width = rows.shape
    columns = weights[0].shape[1] // 3
    block = 256 if columns % 256 == 0 else columns
    steps = columns // block
    specs = []
    for part in range(3):
        specs += [
            pl.BlockSpec((width // 2, block), lambda k, part=part: (0, part * steps + k))
        ] * 2
    whole = pl.BlockSpec((row_len, width), lambda k: (0, 0))
    return pl.pallas_call(
        hidden_kernel,
        grid=(steps,),
        in_specs=specs + [whole, whole],
        out_specs=[pl.BlockSpec((row_len, block), lambda k: (0, k))] * 3,
        out_shape=[jax.ShapeDtypeStruct((row_len, columns), BF16)] * 3,
        compiler_params=pltpu.CompilerParams(vmem_limit_bytes=VMEM_BYTES),
        cost_estimate=LIGHT,
    )(*weights, *weights, *weights, rows, cot_rows)


def row_places(own_rows):
    own = jnp.arange(own_rows, dtype=jnp.int32)
    index = lax.axis_index("tp")
    return jnp.concatenate([own + index * own_rows, own + (1 - index) * own_rows])


def document_tables(starts, places):
    inside = places[:, None] >= starts[None, :]
    firsts = jnp.max(jnp.where(inside, starts[None, :], 0), axis=1)
    return firsts, places - firsts


def meet_kernel(count, *refs):
    total = refs[0][...]
    for other_ref in refs[1:count]:
        total = total + other_ref[...].astype(F32)
    outs = refs[count:]
    if len(outs) == 1:
        outs[0][...] = total.astype(outs[0].dtype)
        return
    half = total.shape[0] // 2
    outs[0][...] = total[half:].astype(BF16)
    outs[1][...] = total[:half]


def meet(values, kind):
    rows, columns = values[0].shape
    steps = 3 if columns % 384 == 0 else 1
    block = columns // steps
    shapes = [(rows, kind)] if kind is not None else [(rows // 2, BF16), (rows // 2, F32)]
    return pl.pallas_call(
        functools.partial(meet_kernel, len(values)),
        grid=(steps,),
        in_specs=[pl.BlockSpec((rows, block), lambda k: (0, k))] * len(values),
        out_specs=[pl.BlockSpec((size, block), lambda k: (0, k)) for size, _ in shapes],
        out_shape=[jax.ShapeDtypeStruct((size, columns), kind) for size, kind in shapes],
        compiler_params=pltpu.CompilerParams(vmem_limit_bytes=VMEM_BYTES),
        cost_estimate=LIGHT,
    )(*values)


def norm_kernel(inputs_ref, kept_ref, other_ref, gain_ref, normed_ref, hat_ref, inv_ref, hidden_ref):
    hidden = inputs_ref[...] + kept_ref[...] + other_ref[...].astype(F32)
    normed, hat, inverse = norm_forward(hidden, gain_ref[...])
    normed_ref[...] = normed.astype(BF16)
    hat_ref[...] = hat
    inv_ref[...] = inverse
    hidden_ref[...] = hidden


def norm_hidden(inputs, kept, other, gain):
    rows, width = inputs.shape
    shapes = [(width, BF16), (width, F32), (1, F32), (width, F32)]
    return pl.pallas_call(
        norm_kernel,
        out_shape=[jax.ShapeDtypeStruct((rows, size), kind) for size, kind in shapes],
        compiler_params=pltpu.CompilerParams(vmem_limit_bytes=VMEM_BYTES),
        cost_estimate=LIGHT,
    )(inputs, kept, other, gain)


def norm_back_kernel(kept_ref, other_ref, hat_ref, inv_ref, gain_ref, base_ref, *outs):
    low_ref, grad_ref, gain_part_ref = outs
    incoming = kept_ref[...] + other_ref[...].astype(F32)
    hat = hat_ref[...]
    grad_hat = incoming * gain_ref[...]
    inner = jnp.mean(grad_hat * hat, axis=-1, keepdims=True)
    grad = base_ref[...].astype(F32) + inv_ref[...] * (grad_hat - hat * inner)
    low_ref[...] = grad.astype(BF16)
    grad_ref[...] = grad
    gain_part_ref[...] = jnp.sum(incoming * hat, axis=0, keepdims=True)


def norm_back(kept, other, hat, inverse, gain, base):
    rows, width = kept.shape
    shapes = [(rows, BF16), (rows, F32), (1, F32)]
    return pl.pallas_call(
        norm_back_kernel,
        out_shape=[jax.ShapeDtypeStruct((size, width), kind) for size, kind in shapes],
        compiler_params=pltpu.CompilerParams(vmem_limit_bytes=VMEM_BYTES),
        cost_estimate=LIGHT,
    )(kept, other, hat, inverse, gain, base)


class Gather:
    def __init__(self, program, shard):
        self.program = program
        self.near = shard

    def start(self, mask):
        if mask == 8:
            self.far = self.program.send(self.near, 8)
        elif mask == 4:
            self.next = self.program.send(self.near, 4)
        elif mask == 2:
            self.across = self.program.send(self.near, 2)
        else:
            self.other = self.program.send(self.own, 1)

    def start_last(self):
        self.last = self.program.send(self.next, 2)

    def arrive(self, mask):
        program = self.program
        if mask == 8:
            far = program.arrive(self.far)
            self.near = program.run(lambda *parts: jnp.concatenate(parts), self.near, far)
        elif mask == 4:
            self.next = program.arrive(self.next)
        elif mask == 2:
            self.across = program.arrive(self.across)
        else:
            self.halves = [self.own, program.arrive(self.other)]

    def arrive_last(self):
        last = self.program.arrive(self.last)
        parts = (self.near, self.next, self.across, last)
        self.own = self.program.run(lambda *parts: jnp.concatenate(parts), *parts)


class GatherAcross:
    def __init__(self, program, shard):
        self.program = program
        self.parts = [shard, None]
        self.sent = [None, None]
        self.next = [None, None]

    def start_across(self):
        self.sent[1] = self.program.send(self.parts[0], 2)

    def arrive_across(self):
        self.parts[1] = self.program.arrive(self.sent[1])

    def start(self, mask, part):
        self.sent[part] = self.program.send(self.parts[part], mask)

    def arrive(self, mask, part):
        other = self.program.arrive(self.sent[part])
        if mask == 8:
            self.parts[part] = self.program.run(
                lambda *parts: jnp.concatenate(parts), self.parts[part], other
            )
        else:
            self.next[part] = other

    def join(self):
        parts = (self.parts[0], self.next[0], self.parts[1], self.next[1])
        self.own = self.program.run(lambda *parts: jnp.concatenate(parts), *parts)

    def start_core(self):
        self.other = self.program.send(self.own, 1)

    def arrive_core(self):
        self.halves = [self.own, self.program.arrive(self.other)]


class Scatter:
    def __init__(self, program, pairs, flipped=False):
        self.program, self.flipped = program, flipped
        self.arrays = [pair[:2] for pair in pairs]
        self.blocks = [pair[2:] for pair in pairs]

    def half(self, side, added):
        def step(arrays, added):
            pairs = [(*pair, *block) for pair, block in zip(arrays, self.blocks)]
            return grad_half(pairs, side, added, self.flipped)

        return self.program.run(step, self.arrays, added)

    def core(self):
        self.core_step()
        self.core_send()

    def core_step(self):
        self.near = self.half(1, None)[0]

    def core_send(self):
        self.other = self.program.send(self.near, 1)

    def beside(self):
        parts = self.half(0, self.other)
        self.kept, self.kept_far, self.low, self.high = parts

    def arrive_core(self):
        self.other = self.program.arrive(self.other)

    def arrive_far(self):
        self.other = self.program.arrive(self.other)

    def send_high(self):
        self.other = self.program.send(self.high, 2)

    def send_low(self):
        self.across = self.program.send(self.low, 2)

    def meet_high(self):
        arrays = [self.kept_far, self.program.arrive(self.other)]
        self.near = self.program.run(lambda *arrays: meet(arrays, BF16)[0], *arrays)

    def arrive_low(self):
        self.across = self.program.arrive(self.across)

    def send(self, mask):
        self.other = self.program.send(self.near, mask)

    def meet_far(self):
        arrays = [self.kept, self.across, self.other]
        self.near, self.kept = self.program.run(lambda *arrays: meet(arrays, None), *arrays)

    def finish(self):
        arrays = [self.kept, self.other]
        self.kept = self.program.run(lambda *arrays: meet(arrays, F32)[0], *arrays)


def local_small(
    tokens,
    doc_starts,
    attn_gain,
    w_query,
    w_key,
    w_value,
    q_gain,
    k_gain,
    w_out,
    mlp_gain,
    w_gate,
    w_up,
    w_down,
    out_grad,
):
    width = tokens.shape[-1]
    own_rows = tokens.shape[1]
    groups = w_key.shape[1] // HD
    repeat = w_query.shape[1] // w_key.shape[1]
    query_cols, key_cols = w_query.shape[1], w_key.shape[1]
    columns = query_cols + 2 * key_cols
    ff_cols = w_gate.shape[1]
    cut = ff_cols // 3
    program = Program()
    run, send, arrive = program.run, program.send, program.arrive

    shards = [w_query, w_key, w_value, w_out]
    plan = [(one, 0, shard.shape[1]) for one, shard in enumerate(shards)]
    attn = Gather(program, run(lambda *parts: pack(parts, [plan]), *shards)[0])
    attn.start(8)
    plans = [[(one, at, at + cut) for one in range(3)] for at in range(0, ff_cols, cut)]
    packed = run(lambda *parts: pack(parts, plans), w_gate, w_up, w_down)
    first, second = (Gather(program, one) for one in packed[:2])
    third = GatherAcross(program, packed[2])

    matrix = order_matrix(width, BF16)
    places = row_places(own_rows)
    firsts, position = document_tables(doc_starts[0], places)
    cosine, sine = rope_tables(position, HD)

    def norm_tokens(tokens, attn_gain, mlp_gain):
        gains = reorder(jnp.stack([attn_gain, mlp_gain]), matrix)
        inputs = reorder(tokens, matrix).astype(F32)
        normed, hat, inverse = norm_forward(inputs, gains[0])
        return normed.astype(BF16), hat, inverse, inputs, gains

    normed_first, hat_first, inv_first, inputs, gains = run(
        norm_tokens, tokens[0], attn_gain, mlp_gain
    )
    attn_gain, mlp_gain = gains[0], gains[1]
    cotangent = run(lambda rows: reorder(rows, matrix), out_grad[0])

    def join_rows(own, other):
        return jnp.concatenate([own, other], axis=0)

    attn.arrive(8)
    attn.start(4)
    attn.start(2)
    first.start(8)
    rows_sent = send(normed_first, 0, 1)
    third.start_across()
    attn.arrive(4)
    attn.arrive(2)
    first.arrive(8)
    rows_first = run(join_rows, normed_first, arrive(rows_sent))
    third.arrive_across()
    attn.start_last()
    first.start(4)
    cot_sent = send(cotangent, 0, 1)
    third.start(8, 0)
    attn.arrive_last()
    first.arrive(4)
    cot_rows = run(join_rows, cotangent, arrive(cot_sent))
    third.arrive(8, 0)
    attn.start(1)
    tables = (
        cosine.T,
        sine.T,
        q_gain[:, None],
        k_gain[:, None],
        places[None, :],
        firsts[None, :],
        places[:, None],
    )
    attn.arrive(1)
    first.start(2)
    second.start(8)
    raw, queries, keys, values, logs, attended = run(
        lambda weights, rows: attend_rows(weights, rows, tables, groups, repeat),
        attn.halves,
        rows_first,
    )

    def back_rows(lefts, weights, parts, flipped=False):
        return run(
            lambda lefts, weights: project_back(lefts, weights, parts, flipped)[::-1],
            lefts,
            weights,
        )

    sent, kept = back_rows([attended], [attn.halves], [columns // query_cols], True)
    first.arrive(2)
    second.arrive(8)
    branch_sent = send(sent, 0, 1)
    first.start_last()
    second.start(4)
    third.start(8, 1)

    normed_second, hat_second, inv_second, hidden = run(
        norm_hidden, inputs, kept, arrive(branch_sent), mlp_gain[None]
    )
    first.arrive_last()
    second.arrive(4)
    third.arrive(8, 1)
    rows_sent = send(normed_second, 0, 1)
    first.start(1)
    second.start(2)
    third.start(4, 0)
    rows_second = run(join_rows, normed_second, arrive(rows_sent))
    first.arrive(1)
    second.arrive(2)
    third.arrive(4, 0)
    second.start_last()
    third.start(4, 1)

    def hidden_third(one):
        parts = run(hidden_small, one.halves, rows_second, cot_rows)
        return parts, [(rows_second, parts[0]), (rows_second, parts[1]), (cot_rows, parts[2])]

    parts_one, pairs = hidden_third(first)
    sum_one = Scatter(program, pairs)
    sum_one.core()
    second.arrive_last()
    third.arrive(4, 1)
    third.join()
    sum_one.arrive_core()
    sum_one.beside()
    second.start(1)
    third.start_core()
    second.arrive(1)
    parts_two, pairs = hidden_third(second)
    sum_two = Scatter(program, pairs)
    third.arrive_core()
    sum_two.core_step()
    sum_one.send_high()
    sum_two.core_send()
    parts_three, pairs = hidden_third(third)
    sum_three = Scatter(program, pairs)
    sum_three.core_step()
    parts = (parts_one, parts_two, parts_three)
    thirds_halves = [first.halves, second.halves, third.halves]
    sent, kept = back_rows(
        [one for part in parts for one in part[:2]],
        [halves for halves in thirds_halves for _ in range(2)],
        [0, 1] * 3,
    )
    sum_one.meet_high()
    sum_two.arrive_core()
    grad_sent = send(sent, 0, 1)
    sum_one.send_low()
    sum_one.send(4)
    sum_three.core_send()
    sum_two.beside()
    result_part = back_rows([part[2] for part in parts], thirds_halves, [2] * 3)
    sum_three.arrive_core()
    sum_one.arrive_low()
    sum_one.arrive_far()
    grad_branch, grad_hidden, mlp_gain_part = run(
        norm_back, kept, arrive(grad_sent), hat_second, inv_second, mlp_gain[None], cotangent
    )
    rows_sent = send(grad_branch, 0, 1)
    sum_two.send_high()
    sum_one.meet_far()
    sum_three.beside()
    sum_two.meet_high()
    branch_rows = run(join_rows, grad_branch, arrive(rows_sent))
    sum_two.send_low()
    sum_two.send(4)
    sum_one.send(8)
    result_sent = send(result_part[0], 0, 1)
    grads, q_gain_part, k_gain_part = run(
        lambda weights, rows, kept: attend_rows_back(weights, rows, tables, kept, groups, repeat),
        attn.halves,
        branch_rows,
        (raw, queries, keys, values, logs),
    )
    sent, kept = back_rows([grads], [attn.halves], [0], True)
    pairs = [(rows_first, grads, block) for block in range(columns // query_cols)]
    sum_attn = Scatter(program, [*pairs, (branch_rows, attended)], True)
    sum_attn.core_step()
    sum_two.arrive_low()
    sum_two.arrive_far()
    sum_one.arrive_far()
    result_other = arrive(result_sent)
    sum_attn.core_send()
    sum_two.meet_far()
    sum_attn.arrive_core()
    sum_attn.beside()
    grad_sent = send(sent, 0, 1)
    sum_three.send_high()
    sum_attn.send_high()
    sum_two.send(8)
    sum_one.finish()
    result = run(
        lambda hidden, kept, other: restore((hidden + kept + other.astype(F32)).astype(BF16), matrix),
        hidden,
        result_part[1],
        result_other,
    )
    sum_three.meet_high()
    sum_attn.meet_high()
    grad_other = arrive(grad_sent)
    sum_two.arrive_far()
    sum_three.send_low()
    sum_three.send(4)
    sum_attn.send_low()
    sum_attn.send(4)
    sum_two.finish()
    tokens_grad, _, attn_gain_part = run(
        norm_back, kept, grad_other, hat_first, inv_first, attn_gain[None], grad_hidden
    )

    def gain_parts(attn_part, mlp_part, q_part, k_part):
        both = restore(jnp.concatenate([attn_part, mlp_part]), matrix)
        return jnp.concatenate([both[0], both[1], q_part[:, 0], k_part[:, 0]])

    total = run(gain_parts, attn_gain_part, mlp_gain_part, q_gain_part, k_gain_part)

    def total_send(*partners):
        return [send(total, *partner) for partner in partners]

    def total_arrive(sent):
        return run(sum, [total] + [arrive(one) for one in sent])

    gains_sent = total_send((0, 1))
    sum_three.arrive_low()
    sum_three.arrive_far()
    sum_three.meet_far()
    sum_attn.arrive_low()
    sum_attn.arrive_far()
    sum_attn.meet_far()
    total = total_arrive(gains_sent)
    sum_three.send(8)
    sum_attn.send(8)
    gains_sent = total_send((1,), (2,), (3,))
    sum_three.arrive_far()
    sum_three.finish()
    sum_attn.arrive_far()
    sum_attn.finish()
    total = total_arrive(gains_sent)
    gains_sent = total_send((4,), (8,), (12,))
    total = total_arrive(gains_sent)

    sums = [one.kept for one in (sum_one, sum_two, sum_three)]
    gate_grad, up_grad, down_grad = (
        jnp.concatenate([one[:, part * cut : (part + 1) * cut] for one in sums], axis=1)
        for part in range(3)
    )
    kept = sum_attn.kept
    return (
        result[None],
        restore(tokens_grad, matrix)[None],
        total[:width],
        kept[:, :query_cols],
        kept[:, query_cols : query_cols + key_cols],
        kept[:, query_cols + key_cols : columns],
        total[2 * width : 2 * width + HD],
        total[2 * width + HD :],
        kept[:, columns:],
        total[width : 2 * width],
        gate_grad,
        up_grad,
        down_grad,
    )


def local(*arrays):
    small = lax.axis_size("dp") == DEVICES and lax.axis_size("tp") == 2
    if small and arrays[0].shape[1:] == (256, 1024):
        return local_small(*arrays)
    return local_large(*arrays)


def solution(mesh):
    in_specs = (
        P("dp", "tp", None),
        P("dp", None),
        P(),
        P("dp", "tp"),
        P("dp", "tp"),
        P("dp", "tp"),
        P(),
        P(),
        P("dp", "tp"),
        P(),
        P("dp", "tp"),
        P("dp", "tp"),
        P("dp", "tp"),
        P("dp", "tp", None),
    )
    out_specs = (
        P("dp", "tp", None),
        P("dp", "tp", None),
        P(),
        P("dp", "tp"),
        P("dp", "tp"),
        P("dp", "tp"),
        P(),
        P(),
        P("dp", "tp"),
        P(),
        P("dp", "tp"),
        P("dp", "tp"),
        P("dp", "tp"),
    )
    return jax.shard_map(local, mesh=mesh, in_specs=in_specs, out_specs=out_specs, check_vma=False)
```

```python
import functools

import jax
import jax.numpy as jnp
from jax import lax
from jax.experimental import pallas as pl
from jax.experimental.pallas import tpu as pltpu
from jax.sharding import PartitionSpec as P

HD = 64


EPSILON = 1e-05
THETA = 1000000.0


def documents(starts, length):
    places = jnp.arange(length, dtype=jnp.int32)
    inside = places[:, None] >= starts[None, :]
    segment = jnp.sum(inside.astype(jnp.int32), axis=1) - 1
    firsts = jnp.max(jnp.where(inside, starts[None, :], 0), axis=1)
    return (segment, places - firsts)


def rope_tables(position, width):
    half_width = width // 2
    freqs = THETA ** (-(jnp.arange(half_width, dtype=jnp.float32) * 2.0 / width))
    angles = position.astype(jnp.float32)[:, None] * freqs[None, :]
    return (jnp.cos(angles), jnp.sin(angles))


def rotate(values, cosine, sine):
    half_width = values.shape[-1] // 2
    first_half = values[..., :half_width]
    second_half = values[..., half_width:]
    tile_shape = (values.shape[0],) + (1,) * (values.ndim - 2) + (half_width,)
    cos_tile = cosine.reshape(tile_shape)
    sin_tile = sine.reshape(tile_shape)
    return jnp.concatenate(
        [
            first_half * cos_tile - second_half * sin_tile,
            second_half * cos_tile + first_half * sin_tile,
        ],
        axis=-1,
    )


def norm_forward(values, gain):
    inverse = lax.rsqrt(jnp.mean(values * values, axis=-1, keepdims=True) + EPSILON)
    normed_hat = values * inverse
    return (normed_hat * gain, normed_hat, inverse)


def norm_backward(grad_normed, normed_hat, inverse, gain):
    grad_hat = grad_normed * gain
    grad_values = inverse * (
        grad_hat - normed_hat * jnp.mean(grad_hat * normed_hat, axis=-1, keepdims=True)
    )
    gain_part = jnp.sum((grad_normed * normed_hat).reshape(-1, normed_hat.shape[-1]), axis=0)
    return (grad_values, gain_part)


def gather_rows(values):
    return lax.all_gather(values, "tp", axis=0, tiled=True)


def sum_rows(left_rows, right_weight):
    return lax.psum_scatter(
        jnp.dot(left_rows, right_weight.T, preferred_element_type=jnp.float32).astype(jnp.bfloat16),
        "tp",
        scatter_dimension=0,
        tiled=True,
    ).astype(jnp.float32)


def masked_scores(query_block, key_rows, block_segment, block_places, segment, places, score_scale):
    scores = (
        jnp.einsum("qgrd,kgd->grqk", query_block, key_rows, preferred_element_type=jnp.float32)
        * score_scale
    )
    allowed = (places[None, :] <= block_places[:, None]) & (
        segment[None, :] == block_segment[:, None]
    )
    return jnp.where(allowed, scores, -1e30)


def attend(query_rows, key_rows, value_rows, segment, block_rows):
    row_len = query_rows.shape[0]
    blocks = row_len // block_rows
    places = jnp.arange(row_len, dtype=jnp.int32)
    score_scale = query_rows.shape[-1] ** (-0.5)

    def block_out(block_item):
        query_block, block_segment, block_places = block_item
        scores = masked_scores(
            query_block, key_rows, block_segment, block_places, segment, places, score_scale
        )
        peaks = jnp.max(scores, axis=-1, keepdims=True)
        shifted = jnp.exp(scores - peaks)
        totals = jnp.sum(shifted, axis=-1, keepdims=True)
        attn_probs = (shifted / totals).astype(jnp.bfloat16)
        outputs = jnp.einsum(
            "grqk,kgd->qgrd", attn_probs, value_rows, preferred_element_type=jnp.float32
        )
        return (outputs, (peaks + jnp.log(totals))[..., 0])

    outputs, log_totals = lax.map(
        block_out,
        (
            query_rows.reshape((blocks, block_rows) + query_rows.shape[1:]),
            segment.reshape(blocks, block_rows),
            places.reshape(blocks, block_rows),
        ),
    )
    return (outputs.reshape(query_rows.shape), log_totals)


def attend_back(query_rows, key_rows, value_rows, grad_out, log_totals, segment, block_rows):
    row_len = query_rows.shape[0]
    blocks = row_len // block_rows
    places = jnp.arange(row_len, dtype=jnp.int32)
    score_scale = query_rows.shape[-1] ** (-0.5)

    def block_back(carry, block_item):
        grad_keys, grad_values = carry
        query_block, grad_block, total_block, block_segment, block_places = block_item
        scores = masked_scores(
            query_block, key_rows, block_segment, block_places, segment, places, score_scale
        )
        attn_probs = jnp.exp(scores - total_block[..., None])
        grad_probs = jnp.einsum(
            "qgrd,kgd->grqk", grad_block, value_rows, preferred_element_type=jnp.float32
        )
        inner = jnp.sum(attn_probs * grad_probs, axis=-1, keepdims=True)
        grad_scores = (attn_probs * (grad_probs - inner)).astype(jnp.bfloat16)
        grad_query = (
            jnp.einsum("grqk,kgd->qgrd", grad_scores, key_rows, preferred_element_type=jnp.float32)
            * score_scale
        )
        grad_keys = (
            grad_keys
            + jnp.einsum(
                "grqk,qgrd->kgd", grad_scores, query_block, preferred_element_type=jnp.float32
            )
            * score_scale
        )
        grad_values = grad_values + jnp.einsum(
            "grqk,qgrd->kgd",
            attn_probs.astype(jnp.bfloat16),
            grad_block,
            preferred_element_type=jnp.float32,
        )
        return ((grad_keys, grad_values), grad_query)

    zeros_kv = jnp.zeros(key_rows.shape, jnp.float32)
    block_shape = (blocks, block_rows) + query_rows.shape[1:]
    (grad_keys, grad_values), grad_queries = lax.scan(
        block_back,
        (zeros_kv, zeros_kv),
        (
            query_rows.reshape(block_shape),
            grad_out.reshape(block_shape),
            log_totals,
            segment.reshape(blocks, block_rows),
            places.reshape(blocks, block_rows),
        ),
    )
    return (grad_queries.reshape(query_rows.shape), grad_keys, grad_values)


def local_large(
    tokens,
    doc_starts,
    attn_gain,
    w_query,
    w_key,
    w_value,
    q_gain,
    k_gain,
    w_out,
    mlp_gain,
    w_gate,
    w_up,
    w_down,
    out_grad,
):
    query_w, key_w, value_w, out_w, gate_w, up_w, down_w = (
        lax.all_gather(w_query, "dp", axis=0, tiled=True),
        lax.all_gather(w_key, "dp", axis=0, tiled=True),
        lax.all_gather(w_value, "dp", axis=0, tiled=True),
        lax.all_gather(w_out, "dp", axis=0, tiled=True),
        lax.all_gather(w_gate, "dp", axis=0, tiled=True),
        lax.all_gather(w_up, "dp", axis=0, tiled=True),
        lax.all_gather(w_down, "dp", axis=0, tiled=True),
    )
    inputs = tokens[0].astype(jnp.float32)
    cotangent = out_grad[0]
    own_rows = inputs.shape[0]
    row_len = own_rows * lax.axis_size("tp")
    head_dim = HD
    groups = key_w.shape[1] // head_dim
    repeat = query_w.shape[1] // key_w.shape[1]
    query_cols = query_w.shape[1]
    key_cols = key_w.shape[1]
    ff_cols = gate_w.shape[1]
    block_rows = min(512, row_len)
    segment, position = documents(doc_starts[0], row_len)
    cosine, sine = rope_tables(position, head_dim)
    qkv_weight = jnp.concatenate([query_w, key_w, value_w], axis=1)
    gate_up_weight = jnp.concatenate([gate_w, up_w], axis=1)
    normed_first, hat_first, inv_first = norm_forward(inputs, attn_gain)
    rows_first = gather_rows(normed_first.astype(jnp.bfloat16))
    projected = jnp.dot(rows_first, qkv_weight, preferred_element_type=jnp.float32)
    query_raw = projected[:, :query_cols].reshape(row_len, groups, repeat, head_dim)
    key_raw = projected[:, query_cols : query_cols + key_cols].reshape(row_len, groups, head_dim)
    value_rows = (
        projected[:, query_cols + key_cols :]
        .astype(jnp.bfloat16)
        .reshape(row_len, groups, head_dim)
    )
    query_normed, query_hat, query_inv = norm_forward(query_raw, q_gain)
    key_normed, key_hat, key_inv = norm_forward(key_raw, k_gain)
    query_rows = rotate(query_normed, cosine, sine).astype(jnp.bfloat16)
    key_rows = rotate(key_normed, cosine, sine).astype(jnp.bfloat16)
    attended, log_totals = attend(query_rows, key_rows, value_rows, segment, block_rows)
    attended = attended.reshape(row_len, query_cols).astype(jnp.bfloat16)
    branch_out = sum_rows(attended, out_w)
    hidden = inputs + branch_out
    normed_second, hat_second, inv_second = norm_forward(hidden, mlp_gain)
    rows_second = gather_rows(normed_second.astype(jnp.bfloat16))
    gate_up = jnp.dot(rows_second, gate_up_weight, preferred_element_type=jnp.float32)
    gate_pre = gate_up[:, :ff_cols]
    up_pre = gate_up[:, ff_cols:]
    sigmoid_gate = jax.nn.sigmoid(gate_pre)
    activated = (gate_pre * sigmoid_gate * up_pre).astype(jnp.bfloat16)
    result = hidden + sum_rows(activated, down_w)
    cot_rows = gather_rows(cotangent)
    grad_act = jnp.dot(cot_rows, down_w, preferred_element_type=jnp.float32)
    grad_down = jnp.einsum("rd,rf->df", cot_rows, activated, preferred_element_type=jnp.float32)
    grad_gate = grad_act * up_pre * sigmoid_gate * (1.0 + gate_pre * (1.0 - sigmoid_gate))
    grad_up = grad_act * gate_pre * sigmoid_gate
    grad_gate_up = jnp.concatenate([grad_gate, grad_up], axis=1).astype(jnp.bfloat16)
    grad_gate_up_w = jnp.einsum(
        "rd,rf->df", rows_second, grad_gate_up, preferred_element_type=jnp.float32
    )
    grad_normed_second = sum_rows(grad_gate_up, gate_up_weight)
    grad_hidden_norm, mlp_gain_part = norm_backward(
        grad_normed_second, hat_second, inv_second, mlp_gain
    )
    grad_hidden = cotangent.astype(jnp.float32) + grad_hidden_norm
    grad_branch = grad_hidden.astype(jnp.bfloat16)
    branch_rows = gather_rows(grad_branch)
    grad_out_w = jnp.einsum("rd,rq->dq", branch_rows, attended, preferred_element_type=jnp.float32)
    grad_attended = jnp.dot(branch_rows, out_w, preferred_element_type=jnp.float32).astype(
        jnp.bfloat16
    )
    grad_query_rot, grad_key_rot, grad_value = attend_back(
        query_rows,
        key_rows,
        value_rows,
        grad_attended.reshape(row_len, groups, repeat, head_dim),
        log_totals,
        segment,
        block_rows,
    )
    grad_query_norm = rotate(grad_query_rot, cosine, -sine)
    grad_key_norm = rotate(grad_key_rot, cosine, -sine)
    grad_query_raw, q_gain_part = norm_backward(grad_query_norm, query_hat, query_inv, q_gain)
    grad_key_raw, k_gain_part = norm_backward(grad_key_norm, key_hat, key_inv, k_gain)
    grad_projected = jnp.concatenate(
        [
            grad_query_raw.reshape(row_len, query_cols),
            grad_key_raw.reshape(row_len, key_cols),
            grad_value.reshape(row_len, key_cols),
        ],
        axis=1,
    ).astype(jnp.bfloat16)
    grad_qkv_w = jnp.einsum(
        "rd,rf->df", rows_first, grad_projected, preferred_element_type=jnp.float32
    )
    grad_normed_first = sum_rows(grad_projected, qkv_weight)
    grad_input_norm, attn_gain_part = norm_backward(
        grad_normed_first, hat_first, inv_first, attn_gain
    )
    grad_inputs = grad_hidden + grad_input_norm
    summed = (
        lax.psum_scatter(
            grad_qkv_w[:, :query_cols].astype(jnp.bfloat16), "dp", scatter_dimension=0, tiled=True
        ).astype(jnp.float32),
        lax.psum_scatter(
            grad_qkv_w[:, query_cols : query_cols + key_cols].astype(jnp.bfloat16),
            "dp",
            scatter_dimension=0,
            tiled=True,
        ).astype(jnp.float32),
        lax.psum_scatter(
            grad_qkv_w[:, query_cols + key_cols :].astype(jnp.bfloat16),
            "dp",
            scatter_dimension=0,
            tiled=True,
        ).astype(jnp.float32),
        lax.psum_scatter(
            grad_out_w.astype(jnp.bfloat16), "dp", scatter_dimension=0, tiled=True
        ).astype(jnp.float32),
        lax.psum_scatter(
            grad_gate_up_w[:, :ff_cols].astype(jnp.bfloat16), "dp", scatter_dimension=0, tiled=True
        ).astype(jnp.float32),
        lax.psum_scatter(
            grad_gate_up_w[:, ff_cols:].astype(jnp.bfloat16), "dp", scatter_dimension=0, tiled=True
        ).astype(jnp.float32),
        lax.psum_scatter(
            grad_down.astype(jnp.bfloat16), "dp", scatter_dimension=0, tiled=True
        ).astype(jnp.float32),
    )
    gains = lax.psum((attn_gain_part, q_gain_part, k_gain_part, mlp_gain_part), ("dp", "tp"))
    return (
        result.astype(jnp.bfloat16)[None],
        grad_inputs.astype(jnp.bfloat16)[None],
        gains[0],
        summed[0],
        summed[1],
        summed[2],
        gains[1],
        gains[2],
        summed[3],
        gains[3],
        summed[4],
        summed[5],
        summed[6],
    )


F32 = jnp.float32
BF16 = jnp.bfloat16
VMEM_BYTES = 26 * 1024 * 1024
LIGHT = pl.CostEstimate(flops=1000, bytes_accessed=1000, transcendentals=0)


DEVICES = 16
MASKS = (1, 2, 4, 8)


def tied(values, *others):
    return lax.optimization_barrier((values, *others))[0]


class Program:
    def __init__(self):
        self.arrival = None
        self.step = None

    def begun(self):
        return [one for one in (self.arrival, self.step) if one is not None]

    def ready(self, *values):
        out = lax.optimization_barrier((*values, *self.begun()))[: len(values)]
        return out if len(out) > 1 else out[0]

    def run(self, function, *values):
        flat, tree = jax.tree.flatten(values)
        flat = lax.optimization_barrier((*flat, *self.begun()))[: len(flat)]
        out = function(*jax.tree.unflatten(tree, flat))
        self.step = jax.tree.leaves(out)[0]
        return out

    def send(self, values, mask, across=0):
        pairs = []
        for own in range(DEVICES):
            for side in range(2):
                pairs.append((own * 2 + side, (own ^ mask) * 2 + (side ^ across)))
        return lax.ppermute(self.ready(values), ("dp", "tp"), pairs)

    def arrive(self, other):
        if self.arrival is not None:
            other = tied(other, self.arrival)
        self.arrival = other
        return other


def copy_kernel(count, moves, *refs):
    semaphores = refs[-1]
    copies = []
    for place, (source, rows, columns, target, row, column) in enumerate(moves):
        size, width = rows[1] - rows[0], columns[1] - columns[0]
        copies.append(
            pltpu.make_async_copy(
                refs[source].at[rows[0] : rows[1], columns[0] : columns[1]],
                refs[count + target].at[row : row + size, column : column + width],
                semaphores.at[place],
            )
        )
    for copy in copies:
        copy.start()
    for copy in copies:
        copy.wait()


def copy_blocks(arrays, moves, shapes):
    return pl.pallas_call(
        functools.partial(copy_kernel, len(arrays), moves),
        in_specs=[pl.BlockSpec(memory_space=pl.ANY)] * len(arrays),
        out_specs=[pl.BlockSpec(memory_space=pl.ANY)] * len(shapes),
        out_shape=[jax.ShapeDtypeStruct(shape, arrays[0].dtype) for shape in shapes],
        scratch_shapes=[pltpu.SemaphoreType.DMA((len(moves),))],
        compiler_params=pltpu.CompilerParams(vmem_limit_bytes=VMEM_BYTES),
        cost_estimate=LIGHT,
    )(*arrays)


def pack(shards, plans):
    rows = shards[0].shape[0]
    moves, shapes = [], []
    for target, plan in enumerate(plans):
        column = 0
        for source, start, stop in plan:
            moves.append((source, (0, rows), (start, stop), target, 0, column))
            column += stop - start
        shapes.append((rows, column))
    return copy_blocks(shards, moves, shapes)


def stack(*parts):
    moves, row = [], 0
    for source, part in enumerate(parts):
        moves.append((source, (0, part.shape[0]), (0, part.shape[1]), 0, row, 0))
        row += part.shape[0]
    return copy_blocks(parts, moves, [(row, parts[0].shape[1])])[0]


def grad_kernel(count, flipped, added, *refs):
    lefts, rights = refs[:count], refs[count : 2 * count]
    outs = refs[2 * count + (1 if added else 0) :]
    step = pl.program_id(0)
    for one in range(count):

        @pl.when(step == one)
        def _(one=one):
            value = lax.dot_general(
                lefts[one][...],
                rights[one][...],
                (((0,), (1 if flipped else 0,)), ((), ())),
                preferred_element_type=F32,
            )
            if added:
                value = value + refs[2 * count][...].astype(F32)
            rows = value.shape[0] // len(outs)
            for place, out_ref in enumerate(outs):
                out_ref[...] = value[place * rows : (place + 1) * rows].astype(out_ref.dtype)


def grad_half(pairs, side, added, flipped, across=False):
    count = len(pairs)
    row_len, width = pairs[0][0].shape
    half = width // 2
    blocks = [pair[2] if len(pair) > 2 else 0 for pair in pairs]
    pairs = [pair[:2] for pair in pairs]
    columns = pairs[-1][1].shape[0 if flipped else 1]
    arrays = [left for left, _ in pairs] + [right for _, right in pairs]
    specs = [pl.BlockSpec((row_len, half), lambda k: (0, side))] * count
    for block in blocks:
        shape = (columns, row_len) if flipped else (row_len, columns)
        specs.append(pl.BlockSpec(shape, lambda k, block=block: (block, 0)))
    if added is None:
        types = [BF16]
    else:
        arrays.append(added)
        specs.append(pl.BlockSpec((half, columns), lambda k: (0, k)))
        types = [F32, BF16, F32, BF16] if across else [F32, F32, BF16, BF16]
    rows = half // len(types)
    return pl.pallas_call(
        functools.partial(grad_kernel, count, flipped, added is not None),
        grid=(count,),
        in_specs=specs,
        out_specs=[pl.BlockSpec((rows, columns), lambda k: (0, k))] * len(types),
        out_shape=[jax.ShapeDtypeStruct((rows, count * columns), kind) for kind in types],
        compiler_params=pltpu.CompilerParams(vmem_limit_bytes=VMEM_BYTES),
        cost_estimate=LIGHT,
    )(*arrays)


def reversed_bits(block):
    masks = MASKS
    flipped = jnp.zeros_like(block)
    for rank, mask in enumerate(masks):
        flipped = flipped + ((block >> (len(masks) - 1 - rank)) & 1) * mask
    return flipped


def order_matrix(width, dtype):
    chunk = width // DEVICES
    place = lax.broadcasted_iota(jnp.int32, (width, width), 1)
    source = lax.broadcasted_iota(jnp.int32, (width, width), 0)
    entry = (lax.axis_index("dp") ^ reversed_bits(place // chunk)) * chunk + place % chunk
    return (source == entry).astype(dtype)


def thirds(values):
    high = values.astype(BF16)
    rest = values - high.astype(F32)
    middle = rest.astype(BF16)
    return jnp.concatenate([high, middle, (rest - middle.astype(F32)).astype(BF16)], axis=0)


def reorder(values, matrix):
    if values.dtype == F32:
        rows = values.shape[0]
        value = jnp.dot(thirds(values), matrix, preferred_element_type=F32)
        return value[:rows] + value[rows : 2 * rows] + value[2 * rows :]
    return jnp.dot(values, matrix, preferred_element_type=F32).astype(values.dtype)


def restore(values, matrix):
    dims = (((1,), (1,)), ((), ()))
    if values.dtype == F32:
        rows = values.shape[0]
        value = lax.dot_general(thirds(values), matrix, dims, preferred_element_type=F32)
        return value[:rows] + value[rows : 2 * rows] + value[2 * rows :]
    return lax.dot_general(values, matrix, dims, preferred_element_type=F32).astype(values.dtype)


def back_kernel(count, flipped, *refs):
    lefts, weights = refs[:count], refs[count : 3 * count]
    kept_ref, sent_ref = refs[3 * count :]
    rows = kept_ref.shape[0]
    block = weights[0].shape[0]
    step = pl.program_id(0)
    for side in range(2):
        value = None
        for one in range(count):
            term = lax.dot_general(
                lefts[one][...],
                weights[2 * one + side][...],
                (((0 if flipped else 1,), (1,)), ((), ())),
                preferred_element_type=F32,
            )
            value = term if value is None else value + term
        start = pl.multiple_of((side * pl.num_programs(0) + step) * block, block)
        kept_ref[:, pl.ds(start, block)] = value[:rows]
        sent_ref[:, pl.ds(start, block)] = value[rows:].astype(BF16)


def project_back(lefts, weights, parts, flipped=False):
    count = len(lefts)
    half = weights[0][0].shape[0]
    block = half // 2
    row_len, inner = lefts[0].shape[::-1] if flipped else lefts[0].shape
    specs = [pl.BlockSpec(left.shape, lambda k: (0, 0)) for left in lefts]
    for part in parts:
        specs += [pl.BlockSpec((block, inner), lambda k, part=part: (k, part))] * 2
    flat = [side for halves in weights for side in halves]
    whole = pl.BlockSpec((row_len // 2, 2 * half), lambda k: (0, 0))
    return pl.pallas_call(
        functools.partial(back_kernel, count, flipped),
        grid=(2,),
        in_specs=specs,
        out_specs=[whole, whole],
        out_shape=[
            jax.ShapeDtypeStruct((row_len // 2, 2 * half), F32),
            jax.ShapeDtypeStruct((row_len // 2, 2 * half), BF16),
        ],
        compiler_params=pltpu.CompilerParams(vmem_limit_bytes=VMEM_BYTES),
        cost_estimate=LIGHT,
    )(*lefts, *flat)


def head_normed(raw, gain, cosine, sine):
    inverse = lax.rsqrt(jnp.mean(raw * raw, axis=0, keepdims=True) + EPSILON)
    normed = raw * inverse * gain
    half = raw.shape[0] // 2
    first, second = normed[:half], normed[half:]
    return jnp.concatenate(
        [first * cosine - second * sine, second * cosine + first * sine], axis=0
    )


def weighted_columns(weights, rows_ref, target_ref):
    width = weights[0].shape[0]
    value = None
    for part in range(len(weights)):
        term = lax.dot_general(
            weights[part][...],
            rows_ref[:, part * width : (part + 1) * width],
            (((0,), (1,)), ((), ())),
            preferred_element_type=F32,
        )
        value = term if value is None else value + term
    target_ref[...] = value.astype(target_ref.dtype)


def attend_kernel(
    groups,
    repeat,
    w0,
    w1,
    rows_ref,
    table_ref,
    bias_ref,
    raw_ref,
    q_ref,
    k_ref,
    v_ref,
    log_ref,
    out_ref,
):
    weighted_columns((w0, w1), rows_ref, raw_ref)
    half = HD // 2
    cosine, sine = table_ref[:half, :], table_ref[half:HD, :]
    q_gain, k_gain = table_ref[HD : 2 * HD, :], table_ref[2 * HD :, :]
    heads = groups * repeat

    def group_step(group, carry):
        k_row = pl.multiple_of(group * HD, HD)
        keys = head_normed(
            raw_ref[pl.ds(heads * HD + k_row, HD), :], k_gain, cosine, sine
        ).astype(BF16)
        values = raw_ref[pl.ds((heads + groups) * HD + k_row, HD), :].astype(BF16)
        k_ref[pl.ds(k_row, HD), :] = keys
        v_ref[pl.ds(k_row, HD), :] = values
        for one in range(repeat):
            q_row = pl.multiple_of((group * repeat + one) * HD, HD)
            queries = head_normed(
                raw_ref[pl.ds(q_row, HD), :], q_gain, cosine, sine
            ).astype(BF16)
            queries = queries * jnp.asarray(HD ** (-0.5), BF16)
            q_ref[pl.ds(q_row, HD), :] = queries
            scores = (
                lax.dot_general(
                    keys, queries, (((0,), (0,)), ((), ())), preferred_element_type=F32
                )
                + bias_ref[...].astype(F32)
            )
            peaks = jnp.max(scores, axis=0, keepdims=True)
            shifted = jnp.exp(scores - peaks)
            totals = jnp.sum(shifted, axis=0, keepdims=True)
            outputs = jnp.dot(values, shifted.astype(BF16), preferred_element_type=F32)
            out_ref[pl.ds(q_row, HD), :] = (outputs / totals).astype(BF16)
            log_ref[group * repeat + one] = peaks + jnp.log(totals)
        return carry

    lax.fori_loop(0, groups, group_step, 0)


def whole_block(value):
    return pl.BlockSpec(value.shape, lambda k: (0,) * len(value.shape))


def attend_rows(weights, rows, tables, groups, repeat):
    row_len = rows.shape[0]
    heads = groups * repeat
    columns = (heads + 2 * groups) * HD
    shapes = [
        jax.ShapeDtypeStruct((columns, row_len), F32),
        jax.ShapeDtypeStruct((heads * HD, row_len), BF16),
        jax.ShapeDtypeStruct((groups * HD, row_len), BF16),
        jax.ShapeDtypeStruct((groups * HD, row_len), BF16),
        jax.ShapeDtypeStruct((heads, 1, row_len), F32),
        jax.ShapeDtypeStruct((heads * HD, row_len), BF16),
    ]
    return pl.pallas_call(
        functools.partial(attend_kernel, groups, repeat),
        grid=(1,),
        in_specs=[pl.BlockSpec((weights[0].shape[0], columns), lambda k: (0, 0))] * 2
        + [whole_block(one) for one in (rows, *tables)],
        out_specs=[whole_block(one) for one in shapes],
        out_shape=shapes,
        compiler_params=pltpu.CompilerParams(vmem_limit_bytes=VMEM_BYTES),
        cost_estimate=LIGHT,
    )(*weights, rows, *tables)


def head_back(raw, gain, grad_rot, cosine, sine):
    half = raw.shape[0] // 2
    first, second = grad_rot[:half], grad_rot[half:]
    grad = jnp.concatenate(
        [first * cosine + second * sine, second * cosine - first * sine], axis=0
    )
    inverse = lax.rsqrt(jnp.mean(raw * raw, axis=0, keepdims=True) + EPSILON)
    hat = raw * inverse
    terms = grad * hat
    grad_hat = grad * gain
    inner = jnp.mean(terms * gain, axis=0, keepdims=True)
    return inverse * (grad_hat - hat * inner), terms


def attend_back_kernel(
    groups,
    repeat,
    w0,
    w1,
    rows_ref,
    table_ref,
    bias_ref,
    raw_ref,
    q_ref,
    k_ref,
    v_ref,
    log_ref,
    grad_ref,
    q_terms_ref,
    k_terms_ref,
    outer_ref,
):
    weighted_columns((w0, w1), rows_ref, outer_ref)
    half = HD // 2
    cosine, sine = table_ref[:half, :], table_ref[half:HD, :]
    q_gain, k_gain = table_ref[HD : 2 * HD, :], table_ref[2 * HD :, :]
    heads = groups * repeat
    q_terms_ref[...] = jnp.zeros_like(q_terms_ref)
    k_terms_ref[...] = jnp.zeros_like(k_terms_ref)

    def group_step(group, carry):
        k_row = pl.multiple_of(group * HD, HD)
        keys = k_ref[pl.ds(k_row, HD), :]
        values = v_ref[pl.ds(k_row, HD), :]
        grad_keys = None
        for one in range(repeat):
            q_row = pl.multiple_of((group * repeat + one) * HD, HD)
            queries = q_ref[pl.ds(q_row, HD), :]
            outer = outer_ref[pl.ds(q_row, HD), :]
            scores = (
                lax.dot_general(
                    keys, queries, (((0,), (0,)), ((), ())), preferred_element_type=F32
                )
                + bias_ref[...].astype(F32)
            )
            attn_probs = jnp.exp(scores - log_ref[group * repeat + one])
            grad_probs = lax.dot_general(
                values, outer, (((0,), (0,)), ((), ())), preferred_element_type=F32
            )
            inner = jnp.sum(attn_probs * grad_probs, axis=0, keepdims=True)
            grad_scores = (attn_probs * (grad_probs - inner)).astype(BF16)
            grad_query = jnp.dot(keys, grad_scores, preferred_element_type=F32) * (HD ** (-0.5))
            grad_key = lax.dot_general(
                queries, grad_scores, (((1,), (1,)), ((), ())), preferred_element_type=F32
            )
            grad_value = lax.dot_general(
                outer,
                attn_probs.astype(BF16),
                (((1,), (1,)), ((), ())),
                preferred_element_type=F32,
            )
            grad_raw, terms = head_back(
                raw_ref[pl.ds(q_row, HD), :], q_gain, grad_query, cosine, sine
            )
            grad_ref[pl.ds(q_row, HD), :] = grad_raw.astype(BF16)
            q_terms_ref[...] += terms
            if grad_keys is None:
                grad_keys, grad_values = grad_key, grad_value
            else:
                grad_keys, grad_values = grad_keys + grad_key, grad_values + grad_value
        grad_raw, terms = head_back(
            raw_ref[pl.ds(heads * HD + k_row, HD), :], k_gain, grad_keys, cosine, sine
        )
        k_terms_ref[...] += terms
        grad_ref[pl.ds(heads * HD + k_row, HD), :] = grad_raw.astype(BF16)
        grad_ref[pl.ds((heads + groups) * HD + k_row, HD), :] = grad_values.astype(BF16)
        return carry

    lax.fori_loop(0, groups, group_step, 0)


def attend_rows_back(weights, rows, tables, kept, groups, repeat):
    row_len = rows.shape[0]
    heads = groups * repeat
    columns = (heads + 2 * groups) * HD
    shapes = [
        jax.ShapeDtypeStruct((columns, row_len), BF16),
        jax.ShapeDtypeStruct((HD, row_len), F32),
        jax.ShapeDtypeStruct((HD, row_len), F32),
    ]
    return pl.pallas_call(
        functools.partial(attend_back_kernel, groups, repeat),
        grid=(1,),
        in_specs=[
            pl.BlockSpec(
                (weights[0].shape[0], heads * HD), lambda k: (0, columns // (heads * HD))
            )
        ]
        * 2
        + [whole_block(one) for one in (rows, *tables, *kept)],
        out_specs=[whole_block(one) for one in shapes],
        out_shape=shapes,
        scratch_shapes=[
            pltpu.VMEM((heads * HD, row_len), BF16),
        ],
        compiler_params=pltpu.CompilerParams(vmem_limit_bytes=VMEM_BYTES),
        cost_estimate=LIGHT,
    )(*weights, rows, *tables, *kept)


def hidden_kernel(
    gate_own, gate_other, up_own, up_other, down_own, down_other, rows_ref, cot_ref, *outs
):
    gate_grad_ref, up_grad_ref, act_ref = outs
    width = gate_own.shape[0]

    def summed(source_ref, own_ref, other_ref):
        return jnp.dot(
            source_ref[:, :width], own_ref[...], preferred_element_type=F32
        ) + jnp.dot(source_ref[:, width:], other_ref[...], preferred_element_type=F32)

    gate = summed(rows_ref, gate_own, gate_other)
    up = summed(rows_ref, up_own, up_other)
    grad_act = summed(cot_ref, down_own, down_other)
    sigmoid_gate = jax.nn.sigmoid(gate)
    silu = gate * sigmoid_gate
    act_ref[...] = (silu * up).astype(BF16)
    up_grad_ref[...] = (grad_act * silu).astype(BF16)
    gate_grad_ref[...] = (
        grad_act * up * (sigmoid_gate + silu * (1.0 - sigmoid_gate))
    ).astype(BF16)


def hidden_small(weights, rows, cot_rows):
    row_len, width = rows.shape
    columns = weights[0].shape[1] // 3
    block = 256 if columns % 256 == 0 else columns
    steps = columns // block
    specs = []
    for part in range(3):
        specs += [
            pl.BlockSpec((width // 2, block), lambda k, part=part: (0, part * steps + k))
        ] * 2
    whole = pl.BlockSpec((row_len, width), lambda k: (0, 0))
    return pl.pallas_call(
        hidden_kernel,
        grid=(steps,),
        in_specs=specs + [whole, whole],
        out_specs=[pl.BlockSpec((row_len, block), lambda k: (0, k))] * 3,
        out_shape=[jax.ShapeDtypeStruct((row_len, columns), BF16)] * 3,
        compiler_params=pltpu.CompilerParams(vmem_limit_bytes=VMEM_BYTES),
        cost_estimate=LIGHT,
    )(*weights, *weights, *weights, rows, cot_rows)


def row_places(own_rows):
    own = jnp.arange(own_rows, dtype=jnp.int32)
    index = lax.axis_index("tp")
    return jnp.concatenate([own + index * own_rows, own + (1 - index) * own_rows])


def document_tables(starts, places):
    inside = places[:, None] >= starts[None, :]
    firsts = jnp.max(jnp.where(inside, starts[None, :], 0), axis=1)
    return firsts, places - firsts


def meet_kernel(count, *refs):
    total = refs[0][...]
    for other_ref in refs[1:count]:
        total = total + other_ref[...].astype(F32)
    outs = refs[count:]
    if len(outs) == 1:
        outs[0][...] = total.astype(outs[0].dtype)
        return
    half = total.shape[0] // 2
    outs[0][...] = total[half:].astype(BF16)
    outs[1][...] = total[:half]


def meet(values, kind):
    rows, columns = values[0].shape
    steps = 3 if columns % 384 == 0 else 1
    block = columns // steps
    shapes = [(rows, kind)] if kind is not None else [(rows // 2, BF16), (rows // 2, F32)]
    return pl.pallas_call(
        functools.partial(meet_kernel, len(values)),
        grid=(steps,),
        in_specs=[pl.BlockSpec((rows, block), lambda k: (0, k))] * len(values),
        out_specs=[pl.BlockSpec((size, block), lambda k: (0, k)) for size, _ in shapes],
        out_shape=[jax.ShapeDtypeStruct((size, columns), kind) for size, kind in shapes],
        compiler_params=pltpu.CompilerParams(vmem_limit_bytes=VMEM_BYTES),
        cost_estimate=LIGHT,
    )(*values)


def norm_kernel(inputs_ref, kept_ref, other_ref, gain_ref, normed_ref, hat_ref, inv_ref, hidden_ref):
    hidden = inputs_ref[...] + kept_ref[...] + other_ref[...].astype(F32)
    normed, hat, inverse = norm_forward(hidden, gain_ref[...])
    normed_ref[...] = normed.astype(BF16)
    hat_ref[...] = hat
    inv_ref[...] = inverse
    hidden_ref[...] = hidden


def norm_hidden(inputs, kept, other, gain):
    rows, width = inputs.shape
    shapes = [(width, BF16), (width, F32), (1, F32), (width, F32)]
    return pl.pallas_call(
        norm_kernel,
        out_shape=[jax.ShapeDtypeStruct((rows, size), kind) for size, kind in shapes],
        compiler_params=pltpu.CompilerParams(vmem_limit_bytes=VMEM_BYTES),
        cost_estimate=LIGHT,
    )(inputs, kept, other, gain)


def norm_back_kernel(kept_ref, other_ref, hat_ref, inv_ref, gain_ref, base_ref, *outs):
    low_ref, grad_ref, gain_part_ref = outs
    incoming = kept_ref[...] + other_ref[...].astype(F32)
    hat = hat_ref[...]
    grad_hat = incoming * gain_ref[...]
    inner = jnp.mean(grad_hat * hat, axis=-1, keepdims=True)
    grad = base_ref[...].astype(F32) + inv_ref[...] * (grad_hat - hat * inner)
    low_ref[...] = grad.astype(BF16)
    grad_ref[...] = grad
    gain_part_ref[...] = jnp.sum(incoming * hat, axis=0, keepdims=True)


def norm_back(kept, other, hat, inverse, gain, base):
    rows, width = kept.shape
    shapes = [(rows, BF16), (rows, F32), (1, F32)]
    return pl.pallas_call(
        norm_back_kernel,
        out_shape=[jax.ShapeDtypeStruct((size, width), kind) for size, kind in shapes],
        compiler_params=pltpu.CompilerParams(vmem_limit_bytes=VMEM_BYTES),
        cost_estimate=LIGHT,
    )(kept, other, hat, inverse, gain, base)


class Gather:
    def __init__(self, program, shard):
        self.program = program
        self.near = shard

    def start(self, mask):
        if mask == 8:
            self.far = self.program.send(self.near, 8)
        elif mask == 4:
            self.next = self.program.send(self.near, 4)
        elif mask == 2:
            self.across = self.program.send(self.near, 2)
        else:
            self.other = self.program.send(self.own, 1)

    def start_last(self):
        self.last = self.program.send(self.next, 2)

    def arrive(self, mask):
        program = self.program
        if mask == 8:
            far = program.arrive(self.far)
            self.near = program.run(stack, self.near, far)
        elif mask == 4:
            self.next = program.arrive(self.next)
        elif mask == 2:
            self.across = program.arrive(self.across)
        else:
            self.halves = [self.own, program.arrive(self.other)]

    def arrive_last(self):
        last = self.program.arrive(self.last)
        parts = (self.near, self.next, self.across, last)
        self.own = self.program.run(stack, *parts)


class GatherAcross:
    def __init__(self, program, shard):
        self.program = program
        self.parts = [shard, None]
        self.sent = [None, None]
        self.next = [None, None]

    def start_across(self):
        self.sent[1] = self.program.send(self.parts[0], 2)

    def arrive_across(self):
        self.parts[1] = self.program.arrive(self.sent[1])

    def start(self, mask, part):
        self.sent[part] = self.program.send(self.parts[part], mask)

    def arrive(self, mask, part):
        other = self.program.arrive(self.sent[part])
        if mask == 8:
            self.parts[part] = self.program.run(
                stack, self.parts[part], other
            )
        else:
            self.next[part] = other

    def join(self):
        parts = (self.parts[0], self.next[0], self.parts[1], self.next[1])
        self.own = self.program.run(stack, *parts)

    def start_core(self):
        self.other = self.program.send(self.own, 1)

    def arrive_core(self):
        self.halves = [self.own, self.program.arrive(self.other)]


class Scatter:
    across_last = False

    def __init__(self, program, pairs, flipped=False):
        self.program, self.flipped = program, flipped
        self.arrays = [pair[:2] for pair in pairs]
        self.blocks = [pair[2:] for pair in pairs]

    def half(self, side, added):
        def step(arrays, added):
            pairs = [(*pair, *block) for pair, block in zip(arrays, self.blocks)]
            return grad_half(pairs, side, added, self.flipped, self.across_last)

        return self.program.run(step, self.arrays, added)

    def core(self):
        self.core_step()
        self.core_send()

    def core_step(self):
        self.near = self.half(1, None)[0]

    def core_send(self):
        self.other = self.program.send(self.near, 1)

    def beside(self):
        parts = self.half(0, self.other)
        self.kept, self.kept_far, self.low, self.high = parts

    def arrive_core(self):
        self.other = self.program.arrive(self.other)

    def arrive_far(self):
        self.other = self.program.arrive(self.other)

    def send_high(self):
        self.other = self.program.send(self.high, 2)

    def send_low(self):
        self.across = self.program.send(self.low, 2)

    def meet_high(self):
        arrays = [self.kept_far, self.program.arrive(self.other)]
        self.near = self.program.run(lambda *arrays: meet(arrays, BF16)[0], *arrays)

    def arrive_low(self):
        self.across = self.program.arrive(self.across)

    def send(self, mask):
        self.other = self.program.send(self.near, mask)

    def meet_far(self):
        arrays = [self.kept, self.across, self.other]
        self.near, self.kept = self.program.run(lambda *arrays: meet(arrays, None), *arrays)

    def finish(self):
        arrays = [self.kept, self.other]
        self.kept = self.program.run(lambda *arrays: meet(arrays, F32)[0], *arrays)


class ScatterAcross(Scatter):
    across_last = True

    def beside(self):
        parts = self.half(0, self.other)
        self.keep, self.near, self.others = [parts[0], parts[2]], [parts[1], parts[3]], [0, 0]

    def send_part(self, mask, part):
        self.others[part] = self.program.send(self.near[part], mask)

    def arrive_part(self, part):
        self.others[part] = self.program.arrive(self.others[part])

    def meet_part(self, part):
        arrays = [self.keep[part], self.others[part]]
        self.near[part], self.keep[part] = self.program.run(
            lambda *arrays: meet(arrays, None), *arrays
        )

    def meet_across(self):
        arrays = [self.keep[1], self.others[1]]
        self.near[1] = self.program.run(lambda *arrays: meet(arrays, BF16)[0], *arrays)

    def finish(self):
        arrays = [self.keep[0], self.others[0], self.others[1]]
        self.kept = self.program.run(lambda *arrays: meet(arrays, F32)[0], *arrays)


def restore_kernel(count, *refs):
    total = refs[0][...].astype(F32)
    for other_ref in refs[1:count]:
        total = total + other_ref[...].astype(F32)
    matrix_ref, out_ref = refs[count:]
    out_ref[...] = restore(total.astype(BF16), matrix_ref[...])


def restore_sum(matrix, *values):
    return pl.pallas_call(
        functools.partial(restore_kernel, len(values)),
        out_shape=jax.ShapeDtypeStruct(values[0].shape, BF16),
        compiler_params=pltpu.CompilerParams(vmem_limit_bytes=VMEM_BYTES),
        cost_estimate=LIGHT,
    )(*values, matrix)


def gains_kernel(attn_ref, mlp_ref, q_ref, k_ref, matrix_ref, out_ref):
    rows = jnp.concatenate([attn_ref[...], mlp_ref[...]], axis=0)
    out_ref[...] = jnp.zeros_like(out_ref)
    out_ref[0:2, :] = restore(rows, matrix_ref[...])
    ones = jnp.ones((8, q_ref.shape[1]), F32)
    for place, terms_ref in ((2, q_ref), (3, k_ref)):
        sums = lax.dot_general(
            ones,
            terms_ref[...],
            (((1,), (1,)), ((), ())),
            precision=lax.Precision.HIGHEST,
            preferred_element_type=F32,
        )
        out_ref[place : place + 1, : sums.shape[1]] = sums[:1]


def gain_parts(attn_part, mlp_part, q_terms, k_terms, matrix):
    return pl.pallas_call(
        gains_kernel,
        out_shape=jax.ShapeDtypeStruct((8, attn_part.shape[1]), F32),
        compiler_params=pltpu.CompilerParams(vmem_limit_bytes=VMEM_BYTES),
        cost_estimate=LIGHT,
    )(attn_part, mlp_part, q_terms, k_terms, matrix)


def local_small(
    tokens,
    doc_starts,
    attn_gain,
    w_query,
    w_key,
    w_value,
    q_gain,
    k_gain,
    w_out,
    mlp_gain,
    w_gate,
    w_up,
    w_down,
    out_grad,
):
    width = tokens.shape[-1]
    own_rows = tokens.shape[1]
    groups = w_key.shape[1] // HD
    repeat = w_query.shape[1] // w_key.shape[1]
    query_cols, key_cols = w_query.shape[1], w_key.shape[1]
    columns = query_cols + 2 * key_cols
    ff_cols = w_gate.shape[1]
    cut = ff_cols // 3
    program = Program()
    run, send, arrive = program.run, program.send, program.arrive

    shards = [w_query, w_key, w_value, w_out]
    plan = [(one, 0, shard.shape[1]) for one, shard in enumerate(shards)]
    attn = Gather(program, run(lambda *parts: pack(parts, [plan]), *shards)[0])
    attn.start(8)
    plans = [[(one, at, at + cut) for one in range(3)] for at in range(0, ff_cols, cut)]
    packed = run(lambda *parts: pack(parts, plans), w_gate, w_up, w_down)
    first, second = (Gather(program, one) for one in packed[:2])
    third = GatherAcross(program, packed[2])

    matrix = run(lambda: order_matrix(width, BF16))

    def attention_tables(starts, q_gain, k_gain):
        places = row_places(own_rows)
        firsts, position = document_tables(starts, places)
        cosine, sine = rope_tables(position, HD)
        rows = [cosine.T, sine.T]
        rows += [jnp.broadcast_to(gain[:, None], (HD, places.size)) for gain in (q_gain, k_gain)]
        keys = places[:, None]
        allowed = (keys <= places[None, :]) & (keys >= firsts[None, :])
        return jnp.concatenate(rows, axis=0), jnp.where(allowed, 0.0, -1e30).astype(BF16)

    def norm_tokens(tokens, attn_gain, mlp_gain):
        gains = reorder(jnp.stack([attn_gain, mlp_gain]), matrix)
        inputs = reorder(tokens, matrix).astype(F32)
        normed, hat, inverse = norm_forward(inputs, gains[0])
        return normed.astype(BF16), hat, inverse, inputs, gains

    normed_first, hat_first, inv_first, inputs, gains = run(
        norm_tokens, tokens[0], attn_gain, mlp_gain
    )
    attn_gain, mlp_gain = gains[0], gains[1]
    cotangent = run(lambda rows: reorder(rows, matrix), out_grad[0])
    tables = run(attention_tables, doc_starts[0], q_gain, k_gain)

    attn.arrive(8)
    attn.start(4)
    attn.start(2)
    first.start(8)
    rows_sent = send(normed_first, 0, 1)
    third.start_across()
    attn.arrive(4)
    attn.arrive(2)
    first.arrive(8)
    rows_first = run(stack, normed_first, arrive(rows_sent))
    third.arrive_across()
    attn.start_last()
    first.start(4)
    cot_sent = send(cotangent, 0, 1)
    third.start(8, 0)
    attn.arrive_last()
    first.arrive(4)
    cot_rows = run(stack, cotangent, arrive(cot_sent))
    third.arrive(8, 0)
    attn.start(1)
    attn.arrive(1)
    first.start(2)
    second.start(8)
    raw, queries, keys, values, logs, attended = run(
        lambda weights, rows: attend_rows(weights, rows, tables, groups, repeat),
        attn.halves,
        rows_first,
    )

    def back_rows(lefts, weights, parts, flipped=False):
        return run(
            lambda lefts, weights: project_back(lefts, weights, parts, flipped)[::-1],
            lefts,
            weights,
        )

    sent, kept = back_rows([attended], [attn.halves], [columns // query_cols], True)
    first.arrive(2)
    second.arrive(8)
    branch_sent = send(sent, 0, 1)
    first.start_last()
    second.start(4)
    third.start(8, 1)

    normed_second, hat_second, inv_second, hidden = run(
        norm_hidden, inputs, kept, arrive(branch_sent), mlp_gain[None]
    )
    first.arrive_last()
    second.arrive(4)
    third.arrive(8, 1)
    rows_sent = send(normed_second, 0, 1)
    first.start(1)
    second.start(2)
    third.start(4, 0)
    rows_second = run(stack, normed_second, arrive(rows_sent))
    first.arrive(1)
    second.arrive(2)
    third.arrive(4, 0)
    second.start_last()
    third.start(4, 1)

    def hidden_third(one):
        parts = run(hidden_small, one.halves, rows_second, cot_rows)
        return parts, [(rows_second, parts[0]), (rows_second, parts[1]), (cot_rows, parts[2])]

    parts_one, pairs = hidden_third(first)
    sum_one = Scatter(program, pairs)
    sum_one.core_step()
    second.arrive_last()
    third.arrive(4, 1)
    third.join()
    second.start(1)
    third.start_core()
    second.arrive(1)
    sum_one.core_send()
    parts_two, pairs = hidden_third(second)
    sum_two = Scatter(program, pairs)
    third.arrive_core()
    sum_two.core_step()
    sum_one.arrive_core()
    sum_one.beside()
    sum_one.send_high()
    sum_two.core_send()
    parts_three, pairs = hidden_third(third)
    sum_three = ScatterAcross(program, pairs)
    sum_three.core_step()
    parts = (parts_one, parts_two, parts_three)
    thirds_halves = [first.halves, second.halves, third.halves]
    sent, kept = back_rows(
        [one for part in parts for one in part[:2]],
        [halves for halves in thirds_halves for _ in range(2)],
        [0, 1] * 3,
    )
    sum_one.meet_high()
    sum_two.arrive_core()
    grad_sent = send(sent, 0, 1)
    sum_one.send_low()
    sum_one.send(4)
    sum_three.core_send()
    sum_two.beside()
    result_part = back_rows([part[2] for part in parts], thirds_halves, [2] * 3)
    sum_three.arrive_core()
    sum_one.arrive_low()
    sum_one.arrive_far()
    grad_branch, grad_hidden, mlp_gain_part = run(
        norm_back, kept, arrive(grad_sent), hat_second, inv_second, mlp_gain[None], cotangent
    )
    rows_sent = send(grad_branch, 0, 1)
    sum_two.send_high()
    sum_one.meet_far()
    sum_three.beside()
    sum_one.send(8)
    sum_three.send_part(4, 0)
    branch_rows = run(stack, grad_branch, arrive(rows_sent))
    sum_two.meet_high()
    sum_three.arrive_part(0)
    sum_one.arrive_far()
    sum_three.meet_part(0)
    sum_two.send_low()
    sum_two.send(4)
    sum_three.send_part(8, 0)
    result_sent = send(result_part[0], 0, 1)
    grads, q_terms, k_terms = run(
        lambda weights, rows, kept: attend_rows_back(weights, rows, tables, kept, groups, repeat),
        attn.halves,
        branch_rows,
        (raw, queries, keys, values, logs),
    )
    sent, kept = back_rows([grads], [attn.halves], [0], True)
    pairs = [(rows_first, grads, block) for block in range(columns // query_cols)]
    sum_attn = Scatter(program, [*pairs, (branch_rows, attended)], True)
    sum_attn.core_step()
    sum_two.arrive_low()
    sum_two.arrive_far()
    sum_three.arrive_part(0)
    result_other = arrive(result_sent)
    sum_attn.core_send()
    sum_two.meet_far()
    sum_attn.arrive_core()
    sum_attn.beside()
    grad_sent = send(sent, 0, 1)
    sum_attn.send_high()
    sum_attn.send_low()
    sum_three.send_part(4, 1)
    sum_two.send(8)
    sum_one.finish()
    result = run(restore_sum, matrix, hidden, result_part[1], result_other)
    sum_attn.meet_high()
    sum_attn.arrive_low()
    grad_other = arrive(grad_sent)
    sum_three.arrive_part(1)
    sum_two.arrive_far()
    sum_three.meet_part(1)
    sum_attn.send(4)
    sum_three.send_part(8, 1)
    tokens_low, _, attn_gain_part = run(
        norm_back, kept, grad_other, hat_first, inv_first, attn_gain[None], grad_hidden
    )
    total = run(gain_parts, attn_gain_part, mlp_gain_part, q_terms, k_terms, matrix)

    def total_send(*partners):
        return [send(total, *partner) for partner in partners]

    def total_arrive(sent):
        return run(lambda *arrays: meet(arrays, F32)[0], total, *[arrive(one) for one in sent])

    gains_sent = total_send((0, 1))
    sum_two.finish()
    tokens_grad = run(restore_sum, matrix, tokens_low)
    sum_attn.arrive_far()
    sum_attn.meet_far()
    sum_three.arrive_part(1)
    sum_three.meet_across()
    total = total_arrive(gains_sent)
    sum_attn.send(8)
    sum_three.send_part(2, 1)
    gains_sent = total_send((1,), (2,), (3,))
    sum_attn.arrive_far()
    sum_attn.finish()
    sum_three.arrive_part(1)
    total = total_arrive(gains_sent)
    gains_sent = total_send((4,), (8,), (12,))
    sum_three.finish()

    def split_sums(*sums):
        rows = sums[0].shape[0]
        moves = [
            (source, (0, rows), (part * cut, (part + 1) * cut), part, 0, source * cut)
            for source in range(3)
            for part in range(3)
        ]
        return copy_blocks(sums, moves, [(rows, ff_cols)] * 3)

    weights = run(split_sums, sum_one.kept, sum_two.kept, sum_three.kept)
    total = total_arrive(gains_sent)

    gate_grad, up_grad, down_grad = weights
    kept = sum_attn.kept
    return (
        result[None],
        tokens_grad[None],
        total[0],
        kept[:, :query_cols],
        kept[:, query_cols : query_cols + key_cols],
        kept[:, query_cols + key_cols : columns],
        total[2, :HD],
        total[3, :HD],
        kept[:, columns:],
        total[1],
        gate_grad,
        up_grad,
        down_grad,
    )


def local(*arrays):
    small = lax.axis_size("dp") == DEVICES and lax.axis_size("tp") == 2
    if small and arrays[0].shape[1:] == (256, 1024):
        return local_small(*arrays)
    return local_large(*arrays)


def solution(mesh):
    in_specs = (
        P("dp", "tp", None),
        P("dp", None),
        P(),
        P("dp", "tp"),
        P("dp", "tp"),
        P("dp", "tp"),
        P(),
        P(),
        P("dp", "tp"),
        P(),
        P("dp", "tp"),
        P("dp", "tp"),
        P("dp", "tp"),
        P("dp", "tp", None),
    )
    out_specs = (
        P("dp", "tp", None),
        P("dp", "tp", None),
        P(),
        P("dp", "tp"),
        P("dp", "tp"),
        P("dp", "tp"),
        P(),
        P(),
        P("dp", "tp"),
        P(),
        P("dp", "tp"),
        P("dp", "tp"),
        P("dp", "tp"),
    )
    return jax.shard_map(local, mesh=mesh, in_specs=in_specs, out_specs=out_specs, check_vma=False)
```

```python
import functools

import jax
import jax.numpy as jnp
from jax import lax
from jax.experimental import pallas as pl
from jax.experimental.pallas import tpu as pltpu
from jax.sharding import PartitionSpec as P

HD = 64


EPSILON = 1e-05
THETA = 1000000.0


def documents(starts, length):
    places = jnp.arange(length, dtype=jnp.int32)
    inside = places[:, None] >= starts[None, :]
    segment = jnp.sum(inside.astype(jnp.int32), axis=1) - 1
    firsts = jnp.max(jnp.where(inside, starts[None, :], 0), axis=1)
    return (segment, places - firsts)


def rope_tables(position, width):
    half_width = width // 2
    freqs = THETA ** (-(jnp.arange(half_width, dtype=jnp.float32) * 2.0 / width))
    angles = position.astype(jnp.float32)[:, None] * freqs[None, :]
    return (jnp.cos(angles), jnp.sin(angles))


def rotate(values, cosine, sine):
    half_width = values.shape[-1] // 2
    first_half = values[..., :half_width]
    second_half = values[..., half_width:]
    tile_shape = (values.shape[0],) + (1,) * (values.ndim - 2) + (half_width,)
    cos_tile = cosine.reshape(tile_shape)
    sin_tile = sine.reshape(tile_shape)
    return jnp.concatenate(
        [
            first_half * cos_tile - second_half * sin_tile,
            second_half * cos_tile + first_half * sin_tile,
        ],
        axis=-1,
    )


def norm_forward(values, gain):
    inverse = lax.rsqrt(jnp.mean(values * values, axis=-1, keepdims=True) + EPSILON)
    normed_hat = values * inverse
    return (normed_hat * gain, normed_hat, inverse)


def norm_backward(grad_normed, normed_hat, inverse, gain):
    grad_hat = grad_normed * gain
    grad_values = inverse * (
        grad_hat - normed_hat * jnp.mean(grad_hat * normed_hat, axis=-1, keepdims=True)
    )
    gain_part = jnp.sum((grad_normed * normed_hat).reshape(-1, normed_hat.shape[-1]), axis=0)
    return (grad_values, gain_part)


def gather_rows(values):
    return lax.all_gather(values, "tp", axis=0, tiled=True)


def sum_rows(left_rows, right_weight):
    return lax.psum_scatter(
        jnp.dot(left_rows, right_weight.T, preferred_element_type=jnp.float32).astype(jnp.bfloat16),
        "tp",
        scatter_dimension=0,
        tiled=True,
    ).astype(jnp.float32)


def masked_scores(query_block, key_rows, block_segment, block_places, segment, places, score_scale):
    scores = (
        jnp.einsum("qgrd,kgd->grqk", query_block, key_rows, preferred_element_type=jnp.float32)
        * score_scale
    )
    allowed = (places[None, :] <= block_places[:, None]) & (
        segment[None, :] == block_segment[:, None]
    )
    return jnp.where(allowed, scores, -1e30)


def attend(query_rows, key_rows, value_rows, segment, block_rows):
    row_len = query_rows.shape[0]
    blocks = row_len // block_rows
    places = jnp.arange(row_len, dtype=jnp.int32)
    score_scale = query_rows.shape[-1] ** (-0.5)

    def block_out(block_item):
        query_block, block_segment, block_places = block_item
        scores = masked_scores(
            query_block, key_rows, block_segment, block_places, segment, places, score_scale
        )
        peaks = jnp.max(scores, axis=-1, keepdims=True)
        shifted = jnp.exp(scores - peaks)
        totals = jnp.sum(shifted, axis=-1, keepdims=True)
        attn_probs = (shifted / totals).astype(jnp.bfloat16)
        outputs = jnp.einsum(
            "grqk,kgd->qgrd", attn_probs, value_rows, preferred_element_type=jnp.float32
        )
        return (outputs, (peaks + jnp.log(totals))[..., 0])

    outputs, log_totals = lax.map(
        block_out,
        (
            query_rows.reshape((blocks, block_rows) + query_rows.shape[1:]),
            segment.reshape(blocks, block_rows),
            places.reshape(blocks, block_rows),
        ),
    )
    return (outputs.reshape(query_rows.shape), log_totals)


def attend_back(query_rows, key_rows, value_rows, grad_out, log_totals, segment, block_rows):
    row_len = query_rows.shape[0]
    blocks = row_len // block_rows
    places = jnp.arange(row_len, dtype=jnp.int32)
    score_scale = query_rows.shape[-1] ** (-0.5)

    def block_back(carry, block_item):
        grad_keys, grad_values = carry
        query_block, grad_block, total_block, block_segment, block_places = block_item
        scores = masked_scores(
            query_block, key_rows, block_segment, block_places, segment, places, score_scale
        )
        attn_probs = jnp.exp(scores - total_block[..., None])
        grad_probs = jnp.einsum(
            "qgrd,kgd->grqk", grad_block, value_rows, preferred_element_type=jnp.float32
        )
        inner = jnp.sum(attn_probs * grad_probs, axis=-1, keepdims=True)
        grad_scores = (attn_probs * (grad_probs - inner)).astype(jnp.bfloat16)
        grad_query = (
            jnp.einsum("grqk,kgd->qgrd", grad_scores, key_rows, preferred_element_type=jnp.float32)
            * score_scale
        )
        grad_keys = (
            grad_keys
            + jnp.einsum(
                "grqk,qgrd->kgd", grad_scores, query_block, preferred_element_type=jnp.float32
            )
            * score_scale
        )
        grad_values = grad_values + jnp.einsum(
            "grqk,qgrd->kgd",
            attn_probs.astype(jnp.bfloat16),
            grad_block,
            preferred_element_type=jnp.float32,
        )
        return ((grad_keys, grad_values), grad_query)

    zeros_kv = jnp.zeros(key_rows.shape, jnp.float32)
    block_shape = (blocks, block_rows) + query_rows.shape[1:]
    (grad_keys, grad_values), grad_queries = lax.scan(
        block_back,
        (zeros_kv, zeros_kv),
        (
            query_rows.reshape(block_shape),
            grad_out.reshape(block_shape),
            log_totals,
            segment.reshape(blocks, block_rows),
            places.reshape(blocks, block_rows),
        ),
    )
    return (grad_queries.reshape(query_rows.shape), grad_keys, grad_values)


def local_large(
    tokens,
    doc_starts,
    attn_gain,
    w_query,
    w_key,
    w_value,
    q_gain,
    k_gain,
    w_out,
    mlp_gain,
    w_gate,
    w_up,
    w_down,
    out_grad,
):
    query_w, key_w, value_w, out_w, gate_w, up_w, down_w = (
        lax.all_gather(w_query, "dp", axis=0, tiled=True),
        lax.all_gather(w_key, "dp", axis=0, tiled=True),
        lax.all_gather(w_value, "dp", axis=0, tiled=True),
        lax.all_gather(w_out, "dp", axis=0, tiled=True),
        lax.all_gather(w_gate, "dp", axis=0, tiled=True),
        lax.all_gather(w_up, "dp", axis=0, tiled=True),
        lax.all_gather(w_down, "dp", axis=0, tiled=True),
    )
    inputs = tokens[0].astype(jnp.float32)
    cotangent = out_grad[0]
    own_rows = inputs.shape[0]
    row_len = own_rows * lax.axis_size("tp")
    head_dim = HD
    groups = key_w.shape[1] // head_dim
    repeat = query_w.shape[1] // key_w.shape[1]
    query_cols = query_w.shape[1]
    key_cols = key_w.shape[1]
    ff_cols = gate_w.shape[1]
    block_rows = min(512, row_len)
    segment, position = documents(doc_starts[0], row_len)
    cosine, sine = rope_tables(position, head_dim)
    qkv_weight = jnp.concatenate([query_w, key_w, value_w], axis=1)
    gate_up_weight = jnp.concatenate([gate_w, up_w], axis=1)
    normed_first, hat_first, inv_first = norm_forward(inputs, attn_gain)
    rows_first = gather_rows(normed_first.astype(jnp.bfloat16))
    projected = jnp.dot(rows_first, qkv_weight, preferred_element_type=jnp.float32)
    query_raw = projected[:, :query_cols].reshape(row_len, groups, repeat, head_dim)
    key_raw = projected[:, query_cols : query_cols + key_cols].reshape(row_len, groups, head_dim)
    value_rows = (
        projected[:, query_cols + key_cols :]
        .astype(jnp.bfloat16)
        .reshape(row_len, groups, head_dim)
    )
    query_normed, query_hat, query_inv = norm_forward(query_raw, q_gain)
    key_normed, key_hat, key_inv = norm_forward(key_raw, k_gain)
    query_rows = rotate(query_normed, cosine, sine).astype(jnp.bfloat16)
    key_rows = rotate(key_normed, cosine, sine).astype(jnp.bfloat16)
    attended, log_totals = attend(query_rows, key_rows, value_rows, segment, block_rows)
    attended = attended.reshape(row_len, query_cols).astype(jnp.bfloat16)
    branch_out = sum_rows(attended, out_w)
    hidden = inputs + branch_out
    normed_second, hat_second, inv_second = norm_forward(hidden, mlp_gain)
    rows_second = gather_rows(normed_second.astype(jnp.bfloat16))
    gate_up = jnp.dot(rows_second, gate_up_weight, preferred_element_type=jnp.float32)
    gate_pre = gate_up[:, :ff_cols]
    up_pre = gate_up[:, ff_cols:]
    sigmoid_gate = jax.nn.sigmoid(gate_pre)
    activated = (gate_pre * sigmoid_gate * up_pre).astype(jnp.bfloat16)
    result = hidden + sum_rows(activated, down_w)
    cot_rows = gather_rows(cotangent)
    grad_act = jnp.dot(cot_rows, down_w, preferred_element_type=jnp.float32)
    grad_down = jnp.einsum("rd,rf->df", cot_rows, activated, preferred_element_type=jnp.float32)
    grad_gate = grad_act * up_pre * sigmoid_gate * (1.0 + gate_pre * (1.0 - sigmoid_gate))
    grad_up = grad_act * gate_pre * sigmoid_gate
    grad_gate_up = jnp.concatenate([grad_gate, grad_up], axis=1).astype(jnp.bfloat16)
    grad_gate_up_w = jnp.einsum(
        "rd,rf->df", rows_second, grad_gate_up, preferred_element_type=jnp.float32
    )
    grad_normed_second = sum_rows(grad_gate_up, gate_up_weight)
    grad_hidden_norm, mlp_gain_part = norm_backward(
        grad_normed_second, hat_second, inv_second, mlp_gain
    )
    grad_hidden = cotangent.astype(jnp.float32) + grad_hidden_norm
    grad_branch = grad_hidden.astype(jnp.bfloat16)
    branch_rows = gather_rows(grad_branch)
    grad_out_w = jnp.einsum("rd,rq->dq", branch_rows, attended, preferred_element_type=jnp.float32)
    grad_attended = jnp.dot(branch_rows, out_w, preferred_element_type=jnp.float32).astype(
        jnp.bfloat16
    )
    grad_query_rot, grad_key_rot, grad_value = attend_back(
        query_rows,
        key_rows,
        value_rows,
        grad_attended.reshape(row_len, groups, repeat, head_dim),
        log_totals,
        segment,
        block_rows,
    )
    grad_query_norm = rotate(grad_query_rot, cosine, -sine)
    grad_key_norm = rotate(grad_key_rot, cosine, -sine)
    grad_query_raw, q_gain_part = norm_backward(grad_query_norm, query_hat, query_inv, q_gain)
    grad_key_raw, k_gain_part = norm_backward(grad_key_norm, key_hat, key_inv, k_gain)
    grad_projected = jnp.concatenate(
        [
            grad_query_raw.reshape(row_len, query_cols),
            grad_key_raw.reshape(row_len, key_cols),
            grad_value.reshape(row_len, key_cols),
        ],
        axis=1,
    ).astype(jnp.bfloat16)
    grad_qkv_w = jnp.einsum(
        "rd,rf->df", rows_first, grad_projected, preferred_element_type=jnp.float32
    )
    grad_normed_first = sum_rows(grad_projected, qkv_weight)
    grad_input_norm, attn_gain_part = norm_backward(
        grad_normed_first, hat_first, inv_first, attn_gain
    )
    grad_inputs = grad_hidden + grad_input_norm
    summed = (
        lax.psum_scatter(
            grad_qkv_w[:, :query_cols].astype(jnp.bfloat16), "dp", scatter_dimension=0, tiled=True
        ).astype(jnp.float32),
        lax.psum_scatter(
            grad_qkv_w[:, query_cols : query_cols + key_cols].astype(jnp.bfloat16),
            "dp",
            scatter_dimension=0,
            tiled=True,
        ).astype(jnp.float32),
        lax.psum_scatter(
            grad_qkv_w[:, query_cols + key_cols :].astype(jnp.bfloat16),
            "dp",
            scatter_dimension=0,
            tiled=True,
        ).astype(jnp.float32),
        lax.psum_scatter(
            grad_out_w.astype(jnp.bfloat16), "dp", scatter_dimension=0, tiled=True
        ).astype(jnp.float32),
        lax.psum_scatter(
            grad_gate_up_w[:, :ff_cols].astype(jnp.bfloat16), "dp", scatter_dimension=0, tiled=True
        ).astype(jnp.float32),
        lax.psum_scatter(
            grad_gate_up_w[:, ff_cols:].astype(jnp.bfloat16), "dp", scatter_dimension=0, tiled=True
        ).astype(jnp.float32),
        lax.psum_scatter(
            grad_down.astype(jnp.bfloat16), "dp", scatter_dimension=0, tiled=True
        ).astype(jnp.float32),
    )
    gains = lax.psum((attn_gain_part, q_gain_part, k_gain_part, mlp_gain_part), ("dp", "tp"))
    return (
        result.astype(jnp.bfloat16)[None],
        grad_inputs.astype(jnp.bfloat16)[None],
        gains[0],
        summed[0],
        summed[1],
        summed[2],
        gains[1],
        gains[2],
        summed[3],
        gains[3],
        summed[4],
        summed[5],
        summed[6],
    )


F32 = jnp.float32
BF16 = jnp.bfloat16
VMEM_BYTES = 16 * 1024 * 1024
LIGHT = pl.CostEstimate(flops=1000, bytes_accessed=1000, transcendentals=0)
HEAVY = pl.CostEstimate(flops=13000000000, bytes_accessed=1000, transcendentals=0)


DEVICES = 16
MASKS = (1, 2, 4, 8)


def tied(values, *others):
    return lax.optimization_barrier((values, *others))[0]


class Program:
    def __init__(self):
        self.arrival = None
        self.step = None

    def begun(self):
        return [one for one in (self.arrival, self.step) if one is not None]

    def ready(self, *values):
        out = lax.optimization_barrier((*values, *self.begun()))[: len(values)]
        return out if len(out) > 1 else out[0]

    def run(self, function, *values):
        flat, tree = jax.tree.flatten(values)
        flat = lax.optimization_barrier((*flat, *self.begun()))[: len(flat)]
        out = function(*jax.tree.unflatten(tree, flat))
        self.step = jax.tree.leaves(out)[0]
        return out

    def send(self, values, mask, across=0):
        pairs = []
        for own in range(DEVICES):
            for side in range(2):
                pairs.append((own * 2 + side, (own ^ mask) * 2 + (side ^ across)))
        return lax.ppermute(self.ready(values), ("dp", "tp"), pairs)

    def arrive(self, other):
        if self.arrival is not None:
            other = tied(other, self.arrival)
        self.arrival = other
        return other


def copy_kernel(count, moves, *refs):
    semaphores = refs[-1]
    copies = []
    for place, (source, rows, columns, target, row, column) in enumerate(moves):
        size, width = rows[1] - rows[0], columns[1] - columns[0]
        copies.append(
            pltpu.make_async_copy(
                refs[source].at[rows[0] : rows[1], columns[0] : columns[1]],
                refs[count + target].at[row : row + size, column : column + width],
                semaphores.at[place],
            )
        )
    for copy in copies:
        copy.start()
    for copy in copies:
        copy.wait()


def copy_blocks(arrays, moves, shapes, cost=LIGHT):
    return pl.pallas_call(
        functools.partial(copy_kernel, len(arrays), moves),
        in_specs=[pl.BlockSpec(memory_space=pl.ANY)] * len(arrays),
        out_specs=[pl.BlockSpec(memory_space=pl.ANY)] * len(shapes),
        out_shape=[jax.ShapeDtypeStruct(shape, arrays[0].dtype) for shape in shapes],
        scratch_shapes=[pltpu.SemaphoreType.DMA((len(moves),))],
        compiler_params=pltpu.CompilerParams(vmem_limit_bytes=VMEM_BYTES),
        cost_estimate=cost,
    )(*arrays)


def pack(shards, plans):
    rows = shards[0].shape[0]
    moves, shapes = [], []
    for target, plan in enumerate(plans):
        column = 0
        for source, start, stop in plan:
            moves.append((source, (0, rows), (start, stop), target, 0, column))
            column += stop - start
        shapes.append((rows, column))
    return copy_blocks(shards, moves, shapes)


def stack(*parts, cost=LIGHT):
    moves, row = [], 0
    for source, part in enumerate(parts):
        moves.append((source, (0, part.shape[0]), (0, part.shape[1]), 0, row, 0))
        row += part.shape[0]
    return copy_blocks(parts, moves, [(row, parts[0].shape[1])], cost)[0]


def grad_kernel(count, flipped, added, *refs):
    lefts, rights = refs[:count], refs[count : 2 * count]
    outs = refs[2 * count + (1 if added else 0) :]
    step = pl.program_id(0)
    for one in range(count):

        @pl.when(step == one)
        def _(one=one):
            value = lax.dot_general(
                lefts[one][...],
                rights[one][...],
                (((0,), (1 if flipped else 0,)), ((), ())),
                preferred_element_type=F32,
            )
            if added:
                value = value + refs[2 * count][...].astype(F32)
            rows = value.shape[0] // len(outs)
            for place, out_ref in enumerate(outs):
                out_ref[...] = value[place * rows : (place + 1) * rows].astype(out_ref.dtype)


def grad_half(pairs, side, added, flipped, across=False):
    count = len(pairs)
    row_len, width = pairs[0][0].shape
    half = width // 2
    blocks = [pair[2] if len(pair) > 2 else 0 for pair in pairs]
    pairs = [pair[:2] for pair in pairs]
    columns = pairs[-1][1].shape[0 if flipped else 1]
    arrays = [left for left, _ in pairs] + [right for _, right in pairs]
    specs = [pl.BlockSpec((row_len, half), lambda k: (0, side))] * count
    for block in blocks:
        shape = (columns, row_len) if flipped else (row_len, columns)
        specs.append(pl.BlockSpec(shape, lambda k, block=block: (block, 0)))
    if added is None:
        types = [BF16]
    else:
        arrays.append(added)
        specs.append(pl.BlockSpec((half, columns), lambda k: (0, k)))
        types = [F32, BF16, F32, BF16] if across else [F32, F32, BF16, BF16]
    rows = half // len(types)
    return pl.pallas_call(
        functools.partial(grad_kernel, count, flipped, added is not None),
        grid=(count,),
        in_specs=specs,
        out_specs=[pl.BlockSpec((rows, columns), lambda k: (0, k))] * len(types),
        out_shape=[jax.ShapeDtypeStruct((rows, count * columns), kind) for kind in types],
        compiler_params=pltpu.CompilerParams(vmem_limit_bytes=VMEM_BYTES),
        cost_estimate=LIGHT,
    )(*arrays)


def reversed_bits(block):
    masks = MASKS
    flipped = jnp.zeros_like(block)
    for rank, mask in enumerate(masks):
        flipped = flipped + ((block >> (len(masks) - 1 - rank)) & 1) * mask
    return flipped


def order_matrix(width, dtype):
    chunk = width // DEVICES
    place = lax.broadcasted_iota(jnp.int32, (width, width), 1)
    source = lax.broadcasted_iota(jnp.int32, (width, width), 0)
    entry = (lax.axis_index("dp") ^ reversed_bits(place // chunk)) * chunk + place % chunk
    return (source == entry).astype(dtype)


def thirds(values):
    high = values.astype(BF16)
    rest = values - high.astype(F32)
    middle = rest.astype(BF16)
    return jnp.concatenate([high, middle, (rest - middle.astype(F32)).astype(BF16)], axis=0)


def reorder(values, matrix):
    if values.dtype == F32:
        rows = values.shape[0]
        value = jnp.dot(thirds(values), matrix, preferred_element_type=F32)
        return value[:rows] + value[rows : 2 * rows] + value[2 * rows :]
    return jnp.dot(values, matrix, preferred_element_type=F32).astype(values.dtype)


def restore(values, matrix):
    dims = (((1,), (1,)), ((), ()))
    if values.dtype == F32:
        rows = values.shape[0]
        value = lax.dot_general(thirds(values), matrix, dims, preferred_element_type=F32)
        return value[:rows] + value[rows : 2 * rows] + value[2 * rows :]
    return lax.dot_general(values, matrix, dims, preferred_element_type=F32).astype(values.dtype)


def back_kernel(count, flipped, *refs):
    lefts, weights = refs[:count], refs[count : 3 * count]
    kept_ref, sent_ref = refs[3 * count :]
    rows = kept_ref.shape[0]
    block = weights[0].shape[0]
    step = pl.program_id(0)
    for side in range(2):
        value = None
        for one in range(count):
            term = lax.dot_general(
                lefts[one][...],
                weights[2 * one + side][...],
                (((0 if flipped else 1,), (1,)), ((), ())),
                preferred_element_type=F32,
            )
            value = term if value is None else value + term
        start = pl.multiple_of((side * pl.num_programs(0) + step) * block, block)
        kept_ref[:, pl.ds(start, block)] = value[:rows]
        sent_ref[:, pl.ds(start, block)] = value[rows:].astype(BF16)


def project_back(lefts, weights, parts, flipped=False):
    count = len(lefts)
    half = weights[0][0].shape[0]
    block = half // 2
    row_len, inner = lefts[0].shape[::-1] if flipped else lefts[0].shape
    specs = [pl.BlockSpec(left.shape, lambda k: (0, 0)) for left in lefts]
    for part in parts:
        specs += [pl.BlockSpec((block, inner), lambda k, part=part: (k, part))] * 2
    flat = [side for halves in weights for side in halves]
    whole = pl.BlockSpec((row_len // 2, 2 * half), lambda k: (0, 0))
    return pl.pallas_call(
        functools.partial(back_kernel, count, flipped),
        grid=(2,),
        in_specs=specs,
        out_specs=[whole, whole],
        out_shape=[
            jax.ShapeDtypeStruct((row_len // 2, 2 * half), F32),
            jax.ShapeDtypeStruct((row_len // 2, 2 * half), BF16),
        ],
        compiler_params=pltpu.CompilerParams(vmem_limit_bytes=VMEM_BYTES),
        cost_estimate=LIGHT,
    )(*lefts, *flat)


def head_normed(raw, gain, cosine, sine):
    inverse = lax.rsqrt(jnp.mean(raw * raw, axis=0, keepdims=True) + EPSILON)
    normed = raw * inverse * gain
    half = raw.shape[0] // 2
    first, second = normed[:half], normed[half:]
    return jnp.concatenate(
        [first * cosine - second * sine, second * cosine + first * sine], axis=0
    )


def weighted_columns(weights, rows_ref, target_ref):
    width = weights[0].shape[0]
    value = None
    for part in range(len(weights)):
        term = lax.dot_general(
            weights[part][...],
            rows_ref[:, part * width : (part + 1) * width],
            (((0,), (1,)), ((), ())),
            preferred_element_type=F32,
        )
        value = term if value is None else value + term
    target_ref[...] = value.astype(target_ref.dtype)


def attend_kernel(
    groups,
    repeat,
    w0,
    w1,
    rows_ref,
    table_ref,
    bias_ref,
    raw_ref,
    q_ref,
    k_ref,
    v_ref,
    log_ref,
    out_ref,
):
    weighted_columns((w0, w1), rows_ref, raw_ref)
    half = HD // 2
    cosine, sine = table_ref[:half, :], table_ref[half:HD, :]
    q_gain, k_gain = table_ref[HD : 2 * HD, :], table_ref[2 * HD :, :]
    heads = groups * repeat

    def group_step(group, carry):
        k_row = pl.multiple_of(group * HD, HD)
        keys = head_normed(
            raw_ref[pl.ds(heads * HD + k_row, HD), :], k_gain, cosine, sine
        ).astype(BF16)
        values = raw_ref[pl.ds((heads + groups) * HD + k_row, HD), :].astype(BF16)
        k_ref[pl.ds(k_row, HD), :] = keys
        v_ref[pl.ds(k_row, HD), :] = values
        for one in range(repeat):
            q_row = pl.multiple_of((group * repeat + one) * HD, HD)
            queries = head_normed(
                raw_ref[pl.ds(q_row, HD), :], q_gain, cosine, sine
            ).astype(BF16)
            queries = queries * jnp.asarray(HD ** (-0.5), BF16)
            q_ref[pl.ds(q_row, HD), :] = queries
            scores = (
                lax.dot_general(
                    keys, queries, (((0,), (0,)), ((), ())), preferred_element_type=F32
                )
                + bias_ref[...].astype(F32)
            )
            peaks = jnp.max(scores, axis=0, keepdims=True)
            shifted = jnp.exp(scores - peaks)
            totals = jnp.sum(shifted, axis=0, keepdims=True)
            outputs = jnp.dot(values, shifted.astype(BF16), preferred_element_type=F32)
            out_ref[pl.ds(q_row, HD), :] = (outputs / totals).astype(BF16)
            log_ref[group * repeat + one] = peaks + jnp.log(totals)
        return carry

    lax.fori_loop(0, groups, group_step, 0)


def whole_block(value):
    return pl.BlockSpec(value.shape, lambda k: (0,) * len(value.shape))


def attend_rows(weights, rows, tables, groups, repeat):
    row_len = rows.shape[0]
    heads = groups * repeat
    columns = (heads + 2 * groups) * HD
    shapes = [
        jax.ShapeDtypeStruct((columns, row_len), F32),
        jax.ShapeDtypeStruct((heads * HD, row_len), BF16),
        jax.ShapeDtypeStruct((groups * HD, row_len), BF16),
        jax.ShapeDtypeStruct((groups * HD, row_len), BF16),
        jax.ShapeDtypeStruct((heads, 1, row_len), F32),
        jax.ShapeDtypeStruct((heads * HD, row_len), BF16),
    ]
    return pl.pallas_call(
        functools.partial(attend_kernel, groups, repeat),
        grid=(1,),
        in_specs=[pl.BlockSpec((weights[0].shape[0], columns), lambda k: (0, 0))] * 2
        + [whole_block(one) for one in (rows, *tables)],
        out_specs=[whole_block(one) for one in shapes],
        out_shape=shapes,
        compiler_params=pltpu.CompilerParams(vmem_limit_bytes=VMEM_BYTES),
        cost_estimate=LIGHT,
    )(*weights, rows, *tables)


def head_back(raw, gain, grad_rot, cosine, sine):
    half = raw.shape[0] // 2
    first, second = grad_rot[:half], grad_rot[half:]
    grad = jnp.concatenate(
        [first * cosine + second * sine, second * cosine - first * sine], axis=0
    )
    inverse = lax.rsqrt(jnp.mean(raw * raw, axis=0, keepdims=True) + EPSILON)
    hat = raw * inverse
    terms = grad * hat
    grad_hat = grad * gain
    inner = jnp.mean(terms * gain, axis=0, keepdims=True)
    return inverse * (grad_hat - hat * inner), terms


def attend_back_kernel(
    groups,
    repeat,
    w0,
    w1,
    rows_ref,
    table_ref,
    bias_ref,
    raw_ref,
    q_ref,
    k_ref,
    v_ref,
    log_ref,
    grad_ref,
    q_terms_ref,
    k_terms_ref,
    outer_ref,
):
    weighted_columns((w0, w1), rows_ref, outer_ref)
    half = HD // 2
    cosine, sine = table_ref[:half, :], table_ref[half:HD, :]
    q_gain, k_gain = table_ref[HD : 2 * HD, :], table_ref[2 * HD :, :]
    heads = groups * repeat
    q_terms_ref[...] = jnp.zeros_like(q_terms_ref)
    k_terms_ref[...] = jnp.zeros_like(k_terms_ref)

    def group_step(group, carry):
        k_row = pl.multiple_of(group * HD, HD)
        keys = k_ref[pl.ds(k_row, HD), :]
        values = v_ref[pl.ds(k_row, HD), :]
        grad_keys = None
        for one in range(repeat):
            q_row = pl.multiple_of((group * repeat + one) * HD, HD)
            queries = q_ref[pl.ds(q_row, HD), :]
            outer = outer_ref[pl.ds(q_row, HD), :]
            scores = (
                lax.dot_general(
                    keys, queries, (((0,), (0,)), ((), ())), preferred_element_type=F32
                )
                + bias_ref[...].astype(F32)
            )
            attn_probs = jnp.exp(scores - log_ref[group * repeat + one])
            grad_probs = lax.dot_general(
                values, outer, (((0,), (0,)), ((), ())), preferred_element_type=F32
            )
            inner = jnp.sum(attn_probs * grad_probs, axis=0, keepdims=True)
            grad_scores = (attn_probs * (grad_probs - inner)).astype(BF16)
            grad_query = jnp.dot(keys, grad_scores, preferred_element_type=F32) * (HD ** (-0.5))
            grad_key = lax.dot_general(
                queries, grad_scores, (((1,), (1,)), ((), ())), preferred_element_type=F32
            )
            grad_value = lax.dot_general(
                outer,
                attn_probs.astype(BF16),
                (((1,), (1,)), ((), ())),
                preferred_element_type=F32,
            )
            grad_raw, terms = head_back(
                raw_ref[pl.ds(q_row, HD), :], q_gain, grad_query, cosine, sine
            )
            grad_ref[pl.ds(q_row, HD), :] = grad_raw.astype(BF16)
            q_terms_ref[...] += terms
            if grad_keys is None:
                grad_keys, grad_values = grad_key, grad_value
            else:
                grad_keys, grad_values = grad_keys + grad_key, grad_values + grad_value
        grad_raw, terms = head_back(
            raw_ref[pl.ds(heads * HD + k_row, HD), :], k_gain, grad_keys, cosine, sine
        )
        k_terms_ref[...] += terms
        grad_ref[pl.ds(heads * HD + k_row, HD), :] = grad_raw.astype(BF16)
        grad_ref[pl.ds((heads + groups) * HD + k_row, HD), :] = grad_values.astype(BF16)
        return carry

    lax.fori_loop(0, groups, group_step, 0)


def attend_rows_back(weights, rows, tables, kept, groups, repeat):
    row_len = rows.shape[0]
    heads = groups * repeat
    columns = (heads + 2 * groups) * HD
    shapes = [
        jax.ShapeDtypeStruct((columns, row_len), BF16),
        jax.ShapeDtypeStruct((HD, row_len), F32),
        jax.ShapeDtypeStruct((HD, row_len), F32),
    ]
    return pl.pallas_call(
        functools.partial(attend_back_kernel, groups, repeat),
        grid=(1,),
        in_specs=[
            pl.BlockSpec(
                (weights[0].shape[0], heads * HD), lambda k: (0, columns // (heads * HD))
            )
        ]
        * 2
        + [whole_block(one) for one in (rows, *tables, *kept)],
        out_specs=[whole_block(one) for one in shapes],
        out_shape=shapes,
        scratch_shapes=[
            pltpu.VMEM((heads * HD, row_len), BF16),
        ],
        compiler_params=pltpu.CompilerParams(vmem_limit_bytes=VMEM_BYTES),
        cost_estimate=LIGHT,
    )(*weights, rows, *tables, *kept)


def hidden_kernel(
    gate_own, gate_other, up_own, up_other, down_own, down_other, rows_ref, cot_ref, *outs
):
    gate_grad_ref, up_grad_ref, act_ref = outs
    width = gate_own.shape[0]

    def summed(source_ref, own_ref, other_ref):
        return jnp.dot(
            source_ref[:, :width], own_ref[...], preferred_element_type=F32
        ) + jnp.dot(source_ref[:, width:], other_ref[...], preferred_element_type=F32)

    gate = summed(rows_ref, gate_own, gate_other)
    up = summed(rows_ref, up_own, up_other)
    grad_act = summed(cot_ref, down_own, down_other)
    sigmoid_gate = jax.nn.sigmoid(gate)
    silu = gate * sigmoid_gate
    act_ref[...] = (silu * up).astype(BF16)
    up_grad_ref[...] = (grad_act * silu).astype(BF16)
    gate_grad_ref[...] = (
        grad_act * up * (sigmoid_gate + silu * (1.0 - sigmoid_gate))
    ).astype(BF16)


def hidden_small(weights, rows, cot_rows):
    row_len, width = rows.shape
    columns = weights[0].shape[1] // 3
    block = 256 if columns % 256 == 0 else columns
    steps = columns // block
    specs = []
    for part in range(3):
        specs += [
            pl.BlockSpec((width // 2, block), lambda k, part=part: (0, part * steps + k))
        ] * 2
    whole = pl.BlockSpec((row_len, width), lambda k: (0, 0))
    return pl.pallas_call(
        hidden_kernel,
        grid=(steps,),
        in_specs=specs + [whole, whole],
        out_specs=[pl.BlockSpec((row_len, block), lambda k: (0, k))] * 3,
        out_shape=[jax.ShapeDtypeStruct((row_len, columns), BF16)] * 3,
        compiler_params=pltpu.CompilerParams(vmem_limit_bytes=VMEM_BYTES),
        cost_estimate=LIGHT,
    )(*weights, *weights, *weights, rows, cot_rows)


def row_places(own_rows):
    own = jnp.arange(own_rows, dtype=jnp.int32)
    index = lax.axis_index("tp")
    return jnp.concatenate([own + index * own_rows, own + (1 - index) * own_rows])


def document_tables(starts, places):
    inside = places[:, None] >= starts[None, :]
    firsts = jnp.max(jnp.where(inside, starts[None, :], 0), axis=1)
    return firsts, places - firsts


def meet_kernel(count, *refs):
    total = refs[0][...]
    for other_ref in refs[1:count]:
        total = total + other_ref[...].astype(F32)
    outs = refs[count:]
    if len(outs) == 1:
        outs[0][...] = total.astype(outs[0].dtype)
        return
    half = total.shape[0] // 2
    outs[0][...] = total[half:].astype(BF16)
    outs[1][...] = total[:half]


def meet(values, kind, cost=LIGHT):
    rows, columns = values[0].shape
    steps = 3 if columns % 384 == 0 else 1
    block = columns // steps
    shapes = [(rows, kind)] if kind is not None else [(rows // 2, BF16), (rows // 2, F32)]
    return pl.pallas_call(
        functools.partial(meet_kernel, len(values)),
        grid=(steps,),
        in_specs=[pl.BlockSpec((rows, block), lambda k: (0, k))] * len(values),
        out_specs=[pl.BlockSpec((size, block), lambda k: (0, k)) for size, _ in shapes],
        out_shape=[jax.ShapeDtypeStruct((size, columns), kind) for size, kind in shapes],
        compiler_params=pltpu.CompilerParams(vmem_limit_bytes=VMEM_BYTES),
        cost_estimate=cost,
    )(*values)


def norm_kernel(inputs_ref, kept_ref, other_ref, gain_ref, normed_ref, hat_ref, inv_ref, hidden_ref):
    hidden = inputs_ref[...] + kept_ref[...] + other_ref[...].astype(F32)
    normed, hat, inverse = norm_forward(hidden, gain_ref[...])
    normed_ref[...] = normed.astype(BF16)
    hat_ref[...] = hat
    inv_ref[...] = inverse
    hidden_ref[...] = hidden


def norm_hidden(inputs, kept, other, gain):
    rows, width = inputs.shape
    shapes = [(width, BF16), (width, F32), (1, F32), (width, F32)]
    return pl.pallas_call(
        norm_kernel,
        out_shape=[jax.ShapeDtypeStruct((rows, size), kind) for size, kind in shapes],
        compiler_params=pltpu.CompilerParams(vmem_limit_bytes=VMEM_BYTES),
        cost_estimate=LIGHT,
    )(inputs, kept, other, gain)


def norm_back_kernel(kept_ref, other_ref, hat_ref, inv_ref, gain_ref, base_ref, *outs):
    low_ref, grad_ref, gain_part_ref = outs
    incoming = kept_ref[...] + other_ref[...].astype(F32)
    hat = hat_ref[...]
    grad_hat = incoming * gain_ref[...]
    inner = jnp.mean(grad_hat * hat, axis=-1, keepdims=True)
    grad = base_ref[...].astype(F32) + inv_ref[...] * (grad_hat - hat * inner)
    low_ref[...] = grad.astype(BF16)
    grad_ref[...] = grad
    gain_part_ref[...] = jnp.sum(incoming * hat, axis=0, keepdims=True)


def norm_back(kept, other, hat, inverse, gain, base):
    rows, width = kept.shape
    shapes = [(rows, BF16), (rows, F32), (1, F32)]
    return pl.pallas_call(
        norm_back_kernel,
        out_shape=[jax.ShapeDtypeStruct((size, width), kind) for size, kind in shapes],
        compiler_params=pltpu.CompilerParams(vmem_limit_bytes=VMEM_BYTES),
        cost_estimate=LIGHT,
    )(kept, other, hat, inverse, gain, base)


class Gather:
    def __init__(self, program, shard):
        self.program = program
        self.near = shard

    def start(self, mask):
        if mask == 8:
            self.far = self.program.send(self.near, 8)
        elif mask == 4:
            self.next = self.program.send(self.near, 4)
        elif mask == 2:
            self.across = self.program.send(self.near, 2)
        else:
            self.other = self.program.send(self.own, 1)

    def start_last(self):
        self.last = self.program.send(self.next, 2)

    def arrive(self, mask):
        program = self.program
        if mask == 8:
            far = program.arrive(self.far)
            self.near = program.run(stack, self.near, far)
        elif mask == 4:
            self.next = program.arrive(self.next)
        elif mask == 2:
            self.across = program.arrive(self.across)
        else:
            self.halves = [self.own, program.arrive(self.other)]

    def arrive_last(self):
        last = self.program.arrive(self.last)
        parts = (self.near, self.next, self.across, last)
        self.own = self.program.run(stack, *parts)


class GatherAcross:
    def __init__(self, program, shard):
        self.program = program
        self.parts = [shard, None]
        self.sent = [None, None]
        self.next = [None, None]

    def start_across(self):
        self.sent[1] = self.program.send(self.parts[0], 2)

    def arrive_across(self):
        self.parts[1] = self.program.arrive(self.sent[1])

    def start(self, mask, part):
        self.sent[part] = self.program.send(self.parts[part], mask)

    def arrive(self, mask, part):
        other = self.program.arrive(self.sent[part])
        if mask == 8:
            self.parts[part] = self.program.run(
                stack, self.parts[part], other
            )
        else:
            self.next[part] = other

    def join(self, cost=LIGHT):
        parts = (self.parts[0], self.next[0], self.parts[1], self.next[1])
        self.own = self.program.run(functools.partial(stack, cost=cost), *parts)

    def start_core(self):
        self.other = self.program.send(self.own, 1)

    def arrive_core(self):
        self.halves = [self.own, self.program.arrive(self.other)]


class Scatter:
    across_last = False

    def __init__(self, program, pairs, flipped=False):
        self.program, self.flipped = program, flipped
        self.arrays = [pair[:2] for pair in pairs]
        self.blocks = [pair[2:] for pair in pairs]

    def half(self, side, added):
        def step(arrays, added):
            pairs = [(*pair, *block) for pair, block in zip(arrays, self.blocks)]
            return grad_half(pairs, side, added, self.flipped, self.across_last)

        return self.program.run(step, self.arrays, added)

    def core(self):
        self.core_step()
        self.core_send()

    def core_step(self):
        self.near = self.half(1, None)[0]

    def core_send(self):
        self.other = self.program.send(self.near, 1)

    def beside(self):
        parts = self.half(0, self.other)
        self.kept, self.kept_far, self.low, self.high = parts

    def arrive_core(self):
        self.other = self.program.arrive(self.other)

    def arrive_far(self):
        self.other = self.program.arrive(self.other)

    def send_high(self):
        self.other = self.program.send(self.high, 2)

    def send_low(self):
        self.across = self.program.send(self.low, 2)

    def meet_high(self, cost=LIGHT):
        arrays = [self.kept_far, self.program.arrive(self.other)]
        self.near = self.program.run(lambda *arrays: meet(arrays, BF16, cost)[0], *arrays)

    def arrive_low(self):
        self.across = self.program.arrive(self.across)

    def send(self, mask):
        self.other = self.program.send(self.near, mask)

    def meet_far(self):
        arrays = [self.kept, self.across, self.other]
        self.near, self.kept = self.program.run(lambda *arrays: meet(arrays, None), *arrays)

    def finish(self):
        arrays = [self.kept, self.other]
        self.kept = self.program.run(lambda *arrays: meet(arrays, F32)[0], *arrays)


class ScatterAcross(Scatter):
    across_last = True

    def beside(self):
        parts = self.half(0, self.other)
        self.keep, self.near, self.others = [parts[0], parts[2]], [parts[1], parts[3]], [0, 0]

    def send_part(self, mask, part):
        self.others[part] = self.program.send(self.near[part], mask)

    def arrive_part(self, part):
        self.others[part] = self.program.arrive(self.others[part])

    def meet_part(self, part):
        arrays = [self.keep[part], self.others[part]]
        self.near[part], self.keep[part] = self.program.run(
            lambda *arrays: meet(arrays, None), *arrays
        )

    def meet_across(self):
        arrays = [self.keep[1], self.others[1]]
        self.near[1] = self.program.run(lambda *arrays: meet(arrays, BF16)[0], *arrays)

    def finish(self):
        arrays = [self.keep[0], self.others[0], self.others[1]]
        self.kept = self.program.run(lambda *arrays: meet(arrays, F32)[0], *arrays)


def restore_kernel(count, *refs):
    total = refs[0][...].astype(F32)
    for other_ref in refs[1:count]:
        total = total + other_ref[...].astype(F32)
    matrix_ref, out_ref = refs[count:]
    out_ref[...] = restore(total.astype(BF16), matrix_ref[...])


def restore_sum(matrix, *values):
    return pl.pallas_call(
        functools.partial(restore_kernel, len(values)),
        out_shape=jax.ShapeDtypeStruct(values[0].shape, BF16),
        compiler_params=pltpu.CompilerParams(vmem_limit_bytes=VMEM_BYTES),
        cost_estimate=LIGHT,
    )(*values, matrix)


def gains_kernel(attn_ref, mlp_ref, q_ref, k_ref, matrix_ref, out_ref):
    rows = jnp.concatenate([attn_ref[...], mlp_ref[...]], axis=0)
    out_ref[...] = jnp.zeros_like(out_ref)
    out_ref[0:2, :] = restore(rows, matrix_ref[...])
    ones = jnp.ones((8, q_ref.shape[1]), F32)
    for place, terms_ref in ((2, q_ref), (3, k_ref)):
        sums = lax.dot_general(
            ones,
            terms_ref[...],
            (((1,), (1,)), ((), ())),
            precision=lax.Precision.HIGHEST,
            preferred_element_type=F32,
        )
        out_ref[place : place + 1, : sums.shape[1]] = sums[:1]


def gain_parts(attn_part, mlp_part, q_terms, k_terms, matrix):
    return pl.pallas_call(
        gains_kernel,
        out_shape=jax.ShapeDtypeStruct((8, attn_part.shape[1]), F32),
        compiler_params=pltpu.CompilerParams(vmem_limit_bytes=VMEM_BYTES),
        cost_estimate=LIGHT,
    )(attn_part, mlp_part, q_terms, k_terms, matrix)


def local_small(
    tokens,
    doc_starts,
    attn_gain,
    w_query,
    w_key,
    w_value,
    q_gain,
    k_gain,
    w_out,
    mlp_gain,
    w_gate,
    w_up,
    w_down,
    out_grad,
):
    width = tokens.shape[-1]
    own_rows = tokens.shape[1]
    groups = w_key.shape[1] // HD
    repeat = w_query.shape[1] // w_key.shape[1]
    query_cols, key_cols = w_query.shape[1], w_key.shape[1]
    columns = query_cols + 2 * key_cols
    ff_cols = w_gate.shape[1]
    cut = ff_cols // 3
    program = Program()
    run, send, arrive = program.run, program.send, program.arrive

    shards = [w_query, w_key, w_value, w_out]
    plan = [(one, 0, shard.shape[1]) for one, shard in enumerate(shards)]
    attn = Gather(program, run(lambda *parts: pack(parts, [plan]), *shards)[0])
    attn.start(8)
    plans = [[(one, at, at + cut) for one in range(3)] for at in range(0, ff_cols, cut)]
    packed = run(lambda *parts: pack(parts, plans), w_gate, w_up, w_down)
    first, second = (Gather(program, one) for one in packed[:2])
    third = GatherAcross(program, packed[2])

    matrix = run(lambda: order_matrix(width, BF16))

    def attention_tables(starts, q_gain, k_gain):
        places = row_places(own_rows)
        firsts, position = document_tables(starts, places)
        cosine, sine = rope_tables(position, HD)
        rows = [cosine.T, sine.T]
        rows += [jnp.broadcast_to(gain[:, None], (HD, places.size)) for gain in (q_gain, k_gain)]
        keys = places[:, None]
        allowed = (keys <= places[None, :]) & (keys >= firsts[None, :])
        return jnp.concatenate(rows, axis=0), jnp.where(allowed, 0.0, -1e30).astype(BF16)

    def norm_tokens(tokens, attn_gain, mlp_gain):
        gains = reorder(jnp.stack([attn_gain, mlp_gain]), matrix)
        inputs = reorder(tokens, matrix).astype(F32)
        normed, hat, inverse = norm_forward(inputs, gains[0])
        return normed.astype(BF16), hat, inverse, inputs, gains

    normed_first, hat_first, inv_first, inputs, gains = run(
        norm_tokens, tokens[0], attn_gain, mlp_gain
    )
    attn_gain, mlp_gain = gains[0], gains[1]
    cotangent = run(lambda rows: reorder(rows, matrix), out_grad[0])
    tables = run(attention_tables, doc_starts[0], q_gain, k_gain)

    attn.arrive(8)
    attn.start(4)
    attn.start(2)
    first.start(8)
    rows_sent = send(normed_first, 0, 1)
    third.start_across()
    attn.arrive(4)
    attn.arrive(2)
    first.arrive(8)
    rows_first = run(stack, normed_first, arrive(rows_sent))
    third.arrive_across()
    attn.start_last()
    first.start(4)
    cot_sent = send(cotangent, 0, 1)
    third.start(8, 0)
    attn.arrive_last()
    first.arrive(4)
    cot_rows = run(stack, cotangent, arrive(cot_sent))
    third.arrive(8, 0)
    attn.start(1)
    attn.arrive(1)
    first.start(2)
    second.start(8)
    raw, queries, keys, values, logs, attended = run(
        lambda weights, rows: attend_rows(weights, rows, tables, groups, repeat),
        attn.halves,
        rows_first,
    )

    def back_rows(lefts, weights, parts, flipped=False):
        return run(
            lambda lefts, weights: project_back(lefts, weights, parts, flipped)[::-1],
            lefts,
            weights,
        )

    sent, kept = back_rows([attended], [attn.halves], [columns // query_cols], True)
    first.arrive(2)
    second.arrive(8)
    branch_sent = send(sent, 0, 1)
    first.start_last()
    second.start(4)
    third.start(8, 1)

    normed_second, hat_second, inv_second, hidden = run(
        norm_hidden, inputs, kept, arrive(branch_sent), mlp_gain[None]
    )
    first.arrive_last()
    second.arrive(4)
    third.arrive(8, 1)
    rows_sent = send(normed_second, 0, 1)
    first.start(1)
    second.start(2)
    third.start(4, 0)
    rows_second = run(stack, normed_second, arrive(rows_sent))
    first.arrive(1)
    second.arrive(2)
    third.arrive(4, 0)
    second.start_last()
    third.start(4, 1)

    def hidden_third(one):
        parts = run(hidden_small, one.halves, rows_second, cot_rows)
        return parts, [(rows_second, parts[0]), (rows_second, parts[1]), (cot_rows, parts[2])]

    parts_one, pairs = hidden_third(first)
    sum_one = Scatter(program, pairs)
    sum_one.core()
    second.arrive_last()
    third.arrive(4, 1)
    third.join(HEAVY)
    second.start(1)
    third.start_core()
    sum_one.arrive_core()
    sum_one.beside()
    second.arrive(1)
    sum_one.send_high()
    parts_two, pairs = hidden_third(second)
    sum_two = Scatter(program, pairs)
    third.arrive_core()
    sum_two.core_step()
    parts_three, pairs = hidden_third(third)
    sum_three = ScatterAcross(program, pairs)
    sum_three.core_step()
    sum_two.core_send()
    sum_three.core_send()
    sum_one.meet_high(HEAVY)
    sum_one.send_low()
    sum_one.send(4)
    parts = (parts_one, parts_two, parts_three)
    thirds_halves = [first.halves, second.halves, third.halves]
    sent, kept = back_rows(
        [one for part in parts for one in part[:2]],
        [halves for halves in thirds_halves for _ in range(2)],
        [0, 1] * 3,
    )
    grad_sent = send(sent, 0, 1)
    sum_two.arrive_core()
    sum_three.arrive_core()
    sum_two.beside()
    sum_three.beside()
    sum_one.arrive_low()
    sum_one.arrive_far()
    sum_two.send_high()
    sum_one.meet_far()
    sum_one.send(8)
    sum_three.send_part(4, 0)
    grad_branch, grad_hidden, mlp_gain_part = run(
        norm_back, kept, arrive(grad_sent), hat_second, inv_second, mlp_gain[None], cotangent
    )
    rows_sent = send(grad_branch, 0, 1)
    result_part = back_rows([part[2] for part in parts], thirds_halves, [2] * 3)
    sum_two.meet_high()
    sum_two.send_low()
    sum_two.send(4)
    sum_one.arrive_far()
    sum_one.finish()
    sum_three.arrive_part(0)
    sum_three.meet_part(0)
    sum_three.send_part(8, 0)
    branch_rows = run(stack, grad_branch, arrive(rows_sent))
    result_sent = send(result_part[0], 0, 1)
    grads, q_terms, k_terms = run(
        lambda weights, rows, kept: attend_rows_back(weights, rows, tables, kept, groups, repeat),
        attn.halves,
        branch_rows,
        (raw, queries, keys, values, logs),
    )
    sent, kept = back_rows([grads], [attn.halves], [0], True)
    pairs = [(rows_first, grads, block) for block in range(columns // query_cols)]
    sum_attn = Scatter(program, [*pairs, (branch_rows, attended)], True)
    sum_attn.core_step()
    sum_two.arrive_low()
    sum_two.arrive_far()
    sum_three.arrive_part(0)
    result_other = arrive(result_sent)
    sum_attn.core_send()
    sum_two.meet_far()
    sum_attn.arrive_core()
    sum_attn.beside()
    grad_sent = send(sent, 0, 1)
    sum_attn.send_high()
    sum_attn.send_low()
    sum_three.send_part(4, 1)
    sum_two.send(8)
    result = run(restore_sum, matrix, hidden, result_part[1], result_other)
    sum_attn.meet_high()
    sum_attn.arrive_low()
    grad_other = arrive(grad_sent)
    sum_three.arrive_part(1)
    sum_two.arrive_far()
    sum_three.meet_part(1)
    sum_attn.send(4)
    sum_three.send_part(8, 1)
    tokens_low, _, attn_gain_part = run(
        norm_back, kept, grad_other, hat_first, inv_first, attn_gain[None], grad_hidden
    )
    total = run(gain_parts, attn_gain_part, mlp_gain_part, q_terms, k_terms, matrix)

    def total_send(*partners):
        return [send(total, *partner) for partner in partners]

    def total_arrive(sent):
        return run(lambda *arrays: meet(arrays, F32)[0], total, *[arrive(one) for one in sent])

    gains_sent = total_send((0, 1))
    sum_two.finish()
    tokens_grad = run(restore_sum, matrix, tokens_low)
    sum_attn.arrive_far()
    sum_attn.meet_far()
    sum_three.arrive_part(1)
    sum_three.meet_across()
    total = total_arrive(gains_sent)
    sum_attn.send(8)
    sum_three.send_part(2, 1)
    gains_sent = total_send((1,), (2,), (3,))
    total = total_arrive(gains_sent)
    gains_sent = total_send((4,), (8,), (12,))
    sum_attn.arrive_far()
    sum_attn.finish()
    sum_three.arrive_part(1)
    sum_three.finish()

    def split_sums(*sums):
        rows = sums[0].shape[0]
        moves = [
            (source, (0, rows), (part * cut, (part + 1) * cut), part, 0, source * cut)
            for source in range(3)
            for part in range(3)
        ]
        return copy_blocks(sums, moves, [(rows, ff_cols)] * 3)

    weights = run(split_sums, sum_one.kept, sum_two.kept, sum_three.kept)
    total = total_arrive(gains_sent)

    gate_grad, up_grad, down_grad = weights
    kept = sum_attn.kept
    return (
        result[None],
        tokens_grad[None],
        total[0],
        kept[:, :query_cols],
        kept[:, query_cols : query_cols + key_cols],
        kept[:, query_cols + key_cols : columns],
        total[2, :HD],
        total[3, :HD],
        kept[:, columns:],
        total[1],
        gate_grad,
        up_grad,
        down_grad,
    )


def local(*arrays):
    small = lax.axis_size("dp") == DEVICES and lax.axis_size("tp") == 2
    if small and arrays[0].shape[1:] == (256, 1024):
        return local_small(*arrays)
    return local_large(*arrays)


def solution(mesh):
    in_specs = (
        P("dp", "tp", None),
        P("dp", None),
        P(),
        P("dp", "tp"),
        P("dp", "tp"),
        P("dp", "tp"),
        P(),
        P(),
        P("dp", "tp"),
        P(),
        P("dp", "tp"),
        P("dp", "tp"),
        P("dp", "tp"),
        P("dp", "tp", None),
    )
    out_specs = (
        P("dp", "tp", None),
        P("dp", "tp", None),
        P(),
        P("dp", "tp"),
        P("dp", "tp"),
        P("dp", "tp"),
        P(),
        P(),
        P("dp", "tp"),
        P(),
        P("dp", "tp"),
        P("dp", "tp"),
        P("dp", "tp"),
    )
    return jax.shard_map(local, mesh=mesh, in_specs=in_specs, out_specs=out_specs, check_vma=False)
```

```python
import functools

import jax
import jax.numpy as jnp
from jax import lax
from jax.experimental import pallas as pl
from jax.experimental.pallas import tpu as pltpu
from jax.sharding import PartitionSpec as P

HD = 64


EPSILON = 1e-05
THETA = 1000000.0


def documents(starts, length):
    places = jnp.arange(length, dtype=jnp.int32)
    inside = places[:, None] >= starts[None, :]
    segment = jnp.sum(inside.astype(jnp.int32), axis=1) - 1
    firsts = jnp.max(jnp.where(inside, starts[None, :], 0), axis=1)
    return (segment, places - firsts)


def rope_tables(position, width):
    half_width = width // 2
    freqs = THETA ** (-(jnp.arange(half_width, dtype=jnp.float32) * 2.0 / width))
    angles = position.astype(jnp.float32)[:, None] * freqs[None, :]
    return (jnp.cos(angles), jnp.sin(angles))


def rotate(values, cosine, sine):
    half_width = values.shape[-1] // 2
    first_half = values[..., :half_width]
    second_half = values[..., half_width:]
    tile_shape = (values.shape[0],) + (1,) * (values.ndim - 2) + (half_width,)
    cos_tile = cosine.reshape(tile_shape)
    sin_tile = sine.reshape(tile_shape)
    return jnp.concatenate(
        [
            first_half * cos_tile - second_half * sin_tile,
            second_half * cos_tile + first_half * sin_tile,
        ],
        axis=-1,
    )


def norm_forward(values, gain):
    inverse = lax.rsqrt(jnp.mean(values * values, axis=-1, keepdims=True) + EPSILON)
    normed_hat = values * inverse
    return (normed_hat * gain, normed_hat, inverse)


def norm_backward(grad_normed, normed_hat, inverse, gain):
    grad_hat = grad_normed * gain
    grad_values = inverse * (
        grad_hat - normed_hat * jnp.mean(grad_hat * normed_hat, axis=-1, keepdims=True)
    )
    gain_part = jnp.sum((grad_normed * normed_hat).reshape(-1, normed_hat.shape[-1]), axis=0)
    return (grad_values, gain_part)


def gather_rows(values):
    return lax.all_gather(values, "tp", axis=0, tiled=True)


def sum_rows(left_rows, right_weight):
    return lax.psum_scatter(
        jnp.dot(left_rows, right_weight.T, preferred_element_type=jnp.float32).astype(jnp.bfloat16),
        "tp",
        scatter_dimension=0,
        tiled=True,
    ).astype(jnp.float32)


def masked_scores(query_block, key_rows, block_segment, block_places, segment, places, score_scale):
    scores = (
        jnp.einsum("qgrd,kgd->grqk", query_block, key_rows, preferred_element_type=jnp.float32)
        * score_scale
    )
    allowed = (places[None, :] <= block_places[:, None]) & (
        segment[None, :] == block_segment[:, None]
    )
    return jnp.where(allowed, scores, -1e30)


def attend(query_rows, key_rows, value_rows, segment, block_rows):
    row_len = query_rows.shape[0]
    blocks = row_len // block_rows
    places = jnp.arange(row_len, dtype=jnp.int32)
    score_scale = query_rows.shape[-1] ** (-0.5)

    def block_out(block_item):
        query_block, block_segment, block_places = block_item
        scores = masked_scores(
            query_block, key_rows, block_segment, block_places, segment, places, score_scale
        )
        peaks = jnp.max(scores, axis=-1, keepdims=True)
        shifted = jnp.exp(scores - peaks)
        totals = jnp.sum(shifted, axis=-1, keepdims=True)
        attn_probs = (shifted / totals).astype(jnp.bfloat16)
        outputs = jnp.einsum(
            "grqk,kgd->qgrd", attn_probs, value_rows, preferred_element_type=jnp.float32
        )
        return (outputs, (peaks + jnp.log(totals))[..., 0])

    outputs, log_totals = lax.map(
        block_out,
        (
            query_rows.reshape((blocks, block_rows) + query_rows.shape[1:]),
            segment.reshape(blocks, block_rows),
            places.reshape(blocks, block_rows),
        ),
    )
    return (outputs.reshape(query_rows.shape), log_totals)


def attend_back(query_rows, key_rows, value_rows, grad_out, log_totals, segment, block_rows):
    row_len = query_rows.shape[0]
    blocks = row_len // block_rows
    places = jnp.arange(row_len, dtype=jnp.int32)
    score_scale = query_rows.shape[-1] ** (-0.5)

    def block_back(carry, block_item):
        grad_keys, grad_values = carry
        query_block, grad_block, total_block, block_segment, block_places = block_item
        scores = masked_scores(
            query_block, key_rows, block_segment, block_places, segment, places, score_scale
        )
        attn_probs = jnp.exp(scores - total_block[..., None])
        grad_probs = jnp.einsum(
            "qgrd,kgd->grqk", grad_block, value_rows, preferred_element_type=jnp.float32
        )
        inner = jnp.sum(attn_probs * grad_probs, axis=-1, keepdims=True)
        grad_scores = (attn_probs * (grad_probs - inner)).astype(jnp.bfloat16)
        grad_query = (
            jnp.einsum("grqk,kgd->qgrd", grad_scores, key_rows, preferred_element_type=jnp.float32)
            * score_scale
        )
        grad_keys = (
            grad_keys
            + jnp.einsum(
                "grqk,qgrd->kgd", grad_scores, query_block, preferred_element_type=jnp.float32
            )
            * score_scale
        )
        grad_values = grad_values + jnp.einsum(
            "grqk,qgrd->kgd",
            attn_probs.astype(jnp.bfloat16),
            grad_block,
            preferred_element_type=jnp.float32,
        )
        return ((grad_keys, grad_values), grad_query)

    zeros_kv = jnp.zeros(key_rows.shape, jnp.float32)
    block_shape = (blocks, block_rows) + query_rows.shape[1:]
    (grad_keys, grad_values), grad_queries = lax.scan(
        block_back,
        (zeros_kv, zeros_kv),
        (
            query_rows.reshape(block_shape),
            grad_out.reshape(block_shape),
            log_totals,
            segment.reshape(blocks, block_rows),
            places.reshape(blocks, block_rows),
        ),
    )
    return (grad_queries.reshape(query_rows.shape), grad_keys, grad_values)


def local_large(
    tokens,
    doc_starts,
    attn_gain,
    w_query,
    w_key,
    w_value,
    q_gain,
    k_gain,
    w_out,
    mlp_gain,
    w_gate,
    w_up,
    w_down,
    out_grad,
):
    query_w, key_w, value_w, out_w, gate_w, up_w, down_w = (
        lax.all_gather(w_query, "dp", axis=0, tiled=True),
        lax.all_gather(w_key, "dp", axis=0, tiled=True),
        lax.all_gather(w_value, "dp", axis=0, tiled=True),
        lax.all_gather(w_out, "dp", axis=0, tiled=True),
        lax.all_gather(w_gate, "dp", axis=0, tiled=True),
        lax.all_gather(w_up, "dp", axis=0, tiled=True),
        lax.all_gather(w_down, "dp", axis=0, tiled=True),
    )
    inputs = tokens[0].astype(jnp.float32)
    cotangent = out_grad[0]
    own_rows = inputs.shape[0]
    row_len = own_rows * lax.axis_size("tp")
    head_dim = HD
    groups = key_w.shape[1] // head_dim
    repeat = query_w.shape[1] // key_w.shape[1]
    query_cols = query_w.shape[1]
    key_cols = key_w.shape[1]
    ff_cols = gate_w.shape[1]
    block_rows = min(512, row_len)
    segment, position = documents(doc_starts[0], row_len)
    cosine, sine = rope_tables(position, head_dim)
    qkv_weight = jnp.concatenate([query_w, key_w, value_w], axis=1)
    gate_up_weight = jnp.concatenate([gate_w, up_w], axis=1)
    normed_first, hat_first, inv_first = norm_forward(inputs, attn_gain)
    rows_first = gather_rows(normed_first.astype(jnp.bfloat16))
    projected = jnp.dot(rows_first, qkv_weight, preferred_element_type=jnp.float32)
    query_raw = projected[:, :query_cols].reshape(row_len, groups, repeat, head_dim)
    key_raw = projected[:, query_cols : query_cols + key_cols].reshape(row_len, groups, head_dim)
    value_rows = (
        projected[:, query_cols + key_cols :]
        .astype(jnp.bfloat16)
        .reshape(row_len, groups, head_dim)
    )
    query_normed, query_hat, query_inv = norm_forward(query_raw, q_gain)
    key_normed, key_hat, key_inv = norm_forward(key_raw, k_gain)
    query_rows = rotate(query_normed, cosine, sine).astype(jnp.bfloat16)
    key_rows = rotate(key_normed, cosine, sine).astype(jnp.bfloat16)
    attended, log_totals = attend(query_rows, key_rows, value_rows, segment, block_rows)
    attended = attended.reshape(row_len, query_cols).astype(jnp.bfloat16)
    branch_out = sum_rows(attended, out_w)
    hidden = inputs + branch_out
    normed_second, hat_second, inv_second = norm_forward(hidden, mlp_gain)
    rows_second = gather_rows(normed_second.astype(jnp.bfloat16))
    gate_up = jnp.dot(rows_second, gate_up_weight, preferred_element_type=jnp.float32)
    gate_pre = gate_up[:, :ff_cols]
    up_pre = gate_up[:, ff_cols:]
    sigmoid_gate = jax.nn.sigmoid(gate_pre)
    activated = (gate_pre * sigmoid_gate * up_pre).astype(jnp.bfloat16)
    result = hidden + sum_rows(activated, down_w)
    cot_rows = gather_rows(cotangent)
    grad_act = jnp.dot(cot_rows, down_w, preferred_element_type=jnp.float32)
    grad_down = jnp.einsum("rd,rf->df", cot_rows, activated, preferred_element_type=jnp.float32)
    grad_gate = grad_act * up_pre * sigmoid_gate * (1.0 + gate_pre * (1.0 - sigmoid_gate))
    grad_up = grad_act * gate_pre * sigmoid_gate
    grad_gate_up = jnp.concatenate([grad_gate, grad_up], axis=1).astype(jnp.bfloat16)
    grad_gate_up_w = jnp.einsum(
        "rd,rf->df", rows_second, grad_gate_up, preferred_element_type=jnp.float32
    )
    grad_normed_second = sum_rows(grad_gate_up, gate_up_weight)
    grad_hidden_norm, mlp_gain_part = norm_backward(
        grad_normed_second, hat_second, inv_second, mlp_gain
    )
    grad_hidden = cotangent.astype(jnp.float32) + grad_hidden_norm
    grad_branch = grad_hidden.astype(jnp.bfloat16)
    branch_rows = gather_rows(grad_branch)
    grad_out_w = jnp.einsum("rd,rq->dq", branch_rows, attended, preferred_element_type=jnp.float32)
    grad_attended = jnp.dot(branch_rows, out_w, preferred_element_type=jnp.float32).astype(
        jnp.bfloat16
    )
    grad_query_rot, grad_key_rot, grad_value = attend_back(
        query_rows,
        key_rows,
        value_rows,
        grad_attended.reshape(row_len, groups, repeat, head_dim),
        log_totals,
        segment,
        block_rows,
    )
    grad_query_norm = rotate(grad_query_rot, cosine, -sine)
    grad_key_norm = rotate(grad_key_rot, cosine, -sine)
    grad_query_raw, q_gain_part = norm_backward(grad_query_norm, query_hat, query_inv, q_gain)
    grad_key_raw, k_gain_part = norm_backward(grad_key_norm, key_hat, key_inv, k_gain)
    grad_projected = jnp.concatenate(
        [
            grad_query_raw.reshape(row_len, query_cols),
            grad_key_raw.reshape(row_len, key_cols),
            grad_value.reshape(row_len, key_cols),
        ],
        axis=1,
    ).astype(jnp.bfloat16)
    grad_qkv_w = jnp.einsum(
        "rd,rf->df", rows_first, grad_projected, preferred_element_type=jnp.float32
    )
    grad_normed_first = sum_rows(grad_projected, qkv_weight)
    grad_input_norm, attn_gain_part = norm_backward(
        grad_normed_first, hat_first, inv_first, attn_gain
    )
    grad_inputs = grad_hidden + grad_input_norm
    summed = (
        lax.psum_scatter(
            grad_qkv_w[:, :query_cols].astype(jnp.bfloat16), "dp", scatter_dimension=0, tiled=True
        ).astype(jnp.float32),
        lax.psum_scatter(
            grad_qkv_w[:, query_cols : query_cols + key_cols].astype(jnp.bfloat16),
            "dp",
            scatter_dimension=0,
            tiled=True,
        ).astype(jnp.float32),
        lax.psum_scatter(
            grad_qkv_w[:, query_cols + key_cols :].astype(jnp.bfloat16),
            "dp",
            scatter_dimension=0,
            tiled=True,
        ).astype(jnp.float32),
        lax.psum_scatter(
            grad_out_w.astype(jnp.bfloat16), "dp", scatter_dimension=0, tiled=True
        ).astype(jnp.float32),
        lax.psum_scatter(
            grad_gate_up_w[:, :ff_cols].astype(jnp.bfloat16), "dp", scatter_dimension=0, tiled=True
        ).astype(jnp.float32),
        lax.psum_scatter(
            grad_gate_up_w[:, ff_cols:].astype(jnp.bfloat16), "dp", scatter_dimension=0, tiled=True
        ).astype(jnp.float32),
        lax.psum_scatter(
            grad_down.astype(jnp.bfloat16), "dp", scatter_dimension=0, tiled=True
        ).astype(jnp.float32),
    )
    gains = lax.psum((attn_gain_part, q_gain_part, k_gain_part, mlp_gain_part), ("dp", "tp"))
    return (
        result.astype(jnp.bfloat16)[None],
        grad_inputs.astype(jnp.bfloat16)[None],
        gains[0],
        summed[0],
        summed[1],
        summed[2],
        gains[1],
        gains[2],
        summed[3],
        gains[3],
        summed[4],
        summed[5],
        summed[6],
    )


F32 = jnp.float32
BF16 = jnp.bfloat16
VMEM_BYTES = 16 * 1024 * 1024
LIGHT = pl.CostEstimate(flops=1000, bytes_accessed=1000, transcendentals=0)
HEAVY = pl.CostEstimate(flops=13000000000, bytes_accessed=1000, transcendentals=0)


DEVICES = 16
MASKS = (1, 2, 4, 8)


def tied(values, *others):
    return lax.optimization_barrier((values, *others))[0]


class Program:
    def __init__(self):
        self.arrival = None
        self.step = None

    def begun(self):
        return [one for one in (self.arrival, self.step) if one is not None]

    def ready(self, *values):
        out = lax.optimization_barrier((*values, *self.begun()))[: len(values)]
        return out if len(out) > 1 else out[0]

    def run(self, function, *values):
        flat, tree = jax.tree.flatten(values)
        flat = lax.optimization_barrier((*flat, *self.begun()))[: len(flat)]
        out = function(*jax.tree.unflatten(tree, flat))
        self.step = jax.tree.leaves(out)[0]
        return out

    def send(self, values, mask, across=0):
        pairs = []
        for own in range(DEVICES):
            for side in range(2):
                pairs.append((own * 2 + side, (own ^ mask) * 2 + (side ^ across)))
        return lax.ppermute(self.ready(values), ("dp", "tp"), pairs)

    def arrive(self, other):
        if self.arrival is not None:
            other = tied(other, self.arrival)
        self.arrival = other
        return other


def copy_kernel(count, moves, *refs):
    semaphores = refs[-1]
    copies = []
    for place, (source, rows, columns, target, row, column) in enumerate(moves):
        size, width = rows[1] - rows[0], columns[1] - columns[0]
        copies.append(
            pltpu.make_async_copy(
                refs[source].at[rows[0] : rows[1], columns[0] : columns[1]],
                refs[count + target].at[row : row + size, column : column + width],
                semaphores.at[place],
            )
        )
    for copy in copies:
        copy.start()
    for copy in copies:
        copy.wait()


def copy_blocks(arrays, moves, shapes, cost=LIGHT):
    return pl.pallas_call(
        functools.partial(copy_kernel, len(arrays), moves),
        in_specs=[pl.BlockSpec(memory_space=pl.ANY)] * len(arrays),
        out_specs=[pl.BlockSpec(memory_space=pl.ANY)] * len(shapes),
        out_shape=[jax.ShapeDtypeStruct(shape, arrays[0].dtype) for shape in shapes],
        scratch_shapes=[pltpu.SemaphoreType.DMA((len(moves),))],
        compiler_params=pltpu.CompilerParams(vmem_limit_bytes=VMEM_BYTES),
        cost_estimate=cost,
    )(*arrays)


def pack(shards, plans):
    rows = shards[0].shape[0]
    moves, shapes = [], []
    for target, plan in enumerate(plans):
        column = 0
        for source, start, stop in plan:
            moves.append((source, (0, rows), (start, stop), target, 0, column))
            column += stop - start
        shapes.append((rows, column))
    return copy_blocks(shards, moves, shapes)


def stack(*parts, cost=LIGHT):
    moves, row = [], 0
    for source, part in enumerate(parts):
        moves.append((source, (0, part.shape[0]), (0, part.shape[1]), 0, row, 0))
        row += part.shape[0]
    return copy_blocks(parts, moves, [(row, parts[0].shape[1])], cost)[0]


def grad_kernel(count, flipped, added, *refs):
    lefts, rights = refs[:count], refs[count : 2 * count]
    outs = refs[2 * count + (1 if added else 0) :]
    step = pl.program_id(0)
    for one in range(count):

        @pl.when(step == one)
        def _(one=one):
            value = lax.dot_general(
                lefts[one][...],
                rights[one][...],
                (((0,), (1 if flipped else 0,)), ((), ())),
                preferred_element_type=F32,
            )
            if added:
                value = value + refs[2 * count][...].astype(F32)
            rows = value.shape[0] // len(outs)
            for place, out_ref in enumerate(outs):
                out_ref[...] = value[place * rows : (place + 1) * rows].astype(out_ref.dtype)


def grad_half(pairs, side, added, flipped, across=False):
    count = len(pairs)
    row_len, width = pairs[0][0].shape
    half = width // 2
    blocks = [pair[2] if len(pair) > 2 else 0 for pair in pairs]
    pairs = [pair[:2] for pair in pairs]
    columns = pairs[-1][1].shape[0 if flipped else 1]
    arrays = [left for left, _ in pairs] + [right for _, right in pairs]
    specs = [pl.BlockSpec((row_len, half), lambda k: (0, side))] * count
    for block in blocks:
        shape = (columns, row_len) if flipped else (row_len, columns)
        specs.append(pl.BlockSpec(shape, lambda k, block=block: (block, 0)))
    if added is None:
        types = [BF16]
    else:
        arrays.append(added)
        specs.append(pl.BlockSpec((half, columns), lambda k: (0, k)))
        types = [F32, BF16, F32, BF16] if across else [F32, F32, BF16, BF16]
    rows = half // len(types)
    return pl.pallas_call(
        functools.partial(grad_kernel, count, flipped, added is not None),
        grid=(count,),
        in_specs=specs,
        out_specs=[pl.BlockSpec((rows, columns), lambda k: (0, k))] * len(types),
        out_shape=[jax.ShapeDtypeStruct((rows, count * columns), kind) for kind in types],
        compiler_params=pltpu.CompilerParams(vmem_limit_bytes=VMEM_BYTES),
        cost_estimate=LIGHT,
    )(*arrays)


def reversed_bits(block):
    masks = MASKS
    flipped = jnp.zeros_like(block)
    for rank, mask in enumerate(masks):
        flipped = flipped + ((block >> (len(masks) - 1 - rank)) & 1) * mask
    return flipped


def order_matrix(width, dtype):
    chunk = width // DEVICES
    place = lax.broadcasted_iota(jnp.int32, (width, width), 1)
    source = lax.broadcasted_iota(jnp.int32, (width, width), 0)
    entry = (lax.axis_index("dp") ^ reversed_bits(place // chunk)) * chunk + place % chunk
    return (source == entry).astype(dtype)


def thirds(values):
    high = values.astype(BF16)
    rest = values - high.astype(F32)
    middle = rest.astype(BF16)
    return jnp.concatenate([high, middle, (rest - middle.astype(F32)).astype(BF16)], axis=0)


def reorder(values, matrix):
    if values.dtype == F32:
        rows = values.shape[0]
        value = jnp.dot(thirds(values), matrix, preferred_element_type=F32)
        return value[:rows] + value[rows : 2 * rows] + value[2 * rows :]
    return jnp.dot(values, matrix, preferred_element_type=F32).astype(values.dtype)


def restore(values, matrix):
    dims = (((1,), (1,)), ((), ()))
    if values.dtype == F32:
        rows = values.shape[0]
        value = lax.dot_general(thirds(values), matrix, dims, preferred_element_type=F32)
        return value[:rows] + value[rows : 2 * rows] + value[2 * rows :]
    return lax.dot_general(values, matrix, dims, preferred_element_type=F32).astype(values.dtype)


def back_kernel(count, flipped, *refs):
    lefts, weights = refs[:count], refs[count : 3 * count]
    kept_ref, sent_ref = refs[3 * count :]
    rows = kept_ref.shape[0]
    block = weights[0].shape[0]
    step = pl.program_id(0)
    for side in range(2):
        value = None
        for one in range(count):
            term = lax.dot_general(
                lefts[one][...],
                weights[2 * one + side][...],
                (((0 if flipped else 1,), (1,)), ((), ())),
                preferred_element_type=F32,
            )
            value = term if value is None else value + term
        start = pl.multiple_of((side * pl.num_programs(0) + step) * block, block)
        kept_ref[:, pl.ds(start, block)] = value[:rows]
        sent_ref[:, pl.ds(start, block)] = value[rows:].astype(BF16)


def project_back(lefts, weights, parts, flipped=False):
    count = len(lefts)
    half = weights[0][0].shape[0]
    block = half // 2
    row_len, inner = lefts[0].shape[::-1] if flipped else lefts[0].shape
    specs = [pl.BlockSpec(left.shape, lambda k: (0, 0)) for left in lefts]
    for part in parts:
        specs += [pl.BlockSpec((block, inner), lambda k, part=part: (k, part))] * 2
    flat = [side for halves in weights for side in halves]
    whole = pl.BlockSpec((row_len // 2, 2 * half), lambda k: (0, 0))
    return pl.pallas_call(
        functools.partial(back_kernel, count, flipped),
        grid=(2,),
        in_specs=specs,
        out_specs=[whole, whole],
        out_shape=[
            jax.ShapeDtypeStruct((row_len // 2, 2 * half), F32),
            jax.ShapeDtypeStruct((row_len // 2, 2 * half), BF16),
        ],
        compiler_params=pltpu.CompilerParams(vmem_limit_bytes=VMEM_BYTES),
        cost_estimate=LIGHT,
    )(*lefts, *flat)


def head_normed(raw, gain, cosine, sine):
    inverse = lax.rsqrt(jnp.mean(raw * raw, axis=0, keepdims=True) + EPSILON)
    normed = raw * inverse * gain
    half = raw.shape[0] // 2
    first, second = normed[:half], normed[half:]
    return jnp.concatenate(
        [first * cosine - second * sine, second * cosine + first * sine], axis=0
    )


def weighted_columns(weights, rows_ref, target_ref):
    width = weights[0].shape[0]
    value = None
    for part in range(len(weights)):
        term = lax.dot_general(
            weights[part][...],
            rows_ref[:, part * width : (part + 1) * width],
            (((0,), (1,)), ((), ())),
            preferred_element_type=F32,
        )
        value = term if value is None else value + term
    target_ref[...] = value.astype(target_ref.dtype)


def attend_kernel(
    groups,
    repeat,
    w0,
    w1,
    rows_ref,
    table_ref,
    bias_ref,
    raw_ref,
    q_ref,
    k_ref,
    v_ref,
    log_ref,
    out_ref,
):
    weighted_columns((w0, w1), rows_ref, raw_ref)
    half = HD // 2
    cosine, sine = table_ref[:half, :], table_ref[half:HD, :]
    q_gain, k_gain = table_ref[HD : 2 * HD, :], table_ref[2 * HD :, :]
    heads = groups * repeat

    def group_step(group, carry):
        k_row = pl.multiple_of(group * HD, HD)
        keys = head_normed(
            raw_ref[pl.ds(heads * HD + k_row, HD), :], k_gain, cosine, sine
        ).astype(BF16)
        values = raw_ref[pl.ds((heads + groups) * HD + k_row, HD), :].astype(BF16)
        k_ref[pl.ds(k_row, HD), :] = keys
        v_ref[pl.ds(k_row, HD), :] = values
        for one in range(repeat):
            q_row = pl.multiple_of((group * repeat + one) * HD, HD)
            queries = head_normed(
                raw_ref[pl.ds(q_row, HD), :], q_gain, cosine, sine
            ).astype(BF16)
            queries = queries * jnp.asarray(HD ** (-0.5), BF16)
            q_ref[pl.ds(q_row, HD), :] = queries
            scores = (
                lax.dot_general(
                    keys, queries, (((0,), (0,)), ((), ())), preferred_element_type=F32
                )
                + bias_ref[...].astype(F32)
            )
            peaks = jnp.max(scores, axis=0, keepdims=True)
            shifted = jnp.exp(scores - peaks)
            totals = jnp.sum(shifted, axis=0, keepdims=True)
            outputs = jnp.dot(values, shifted.astype(BF16), preferred_element_type=F32)
            out_ref[pl.ds(q_row, HD), :] = (outputs / totals).astype(BF16)
            log_ref[group * repeat + one] = peaks + jnp.log(totals)
        return carry

    lax.fori_loop(0, groups, group_step, 0)


def whole_block(value):
    return pl.BlockSpec(value.shape, lambda k: (0,) * len(value.shape))


def attend_rows(weights, rows, tables, groups, repeat):
    row_len = rows.shape[0]
    heads = groups * repeat
    columns = (heads + 2 * groups) * HD
    shapes = [
        jax.ShapeDtypeStruct((columns, row_len), F32),
        jax.ShapeDtypeStruct((heads * HD, row_len), BF16),
        jax.ShapeDtypeStruct((groups * HD, row_len), BF16),
        jax.ShapeDtypeStruct((groups * HD, row_len), BF16),
        jax.ShapeDtypeStruct((heads, 1, row_len), F32),
        jax.ShapeDtypeStruct((heads * HD, row_len), BF16),
    ]
    return pl.pallas_call(
        functools.partial(attend_kernel, groups, repeat),
        grid=(1,),
        in_specs=[pl.BlockSpec((weights[0].shape[0], columns), lambda k: (0, 0))] * 2
        + [whole_block(one) for one in (rows, *tables)],
        out_specs=[whole_block(one) for one in shapes],
        out_shape=shapes,
        compiler_params=pltpu.CompilerParams(vmem_limit_bytes=VMEM_BYTES),
        cost_estimate=LIGHT,
    )(*weights, rows, *tables)


def head_back(raw, gain, grad_rot, cosine, sine):
    half = raw.shape[0] // 2
    first, second = grad_rot[:half], grad_rot[half:]
    grad = jnp.concatenate(
        [first * cosine + second * sine, second * cosine - first * sine], axis=0
    )
    inverse = lax.rsqrt(jnp.mean(raw * raw, axis=0, keepdims=True) + EPSILON)
    hat = raw * inverse
    terms = grad * hat
    grad_hat = grad * gain
    inner = jnp.mean(terms * gain, axis=0, keepdims=True)
    return inverse * (grad_hat - hat * inner), terms


def attend_back_kernel(
    groups,
    repeat,
    w0,
    w1,
    rows_ref,
    table_ref,
    bias_ref,
    raw_ref,
    q_ref,
    k_ref,
    v_ref,
    log_ref,
    grad_ref,
    q_terms_ref,
    k_terms_ref,
    outer_ref,
):
    weighted_columns((w0, w1), rows_ref, outer_ref)
    half = HD // 2
    cosine, sine = table_ref[:half, :], table_ref[half:HD, :]
    q_gain, k_gain = table_ref[HD : 2 * HD, :], table_ref[2 * HD :, :]
    heads = groups * repeat
    q_terms_ref[...] = jnp.zeros_like(q_terms_ref)
    k_terms_ref[...] = jnp.zeros_like(k_terms_ref)

    def group_step(group, carry):
        k_row = pl.multiple_of(group * HD, HD)
        keys = k_ref[pl.ds(k_row, HD), :]
        values = v_ref[pl.ds(k_row, HD), :]
        grad_keys = None
        for one in range(repeat):
            q_row = pl.multiple_of((group * repeat + one) * HD, HD)
            queries = q_ref[pl.ds(q_row, HD), :]
            outer = outer_ref[pl.ds(q_row, HD), :]
            scores = (
                lax.dot_general(
                    keys, queries, (((0,), (0,)), ((), ())), preferred_element_type=F32
                )
                + bias_ref[...].astype(F32)
            )
            attn_probs = jnp.exp(scores - log_ref[group * repeat + one])
            grad_probs = lax.dot_general(
                values, outer, (((0,), (0,)), ((), ())), preferred_element_type=F32
            )
            inner = jnp.sum(attn_probs * grad_probs, axis=0, keepdims=True)
            grad_scores = (attn_probs * (grad_probs - inner)).astype(BF16)
            grad_query = jnp.dot(keys, grad_scores, preferred_element_type=F32) * (HD ** (-0.5))
            grad_key = lax.dot_general(
                queries, grad_scores, (((1,), (1,)), ((), ())), preferred_element_type=F32
            )
            grad_value = lax.dot_general(
                outer,
                attn_probs.astype(BF16),
                (((1,), (1,)), ((), ())),
                preferred_element_type=F32,
            )
            grad_raw, terms = head_back(
                raw_ref[pl.ds(q_row, HD), :], q_gain, grad_query, cosine, sine
            )
            grad_ref[pl.ds(q_row, HD), :] = grad_raw.astype(BF16)
            q_terms_ref[...] += terms
            if grad_keys is None:
                grad_keys, grad_values = grad_key, grad_value
            else:
                grad_keys, grad_values = grad_keys + grad_key, grad_values + grad_value
        grad_raw, terms = head_back(
            raw_ref[pl.ds(heads * HD + k_row, HD), :], k_gain, grad_keys, cosine, sine
        )
        k_terms_ref[...] += terms
        grad_ref[pl.ds(heads * HD + k_row, HD), :] = grad_raw.astype(BF16)
        grad_ref[pl.ds((heads + groups) * HD + k_row, HD), :] = grad_values.astype(BF16)
        return carry

    lax.fori_loop(0, groups, group_step, 0)


def attend_rows_back(weights, rows, tables, kept, groups, repeat):
    row_len = rows.shape[0]
    heads = groups * repeat
    columns = (heads + 2 * groups) * HD
    shapes = [
        jax.ShapeDtypeStruct((columns, row_len), BF16),
        jax.ShapeDtypeStruct((HD, row_len), F32),
        jax.ShapeDtypeStruct((HD, row_len), F32),
    ]
    return pl.pallas_call(
        functools.partial(attend_back_kernel, groups, repeat),
        grid=(1,),
        in_specs=[
            pl.BlockSpec(
                (weights[0].shape[0], heads * HD), lambda k: (0, columns // (heads * HD))
            )
        ]
        * 2
        + [whole_block(one) for one in (rows, *tables, *kept)],
        out_specs=[whole_block(one) for one in shapes],
        out_shape=shapes,
        scratch_shapes=[
            pltpu.VMEM((heads * HD, row_len), BF16),
        ],
        compiler_params=pltpu.CompilerParams(vmem_limit_bytes=VMEM_BYTES),
        cost_estimate=LIGHT,
    )(*weights, rows, *tables, *kept)


def hidden_kernel(
    gate_own, gate_other, up_own, up_other, down_own, down_other, rows_ref, cot_ref, *outs
):
    gate_grad_ref, up_grad_ref, act_ref = outs
    width = gate_own.shape[0]

    def summed(source_ref, own_ref, other_ref):
        return jnp.dot(
            source_ref[:, :width], own_ref[...], preferred_element_type=F32
        ) + jnp.dot(source_ref[:, width:], other_ref[...], preferred_element_type=F32)

    gate = summed(rows_ref, gate_own, gate_other)
    up = summed(rows_ref, up_own, up_other)
    grad_act = summed(cot_ref, down_own, down_other)
    sigmoid_gate = jax.nn.sigmoid(gate)
    silu = gate * sigmoid_gate
    act_ref[...] = (silu * up).astype(BF16)
    up_grad_ref[...] = (grad_act * silu).astype(BF16)
    gate_grad_ref[...] = (
        grad_act * up * (sigmoid_gate + silu * (1.0 - sigmoid_gate))
    ).astype(BF16)


def hidden_small(weights, rows, cot_rows):
    row_len, width = rows.shape
    columns = weights[0].shape[1] // 3
    block = 256 if columns % 256 == 0 else columns
    steps = columns // block
    specs = []
    for part in range(3):
        specs += [
            pl.BlockSpec((width // 2, block), lambda k, part=part: (0, part * steps + k))
        ] * 2
    whole = pl.BlockSpec((row_len, width), lambda k: (0, 0))
    return pl.pallas_call(
        hidden_kernel,
        grid=(steps,),
        in_specs=specs + [whole, whole],
        out_specs=[pl.BlockSpec((row_len, block), lambda k: (0, k))] * 3,
        out_shape=[jax.ShapeDtypeStruct((row_len, columns), BF16)] * 3,
        compiler_params=pltpu.CompilerParams(vmem_limit_bytes=VMEM_BYTES),
        cost_estimate=LIGHT,
    )(*weights, *weights, *weights, rows, cot_rows)


def row_places(own_rows):
    own = jnp.arange(own_rows, dtype=jnp.int32)
    index = lax.axis_index("tp")
    return jnp.concatenate([own + index * own_rows, own + (1 - index) * own_rows])


def document_tables(starts, places):
    inside = places[:, None] >= starts[None, :]
    firsts = jnp.max(jnp.where(inside, starts[None, :], 0), axis=1)
    return firsts, places - firsts


def meet_kernel(count, *refs):
    total = refs[0][...]
    for other_ref in refs[1:count]:
        total = total + other_ref[...].astype(F32)
    outs = refs[count:]
    if len(outs) == 1:
        outs[0][...] = total.astype(outs[0].dtype)
        return
    half = total.shape[0] // 2
    outs[0][...] = total[half:].astype(BF16)
    outs[1][...] = total[:half]


def meet(values, kind, cost=LIGHT):
    rows, columns = values[0].shape
    steps = 3 if columns % 384 == 0 else 1
    block = columns // steps
    shapes = [(rows, kind)] if kind is not None else [(rows // 2, BF16), (rows // 2, F32)]
    return pl.pallas_call(
        functools.partial(meet_kernel, len(values)),
        grid=(steps,),
        in_specs=[pl.BlockSpec((rows, block), lambda k: (0, k))] * len(values),
        out_specs=[pl.BlockSpec((size, block), lambda k: (0, k)) for size, _ in shapes],
        out_shape=[jax.ShapeDtypeStruct((size, columns), kind) for size, kind in shapes],
        compiler_params=pltpu.CompilerParams(vmem_limit_bytes=VMEM_BYTES),
        cost_estimate=cost,
    )(*values)


def norm_kernel(inputs_ref, kept_ref, other_ref, gain_ref, normed_ref, hat_ref, inv_ref, hidden_ref):
    hidden = inputs_ref[...] + kept_ref[...] + other_ref[...].astype(F32)
    normed, hat, inverse = norm_forward(hidden, gain_ref[...])
    normed_ref[...] = normed.astype(BF16)
    hat_ref[...] = hat
    inv_ref[...] = inverse
    hidden_ref[...] = hidden


def norm_hidden(inputs, kept, other, gain):
    rows, width = inputs.shape
    shapes = [(width, BF16), (width, F32), (1, F32), (width, F32)]
    return pl.pallas_call(
        norm_kernel,
        out_shape=[jax.ShapeDtypeStruct((rows, size), kind) for size, kind in shapes],
        compiler_params=pltpu.CompilerParams(vmem_limit_bytes=VMEM_BYTES),
        cost_estimate=LIGHT,
    )(inputs, kept, other, gain)


def norm_back_kernel(kept_ref, other_ref, hat_ref, inv_ref, gain_ref, base_ref, *outs):
    low_ref, grad_ref, gain_part_ref = outs
    incoming = kept_ref[...] + other_ref[...].astype(F32)
    hat = hat_ref[...]
    grad_hat = incoming * gain_ref[...]
    inner = jnp.mean(grad_hat * hat, axis=-1, keepdims=True)
    grad = base_ref[...].astype(F32) + inv_ref[...] * (grad_hat - hat * inner)
    low_ref[...] = grad.astype(BF16)
    grad_ref[...] = grad
    gain_part_ref[...] = jnp.sum(incoming * hat, axis=0, keepdims=True)


def norm_back(kept, other, hat, inverse, gain, base):
    rows, width = kept.shape
    shapes = [(rows, BF16), (rows, F32), (1, F32)]
    return pl.pallas_call(
        norm_back_kernel,
        out_shape=[jax.ShapeDtypeStruct((size, width), kind) for size, kind in shapes],
        compiler_params=pltpu.CompilerParams(vmem_limit_bytes=VMEM_BYTES),
        cost_estimate=LIGHT,
    )(kept, other, hat, inverse, gain, base)


class Gather:
    def __init__(self, program, shard):
        self.program = program
        self.near = shard

    def start(self, mask):
        if mask == 8:
            self.far = self.program.send(self.near, 8)
        elif mask == 4:
            self.next = self.program.send(self.near, 4)
        elif mask == 2:
            self.across = self.program.send(self.near, 2)
        else:
            self.other = self.program.send(self.own, 1)

    def start_last(self):
        self.last = self.program.send(self.next, 2)

    def arrive(self, mask):
        program = self.program
        if mask == 8:
            far = program.arrive(self.far)
            self.near = program.run(stack, self.near, far)
        elif mask == 4:
            self.next = program.arrive(self.next)
        elif mask == 2:
            self.across = program.arrive(self.across)
        else:
            self.halves = [self.own, program.arrive(self.other)]

    def arrive_last(self):
        last = self.program.arrive(self.last)
        parts = (self.near, self.next, self.across, last)
        self.own = self.program.run(stack, *parts)


class GatherAcross:
    def __init__(self, program, shard):
        self.program = program
        self.parts = [shard, None]
        self.sent = [None, None]
        self.next = [None, None]

    def start_across(self):
        self.sent[1] = self.program.send(self.parts[0], 2)

    def arrive_across(self):
        self.parts[1] = self.program.arrive(self.sent[1])

    def start(self, mask, part):
        self.sent[part] = self.program.send(self.parts[part], mask)

    def arrive(self, mask, part):
        other = self.program.arrive(self.sent[part])
        if mask == 8:
            self.parts[part] = self.program.run(
                stack, self.parts[part], other
            )
        else:
            self.next[part] = other

    def join(self, cost=LIGHT):
        parts = (self.parts[0], self.next[0], self.parts[1], self.next[1])
        self.own = self.program.run(functools.partial(stack, cost=cost), *parts)

    def start_core(self):
        self.other = self.program.send(self.own, 1)

    def arrive_core(self):
        self.halves = [self.own, self.program.arrive(self.other)]


class Scatter:
    across_last = False

    def __init__(self, program, pairs, flipped=False):
        self.program, self.flipped = program, flipped
        self.arrays = [pair[:2] for pair in pairs]
        self.blocks = [pair[2:] for pair in pairs]

    def half(self, side, added):
        def step(arrays, added):
            pairs = [(*pair, *block) for pair, block in zip(arrays, self.blocks)]
            return grad_half(pairs, side, added, self.flipped, self.across_last)

        return self.program.run(step, self.arrays, added)

    def core(self):
        self.core_step()
        self.core_send()

    def core_step(self):
        self.near = self.half(1, None)[0]

    def core_send(self):
        self.other = self.program.send(self.near, 1)

    def beside(self):
        parts = self.half(0, self.other)
        self.kept, self.kept_far, self.low, self.high = parts

    def arrive_core(self):
        self.other = self.program.arrive(self.other)

    def arrive_far(self):
        self.other = self.program.arrive(self.other)

    def send_high(self):
        self.other = self.program.send(self.high, 2)

    def send_low(self):
        self.across = self.program.send(self.low, 2)

    def meet_high(self, cost=LIGHT):
        arrays = [self.kept_far, self.program.arrive(self.other)]
        self.near = self.program.run(lambda *arrays: meet(arrays, BF16, cost)[0], *arrays)

    def arrive_low(self):
        self.across = self.program.arrive(self.across)

    def send(self, mask):
        self.other = self.program.send(self.near, mask)

    def meet_far(self):
        arrays = [self.kept, self.across, self.other]
        self.near, self.kept = self.program.run(lambda *arrays: meet(arrays, None), *arrays)

    def finish(self):
        arrays = [self.kept, self.other]
        self.kept = self.program.run(lambda *arrays: meet(arrays, F32)[0], *arrays)


class ScatterAcross(Scatter):
    across_last = True

    def beside(self):
        parts = self.half(0, self.other)
        self.keep, self.near, self.others = [parts[0], parts[2]], [parts[1], parts[3]], [0, 0]

    def send_part(self, mask, part):
        self.others[part] = self.program.send(self.near[part], mask)

    def arrive_part(self, part):
        self.others[part] = self.program.arrive(self.others[part])

    def meet_part(self, part):
        arrays = [self.keep[part], self.others[part]]
        self.near[part], self.keep[part] = self.program.run(
            lambda *arrays: meet(arrays, None), *arrays
        )

    def meet_across(self):
        arrays = [self.keep[1], self.others[1]]
        self.near[1] = self.program.run(lambda *arrays: meet(arrays, BF16)[0], *arrays)

    def finish(self):
        arrays = [self.keep[0], self.others[0], self.others[1]]
        self.kept = self.program.run(lambda *arrays: meet(arrays, F32)[0], *arrays)


def restore_kernel(count, *refs):
    total = refs[0][...].astype(F32)
    for other_ref in refs[1:count]:
        total = total + other_ref[...].astype(F32)
    matrix_ref, out_ref = refs[count:]
    out_ref[...] = restore(total.astype(BF16), matrix_ref[...])


def restore_sum(matrix, *values):
    return pl.pallas_call(
        functools.partial(restore_kernel, len(values)),
        out_shape=jax.ShapeDtypeStruct(values[0].shape, BF16),
        compiler_params=pltpu.CompilerParams(vmem_limit_bytes=VMEM_BYTES),
        cost_estimate=LIGHT,
    )(*values, matrix)


def gains_kernel(attn_ref, mlp_ref, q_ref, k_ref, matrix_ref, out_ref):
    rows = jnp.concatenate([attn_ref[...], mlp_ref[...]], axis=0)
    out_ref[...] = jnp.zeros_like(out_ref)
    out_ref[0:2, :] = restore(rows, matrix_ref[...])
    ones = jnp.ones((8, q_ref.shape[1]), F32)
    for place, terms_ref in ((2, q_ref), (3, k_ref)):
        sums = lax.dot_general(
            ones,
            terms_ref[...],
            (((1,), (1,)), ((), ())),
            precision=lax.Precision.HIGHEST,
            preferred_element_type=F32,
        )
        out_ref[place : place + 1, : sums.shape[1]] = sums[:1]


def gain_parts(attn_part, mlp_part, q_terms, k_terms, matrix):
    return pl.pallas_call(
        gains_kernel,
        out_shape=jax.ShapeDtypeStruct((8, attn_part.shape[1]), F32),
        compiler_params=pltpu.CompilerParams(vmem_limit_bytes=VMEM_BYTES),
        cost_estimate=LIGHT,
    )(attn_part, mlp_part, q_terms, k_terms, matrix)


def local_small(
    tokens,
    doc_starts,
    attn_gain,
    w_query,
    w_key,
    w_value,
    q_gain,
    k_gain,
    w_out,
    mlp_gain,
    w_gate,
    w_up,
    w_down,
    out_grad,
):
    width = tokens.shape[-1]
    own_rows = tokens.shape[1]
    groups = w_key.shape[1] // HD
    repeat = w_query.shape[1] // w_key.shape[1]
    query_cols, key_cols = w_query.shape[1], w_key.shape[1]
    columns = query_cols + 2 * key_cols
    ff_cols = w_gate.shape[1]
    cut = ff_cols // 3
    program = Program()
    run, send, arrive = program.run, program.send, program.arrive

    shards = [w_query, w_key, w_value, w_out]
    plan = [(one, 0, shard.shape[1]) for one, shard in enumerate(shards)]
    attn = Gather(program, run(lambda *parts: pack(parts, [plan]), *shards)[0])
    attn.start(8)
    plans = [[(one, at, at + cut) for one in range(3)] for at in range(0, ff_cols, cut)]
    packed = run(lambda *parts: pack(parts, plans), w_gate, w_up, w_down)
    first, second = (Gather(program, one) for one in packed[:2])
    third = GatherAcross(program, packed[2])

    matrix = run(lambda: order_matrix(width, BF16))

    def attention_tables(starts, q_gain, k_gain):
        places = row_places(own_rows)
        firsts, position = document_tables(starts, places)
        cosine, sine = rope_tables(position, HD)
        rows = [cosine.T, sine.T]
        rows += [jnp.broadcast_to(gain[:, None], (HD, places.size)) for gain in (q_gain, k_gain)]
        keys = places[:, None]
        allowed = (keys <= places[None, :]) & (keys >= firsts[None, :])
        return jnp.concatenate(rows, axis=0), jnp.where(allowed, 0.0, -1e30).astype(BF16)

    def norm_tokens(tokens, attn_gain, mlp_gain):
        gains = reorder(jnp.stack([attn_gain, mlp_gain]), matrix)
        inputs = reorder(tokens, matrix).astype(F32)
        normed, hat, inverse = norm_forward(inputs, gains[0])
        return normed.astype(BF16), hat, inverse, inputs, gains

    normed_first, hat_first, inv_first, inputs, gains = run(
        norm_tokens, tokens[0], attn_gain, mlp_gain
    )
    attn_gain, mlp_gain = gains[0], gains[1]
    cotangent = run(lambda rows: reorder(rows, matrix), out_grad[0])
    tables = run(attention_tables, doc_starts[0], q_gain, k_gain)

    attn.arrive(8)
    attn.start(4)
    attn.start(2)
    first.start(8)
    rows_sent = send(normed_first, 0, 1)
    third.start_across()
    attn.arrive(4)
    attn.arrive(2)
    first.arrive(8)
    rows_first = run(stack, normed_first, arrive(rows_sent))
    third.arrive_across()
    attn.start_last()
    first.start(4)
    cot_sent = send(cotangent, 0, 1)
    third.start(8, 0)
    attn.arrive_last()
    first.arrive(4)
    cot_rows = run(stack, cotangent, arrive(cot_sent))
    third.arrive(8, 0)
    attn.start(1)
    attn.arrive(1)
    first.start(2)
    second.start(8)
    raw, queries, keys, values, logs, attended = run(
        lambda weights, rows: attend_rows(weights, rows, tables, groups, repeat),
        attn.halves,
        rows_first,
    )

    def back_rows(lefts, weights, parts, flipped=False):
        return run(
            lambda lefts, weights: project_back(lefts, weights, parts, flipped)[::-1],
            lefts,
            weights,
        )

    sent, kept = back_rows([attended], [attn.halves], [columns // query_cols], True)
    first.arrive(2)
    second.arrive(8)
    branch_sent = send(sent, 0, 1)
    first.start_last()
    second.start(4)
    third.start(8, 1)

    normed_second, hat_second, inv_second, hidden = run(
        norm_hidden, inputs, kept, arrive(branch_sent), mlp_gain[None]
    )
    first.arrive_last()
    second.arrive(4)
    third.arrive(8, 1)
    rows_sent = send(normed_second, 0, 1)
    first.start(1)
    second.start(2)
    third.start(4, 0)
    rows_second = run(stack, normed_second, arrive(rows_sent))
    first.arrive(1)
    second.arrive(2)
    third.arrive(4, 0)
    second.start_last()
    third.start(4, 1)

    def hidden_third(one):
        parts = run(hidden_small, one.halves, rows_second, cot_rows)
        return parts, [(rows_second, parts[0]), (rows_second, parts[1]), (cot_rows, parts[2])]

    parts_one, pairs = hidden_third(first)
    sum_one = Scatter(program, pairs)
    sum_one.core()
    second.arrive_last()
    third.arrive(4, 1)
    third.join(HEAVY)
    second.start(1)
    third.start_core()
    sum_one.arrive_core()
    sum_one.beside()
    second.arrive(1)
    sum_one.send_high()
    parts_two, pairs = hidden_third(second)
    sum_two = Scatter(program, pairs)
    third.arrive_core()
    sum_two.core_step()
    parts_three, pairs = hidden_third(third)
    sum_three = ScatterAcross(program, pairs)
    sum_three.core_step()
    sum_two.core_send()
    sum_three.core_send()
    sum_one.meet_high(HEAVY)
    sum_one.send_low()
    sum_one.send(4)
    parts = (parts_one, parts_two, parts_three)
    thirds_halves = [first.halves, second.halves, third.halves]
    sent, kept = back_rows(
        [one for part in parts for one in part[:2]],
        [halves for halves in thirds_halves for _ in range(2)],
        [0, 1] * 3,
    )
    grad_sent = send(sent, 0, 1)
    sum_two.arrive_core()
    sum_three.arrive_core()
    sum_two.beside()
    sum_three.beside()
    sum_one.arrive_low()
    sum_one.arrive_far()
    sum_two.send_high()
    sum_one.meet_far()
    sum_one.send(8)
    sum_three.send_part(4, 0)
    grad_branch, grad_hidden, mlp_gain_part = run(
        norm_back, kept, arrive(grad_sent), hat_second, inv_second, mlp_gain[None], cotangent
    )
    rows_sent = send(grad_branch, 0, 1)
    result_part = back_rows([part[2] for part in parts], thirds_halves, [2] * 3)
    sum_two.meet_high()
    sum_two.send_low()
    sum_two.send(4)
    sum_one.arrive_far()
    sum_one.finish()
    sum_three.arrive_part(0)
    sum_three.meet_part(0)
    sum_three.send_part(8, 0)
    branch_rows = run(stack, grad_branch, arrive(rows_sent))
    result_sent = send(result_part[0], 0, 1)
    grads, q_terms, k_terms = run(
        lambda weights, rows, kept: attend_rows_back(weights, rows, tables, kept, groups, repeat),
        attn.halves,
        branch_rows,
        (raw, queries, keys, values, logs),
    )
    sent, kept = back_rows([grads], [attn.halves], [0], True)
    pairs = [(rows_first, grads, block) for block in range(columns // query_cols)]
    sum_attn = Scatter(program, [*pairs, (branch_rows, attended)], True)
    sum_attn.core_step()
    sum_two.arrive_low()
    sum_two.arrive_far()
    sum_three.arrive_part(0)
    result_other = arrive(result_sent)
    sum_attn.core_send()
    sum_two.meet_far()
    sum_attn.arrive_core()
    sum_attn.beside()
    grad_sent = send(sent, 0, 1)
    sum_attn.send_high()
    sum_attn.send_low()
    sum_three.send_part(4, 1)
    sum_two.send(8)
    result = run(restore_sum, matrix, hidden, result_part[1], result_other)
    sum_attn.meet_high()
    sum_attn.send(4)
    sum_attn.arrive_low()
    grad_other = arrive(grad_sent)
    sum_three.arrive_part(1)
    sum_two.arrive_far()
    sum_three.meet_part(1)
    sum_three.send_part(8, 1)
    tokens_low, _, attn_gain_part = run(
        norm_back, kept, grad_other, hat_first, inv_first, attn_gain[None], grad_hidden
    )
    total = run(gain_parts, attn_gain_part, mlp_gain_part, q_terms, k_terms, matrix)

    def total_send(*partners):
        return [send(total, *partner) for partner in partners]

    def total_arrive(sent):
        return run(lambda *arrays: meet(arrays, F32)[0], total, *[arrive(one) for one in sent])

    gains_sent = total_send((0, 1))
    sum_two.finish()
    tokens_grad = run(restore_sum, matrix, tokens_low)
    sum_attn.arrive_far()
    sum_attn.meet_far()
    sum_three.arrive_part(1)
    sum_three.meet_across()
    total = total_arrive(gains_sent)
    sum_attn.send(8)
    sum_three.send_part(2, 1)
    gains_sent = total_send((1,), (2,), (3,))
    total = total_arrive(gains_sent)
    gains_sent = total_send((4,), (8,), (12,))
    sum_attn.arrive_far()
    sum_attn.finish()
    sum_three.arrive_part(1)
    sum_three.finish()

    def split_sums(*sums):
        rows = sums[0].shape[0]
        moves = [
            (source, (0, rows), (part * cut, (part + 1) * cut), part, 0, source * cut)
            for source in range(3)
            for part in range(3)
        ]
        return copy_blocks(sums, moves, [(rows, ff_cols)] * 3)

    weights = run(split_sums, sum_one.kept, sum_two.kept, sum_three.kept)
    total = total_arrive(gains_sent)

    gate_grad, up_grad, down_grad = weights
    kept = sum_attn.kept
    return (
        result[None],
        tokens_grad[None],
        total[0],
        kept[:, :query_cols],
        kept[:, query_cols : query_cols + key_cols],
        kept[:, query_cols + key_cols : columns],
        total[2, :HD],
        total[3, :HD],
        kept[:, columns:],
        total[1],
        gate_grad,
        up_grad,
        down_grad,
    )


def local(*arrays):
    small = lax.axis_size("dp") == DEVICES and lax.axis_size("tp") == 2
    if small and arrays[0].shape[1:] == (256, 1024):
        return local_small(*arrays)
    return local_large(*arrays)


def solution(mesh):
    in_specs = (
        P("dp", "tp", None),
        P("dp", None),
        P(),
        P("dp", "tp"),
        P("dp", "tp"),
        P("dp", "tp"),
        P(),
        P(),
        P("dp", "tp"),
        P(),
        P("dp", "tp"),
        P("dp", "tp"),
        P("dp", "tp"),
        P("dp", "tp", None),
    )
    out_specs = (
        P("dp", "tp", None),
        P("dp", "tp", None),
        P(),
        P("dp", "tp"),
        P("dp", "tp"),
        P("dp", "tp"),
        P(),
        P(),
        P("dp", "tp"),
        P(),
        P("dp", "tp"),
        P("dp", "tp"),
        P("dp", "tp"),
    )
    return jax.shard_map(local, mesh=mesh, in_specs=in_specs, out_specs=out_specs, check_vma=False)
```

```python
import functools

import jax
import jax.numpy as jnp
from jax import lax
from jax.experimental import pallas as pl
from jax.experimental.pallas import tpu as pltpu
from jax.sharding import PartitionSpec as P

HD = 64


EPSILON = 1e-05
THETA = 1000000.0


def documents(starts, length):
    places = jnp.arange(length, dtype=jnp.int32)
    inside = places[:, None] >= starts[None, :]
    segment = jnp.sum(inside.astype(jnp.int32), axis=1) - 1
    firsts = jnp.max(jnp.where(inside, starts[None, :], 0), axis=1)
    return (segment, places - firsts)


def rope_tables(position, width):
    half_width = width // 2
    freqs = THETA ** (-(jnp.arange(half_width, dtype=jnp.float32) * 2.0 / width))
    angles = position.astype(jnp.float32)[:, None] * freqs[None, :]
    return (jnp.cos(angles), jnp.sin(angles))


def rotate(values, cosine, sine):
    half_width = values.shape[-1] // 2
    first_half = values[..., :half_width]
    second_half = values[..., half_width:]
    tile_shape = (values.shape[0],) + (1,) * (values.ndim - 2) + (half_width,)
    cos_tile = cosine.reshape(tile_shape)
    sin_tile = sine.reshape(tile_shape)
    return jnp.concatenate(
        [
            first_half * cos_tile - second_half * sin_tile,
            second_half * cos_tile + first_half * sin_tile,
        ],
        axis=-1,
    )


def norm_forward(values, gain):
    inverse = lax.rsqrt(jnp.mean(values * values, axis=-1, keepdims=True) + EPSILON)
    normed_hat = values * inverse
    return (normed_hat * gain, normed_hat, inverse)


def norm_backward(grad_normed, normed_hat, inverse, gain):
    grad_hat = grad_normed * gain
    grad_values = inverse * (
        grad_hat - normed_hat * jnp.mean(grad_hat * normed_hat, axis=-1, keepdims=True)
    )
    gain_part = jnp.sum((grad_normed * normed_hat).reshape(-1, normed_hat.shape[-1]), axis=0)
    return (grad_values, gain_part)


def gather_rows(values):
    return lax.all_gather(values, "tp", axis=0, tiled=True)


def sum_rows(left_rows, right_weight):
    return lax.psum_scatter(
        jnp.dot(left_rows, right_weight.T, preferred_element_type=jnp.float32).astype(jnp.bfloat16),
        "tp",
        scatter_dimension=0,
        tiled=True,
    ).astype(jnp.float32)


def masked_scores(query_block, key_rows, block_segment, block_places, segment, places, score_scale):
    scores = (
        jnp.einsum("qgrd,kgd->grqk", query_block, key_rows, preferred_element_type=jnp.float32)
        * score_scale
    )
    allowed = (places[None, :] <= block_places[:, None]) & (
        segment[None, :] == block_segment[:, None]
    )
    return jnp.where(allowed, scores, -1e30)


def attend(query_rows, key_rows, value_rows, segment, block_rows):
    row_len = query_rows.shape[0]
    blocks = row_len // block_rows
    places = jnp.arange(row_len, dtype=jnp.int32)
    score_scale = query_rows.shape[-1] ** (-0.5)

    def block_out(block_item):
        query_block, block_segment, block_places = block_item
        scores = masked_scores(
            query_block, key_rows, block_segment, block_places, segment, places, score_scale
        )
        peaks = jnp.max(scores, axis=-1, keepdims=True)
        shifted = jnp.exp(scores - peaks)
        totals = jnp.sum(shifted, axis=-1, keepdims=True)
        attn_probs = (shifted / totals).astype(jnp.bfloat16)
        outputs = jnp.einsum(
            "grqk,kgd->qgrd", attn_probs, value_rows, preferred_element_type=jnp.float32
        )
        return (outputs, (peaks + jnp.log(totals))[..., 0])

    outputs, log_totals = lax.map(
        block_out,
        (
            query_rows.reshape((blocks, block_rows) + query_rows.shape[1:]),
            segment.reshape(blocks, block_rows),
            places.reshape(blocks, block_rows),
        ),
    )
    return (outputs.reshape(query_rows.shape), log_totals)


def attend_back(query_rows, key_rows, value_rows, grad_out, log_totals, segment, block_rows):
    row_len = query_rows.shape[0]
    blocks = row_len // block_rows
    places = jnp.arange(row_len, dtype=jnp.int32)
    score_scale = query_rows.shape[-1] ** (-0.5)

    def block_back(carry, block_item):
        grad_keys, grad_values = carry
        query_block, grad_block, total_block, block_segment, block_places = block_item
        scores = masked_scores(
            query_block, key_rows, block_segment, block_places, segment, places, score_scale
        )
        attn_probs = jnp.exp(scores - total_block[..., None])
        grad_probs = jnp.einsum(
            "qgrd,kgd->grqk", grad_block, value_rows, preferred_element_type=jnp.float32
        )
        inner = jnp.sum(attn_probs * grad_probs, axis=-1, keepdims=True)
        grad_scores = (attn_probs * (grad_probs - inner)).astype(jnp.bfloat16)
        grad_query = (
            jnp.einsum("grqk,kgd->qgrd", grad_scores, key_rows, preferred_element_type=jnp.float32)
            * score_scale
        )
        grad_keys = (
            grad_keys
            + jnp.einsum(
                "grqk,qgrd->kgd", grad_scores, query_block, preferred_element_type=jnp.float32
            )
            * score_scale
        )
        grad_values = grad_values + jnp.einsum(
            "grqk,qgrd->kgd",
            attn_probs.astype(jnp.bfloat16),
            grad_block,
            preferred_element_type=jnp.float32,
        )
        return ((grad_keys, grad_values), grad_query)

    zeros_kv = jnp.zeros(key_rows.shape, jnp.float32)
    block_shape = (blocks, block_rows) + query_rows.shape[1:]
    (grad_keys, grad_values), grad_queries = lax.scan(
        block_back,
        (zeros_kv, zeros_kv),
        (
            query_rows.reshape(block_shape),
            grad_out.reshape(block_shape),
            log_totals,
            segment.reshape(blocks, block_rows),
            places.reshape(blocks, block_rows),
        ),
    )
    return (grad_queries.reshape(query_rows.shape), grad_keys, grad_values)


def local_large(
    tokens,
    doc_starts,
    attn_gain,
    w_query,
    w_key,
    w_value,
    q_gain,
    k_gain,
    w_out,
    mlp_gain,
    w_gate,
    w_up,
    w_down,
    out_grad,
):
    query_w, key_w, value_w, out_w, gate_w, up_w, down_w = (
        lax.all_gather(w_query, "dp", axis=0, tiled=True),
        lax.all_gather(w_key, "dp", axis=0, tiled=True),
        lax.all_gather(w_value, "dp", axis=0, tiled=True),
        lax.all_gather(w_out, "dp", axis=0, tiled=True),
        lax.all_gather(w_gate, "dp", axis=0, tiled=True),
        lax.all_gather(w_up, "dp", axis=0, tiled=True),
        lax.all_gather(w_down, "dp", axis=0, tiled=True),
    )
    inputs = tokens[0].astype(jnp.float32)
    cotangent = out_grad[0]
    own_rows = inputs.shape[0]
    row_len = own_rows * lax.axis_size("tp")
    head_dim = HD
    groups = key_w.shape[1] // head_dim
    repeat = query_w.shape[1] // key_w.shape[1]
    query_cols = query_w.shape[1]
    key_cols = key_w.shape[1]
    ff_cols = gate_w.shape[1]
    block_rows = min(512, row_len)
    segment, position = documents(doc_starts[0], row_len)
    cosine, sine = rope_tables(position, head_dim)
    qkv_weight = jnp.concatenate([query_w, key_w, value_w], axis=1)
    gate_up_weight = jnp.concatenate([gate_w, up_w], axis=1)
    normed_first, hat_first, inv_first = norm_forward(inputs, attn_gain)
    rows_first = gather_rows(normed_first.astype(jnp.bfloat16))
    projected = jnp.dot(rows_first, qkv_weight, preferred_element_type=jnp.float32)
    query_raw = projected[:, :query_cols].reshape(row_len, groups, repeat, head_dim)
    key_raw = projected[:, query_cols : query_cols + key_cols].reshape(row_len, groups, head_dim)
    value_rows = (
        projected[:, query_cols + key_cols :]
        .astype(jnp.bfloat16)
        .reshape(row_len, groups, head_dim)
    )
    query_normed, query_hat, query_inv = norm_forward(query_raw, q_gain)
    key_normed, key_hat, key_inv = norm_forward(key_raw, k_gain)
    query_rows = rotate(query_normed, cosine, sine).astype(jnp.bfloat16)
    key_rows = rotate(key_normed, cosine, sine).astype(jnp.bfloat16)
    attended, log_totals = attend(query_rows, key_rows, value_rows, segment, block_rows)
    attended = attended.reshape(row_len, query_cols).astype(jnp.bfloat16)
    branch_out = sum_rows(attended, out_w)
    hidden = inputs + branch_out
    normed_second, hat_second, inv_second = norm_forward(hidden, mlp_gain)
    rows_second = gather_rows(normed_second.astype(jnp.bfloat16))
    gate_up = jnp.dot(rows_second, gate_up_weight, preferred_element_type=jnp.float32)
    gate_pre = gate_up[:, :ff_cols]
    up_pre = gate_up[:, ff_cols:]
    sigmoid_gate = jax.nn.sigmoid(gate_pre)
    activated = (gate_pre * sigmoid_gate * up_pre).astype(jnp.bfloat16)
    result = hidden + sum_rows(activated, down_w)
    cot_rows = gather_rows(cotangent)
    grad_act = jnp.dot(cot_rows, down_w, preferred_element_type=jnp.float32)
    grad_down = jnp.einsum("rd,rf->df", cot_rows, activated, preferred_element_type=jnp.float32)
    grad_gate = grad_act * up_pre * sigmoid_gate * (1.0 + gate_pre * (1.0 - sigmoid_gate))
    grad_up = grad_act * gate_pre * sigmoid_gate
    grad_gate_up = jnp.concatenate([grad_gate, grad_up], axis=1).astype(jnp.bfloat16)
    grad_gate_up_w = jnp.einsum(
        "rd,rf->df", rows_second, grad_gate_up, preferred_element_type=jnp.float32
    )
    grad_normed_second = sum_rows(grad_gate_up, gate_up_weight)
    grad_hidden_norm, mlp_gain_part = norm_backward(
        grad_normed_second, hat_second, inv_second, mlp_gain
    )
    grad_hidden = cotangent.astype(jnp.float32) + grad_hidden_norm
    grad_branch = grad_hidden.astype(jnp.bfloat16)
    branch_rows = gather_rows(grad_branch)
    grad_out_w = jnp.einsum("rd,rq->dq", branch_rows, attended, preferred_element_type=jnp.float32)
    grad_attended = jnp.dot(branch_rows, out_w, preferred_element_type=jnp.float32).astype(
        jnp.bfloat16
    )
    grad_query_rot, grad_key_rot, grad_value = attend_back(
        query_rows,
        key_rows,
        value_rows,
        grad_attended.reshape(row_len, groups, repeat, head_dim),
        log_totals,
        segment,
        block_rows,
    )
    grad_query_norm = rotate(grad_query_rot, cosine, -sine)
    grad_key_norm = rotate(grad_key_rot, cosine, -sine)
    grad_query_raw, q_gain_part = norm_backward(grad_query_norm, query_hat, query_inv, q_gain)
    grad_key_raw, k_gain_part = norm_backward(grad_key_norm, key_hat, key_inv, k_gain)
    grad_projected = jnp.concatenate(
        [
            grad_query_raw.reshape(row_len, query_cols),
            grad_key_raw.reshape(row_len, key_cols),
            grad_value.reshape(row_len, key_cols),
        ],
        axis=1,
    ).astype(jnp.bfloat16)
    grad_qkv_w = jnp.einsum(
        "rd,rf->df", rows_first, grad_projected, preferred_element_type=jnp.float32
    )
    grad_normed_first = sum_rows(grad_projected, qkv_weight)
    grad_input_norm, attn_gain_part = norm_backward(
        grad_normed_first, hat_first, inv_first, attn_gain
    )
    grad_inputs = grad_hidden + grad_input_norm
    summed = (
        lax.psum_scatter(
            grad_qkv_w[:, :query_cols].astype(jnp.bfloat16), "dp", scatter_dimension=0, tiled=True
        ).astype(jnp.float32),
        lax.psum_scatter(
            grad_qkv_w[:, query_cols : query_cols + key_cols].astype(jnp.bfloat16),
            "dp",
            scatter_dimension=0,
            tiled=True,
        ).astype(jnp.float32),
        lax.psum_scatter(
            grad_qkv_w[:, query_cols + key_cols :].astype(jnp.bfloat16),
            "dp",
            scatter_dimension=0,
            tiled=True,
        ).astype(jnp.float32),
        lax.psum_scatter(
            grad_out_w.astype(jnp.bfloat16), "dp", scatter_dimension=0, tiled=True
        ).astype(jnp.float32),
        lax.psum_scatter(
            grad_gate_up_w[:, :ff_cols].astype(jnp.bfloat16), "dp", scatter_dimension=0, tiled=True
        ).astype(jnp.float32),
        lax.psum_scatter(
            grad_gate_up_w[:, ff_cols:].astype(jnp.bfloat16), "dp", scatter_dimension=0, tiled=True
        ).astype(jnp.float32),
        lax.psum_scatter(
            grad_down.astype(jnp.bfloat16), "dp", scatter_dimension=0, tiled=True
        ).astype(jnp.float32),
    )
    gains = lax.psum((attn_gain_part, q_gain_part, k_gain_part, mlp_gain_part), ("dp", "tp"))
    return (
        result.astype(jnp.bfloat16)[None],
        grad_inputs.astype(jnp.bfloat16)[None],
        gains[0],
        summed[0],
        summed[1],
        summed[2],
        gains[1],
        gains[2],
        summed[3],
        gains[3],
        summed[4],
        summed[5],
        summed[6],
    )


F32 = jnp.float32
BF16 = jnp.bfloat16
VMEM_BYTES = 16 * 1024 * 1024
LIGHT = pl.CostEstimate(flops=1000, bytes_accessed=1000, transcendentals=0)
HEAVY = pl.CostEstimate(flops=13000000000, bytes_accessed=1000, transcendentals=0)


DEVICES = 16
MASKS = (1, 2, 4, 8)


def tied(values, *others):
    return lax.optimization_barrier((values, *others))[0]


class Program:
    def __init__(self):
        self.arrival = None
        self.step = None

    def begun(self):
        return [one for one in (self.arrival, self.step) if one is not None]

    def ready(self, *values):
        out = lax.optimization_barrier((*values, *self.begun()))[: len(values)]
        return out if len(out) > 1 else out[0]

    def run(self, function, *values):
        flat, tree = jax.tree.flatten(values)
        flat = lax.optimization_barrier((*flat, *self.begun()))[: len(flat)]
        out = function(*jax.tree.unflatten(tree, flat))
        self.step = jax.tree.leaves(out)[0]
        return out

    def send(self, values, mask, across=0):
        pairs = []
        for own in range(DEVICES):
            for side in range(2):
                pairs.append((own * 2 + side, (own ^ mask) * 2 + (side ^ across)))
        return lax.ppermute(self.ready(values), ("dp", "tp"), pairs)

    def arrive(self, other):
        if self.arrival is not None:
            other = tied(other, self.arrival)
        self.arrival = other
        return other


def copy_kernel(count, moves, *refs):
    semaphores = refs[-1]
    copies = []
    for place, (source, rows, columns, target, row, column) in enumerate(moves):
        size, width = rows[1] - rows[0], columns[1] - columns[0]
        copies.append(
            pltpu.make_async_copy(
                refs[source].at[rows[0] : rows[1], columns[0] : columns[1]],
                refs[count + target].at[row : row + size, column : column + width],
                semaphores.at[place],
            )
        )
    for copy in copies:
        copy.start()
    for copy in copies:
        copy.wait()


def copy_blocks(arrays, moves, shapes, cost=LIGHT):
    return pl.pallas_call(
        functools.partial(copy_kernel, len(arrays), moves),
        in_specs=[pl.BlockSpec(memory_space=pl.ANY)] * len(arrays),
        out_specs=[pl.BlockSpec(memory_space=pl.ANY)] * len(shapes),
        out_shape=[jax.ShapeDtypeStruct(shape, arrays[0].dtype) for shape in shapes],
        scratch_shapes=[pltpu.SemaphoreType.DMA((len(moves),))],
        compiler_params=pltpu.CompilerParams(vmem_limit_bytes=VMEM_BYTES),
        cost_estimate=cost,
    )(*arrays)


def pack(shards, plans):
    rows = shards[0].shape[0]
    moves, shapes = [], []
    for target, plan in enumerate(plans):
        column = 0
        for source, start, stop in plan:
            moves.append((source, (0, rows), (start, stop), target, 0, column))
            column += stop - start
        shapes.append((rows, column))
    return copy_blocks(shards, moves, shapes)


def stack(*parts, cost=LIGHT):
    moves, row = [], 0
    for source, part in enumerate(parts):
        moves.append((source, (0, part.shape[0]), (0, part.shape[1]), 0, row, 0))
        row += part.shape[0]
    return copy_blocks(parts, moves, [(row, parts[0].shape[1])], cost)[0]


def grad_kernel(count, flipped, added, *refs):
    lefts, rights = refs[:count], refs[count : 2 * count]
    outs = refs[2 * count + (1 if added else 0) :]
    step = pl.program_id(0)
    for one in range(count):

        @pl.when(step == one)
        def _(one=one):
            value = lax.dot_general(
                lefts[one][...],
                rights[one][...],
                (((0,), (1 if flipped else 0,)), ((), ())),
                preferred_element_type=F32,
            )
            if added:
                value = value + refs[2 * count][...].astype(F32)
            rows = value.shape[0] // len(outs)
            for place, out_ref in enumerate(outs):
                out_ref[...] = value[place * rows : (place + 1) * rows].astype(out_ref.dtype)


def grad_half(pairs, side, added, flipped, across=False):
    count = len(pairs)
    row_len, width = pairs[0][0].shape
    half = width // 2
    blocks = [pair[2] if len(pair) > 2 else 0 for pair in pairs]
    pairs = [pair[:2] for pair in pairs]
    columns = pairs[-1][1].shape[0 if flipped else 1]
    arrays = [left for left, _ in pairs] + [right for _, right in pairs]
    specs = [pl.BlockSpec((row_len, half), lambda k: (0, side))] * count
    for block in blocks:
        shape = (columns, row_len) if flipped else (row_len, columns)
        specs.append(pl.BlockSpec(shape, lambda k, block=block: (block, 0)))
    if added is None:
        types = [BF16]
    else:
        arrays.append(added)
        specs.append(pl.BlockSpec((half, columns), lambda k: (0, k)))
        types = [F32, BF16, F32, BF16] if across else [F32, F32, BF16, BF16]
    rows = half // len(types)
    return pl.pallas_call(
        functools.partial(grad_kernel, count, flipped, added is not None),
        grid=(count,),
        in_specs=specs,
        out_specs=[pl.BlockSpec((rows, columns), lambda k: (0, k))] * len(types),
        out_shape=[jax.ShapeDtypeStruct((rows, count * columns), kind) for kind in types],
        compiler_params=pltpu.CompilerParams(vmem_limit_bytes=VMEM_BYTES),
        cost_estimate=LIGHT,
    )(*arrays)


def reversed_bits(block):
    masks = MASKS
    flipped = jnp.zeros_like(block)
    for rank, mask in enumerate(masks):
        flipped = flipped + ((block >> (len(masks) - 1 - rank)) & 1) * mask
    return flipped


def order_matrix(width, dtype):
    chunk = width // DEVICES
    place = lax.broadcasted_iota(jnp.int32, (width, width), 1)
    source = lax.broadcasted_iota(jnp.int32, (width, width), 0)
    entry = (lax.axis_index("dp") ^ reversed_bits(place // chunk)) * chunk + place % chunk
    return (source == entry).astype(dtype)


def thirds(values):
    high = values.astype(BF16)
    rest = values - high.astype(F32)
    middle = rest.astype(BF16)
    return jnp.concatenate([high, middle, (rest - middle.astype(F32)).astype(BF16)], axis=0)


def reorder(values, matrix):
    if values.dtype == F32:
        rows = values.shape[0]
        value = jnp.dot(thirds(values), matrix, preferred_element_type=F32)
        return value[:rows] + value[rows : 2 * rows] + value[2 * rows :]
    return jnp.dot(values, matrix, preferred_element_type=F32).astype(values.dtype)


def restore(values, matrix):
    dims = (((1,), (1,)), ((), ()))
    if values.dtype == F32:
        rows = values.shape[0]
        value = lax.dot_general(thirds(values), matrix, dims, preferred_element_type=F32)
        return value[:rows] + value[rows : 2 * rows] + value[2 * rows :]
    return lax.dot_general(values, matrix, dims, preferred_element_type=F32).astype(values.dtype)


def back_kernel(count, flipped, *refs):
    lefts, weights = refs[:count], refs[count : 3 * count]
    kept_ref, sent_ref = refs[3 * count :]
    rows = kept_ref.shape[0]
    block = weights[0].shape[0]
    step = pl.program_id(0)
    for side in range(2):
        value = None
        for one in range(count):
            term = lax.dot_general(
                lefts[one][...],
                weights[2 * one + side][...],
                (((0 if flipped else 1,), (1,)), ((), ())),
                preferred_element_type=F32,
            )
            value = term if value is None else value + term
        start = pl.multiple_of((side * pl.num_programs(0) + step) * block, block)
        kept_ref[:, pl.ds(start, block)] = value[:rows]
        sent_ref[:, pl.ds(start, block)] = value[rows:].astype(BF16)


def project_back(lefts, weights, parts, flipped=False):
    count = len(lefts)
    half = weights[0][0].shape[0]
    block = half // 2
    row_len, inner = lefts[0].shape[::-1] if flipped else lefts[0].shape
    specs = [pl.BlockSpec(left.shape, lambda k: (0, 0)) for left in lefts]
    for part in parts:
        specs += [pl.BlockSpec((block, inner), lambda k, part=part: (k, part))] * 2
    flat = [side for halves in weights for side in halves]
    whole = pl.BlockSpec((row_len // 2, 2 * half), lambda k: (0, 0))
    return pl.pallas_call(
        functools.partial(back_kernel, count, flipped),
        grid=(2,),
        in_specs=specs,
        out_specs=[whole, whole],
        out_shape=[
            jax.ShapeDtypeStruct((row_len // 2, 2 * half), F32),
            jax.ShapeDtypeStruct((row_len // 2, 2 * half), BF16),
        ],
        compiler_params=pltpu.CompilerParams(vmem_limit_bytes=VMEM_BYTES),
        cost_estimate=LIGHT,
    )(*lefts, *flat)


def head_normed(raw, gain, cosine, sine):
    inverse = lax.rsqrt(jnp.mean(raw * raw, axis=0, keepdims=True) + EPSILON)
    normed = raw * inverse * gain
    half = raw.shape[0] // 2
    first, second = normed[:half], normed[half:]
    return jnp.concatenate(
        [first * cosine - second * sine, second * cosine + first * sine], axis=0
    )


def weighted_columns(weights, rows_ref, target_ref):
    width = weights[0].shape[0]
    value = None
    for part in range(len(weights)):
        term = lax.dot_general(
            weights[part][...],
            rows_ref[:, part * width : (part + 1) * width],
            (((0,), (1,)), ((), ())),
            preferred_element_type=F32,
        )
        value = term if value is None else value + term
    target_ref[...] = value.astype(target_ref.dtype)


def attend_kernel(
    groups,
    repeat,
    w0,
    w1,
    rows_ref,
    table_ref,
    bias_ref,
    raw_ref,
    q_ref,
    k_ref,
    v_ref,
    log_ref,
    out_ref,
):
    weighted_columns((w0, w1), rows_ref, raw_ref)
    half = HD // 2
    cosine, sine = table_ref[:half, :], table_ref[half:HD, :]
    q_gain, k_gain = table_ref[HD : 2 * HD, :], table_ref[2 * HD :, :]
    heads = groups * repeat

    def group_step(group, carry):
        k_row = pl.multiple_of(group * HD, HD)
        keys = head_normed(
            raw_ref[pl.ds(heads * HD + k_row, HD), :], k_gain, cosine, sine
        ).astype(BF16)
        values = raw_ref[pl.ds((heads + groups) * HD + k_row, HD), :].astype(BF16)
        k_ref[pl.ds(k_row, HD), :] = keys
        v_ref[pl.ds(k_row, HD), :] = values
        for one in range(repeat):
            q_row = pl.multiple_of((group * repeat + one) * HD, HD)
            queries = head_normed(
                raw_ref[pl.ds(q_row, HD), :], q_gain, cosine, sine
            ).astype(BF16)
            queries = queries * jnp.asarray(HD ** (-0.5), BF16)
            q_ref[pl.ds(q_row, HD), :] = queries
            scores = (
                lax.dot_general(
                    keys, queries, (((0,), (0,)), ((), ())), preferred_element_type=F32
                )
                + bias_ref[...].astype(F32)
            )
            peaks = jnp.max(scores, axis=0, keepdims=True)
            shifted = jnp.exp(scores - peaks)
            totals = jnp.sum(shifted, axis=0, keepdims=True)
            outputs = jnp.dot(values, shifted.astype(BF16), preferred_element_type=F32)
            out_ref[pl.ds(q_row, HD), :] = (outputs / totals).astype(BF16)
            log_ref[group * repeat + one] = peaks + jnp.log(totals)
        return carry

    lax.fori_loop(0, groups, group_step, 0)


def whole_block(value):
    return pl.BlockSpec(value.shape, lambda k: (0,) * len(value.shape))


def attend_rows(weights, rows, tables, groups, repeat):
    row_len = rows.shape[0]
    heads = groups * repeat
    columns = (heads + 2 * groups) * HD
    shapes = [
        jax.ShapeDtypeStruct((columns, row_len), F32),
        jax.ShapeDtypeStruct((heads * HD, row_len), BF16),
        jax.ShapeDtypeStruct((groups * HD, row_len), BF16),
        jax.ShapeDtypeStruct((groups * HD, row_len), BF16),
        jax.ShapeDtypeStruct((heads, 1, row_len), F32),
        jax.ShapeDtypeStruct((heads * HD, row_len), BF16),
    ]
    return pl.pallas_call(
        functools.partial(attend_kernel, groups, repeat),
        grid=(1,),
        in_specs=[pl.BlockSpec((weights[0].shape[0], columns), lambda k: (0, 0))] * 2
        + [whole_block(one) for one in (rows, *tables)],
        out_specs=[whole_block(one) for one in shapes],
        out_shape=shapes,
        compiler_params=pltpu.CompilerParams(vmem_limit_bytes=VMEM_BYTES),
        cost_estimate=LIGHT,
    )(*weights, rows, *tables)


def head_back(raw, gain, grad_rot, cosine, sine):
    half = raw.shape[0] // 2
    first, second = grad_rot[:half], grad_rot[half:]
    grad = jnp.concatenate(
        [first * cosine + second * sine, second * cosine - first * sine], axis=0
    )
    inverse = lax.rsqrt(jnp.mean(raw * raw, axis=0, keepdims=True) + EPSILON)
    hat = raw * inverse
    terms = grad * hat
    grad_hat = grad * gain
    inner = jnp.mean(terms * gain, axis=0, keepdims=True)
    return inverse * (grad_hat - hat * inner), terms


def attend_back_kernel(
    groups,
    repeat,
    w0,
    w1,
    rows_ref,
    table_ref,
    bias_ref,
    raw_ref,
    q_ref,
    k_ref,
    v_ref,
    log_ref,
    grad_ref,
    q_terms_ref,
    k_terms_ref,
    outer_ref,
):
    weighted_columns((w0, w1), rows_ref, outer_ref)
    half = HD // 2
    cosine, sine = table_ref[:half, :], table_ref[half:HD, :]
    q_gain, k_gain = table_ref[HD : 2 * HD, :], table_ref[2 * HD :, :]
    heads = groups * repeat
    q_terms_ref[...] = jnp.zeros_like(q_terms_ref)
    k_terms_ref[...] = jnp.zeros_like(k_terms_ref)

    def group_step(group, carry):
        k_row = pl.multiple_of(group * HD, HD)
        keys = k_ref[pl.ds(k_row, HD), :]
        values = v_ref[pl.ds(k_row, HD), :]
        grad_keys = None
        for one in range(repeat):
            q_row = pl.multiple_of((group * repeat + one) * HD, HD)
            queries = q_ref[pl.ds(q_row, HD), :]
            outer = outer_ref[pl.ds(q_row, HD), :]
            scores = (
                lax.dot_general(
                    keys, queries, (((0,), (0,)), ((), ())), preferred_element_type=F32
                )
                + bias_ref[...].astype(F32)
            )
            attn_probs = jnp.exp(scores - log_ref[group * repeat + one])
            grad_probs = lax.dot_general(
                values, outer, (((0,), (0,)), ((), ())), preferred_element_type=F32
            )
            inner = jnp.sum(attn_probs * grad_probs, axis=0, keepdims=True)
            grad_scores = (attn_probs * (grad_probs - inner)).astype(BF16)
            grad_query = jnp.dot(keys, grad_scores, preferred_element_type=F32) * (HD ** (-0.5))
            grad_key = lax.dot_general(
                queries, grad_scores, (((1,), (1,)), ((), ())), preferred_element_type=F32
            )
            grad_value = lax.dot_general(
                outer,
                attn_probs.astype(BF16),
                (((1,), (1,)), ((), ())),
                preferred_element_type=F32,
            )
            grad_raw, terms = head_back(
                raw_ref[pl.ds(q_row, HD), :], q_gain, grad_query, cosine, sine
            )
            grad_ref[pl.ds(q_row, HD), :] = grad_raw.astype(BF16)
            q_terms_ref[...] += terms
            if grad_keys is None:
                grad_keys, grad_values = grad_key, grad_value
            else:
                grad_keys, grad_values = grad_keys + grad_key, grad_values + grad_value
        grad_raw, terms = head_back(
            raw_ref[pl.ds(heads * HD + k_row, HD), :], k_gain, grad_keys, cosine, sine
        )
        k_terms_ref[...] += terms
        grad_ref[pl.ds(heads * HD + k_row, HD), :] = grad_raw.astype(BF16)
        grad_ref[pl.ds((heads + groups) * HD + k_row, HD), :] = grad_values.astype(BF16)
        return carry

    lax.fori_loop(0, groups, group_step, 0)


def attend_rows_back(weights, rows, tables, kept, groups, repeat):
    row_len = rows.shape[0]
    heads = groups * repeat
    columns = (heads + 2 * groups) * HD
    shapes = [
        jax.ShapeDtypeStruct((columns, row_len), BF16),
        jax.ShapeDtypeStruct((HD, row_len), F32),
        jax.ShapeDtypeStruct((HD, row_len), F32),
    ]
    return pl.pallas_call(
        functools.partial(attend_back_kernel, groups, repeat),
        grid=(1,),
        in_specs=[
            pl.BlockSpec(
                (weights[0].shape[0], heads * HD), lambda k: (0, columns // (heads * HD))
            )
        ]
        * 2
        + [whole_block(one) for one in (rows, *tables, *kept)],
        out_specs=[whole_block(one) for one in shapes],
        out_shape=shapes,
        scratch_shapes=[
            pltpu.VMEM((heads * HD, row_len), BF16),
        ],
        compiler_params=pltpu.CompilerParams(vmem_limit_bytes=VMEM_BYTES),
        cost_estimate=LIGHT,
    )(*weights, rows, *tables, *kept)


def hidden_kernel(
    gate_own, gate_other, up_own, up_other, down_own, down_other, rows_ref, cot_ref, *outs
):
    gate_grad_ref, up_grad_ref, act_ref = outs
    width = gate_own.shape[0]

    def summed(source_ref, own_ref, other_ref):
        return jnp.dot(
            source_ref[:, :width], own_ref[...], preferred_element_type=F32
        ) + jnp.dot(source_ref[:, width:], other_ref[...], preferred_element_type=F32)

    gate = summed(rows_ref, gate_own, gate_other)
    up = summed(rows_ref, up_own, up_other)
    grad_act = summed(cot_ref, down_own, down_other)
    sigmoid_gate = jax.nn.sigmoid(gate)
    silu = gate * sigmoid_gate
    act_ref[...] = (silu * up).astype(BF16)
    up_grad_ref[...] = (grad_act * silu).astype(BF16)
    gate_grad_ref[...] = (
        grad_act * up * (sigmoid_gate + silu * (1.0 - sigmoid_gate))
    ).astype(BF16)


def hidden_small(weights, rows, cot_rows):
    row_len, width = rows.shape
    columns = weights[0].shape[1] // 3
    block = 384 if columns % 384 == 0 else columns
    steps = columns // block
    specs = []
    for part in range(3):
        specs += [
            pl.BlockSpec((width // 2, block), lambda k, part=part: (0, part * steps + k))
        ] * 2
    whole = pl.BlockSpec((row_len, width), lambda k: (0, 0))
    return pl.pallas_call(
        hidden_kernel,
        grid=(steps,),
        in_specs=specs + [whole, whole],
        out_specs=[pl.BlockSpec((row_len, block), lambda k: (0, k))] * 3,
        out_shape=[jax.ShapeDtypeStruct((row_len, columns), BF16)] * 3,
        compiler_params=pltpu.CompilerParams(vmem_limit_bytes=VMEM_BYTES),
        cost_estimate=LIGHT,
    )(*weights, *weights, *weights, rows, cot_rows)


def row_places(own_rows):
    own = jnp.arange(own_rows, dtype=jnp.int32)
    index = lax.axis_index("tp")
    return jnp.concatenate([own + index * own_rows, own + (1 - index) * own_rows])


def document_tables(starts, places):
    inside = places[:, None] >= starts[None, :]
    firsts = jnp.max(jnp.where(inside, starts[None, :], 0), axis=1)
    return firsts, places - firsts


def meet_kernel(count, *refs):
    total = refs[0][...]
    for other_ref in refs[1:count]:
        total = total + other_ref[...].astype(F32)
    outs = refs[count:]
    if len(outs) == 1:
        outs[0][...] = total.astype(outs[0].dtype)
        return
    half = total.shape[0] // 2
    outs[0][...] = total[half:].astype(BF16)
    outs[1][...] = total[:half]


def meet(values, kind, cost=LIGHT):
    rows, columns = values[0].shape
    steps = 3 if columns % 384 == 0 and rows > 128 else 1
    block = columns // steps
    shapes = [(rows, kind)] if kind is not None else [(rows // 2, BF16), (rows // 2, F32)]
    return pl.pallas_call(
        functools.partial(meet_kernel, len(values)),
        grid=(steps,),
        in_specs=[pl.BlockSpec((rows, block), lambda k: (0, k))] * len(values),
        out_specs=[pl.BlockSpec((size, block), lambda k: (0, k)) for size, _ in shapes],
        out_shape=[jax.ShapeDtypeStruct((size, columns), kind) for size, kind in shapes],
        compiler_params=pltpu.CompilerParams(vmem_limit_bytes=VMEM_BYTES),
        cost_estimate=cost,
    )(*values)


def norm_kernel(inputs_ref, kept_ref, other_ref, gain_ref, normed_ref, hat_ref, inv_ref, hidden_ref):
    hidden = inputs_ref[...] + kept_ref[...] + other_ref[...].astype(F32)
    normed, hat, inverse = norm_forward(hidden, gain_ref[...])
    normed_ref[...] = normed.astype(BF16)
    hat_ref[...] = hat
    inv_ref[...] = inverse
    hidden_ref[...] = hidden


def norm_hidden(inputs, kept, other, gain):
    rows, width = inputs.shape
    shapes = [(width, BF16), (width, F32), (1, F32), (width, F32)]
    return pl.pallas_call(
        norm_kernel,
        out_shape=[jax.ShapeDtypeStruct((rows, size), kind) for size, kind in shapes],
        compiler_params=pltpu.CompilerParams(vmem_limit_bytes=VMEM_BYTES),
        cost_estimate=LIGHT,
    )(inputs, kept, other, gain)


def norm_back_kernel(kept_ref, other_ref, hat_ref, inv_ref, gain_ref, base_ref, *outs):
    low_ref, grad_ref, gain_part_ref = outs
    incoming = kept_ref[...] + other_ref[...].astype(F32)
    hat = hat_ref[...]
    grad_hat = incoming * gain_ref[...]
    inner = jnp.mean(grad_hat * hat, axis=-1, keepdims=True)
    grad = base_ref[...].astype(F32) + inv_ref[...] * (grad_hat - hat * inner)
    low_ref[...] = grad.astype(BF16)
    grad_ref[...] = grad
    gain_part_ref[...] = jnp.sum(incoming * hat, axis=0, keepdims=True)


def norm_back(kept, other, hat, inverse, gain, base):
    rows, width = kept.shape
    shapes = [(rows, BF16), (rows, F32), (1, F32)]
    return pl.pallas_call(
        norm_back_kernel,
        out_shape=[jax.ShapeDtypeStruct((size, width), kind) for size, kind in shapes],
        compiler_params=pltpu.CompilerParams(vmem_limit_bytes=VMEM_BYTES),
        cost_estimate=LIGHT,
    )(kept, other, hat, inverse, gain, base)


class Gather:
    def __init__(self, program, shard):
        self.program = program
        self.near = shard

    def start(self, mask):
        if mask == 8:
            self.far = self.program.send(self.near, 8)
        elif mask == 4:
            self.next = self.program.send(self.near, 4)
        elif mask == 2:
            self.across = self.program.send(self.near, 2)
        else:
            self.other = self.program.send(self.own, 1)

    def start_last(self):
        self.last = self.program.send(self.next, 2)

    def arrive(self, mask):
        program = self.program
        if mask == 8:
            far = program.arrive(self.far)
            self.near = program.run(stack, self.near, far)
        elif mask == 4:
            self.next = program.arrive(self.next)
        elif mask == 2:
            self.across = program.arrive(self.across)
        else:
            self.halves = [self.own, program.arrive(self.other)]

    def arrive_last(self):
        last = self.program.arrive(self.last)
        parts = (self.near, self.next, self.across, last)
        self.own = self.program.run(stack, *parts)


class GatherAcross:
    def __init__(self, program, shard):
        self.program = program
        self.parts = [shard, None]
        self.sent = [None, None]
        self.next = [None, None]

    def start_across(self):
        self.sent[1] = self.program.send(self.parts[0], 2)

    def arrive_across(self):
        self.parts[1] = self.program.arrive(self.sent[1])

    def start(self, mask, part):
        self.sent[part] = self.program.send(self.parts[part], mask)

    def arrive(self, mask, part):
        other = self.program.arrive(self.sent[part])
        if mask == 8:
            self.parts[part] = self.program.run(
                stack, self.parts[part], other
            )
        else:
            self.next[part] = other

    def join(self, cost=LIGHT):
        parts = (self.parts[0], self.next[0], self.parts[1], self.next[1])
        self.own = self.program.run(functools.partial(stack, cost=cost), *parts)

    def start_core(self):
        self.other = self.program.send(self.own, 1)

    def arrive_core(self):
        self.halves = [self.own, self.program.arrive(self.other)]


class Scatter:
    across_last = False

    def __init__(self, program, pairs, flipped=False):
        self.program, self.flipped = program, flipped
        self.arrays = [pair[:2] for pair in pairs]
        self.blocks = [pair[2:] for pair in pairs]

    def half(self, side, added):
        def step(arrays, added):
            pairs = [(*pair, *block) for pair, block in zip(arrays, self.blocks)]
            return grad_half(pairs, side, added, self.flipped, self.across_last)

        return self.program.run(step, self.arrays, added)

    def core(self):
        self.core_step()
        self.core_send()

    def core_step(self):
        self.near = self.half(1, None)[0]

    def core_send(self):
        self.other = self.program.send(self.near, 1)

    def beside(self):
        parts = self.half(0, self.other)
        self.kept, self.kept_far, self.low, self.high = parts

    def arrive_core(self):
        self.other = self.program.arrive(self.other)

    def arrive_far(self):
        self.other = self.program.arrive(self.other)

    def send_high(self):
        self.other = self.program.send(self.high, 2)

    def send_low(self):
        self.across = self.program.send(self.low, 2)

    def meet_high(self, cost=LIGHT):
        arrays = [self.kept_far, self.program.arrive(self.other)]
        self.near = self.program.run(lambda *arrays: meet(arrays, BF16, cost)[0], *arrays)

    def arrive_low(self):
        self.across = self.program.arrive(self.across)

    def send(self, mask):
        self.other = self.program.send(self.near, mask)

    def meet_far(self):
        arrays = [self.kept, self.across, self.other]
        self.near, self.kept = self.program.run(lambda *arrays: meet(arrays, None), *arrays)

    def finish(self):
        arrays = [self.kept, self.other]
        self.kept = self.program.run(lambda *arrays: meet(arrays, F32)[0], *arrays)


class ScatterAcross(Scatter):
    across_last = True

    def beside(self):
        parts = self.half(0, self.other)
        self.keep, self.near, self.others = [parts[0], parts[2]], [parts[1], parts[3]], [0, 0]

    def send_part(self, mask, part):
        self.others[part] = self.program.send(self.near[part], mask)

    def arrive_part(self, part):
        self.others[part] = self.program.arrive(self.others[part])

    def meet_part(self, part):
        arrays = [self.keep[part], self.others[part]]
        self.near[part], self.keep[part] = self.program.run(
            lambda *arrays: meet(arrays, None), *arrays
        )

    def meet_across(self):
        arrays = [self.keep[1], self.others[1]]
        self.near[1] = self.program.run(lambda *arrays: meet(arrays, BF16)[0], *arrays)

    def finish(self):
        arrays = [self.keep[0], self.others[0], self.others[1]]
        self.kept = self.program.run(lambda *arrays: meet(arrays, F32)[0], *arrays)


def restore_kernel(count, *refs):
    total = refs[0][...].astype(F32)
    for other_ref in refs[1:count]:
        total = total + other_ref[...].astype(F32)
    matrix_ref, out_ref = refs[count:]
    out_ref[...] = restore(total.astype(BF16), matrix_ref[...])


def restore_sum(matrix, *values):
    return pl.pallas_call(
        functools.partial(restore_kernel, len(values)),
        out_shape=jax.ShapeDtypeStruct(values[0].shape, BF16),
        compiler_params=pltpu.CompilerParams(vmem_limit_bytes=VMEM_BYTES),
        cost_estimate=LIGHT,
    )(*values, matrix)


def gains_kernel(attn_ref, mlp_ref, q_ref, k_ref, matrix_ref, out_ref):
    rows = jnp.concatenate([attn_ref[...], mlp_ref[...]], axis=0)
    out_ref[...] = jnp.zeros_like(out_ref)
    out_ref[0:2, :] = restore(rows, matrix_ref[...])
    ones = jnp.ones((8, q_ref.shape[1]), F32)
    for place, terms_ref in ((2, q_ref), (3, k_ref)):
        sums = lax.dot_general(
            ones,
            terms_ref[...],
            (((1,), (1,)), ((), ())),
            precision=lax.Precision.HIGHEST,
            preferred_element_type=F32,
        )
        out_ref[place : place + 1, : sums.shape[1]] = sums[:1]


def gain_parts(attn_part, mlp_part, q_terms, k_terms, matrix):
    return pl.pallas_call(
        gains_kernel,
        out_shape=jax.ShapeDtypeStruct((8, attn_part.shape[1]), F32),
        compiler_params=pltpu.CompilerParams(vmem_limit_bytes=VMEM_BYTES),
        cost_estimate=LIGHT,
    )(attn_part, mlp_part, q_terms, k_terms, matrix)


def local_small(
    tokens,
    doc_starts,
    attn_gain,
    w_query,
    w_key,
    w_value,
    q_gain,
    k_gain,
    w_out,
    mlp_gain,
    w_gate,
    w_up,
    w_down,
    out_grad,
):
    width = tokens.shape[-1]
    own_rows = tokens.shape[1]
    groups = w_key.shape[1] // HD
    repeat = w_query.shape[1] // w_key.shape[1]
    query_cols, key_cols = w_query.shape[1], w_key.shape[1]
    columns = query_cols + 2 * key_cols
    ff_cols = w_gate.shape[1]
    cut = ff_cols // 3
    program = Program()
    run, send, arrive = program.run, program.send, program.arrive

    shards = [w_query, w_key, w_value, w_out]
    plan = [(one, 0, shard.shape[1]) for one, shard in enumerate(shards)]
    attn = Gather(program, run(lambda *parts: pack(parts, [plan]), *shards)[0])
    attn.start(8)
    plans = [[(one, at, at + cut) for one in range(3)] for at in range(0, ff_cols, cut)]
    packed = run(lambda *parts: pack(parts, plans), w_gate, w_up, w_down)
    first, second = (Gather(program, one) for one in packed[:2])
    third = GatherAcross(program, packed[2])

    matrix = run(lambda: order_matrix(width, BF16))

    def attention_tables(starts, q_gain, k_gain):
        places = row_places(own_rows)
        firsts, position = document_tables(starts, places)
        cosine, sine = rope_tables(position, HD)
        rows = [cosine.T, sine.T]
        rows += [jnp.broadcast_to(gain[:, None], (HD, places.size)) for gain in (q_gain, k_gain)]
        keys = places[:, None]
        allowed = (keys <= places[None, :]) & (keys >= firsts[None, :])
        return jnp.concatenate(rows, axis=0), jnp.where(allowed, 0.0, -1e30).astype(BF16)

    def norm_tokens(tokens, attn_gain, mlp_gain):
        gains = reorder(jnp.stack([attn_gain, mlp_gain]), matrix)
        inputs = reorder(tokens, matrix).astype(F32)
        normed, hat, inverse = norm_forward(inputs, gains[0])
        return normed.astype(BF16), hat, inverse, inputs, gains

    normed_first, hat_first, inv_first, inputs, gains = run(
        norm_tokens, tokens[0], attn_gain, mlp_gain
    )
    attn_gain, mlp_gain = gains[0], gains[1]
    cotangent = run(lambda rows: reorder(rows, matrix), out_grad[0])
    tables = run(attention_tables, doc_starts[0], q_gain, k_gain)

    attn.arrive(8)
    attn.start(4)
    attn.start(2)
    first.start(8)
    rows_sent = send(normed_first, 0, 1)
    third.start_across()
    attn.arrive(4)
    attn.arrive(2)
    first.arrive(8)
    rows_first = run(stack, normed_first, arrive(rows_sent))
    third.arrive_across()
    attn.start_last()
    first.start(4)
    cot_sent = send(cotangent, 0, 1)
    third.start(8, 0)
    attn.arrive_last()
    first.arrive(4)
    cot_rows = run(stack, cotangent, arrive(cot_sent))
    third.arrive(8, 0)
    attn.start(1)
    attn.arrive(1)
    first.start(2)
    second.start(8)
    raw, queries, keys, values, logs, attended = run(
        lambda weights, rows: attend_rows(weights, rows, tables, groups, repeat),
        attn.halves,
        rows_first,
    )

    def back_rows(lefts, weights, parts, flipped=False):
        return run(
            lambda lefts, weights: project_back(lefts, weights, parts, flipped)[::-1],
            lefts,
            weights,
        )

    sent, kept = back_rows([attended], [attn.halves], [columns // query_cols], True)
    first.arrive(2)
    second.arrive(8)
    branch_sent = send(sent, 0, 1)
    first.start_last()
    second.start(4)
    third.start(8, 1)

    normed_second, hat_second, inv_second, hidden = run(
        norm_hidden, inputs, kept, arrive(branch_sent), mlp_gain[None]
    )
    first.arrive_last()
    second.arrive(4)
    third.arrive(8, 1)
    rows_sent = send(normed_second, 0, 1)
    first.start(1)
    second.start(2)
    third.start(4, 0)
    rows_second = run(stack, normed_second, arrive(rows_sent))
    first.arrive(1)
    second.arrive(2)
    third.arrive(4, 0)
    second.start_last()
    third.start(4, 1)

    def hidden_third(one):
        parts = run(hidden_small, one.halves, rows_second, cot_rows)
        return parts, [(rows_second, parts[0]), (rows_second, parts[1]), (cot_rows, parts[2])]

    parts_one, pairs = hidden_third(first)
    sum_one = Scatter(program, pairs)
    sum_one.core()
    second.arrive_last()
    third.arrive(4, 1)
    third.join(HEAVY)
    second.start(1)
    third.start_core()
    sum_one.arrive_core()
    sum_one.beside()
    second.arrive(1)
    sum_one.send_high()
    parts_two, pairs = hidden_third(second)
    sum_two = Scatter(program, pairs)
    third.arrive_core()
    sum_two.core_step()
    parts_three, pairs = hidden_third(third)
    sum_three = ScatterAcross(program, pairs)
    sum_three.core_step()
    sum_two.core_send()
    sum_three.core_send()
    sum_one.meet_high(HEAVY)
    sum_one.send_low()
    sum_one.send(4)
    parts = (parts_one, parts_two, parts_three)
    thirds_halves = [first.halves, second.halves, third.halves]
    sent, kept = back_rows(
        [one for part in parts for one in part[:2]],
        [halves for halves in thirds_halves for _ in range(2)],
        [0, 1] * 3,
    )
    grad_sent = send(sent, 0, 1)
    sum_two.arrive_core()
    sum_three.arrive_core()
    sum_two.beside()
    sum_three.beside()
    sum_one.arrive_low()
    sum_one.arrive_far()
    sum_two.send_high()
    sum_one.meet_far()
    sum_one.send(8)
    sum_three.send_part(4, 0)
    grad_branch, grad_hidden, mlp_gain_part = run(
        norm_back, kept, arrive(grad_sent), hat_second, inv_second, mlp_gain[None], cotangent
    )
    rows_sent = send(grad_branch, 0, 1)
    result_part = back_rows([part[2] for part in parts], thirds_halves, [2] * 3)
    sum_two.meet_high()
    sum_two.send_low()
    sum_two.send(4)
    sum_one.arrive_far()
    sum_one.finish()
    sum_three.arrive_part(0)
    sum_three.meet_part(0)
    sum_three.send_part(8, 0)
    branch_rows = run(stack, grad_branch, arrive(rows_sent))
    result_sent = send(result_part[0], 0, 1)
    grads, q_terms, k_terms = run(
        lambda weights, rows, kept: attend_rows_back(weights, rows, tables, kept, groups, repeat),
        attn.halves,
        branch_rows,
        (raw, queries, keys, values, logs),
    )
    sent, kept = back_rows([grads], [attn.halves], [0], True)
    pairs = [(rows_first, grads, block) for block in range(columns // query_cols)]
    sum_attn = Scatter(program, [*pairs, (branch_rows, attended)], True)
    sum_attn.core_step()
    sum_two.arrive_low()
    sum_two.arrive_far()
    sum_three.arrive_part(0)
    result_other = arrive(result_sent)
    sum_attn.core_send()
    sum_two.meet_far()
    sum_attn.arrive_core()
    sum_attn.beside()
    grad_sent = send(sent, 0, 1)
    sum_attn.send_high()
    sum_attn.send_low()
    sum_three.send_part(4, 1)
    sum_two.send(8)
    result = run(restore_sum, matrix, hidden, result_part[1], result_other)
    sum_attn.meet_high()
    sum_attn.send(4)
    sum_attn.arrive_low()
    grad_other = arrive(grad_sent)
    sum_three.arrive_part(1)
    sum_two.arrive_far()
    sum_three.meet_part(1)
    sum_three.send_part(8, 1)
    tokens_low, _, attn_gain_part = run(
        norm_back, kept, grad_other, hat_first, inv_first, attn_gain[None], grad_hidden
    )
    total = run(gain_parts, attn_gain_part, mlp_gain_part, q_terms, k_terms, matrix)

    def total_send(*partners):
        return [send(total, *partner) for partner in partners]

    def total_arrive(sent):
        return run(lambda *arrays: meet(arrays, F32)[0], total, *[arrive(one) for one in sent])

    gains_sent = total_send((0, 1))
    sum_two.finish()
    tokens_grad = run(restore_sum, matrix, tokens_low)
    sum_attn.arrive_far()
    sum_attn.meet_far()
    sum_three.arrive_part(1)
    sum_three.meet_across()
    total = total_arrive(gains_sent)
    sum_attn.send(8)
    sum_three.send_part(2, 1)
    gains_sent = total_send((1,), (2,), (3,))
    total = total_arrive(gains_sent)
    gains_sent = total_send((4,), (8,), (12,))
    sum_attn.arrive_far()
    sum_attn.finish()
    sum_three.arrive_part(1)
    sum_three.finish()

    def split_sums(*sums):
        rows = sums[0].shape[0]
        moves = [
            (source, (0, rows), (part * cut, (part + 1) * cut), part, 0, source * cut)
            for source in range(3)
            for part in range(3)
        ]
        return copy_blocks(sums, moves, [(rows, ff_cols)] * 3)

    weights = run(split_sums, sum_one.kept, sum_two.kept, sum_three.kept)
    total = total_arrive(gains_sent)

    gate_grad, up_grad, down_grad = weights
    kept = sum_attn.kept
    return (
        result[None],
        tokens_grad[None],
        total[0],
        kept[:, :query_cols],
        kept[:, query_cols : query_cols + key_cols],
        kept[:, query_cols + key_cols : columns],
        total[2, :HD],
        total[3, :HD],
        kept[:, columns:],
        total[1],
        gate_grad,
        up_grad,
        down_grad,
    )


def local(*arrays):
    small = lax.axis_size("dp") == DEVICES and lax.axis_size("tp") == 2
    if small and arrays[0].shape[1:] == (256, 1024):
        return local_small(*arrays)
    return local_large(*arrays)


def solution(mesh):
    in_specs = (
        P("dp", "tp", None),
        P("dp", None),
        P(),
        P("dp", "tp"),
        P("dp", "tp"),
        P("dp", "tp"),
        P(),
        P(),
        P("dp", "tp"),
        P(),
        P("dp", "tp"),
        P("dp", "tp"),
        P("dp", "tp"),
        P("dp", "tp", None),
    )
    out_specs = (
        P("dp", "tp", None),
        P("dp", "tp", None),
        P(),
        P("dp", "tp"),
        P("dp", "tp"),
        P("dp", "tp"),
        P(),
        P(),
        P("dp", "tp"),
        P(),
        P("dp", "tp"),
        P("dp", "tp"),
        P("dp", "tp"),
    )
    return jax.shard_map(local, mesh=mesh, in_specs=in_specs, out_specs=out_specs, check_vma=False)
```

```python
import functools

import jax
import jax.numpy as jnp
from jax import lax
from jax.experimental import pallas as pl
from jax.experimental.pallas import tpu as pltpu
from jax.sharding import PartitionSpec as P

HD = 64


EPSILON = 1e-05
THETA = 1000000.0


def documents(starts, length):
    places = jnp.arange(length, dtype=jnp.int32)
    inside = places[:, None] >= starts[None, :]
    segment = jnp.sum(inside.astype(jnp.int32), axis=1) - 1
    firsts = jnp.max(jnp.where(inside, starts[None, :], 0), axis=1)
    return (segment, places - firsts)


def rope_tables(position, width):
    half_width = width // 2
    freqs = THETA ** (-(jnp.arange(half_width, dtype=jnp.float32) * 2.0 / width))
    angles = position.astype(jnp.float32)[:, None] * freqs[None, :]
    return (jnp.cos(angles), jnp.sin(angles))


def rotate(values, cosine, sine):
    half_width = values.shape[-1] // 2
    first_half = values[..., :half_width]
    second_half = values[..., half_width:]
    tile_shape = (values.shape[0],) + (1,) * (values.ndim - 2) + (half_width,)
    cos_tile = cosine.reshape(tile_shape)
    sin_tile = sine.reshape(tile_shape)
    return jnp.concatenate(
        [
            first_half * cos_tile - second_half * sin_tile,
            second_half * cos_tile + first_half * sin_tile,
        ],
        axis=-1,
    )


def norm_forward(values, gain):
    inverse = lax.rsqrt(jnp.mean(values * values, axis=-1, keepdims=True) + EPSILON)
    normed_hat = values * inverse
    return (normed_hat * gain, normed_hat, inverse)


def norm_backward(grad_normed, normed_hat, inverse, gain):
    grad_hat = grad_normed * gain
    grad_values = inverse * (
        grad_hat - normed_hat * jnp.mean(grad_hat * normed_hat, axis=-1, keepdims=True)
    )
    gain_part = jnp.sum((grad_normed * normed_hat).reshape(-1, normed_hat.shape[-1]), axis=0)
    return (grad_values, gain_part)


def gather_rows(values):
    return lax.all_gather(values, "tp", axis=0, tiled=True)


def sum_rows(left_rows, right_weight):
    return lax.psum_scatter(
        jnp.dot(left_rows, right_weight.T, preferred_element_type=jnp.float32).astype(jnp.bfloat16),
        "tp",
        scatter_dimension=0,
        tiled=True,
    ).astype(jnp.float32)


def masked_scores(query_block, key_rows, block_segment, block_places, segment, places, score_scale):
    scores = (
        jnp.einsum("qgrd,kgd->grqk", query_block, key_rows, preferred_element_type=jnp.float32)
        * score_scale
    )
    allowed = (places[None, :] <= block_places[:, None]) & (
        segment[None, :] == block_segment[:, None]
    )
    return jnp.where(allowed, scores, -1e30)


def attend(query_rows, key_rows, value_rows, segment, block_rows):
    row_len = query_rows.shape[0]
    blocks = row_len // block_rows
    places = jnp.arange(row_len, dtype=jnp.int32)
    score_scale = query_rows.shape[-1] ** (-0.5)

    def block_out(block_item):
        query_block, block_segment, block_places = block_item
        scores = masked_scores(
            query_block, key_rows, block_segment, block_places, segment, places, score_scale
        )
        peaks = jnp.max(scores, axis=-1, keepdims=True)
        shifted = jnp.exp(scores - peaks)
        totals = jnp.sum(shifted, axis=-1, keepdims=True)
        attn_probs = (shifted / totals).astype(jnp.bfloat16)
        outputs = jnp.einsum(
            "grqk,kgd->qgrd", attn_probs, value_rows, preferred_element_type=jnp.float32
        )
        return (outputs, (peaks + jnp.log(totals))[..., 0])

    outputs, log_totals = lax.map(
        block_out,
        (
            query_rows.reshape((blocks, block_rows) + query_rows.shape[1:]),
            segment.reshape(blocks, block_rows),
            places.reshape(blocks, block_rows),
        ),
    )
    return (outputs.reshape(query_rows.shape), log_totals)


def attend_back(query_rows, key_rows, value_rows, grad_out, log_totals, segment, block_rows):
    row_len = query_rows.shape[0]
    blocks = row_len // block_rows
    places = jnp.arange(row_len, dtype=jnp.int32)
    score_scale = query_rows.shape[-1] ** (-0.5)

    def block_back(carry, block_item):
        grad_keys, grad_values = carry
        query_block, grad_block, total_block, block_segment, block_places = block_item
        scores = masked_scores(
            query_block, key_rows, block_segment, block_places, segment, places, score_scale
        )
        attn_probs = jnp.exp(scores - total_block[..., None])
        grad_probs = jnp.einsum(
            "qgrd,kgd->grqk", grad_block, value_rows, preferred_element_type=jnp.float32
        )
        inner = jnp.sum(attn_probs * grad_probs, axis=-1, keepdims=True)
        grad_scores = (attn_probs * (grad_probs - inner)).astype(jnp.bfloat16)
        grad_query = (
            jnp.einsum("grqk,kgd->qgrd", grad_scores, key_rows, preferred_element_type=jnp.float32)
            * score_scale
        )
        grad_keys = (
            grad_keys
            + jnp.einsum(
                "grqk,qgrd->kgd", grad_scores, query_block, preferred_element_type=jnp.float32
            )
            * score_scale
        )
        grad_values = grad_values + jnp.einsum(
            "grqk,qgrd->kgd",
            attn_probs.astype(jnp.bfloat16),
            grad_block,
            preferred_element_type=jnp.float32,
        )
        return ((grad_keys, grad_values), grad_query)

    zeros_kv = jnp.zeros(key_rows.shape, jnp.float32)
    block_shape = (blocks, block_rows) + query_rows.shape[1:]
    (grad_keys, grad_values), grad_queries = lax.scan(
        block_back,
        (zeros_kv, zeros_kv),
        (
            query_rows.reshape(block_shape),
            grad_out.reshape(block_shape),
            log_totals,
            segment.reshape(blocks, block_rows),
            places.reshape(blocks, block_rows),
        ),
    )
    return (grad_queries.reshape(query_rows.shape), grad_keys, grad_values)


def local_large(
    tokens,
    doc_starts,
    attn_gain,
    w_query,
    w_key,
    w_value,
    q_gain,
    k_gain,
    w_out,
    mlp_gain,
    w_gate,
    w_up,
    w_down,
    out_grad,
):
    query_w, key_w, value_w, out_w, gate_w, up_w, down_w = (
        lax.all_gather(w_query, "dp", axis=0, tiled=True),
        lax.all_gather(w_key, "dp", axis=0, tiled=True),
        lax.all_gather(w_value, "dp", axis=0, tiled=True),
        lax.all_gather(w_out, "dp", axis=0, tiled=True),
        lax.all_gather(w_gate, "dp", axis=0, tiled=True),
        lax.all_gather(w_up, "dp", axis=0, tiled=True),
        lax.all_gather(w_down, "dp", axis=0, tiled=True),
    )
    inputs = tokens[0].astype(jnp.float32)
    cotangent = out_grad[0]
    own_rows = inputs.shape[0]
    row_len = own_rows * lax.axis_size("tp")
    head_dim = HD
    groups = key_w.shape[1] // head_dim
    repeat = query_w.shape[1] // key_w.shape[1]
    query_cols = query_w.shape[1]
    key_cols = key_w.shape[1]
    ff_cols = gate_w.shape[1]
    block_rows = min(512, row_len)
    segment, position = documents(doc_starts[0], row_len)
    cosine, sine = rope_tables(position, head_dim)
    qkv_weight = jnp.concatenate([query_w, key_w, value_w], axis=1)
    gate_up_weight = jnp.concatenate([gate_w, up_w], axis=1)
    normed_first, hat_first, inv_first = norm_forward(inputs, attn_gain)
    rows_first = gather_rows(normed_first.astype(jnp.bfloat16))
    projected = jnp.dot(rows_first, qkv_weight, preferred_element_type=jnp.float32)
    query_raw = projected[:, :query_cols].reshape(row_len, groups, repeat, head_dim)
    key_raw = projected[:, query_cols : query_cols + key_cols].reshape(row_len, groups, head_dim)
    value_rows = (
        projected[:, query_cols + key_cols :]
        .astype(jnp.bfloat16)
        .reshape(row_len, groups, head_dim)
    )
    query_normed, query_hat, query_inv = norm_forward(query_raw, q_gain)
    key_normed, key_hat, key_inv = norm_forward(key_raw, k_gain)
    query_rows = rotate(query_normed, cosine, sine).astype(jnp.bfloat16)
    key_rows = rotate(key_normed, cosine, sine).astype(jnp.bfloat16)
    attended, log_totals = attend(query_rows, key_rows, value_rows, segment, block_rows)
    attended = attended.reshape(row_len, query_cols).astype(jnp.bfloat16)
    branch_out = sum_rows(attended, out_w)
    hidden = inputs + branch_out
    normed_second, hat_second, inv_second = norm_forward(hidden, mlp_gain)
    rows_second = gather_rows(normed_second.astype(jnp.bfloat16))
    gate_up = jnp.dot(rows_second, gate_up_weight, preferred_element_type=jnp.float32)
    gate_pre = gate_up[:, :ff_cols]
    up_pre = gate_up[:, ff_cols:]
    sigmoid_gate = jax.nn.sigmoid(gate_pre)
    activated = (gate_pre * sigmoid_gate * up_pre).astype(jnp.bfloat16)
    result = hidden + sum_rows(activated, down_w)
    cot_rows = gather_rows(cotangent)
    grad_act = jnp.dot(cot_rows, down_w, preferred_element_type=jnp.float32)
    grad_down = jnp.einsum("rd,rf->df", cot_rows, activated, preferred_element_type=jnp.float32)
    grad_gate = grad_act * up_pre * sigmoid_gate * (1.0 + gate_pre * (1.0 - sigmoid_gate))
    grad_up = grad_act * gate_pre * sigmoid_gate
    grad_gate_up = jnp.concatenate([grad_gate, grad_up], axis=1).astype(jnp.bfloat16)
    grad_gate_up_w = jnp.einsum(
        "rd,rf->df", rows_second, grad_gate_up, preferred_element_type=jnp.float32
    )
    grad_normed_second = sum_rows(grad_gate_up, gate_up_weight)
    grad_hidden_norm, mlp_gain_part = norm_backward(
        grad_normed_second, hat_second, inv_second, mlp_gain
    )
    grad_hidden = cotangent.astype(jnp.float32) + grad_hidden_norm
    grad_branch = grad_hidden.astype(jnp.bfloat16)
    branch_rows = gather_rows(grad_branch)
    grad_out_w = jnp.einsum("rd,rq->dq", branch_rows, attended, preferred_element_type=jnp.float32)
    grad_attended = jnp.dot(branch_rows, out_w, preferred_element_type=jnp.float32).astype(
        jnp.bfloat16
    )
    grad_query_rot, grad_key_rot, grad_value = attend_back(
        query_rows,
        key_rows,
        value_rows,
        grad_attended.reshape(row_len, groups, repeat, head_dim),
        log_totals,
        segment,
        block_rows,
    )
    grad_query_norm = rotate(grad_query_rot, cosine, -sine)
    grad_key_norm = rotate(grad_key_rot, cosine, -sine)
    grad_query_raw, q_gain_part = norm_backward(grad_query_norm, query_hat, query_inv, q_gain)
    grad_key_raw, k_gain_part = norm_backward(grad_key_norm, key_hat, key_inv, k_gain)
    grad_projected = jnp.concatenate(
        [
            grad_query_raw.reshape(row_len, query_cols),
            grad_key_raw.reshape(row_len, key_cols),
            grad_value.reshape(row_len, key_cols),
        ],
        axis=1,
    ).astype(jnp.bfloat16)
    grad_qkv_w = jnp.einsum(
        "rd,rf->df", rows_first, grad_projected, preferred_element_type=jnp.float32
    )
    grad_normed_first = sum_rows(grad_projected, qkv_weight)
    grad_input_norm, attn_gain_part = norm_backward(
        grad_normed_first, hat_first, inv_first, attn_gain
    )
    grad_inputs = grad_hidden + grad_input_norm
    summed = (
        lax.psum_scatter(
            grad_qkv_w[:, :query_cols].astype(jnp.bfloat16), "dp", scatter_dimension=0, tiled=True
        ).astype(jnp.float32),
        lax.psum_scatter(
            grad_qkv_w[:, query_cols : query_cols + key_cols].astype(jnp.bfloat16),
            "dp",
            scatter_dimension=0,
            tiled=True,
        ).astype(jnp.float32),
        lax.psum_scatter(
            grad_qkv_w[:, query_cols + key_cols :].astype(jnp.bfloat16),
            "dp",
            scatter_dimension=0,
            tiled=True,
        ).astype(jnp.float32),
        lax.psum_scatter(
            grad_out_w.astype(jnp.bfloat16), "dp", scatter_dimension=0, tiled=True
        ).astype(jnp.float32),
        lax.psum_scatter(
            grad_gate_up_w[:, :ff_cols].astype(jnp.bfloat16), "dp", scatter_dimension=0, tiled=True
        ).astype(jnp.float32),
        lax.psum_scatter(
            grad_gate_up_w[:, ff_cols:].astype(jnp.bfloat16), "dp", scatter_dimension=0, tiled=True
        ).astype(jnp.float32),
        lax.psum_scatter(
            grad_down.astype(jnp.bfloat16), "dp", scatter_dimension=0, tiled=True
        ).astype(jnp.float32),
    )
    gains = lax.psum((attn_gain_part, q_gain_part, k_gain_part, mlp_gain_part), ("dp", "tp"))
    return (
        result.astype(jnp.bfloat16)[None],
        grad_inputs.astype(jnp.bfloat16)[None],
        gains[0],
        summed[0],
        summed[1],
        summed[2],
        gains[1],
        gains[2],
        summed[3],
        gains[3],
        summed[4],
        summed[5],
        summed[6],
    )


F32 = jnp.float32
BF16 = jnp.bfloat16
VMEM_BYTES = 16 * 1024 * 1024
LIGHT = pl.CostEstimate(flops=1000, bytes_accessed=1000, transcendentals=0)
HEAVY = pl.CostEstimate(flops=13000000000, bytes_accessed=1000, transcendentals=0)


DEVICES = 16
MASKS = (1, 2, 4, 8)


def tied(values, *others):
    return lax.optimization_barrier((values, *others))[0]


class Program:
    def __init__(self):
        self.arrival = None
        self.step = None

    def begun(self):
        return [one for one in (self.arrival, self.step) if one is not None]

    def ready(self, *values):
        out = lax.optimization_barrier((*values, *self.begun()))[: len(values)]
        return out if len(out) > 1 else out[0]

    def run(self, function, *values):
        flat, tree = jax.tree.flatten(values)
        flat = lax.optimization_barrier((*flat, *self.begun()))[: len(flat)]
        out = function(*jax.tree.unflatten(tree, flat))
        self.step = jax.tree.leaves(out)[0]
        return out

    def send(self, values, mask, across=0):
        pairs = []
        for own in range(DEVICES):
            for side in range(2):
                pairs.append((own * 2 + side, (own ^ mask) * 2 + (side ^ across)))
        return lax.ppermute(self.ready(values), ("dp", "tp"), pairs)

    def arrive(self, other):
        if self.arrival is not None:
            other = tied(other, self.arrival)
        self.arrival = other
        return other


def copy_kernel(count, moves, *refs):
    semaphores = refs[-1]
    copies = []
    for place, (source, rows, columns, target, row, column) in enumerate(moves):
        size, width = rows[1] - rows[0], columns[1] - columns[0]
        copies.append(
            pltpu.make_async_copy(
                refs[source].at[rows[0] : rows[1], columns[0] : columns[1]],
                refs[count + target].at[row : row + size, column : column + width],
                semaphores.at[place],
            )
        )
    for copy in copies:
        copy.start()
    for copy in copies:
        copy.wait()


def copy_blocks(arrays, moves, shapes, cost=LIGHT):
    return pl.pallas_call(
        functools.partial(copy_kernel, len(arrays), moves),
        in_specs=[pl.BlockSpec(memory_space=pl.ANY)] * len(arrays),
        out_specs=[pl.BlockSpec(memory_space=pl.ANY)] * len(shapes),
        out_shape=[jax.ShapeDtypeStruct(shape, arrays[0].dtype) for shape in shapes],
        scratch_shapes=[pltpu.SemaphoreType.DMA((len(moves),))],
        compiler_params=pltpu.CompilerParams(vmem_limit_bytes=VMEM_BYTES),
        cost_estimate=cost,
    )(*arrays)


def pack(shards, plans):
    rows = shards[0].shape[0]
    moves, shapes = [], []
    for target, plan in enumerate(plans):
        column = 0
        for source, start, stop in plan:
            moves.append((source, (0, rows), (start, stop), target, 0, column))
            column += stop - start
        shapes.append((rows, column))
    return copy_blocks(shards, moves, shapes)


def stack(*parts, cost=LIGHT):
    moves, row = [], 0
    for source, part in enumerate(parts):
        moves.append((source, (0, part.shape[0]), (0, part.shape[1]), 0, row, 0))
        row += part.shape[0]
    return copy_blocks(parts, moves, [(row, parts[0].shape[1])], cost)[0]


def grad_kernel(count, flipped, added, *refs):
    lefts, rights = refs[:count], refs[count : 2 * count]
    outs = refs[2 * count + (1 if added else 0) :]
    step = pl.program_id(0)
    for one in range(count):

        @pl.when(step == one)
        def _(one=one):
            value = lax.dot_general(
                lefts[one][...],
                rights[one][...],
                (((0,), (1 if flipped else 0,)), ((), ())),
                preferred_element_type=F32,
            )
            if added:
                value = value + refs[2 * count][...].astype(F32)
            rows = value.shape[0] // len(outs)
            for place, out_ref in enumerate(outs):
                out_ref[...] = value[place * rows : (place + 1) * rows].astype(out_ref.dtype)


def grad_half(pairs, side, added, flipped, across=False):
    count = len(pairs)
    row_len, width = pairs[0][0].shape
    half = width // 2
    blocks = [pair[2] if len(pair) > 2 else 0 for pair in pairs]
    pairs = [pair[:2] for pair in pairs]
    columns = pairs[-1][1].shape[0 if flipped else 1]
    arrays = [left for left, _ in pairs] + [right for _, right in pairs]
    specs = [pl.BlockSpec((row_len, half), lambda k: (0, side))] * count
    for block in blocks:
        shape = (columns, row_len) if flipped else (row_len, columns)
        specs.append(pl.BlockSpec(shape, lambda k, block=block: (block, 0)))
    if added is None:
        types = [BF16]
    else:
        arrays.append(added)
        specs.append(pl.BlockSpec((half, columns), lambda k: (0, k)))
        types = [F32, BF16, F32, BF16] if across else [F32, F32, BF16, BF16]
    rows = half // len(types)
    return pl.pallas_call(
        functools.partial(grad_kernel, count, flipped, added is not None),
        grid=(count,),
        in_specs=specs,
        out_specs=[pl.BlockSpec((rows, columns), lambda k: (0, k))] * len(types),
        out_shape=[jax.ShapeDtypeStruct((rows, count * columns), kind) for kind in types],
        compiler_params=pltpu.CompilerParams(vmem_limit_bytes=VMEM_BYTES),
        cost_estimate=LIGHT,
    )(*arrays)


def reversed_bits(block):
    masks = MASKS
    flipped = jnp.zeros_like(block)
    for rank, mask in enumerate(masks):
        flipped = flipped + ((block >> (len(masks) - 1 - rank)) & 1) * mask
    return flipped


def order_matrix(width, dtype):
    chunk = width // DEVICES
    place = lax.broadcasted_iota(jnp.int32, (width, width), 1)
    source = lax.broadcasted_iota(jnp.int32, (width, width), 0)
    entry = (lax.axis_index("dp") ^ reversed_bits(place // chunk)) * chunk + place % chunk
    return (source == entry).astype(dtype)


def thirds(values):
    high = values.astype(BF16)
    rest = values - high.astype(F32)
    middle = rest.astype(BF16)
    return jnp.concatenate([high, middle, (rest - middle.astype(F32)).astype(BF16)], axis=0)


def reorder(values, matrix):
    if values.dtype == F32:
        rows = values.shape[0]
        value = jnp.dot(thirds(values), matrix, preferred_element_type=F32)
        return value[:rows] + value[rows : 2 * rows] + value[2 * rows :]
    return jnp.dot(values, matrix, preferred_element_type=F32).astype(values.dtype)


def restore(values, matrix):
    dims = (((1,), (1,)), ((), ()))
    if values.dtype == F32:
        rows = values.shape[0]
        value = lax.dot_general(thirds(values), matrix, dims, preferred_element_type=F32)
        return value[:rows] + value[rows : 2 * rows] + value[2 * rows :]
    return lax.dot_general(values, matrix, dims, preferred_element_type=F32).astype(values.dtype)


def back_kernel(count, flipped, *refs):
    lefts, weights = refs[:count], refs[count : 3 * count]
    kept_ref, sent_ref = refs[3 * count :]
    rows = kept_ref.shape[0]
    block = weights[0].shape[0]
    step = pl.program_id(0)
    for side in range(2):
        value = None
        for one in range(count):
            term = lax.dot_general(
                lefts[one][...],
                weights[2 * one + side][...],
                (((0 if flipped else 1,), (1,)), ((), ())),
                preferred_element_type=F32,
            )
            value = term if value is None else value + term
        start = pl.multiple_of((side * pl.num_programs(0) + step) * block, block)
        kept_ref[:, pl.ds(start, block)] = value[:rows]
        sent_ref[:, pl.ds(start, block)] = value[rows:].astype(BF16)


def project_back(lefts, weights, parts, flipped=False):
    count = len(lefts)
    half = weights[0][0].shape[0]
    block = half // 2 if len(lefts) > 1 else half
    row_len, inner = lefts[0].shape[::-1] if flipped else lefts[0].shape
    specs = [pl.BlockSpec(left.shape, lambda k: (0, 0)) for left in lefts]
    for part in parts:
        specs += [pl.BlockSpec((block, inner), lambda k, part=part: (k, part))] * 2
    flat = [side for halves in weights for side in halves]
    whole = pl.BlockSpec((row_len // 2, 2 * half), lambda k: (0, 0))
    return pl.pallas_call(
        functools.partial(back_kernel, count, flipped),
        grid=(half // block,),
        in_specs=specs,
        out_specs=[whole, whole],
        out_shape=[
            jax.ShapeDtypeStruct((row_len // 2, 2 * half), F32),
            jax.ShapeDtypeStruct((row_len // 2, 2 * half), BF16),
        ],
        compiler_params=pltpu.CompilerParams(vmem_limit_bytes=VMEM_BYTES),
        cost_estimate=LIGHT,
    )(*lefts, *flat)


def head_normed(raw, gain, cosine, sine):
    inverse = lax.rsqrt(jnp.mean(raw * raw, axis=0, keepdims=True) + EPSILON)
    normed = raw * inverse * gain
    half = raw.shape[0] // 2
    first, second = normed[:half], normed[half:]
    return jnp.concatenate(
        [first * cosine - second * sine, second * cosine + first * sine], axis=0
    )


def weighted_columns(weights, rows_ref, target_ref):
    width = weights[0].shape[0]
    value = None
    for part in range(len(weights)):
        term = lax.dot_general(
            weights[part][...],
            rows_ref[:, part * width : (part + 1) * width],
            (((0,), (1,)), ((), ())),
            preferred_element_type=F32,
        )
        value = term if value is None else value + term
    target_ref[...] = value.astype(target_ref.dtype)


def attend_kernel(
    groups,
    repeat,
    w0,
    w1,
    rows_ref,
    table_ref,
    bias_ref,
    raw_ref,
    q_ref,
    k_ref,
    v_ref,
    log_ref,
    out_ref,
):
    weighted_columns((w0, w1), rows_ref, raw_ref)
    half = HD // 2
    cosine, sine = table_ref[:half, :], table_ref[half:HD, :]
    q_gain, k_gain = table_ref[HD : 2 * HD, :], table_ref[2 * HD :, :]
    heads = groups * repeat

    def group_step(group, carry):
        k_row = pl.multiple_of(group * HD, HD)
        keys = head_normed(
            raw_ref[pl.ds(heads * HD + k_row, HD), :], k_gain, cosine, sine
        ).astype(BF16)
        values = raw_ref[pl.ds((heads + groups) * HD + k_row, HD), :].astype(BF16)
        k_ref[pl.ds(k_row, HD), :] = keys
        v_ref[pl.ds(k_row, HD), :] = values
        for one in range(repeat):
            q_row = pl.multiple_of((group * repeat + one) * HD, HD)
            queries = head_normed(
                raw_ref[pl.ds(q_row, HD), :], q_gain, cosine, sine
            ).astype(BF16)
            queries = queries * jnp.asarray(HD ** (-0.5), BF16)
            q_ref[pl.ds(q_row, HD), :] = queries
            scores = (
                lax.dot_general(
                    keys, queries, (((0,), (0,)), ((), ())), preferred_element_type=F32
                )
                + bias_ref[...].astype(F32)
            )
            peaks = jnp.max(scores, axis=0, keepdims=True)
            shifted = jnp.exp(scores - peaks)
            totals = jnp.sum(shifted, axis=0, keepdims=True)
            outputs = jnp.dot(values, shifted.astype(BF16), preferred_element_type=F32)
            out_ref[pl.ds(q_row, HD), :] = (outputs / totals).astype(BF16)
            log_ref[group * repeat + one] = peaks + jnp.log(totals)
        return carry

    lax.fori_loop(0, groups, group_step, 0)


def whole_block(value):
    return pl.BlockSpec(value.shape, lambda k: (0,) * len(value.shape))


def attend_rows(weights, rows, tables, groups, repeat):
    row_len = rows.shape[0]
    heads = groups * repeat
    columns = (heads + 2 * groups) * HD
    shapes = [
        jax.ShapeDtypeStruct((columns, row_len), F32),
        jax.ShapeDtypeStruct((heads * HD, row_len), BF16),
        jax.ShapeDtypeStruct((groups * HD, row_len), BF16),
        jax.ShapeDtypeStruct((groups * HD, row_len), BF16),
        jax.ShapeDtypeStruct((heads, 1, row_len), F32),
        jax.ShapeDtypeStruct((heads * HD, row_len), BF16),
    ]
    return pl.pallas_call(
        functools.partial(attend_kernel, groups, repeat),
        grid=(1,),
        in_specs=[pl.BlockSpec((weights[0].shape[0], columns), lambda k: (0, 0))] * 2
        + [whole_block(one) for one in (rows, *tables)],
        out_specs=[whole_block(one) for one in shapes],
        out_shape=shapes,
        compiler_params=pltpu.CompilerParams(vmem_limit_bytes=VMEM_BYTES),
        cost_estimate=LIGHT,
    )(*weights, rows, *tables)


def head_back(raw, gain, grad_rot, cosine, sine):
    half = raw.shape[0] // 2
    first, second = grad_rot[:half], grad_rot[half:]
    grad = jnp.concatenate(
        [first * cosine + second * sine, second * cosine - first * sine], axis=0
    )
    inverse = lax.rsqrt(jnp.mean(raw * raw, axis=0, keepdims=True) + EPSILON)
    hat = raw * inverse
    terms = grad * hat
    grad_hat = grad * gain
    inner = jnp.mean(terms * gain, axis=0, keepdims=True)
    return inverse * (grad_hat - hat * inner), terms


def attend_back_kernel(
    groups,
    repeat,
    w0,
    w1,
    rows_ref,
    table_ref,
    bias_ref,
    raw_ref,
    q_ref,
    k_ref,
    v_ref,
    log_ref,
    grad_ref,
    q_terms_ref,
    k_terms_ref,
    outer_ref,
):
    weighted_columns((w0, w1), rows_ref, outer_ref)
    half = HD // 2
    cosine, sine = table_ref[:half, :], table_ref[half:HD, :]
    q_gain, k_gain = table_ref[HD : 2 * HD, :], table_ref[2 * HD :, :]
    heads = groups * repeat
    q_terms_ref[...] = jnp.zeros_like(q_terms_ref)
    k_terms_ref[...] = jnp.zeros_like(k_terms_ref)

    def group_step(group, carry):
        k_row = pl.multiple_of(group * HD, HD)
        keys = k_ref[pl.ds(k_row, HD), :]
        values = v_ref[pl.ds(k_row, HD), :]
        grad_keys = None
        for one in range(repeat):
            q_row = pl.multiple_of((group * repeat + one) * HD, HD)
            queries = q_ref[pl.ds(q_row, HD), :]
            outer = outer_ref[pl.ds(q_row, HD), :]
            scores = (
                lax.dot_general(
                    keys, queries, (((0,), (0,)), ((), ())), preferred_element_type=F32
                )
                + bias_ref[...].astype(F32)
            )
            attn_probs = jnp.exp(scores - log_ref[group * repeat + one])
            grad_probs = lax.dot_general(
                values, outer, (((0,), (0,)), ((), ())), preferred_element_type=F32
            )
            inner = jnp.sum(attn_probs * grad_probs, axis=0, keepdims=True)
            grad_scores = (attn_probs * (grad_probs - inner)).astype(BF16)
            grad_query = jnp.dot(keys, grad_scores, preferred_element_type=F32) * (HD ** (-0.5))
            grad_key = lax.dot_general(
                queries, grad_scores, (((1,), (1,)), ((), ())), preferred_element_type=F32
            )
            grad_value = lax.dot_general(
                outer,
                attn_probs.astype(BF16),
                (((1,), (1,)), ((), ())),
                preferred_element_type=F32,
            )
            grad_raw, terms = head_back(
                raw_ref[pl.ds(q_row, HD), :], q_gain, grad_query, cosine, sine
            )
            grad_ref[pl.ds(q_row, HD), :] = grad_raw.astype(BF16)
            q_terms_ref[...] += terms
            if grad_keys is None:
                grad_keys, grad_values = grad_key, grad_value
            else:
                grad_keys, grad_values = grad_keys + grad_key, grad_values + grad_value
        grad_raw, terms = head_back(
            raw_ref[pl.ds(heads * HD + k_row, HD), :], k_gain, grad_keys, cosine, sine
        )
        k_terms_ref[...] += terms
        grad_ref[pl.ds(heads * HD + k_row, HD), :] = grad_raw.astype(BF16)
        grad_ref[pl.ds((heads + groups) * HD + k_row, HD), :] = grad_values.astype(BF16)
        return carry

    lax.fori_loop(0, groups, group_step, 0)


def attend_rows_back(weights, rows, tables, kept, groups, repeat):
    row_len = rows.shape[0]
    heads = groups * repeat
    columns = (heads + 2 * groups) * HD
    shapes = [
        jax.ShapeDtypeStruct((columns, row_len), BF16),
        jax.ShapeDtypeStruct((HD, row_len), F32),
        jax.ShapeDtypeStruct((HD, row_len), F32),
    ]
    return pl.pallas_call(
        functools.partial(attend_back_kernel, groups, repeat),
        grid=(1,),
        in_specs=[
            pl.BlockSpec(
                (weights[0].shape[0], heads * HD), lambda k: (0, columns // (heads * HD))
            )
        ]
        * 2
        + [whole_block(one) for one in (rows, *tables, *kept)],
        out_specs=[whole_block(one) for one in shapes],
        out_shape=shapes,
        scratch_shapes=[
            pltpu.VMEM((heads * HD, row_len), BF16),
        ],
        compiler_params=pltpu.CompilerParams(vmem_limit_bytes=VMEM_BYTES),
        cost_estimate=LIGHT,
    )(*weights, rows, *tables, *kept)


def hidden_kernel(
    gate_own, gate_other, up_own, up_other, down_own, down_other, rows_ref, cot_ref, *outs
):
    gate_grad_ref, up_grad_ref, act_ref = outs
    width = gate_own.shape[0]

    def summed(source_ref, own_ref, other_ref):
        return jnp.dot(
            source_ref[:, :width], own_ref[...], preferred_element_type=F32
        ) + jnp.dot(source_ref[:, width:], other_ref[...], preferred_element_type=F32)

    gate = summed(rows_ref, gate_own, gate_other)
    up = summed(rows_ref, up_own, up_other)
    grad_act = summed(cot_ref, down_own, down_other)
    sigmoid_gate = jax.nn.sigmoid(gate)
    silu = gate * sigmoid_gate
    act_ref[...] = (silu * up).astype(BF16)
    up_grad_ref[...] = (grad_act * silu).astype(BF16)
    gate_grad_ref[...] = (
        grad_act * up * (sigmoid_gate + silu * (1.0 - sigmoid_gate))
    ).astype(BF16)


def hidden_small(weights, rows, cot_rows):
    row_len, width = rows.shape
    columns = weights[0].shape[1] // 3
    block = 384 if columns % 384 == 0 else columns
    steps = columns // block
    specs = []
    for part in range(3):
        specs += [
            pl.BlockSpec((width // 2, block), lambda k, part=part: (0, part * steps + k))
        ] * 2
    whole = pl.BlockSpec((row_len, width), lambda k: (0, 0))
    return pl.pallas_call(
        hidden_kernel,
        grid=(steps,),
        in_specs=specs + [whole, whole],
        out_specs=[pl.BlockSpec((row_len, block), lambda k: (0, k))] * 3,
        out_shape=[jax.ShapeDtypeStruct((row_len, columns), BF16)] * 3,
        compiler_params=pltpu.CompilerParams(vmem_limit_bytes=VMEM_BYTES),
        cost_estimate=LIGHT,
    )(*weights, *weights, *weights, rows, cot_rows)


def row_places(own_rows):
    own = jnp.arange(own_rows, dtype=jnp.int32)
    index = lax.axis_index("tp")
    return jnp.concatenate([own + index * own_rows, own + (1 - index) * own_rows])


def document_tables(starts, places):
    inside = places[:, None] >= starts[None, :]
    firsts = jnp.max(jnp.where(inside, starts[None, :], 0), axis=1)
    return firsts, places - firsts


def meet_kernel(count, *refs):
    total = refs[0][...]
    for other_ref in refs[1:count]:
        total = total + other_ref[...].astype(F32)
    outs = refs[count:]
    if len(outs) == 1:
        outs[0][...] = total.astype(outs[0].dtype)
        return
    half = total.shape[0] // 2
    outs[0][...] = total[half:].astype(BF16)
    outs[1][...] = total[:half]


def meet(values, kind, cost=LIGHT):
    rows, columns = values[0].shape
    steps = 3 if columns % 384 == 0 and rows > 128 else 1
    block = columns // steps
    shapes = [(rows, kind)] if kind is not None else [(rows // 2, BF16), (rows // 2, F32)]
    return pl.pallas_call(
        functools.partial(meet_kernel, len(values)),
        grid=(steps,),
        in_specs=[pl.BlockSpec((rows, block), lambda k: (0, k))] * len(values),
        out_specs=[pl.BlockSpec((size, block), lambda k: (0, k)) for size, _ in shapes],
        out_shape=[jax.ShapeDtypeStruct((size, columns), kind) for size, kind in shapes],
        compiler_params=pltpu.CompilerParams(vmem_limit_bytes=VMEM_BYTES),
        cost_estimate=cost,
    )(*values)


def norm_kernel(inputs_ref, kept_ref, other_ref, gain_ref, normed_ref, hat_ref, inv_ref, hidden_ref):
    hidden = inputs_ref[...] + kept_ref[...] + other_ref[...].astype(F32)
    normed, hat, inverse = norm_forward(hidden, gain_ref[...])
    normed_ref[...] = normed.astype(BF16)
    hat_ref[...] = hat
    inv_ref[...] = inverse
    hidden_ref[...] = hidden


def norm_hidden(inputs, kept, other, gain):
    rows, width = inputs.shape
    shapes = [(width, BF16), (width, F32), (1, F32), (width, F32)]
    return pl.pallas_call(
        norm_kernel,
        out_shape=[jax.ShapeDtypeStruct((rows, size), kind) for size, kind in shapes],
        compiler_params=pltpu.CompilerParams(vmem_limit_bytes=VMEM_BYTES),
        cost_estimate=LIGHT,
    )(inputs, kept, other, gain)


def norm_back_kernel(kept_ref, other_ref, hat_ref, inv_ref, gain_ref, base_ref, *outs):
    low_ref, grad_ref, gain_part_ref = outs
    incoming = kept_ref[...] + other_ref[...].astype(F32)
    hat = hat_ref[...]
    grad_hat = incoming * gain_ref[...]
    inner = jnp.mean(grad_hat * hat, axis=-1, keepdims=True)
    grad = base_ref[...].astype(F32) + inv_ref[...] * (grad_hat - hat * inner)
    low_ref[...] = grad.astype(BF16)
    grad_ref[...] = grad
    gain_part_ref[...] = jnp.sum(incoming * hat, axis=0, keepdims=True)


def norm_back(kept, other, hat, inverse, gain, base):
    rows, width = kept.shape
    shapes = [(rows, BF16), (rows, F32), (1, F32)]
    return pl.pallas_call(
        norm_back_kernel,
        out_shape=[jax.ShapeDtypeStruct((size, width), kind) for size, kind in shapes],
        compiler_params=pltpu.CompilerParams(vmem_limit_bytes=VMEM_BYTES),
        cost_estimate=LIGHT,
    )(kept, other, hat, inverse, gain, base)


class Gather:
    def __init__(self, program, shard):
        self.program = program
        self.near = shard

    def start(self, mask):
        if mask == 8:
            self.far = self.program.send(self.near, 8)
        elif mask == 4:
            self.next = self.program.send(self.near, 4)
        elif mask == 2:
            self.across = self.program.send(self.near, 2)
        else:
            self.other = self.program.send(self.own, 1)

    def start_last(self):
        self.last = self.program.send(self.next, 2)

    def arrive(self, mask):
        program = self.program
        if mask == 8:
            far = program.arrive(self.far)
            self.near = program.run(stack, self.near, far)
        elif mask == 4:
            self.next = program.arrive(self.next)
        elif mask == 2:
            self.across = program.arrive(self.across)
        else:
            self.halves = [self.own, program.arrive(self.other)]

    def arrive_last(self):
        last = self.program.arrive(self.last)
        parts = (self.near, self.next, self.across, last)
        self.own = self.program.run(stack, *parts)


class GatherAcross:
    def __init__(self, program, shard):
        self.program = program
        self.parts = [shard, None]
        self.sent = [None, None]
        self.next = [None, None]

    def start_across(self):
        self.sent[1] = self.program.send(self.parts[0], 2)

    def arrive_across(self):
        self.parts[1] = self.program.arrive(self.sent[1])

    def start(self, mask, part):
        self.sent[part] = self.program.send(self.parts[part], mask)

    def arrive(self, mask, part):
        other = self.program.arrive(self.sent[part])
        if mask == 8:
            self.parts[part] = self.program.run(
                stack, self.parts[part], other
            )
        else:
            self.next[part] = other

    def join(self, cost=LIGHT):
        parts = (self.parts[0], self.next[0], self.parts[1], self.next[1])
        self.own = self.program.run(functools.partial(stack, cost=cost), *parts)

    def start_core(self):
        self.other = self.program.send(self.own, 1)

    def arrive_core(self):
        self.halves = [self.own, self.program.arrive(self.other)]


class Scatter:
    across_last = False

    def __init__(self, program, pairs, flipped=False):
        self.program, self.flipped = program, flipped
        self.arrays = [pair[:2] for pair in pairs]
        self.blocks = [pair[2:] for pair in pairs]

    def half(self, side, added):
        def step(arrays, added):
            pairs = [(*pair, *block) for pair, block in zip(arrays, self.blocks)]
            return grad_half(pairs, side, added, self.flipped, self.across_last)

        return self.program.run(step, self.arrays, added)

    def core(self):
        self.core_step()
        self.core_send()

    def core_step(self):
        self.near = self.half(1, None)[0]

    def core_send(self):
        self.other = self.program.send(self.near, 1)

    def beside(self):
        parts = self.half(0, self.other)
        self.kept, self.kept_far, self.low, self.high = parts

    def arrive_core(self):
        self.other = self.program.arrive(self.other)

    def arrive_far(self):
        self.other = self.program.arrive(self.other)

    def send_high(self):
        self.other = self.program.send(self.high, 2)

    def send_low(self):
        self.across = self.program.send(self.low, 2)

    def meet_high(self, cost=LIGHT):
        arrays = [self.kept_far, self.program.arrive(self.other)]
        self.near = self.program.run(lambda *arrays: meet(arrays, BF16, cost)[0], *arrays)

    def arrive_low(self):
        self.across = self.program.arrive(self.across)

    def send(self, mask):
        self.other = self.program.send(self.near, mask)

    def meet_far(self):
        arrays = [self.kept, self.across, self.other]
        self.near, self.kept = self.program.run(lambda *arrays: meet(arrays, None), *arrays)

    def finish(self):
        arrays = [self.kept, self.other]
        self.kept = self.program.run(lambda *arrays: meet(arrays, F32)[0], *arrays)


class ScatterAcross(Scatter):
    across_last = True

    def beside(self):
        parts = self.half(0, self.other)
        self.keep, self.near, self.others = [parts[0], parts[2]], [parts[1], parts[3]], [0, 0]

    def send_part(self, mask, part):
        self.others[part] = self.program.send(self.near[part], mask)

    def arrive_part(self, part):
        self.others[part] = self.program.arrive(self.others[part])

    def meet_part(self, part):
        arrays = [self.keep[part], self.others[part]]
        self.near[part], self.keep[part] = self.program.run(
            lambda *arrays: meet(arrays, None), *arrays
        )

    def meet_across(self):
        arrays = [self.keep[1], self.others[1]]
        self.near[1] = self.program.run(lambda *arrays: meet(arrays, BF16)[0], *arrays)

    def finish(self):
        arrays = [self.keep[0], self.others[0], self.others[1]]
        self.kept = self.program.run(lambda *arrays: meet(arrays, F32)[0], *arrays)


def restore_kernel(count, *refs):
    total = refs[0][...].astype(F32)
    for other_ref in refs[1:count]:
        total = total + other_ref[...].astype(F32)
    matrix_ref, out_ref = refs[count:]
    out_ref[...] = restore(total.astype(BF16), matrix_ref[...])


def restore_sum(matrix, *values):
    return pl.pallas_call(
        functools.partial(restore_kernel, len(values)),
        out_shape=jax.ShapeDtypeStruct(values[0].shape, BF16),
        compiler_params=pltpu.CompilerParams(vmem_limit_bytes=VMEM_BYTES),
        cost_estimate=LIGHT,
    )(*values, matrix)


def gains_kernel(attn_ref, mlp_ref, q_ref, k_ref, matrix_ref, out_ref):
    rows = jnp.concatenate([attn_ref[...], mlp_ref[...]], axis=0)
    out_ref[...] = jnp.zeros_like(out_ref)
    out_ref[0:2, :] = restore(rows, matrix_ref[...])
    ones = jnp.ones((8, q_ref.shape[1]), F32)
    for place, terms_ref in ((2, q_ref), (3, k_ref)):
        sums = lax.dot_general(
            ones,
            terms_ref[...],
            (((1,), (1,)), ((), ())),
            precision=lax.Precision.HIGHEST,
            preferred_element_type=F32,
        )
        out_ref[place : place + 1, : sums.shape[1]] = sums[:1]


def gain_parts(attn_part, mlp_part, q_terms, k_terms, matrix):
    return pl.pallas_call(
        gains_kernel,
        out_shape=jax.ShapeDtypeStruct((8, attn_part.shape[1]), F32),
        compiler_params=pltpu.CompilerParams(vmem_limit_bytes=VMEM_BYTES),
        cost_estimate=LIGHT,
    )(attn_part, mlp_part, q_terms, k_terms, matrix)


def local_small(
    tokens,
    doc_starts,
    attn_gain,
    w_query,
    w_key,
    w_value,
    q_gain,
    k_gain,
    w_out,
    mlp_gain,
    w_gate,
    w_up,
    w_down,
    out_grad,
):
    width = tokens.shape[-1]
    own_rows = tokens.shape[1]
    groups = w_key.shape[1] // HD
    repeat = w_query.shape[1] // w_key.shape[1]
    query_cols, key_cols = w_query.shape[1], w_key.shape[1]
    columns = query_cols + 2 * key_cols
    ff_cols = w_gate.shape[1]
    cut = ff_cols // 3
    program = Program()
    run, send, arrive = program.run, program.send, program.arrive

    shards = [w_query, w_key, w_value, w_out]
    plan = [(one, 0, shard.shape[1]) for one, shard in enumerate(shards)]
    attn = Gather(program, run(lambda *parts: pack(parts, [plan]), *shards)[0])
    attn.start(8)
    plans = [[(one, at, at + cut) for one in range(3)] for at in range(0, ff_cols, cut)]
    packed = run(lambda *parts: pack(parts, plans), w_gate, w_up, w_down)
    first, second = (Gather(program, one) for one in packed[:2])
    third = GatherAcross(program, packed[2])

    matrix = run(lambda: order_matrix(width, BF16))

    def attention_tables(starts, q_gain, k_gain):
        places = row_places(own_rows)
        firsts, position = document_tables(starts, places)
        cosine, sine = rope_tables(position, HD)
        rows = [cosine.T, sine.T]
        rows += [jnp.broadcast_to(gain[:, None], (HD, places.size)) for gain in (q_gain, k_gain)]
        keys = places[:, None]
        allowed = (keys <= places[None, :]) & (keys >= firsts[None, :])
        return jnp.concatenate(rows, axis=0), jnp.where(allowed, 0.0, -1e30).astype(BF16)

    def norm_tokens(tokens, attn_gain, mlp_gain):
        gains = reorder(jnp.stack([attn_gain, mlp_gain]), matrix)
        inputs = reorder(tokens, matrix).astype(F32)
        normed, hat, inverse = norm_forward(inputs, gains[0])
        return normed.astype(BF16), hat, inverse, inputs, gains

    normed_first, hat_first, inv_first, inputs, gains = run(
        norm_tokens, tokens[0], attn_gain, mlp_gain
    )
    attn_gain, mlp_gain = gains[0], gains[1]
    cotangent = run(lambda rows: reorder(rows, matrix), out_grad[0])
    tables = run(attention_tables, doc_starts[0], q_gain, k_gain)

    attn.arrive(8)
    attn.start(4)
    attn.start(2)
    first.start(8)
    rows_sent = send(normed_first, 0, 1)
    third.start_across()
    attn.arrive(4)
    attn.arrive(2)
    first.arrive(8)
    rows_first = run(stack, normed_first, arrive(rows_sent))
    third.arrive_across()
    attn.start_last()
    first.start(4)
    cot_sent = send(cotangent, 0, 1)
    third.start(8, 0)
    attn.arrive_last()
    first.arrive(4)
    cot_rows = run(stack, cotangent, arrive(cot_sent))
    third.arrive(8, 0)
    attn.start(1)
    attn.arrive(1)
    first.start(2)
    second.start(8)
    raw, queries, keys, values, logs, attended = run(
        lambda weights, rows: attend_rows(weights, rows, tables, groups, repeat),
        attn.halves,
        rows_first,
    )

    def back_rows(lefts, weights, parts, flipped=False):
        return run(
            lambda lefts, weights: project_back(lefts, weights, parts, flipped)[::-1],
            lefts,
            weights,
        )

    sent, kept = back_rows([attended], [attn.halves], [columns // query_cols], True)
    first.arrive(2)
    second.arrive(8)
    branch_sent = send(sent, 0, 1)
    first.start_last()
    second.start(4)
    third.start(8, 1)

    normed_second, hat_second, inv_second, hidden = run(
        norm_hidden, inputs, kept, arrive(branch_sent), mlp_gain[None]
    )
    first.arrive_last()
    second.arrive(4)
    third.arrive(8, 1)
    rows_sent = send(normed_second, 0, 1)
    first.start(1)
    second.start(2)
    third.start(4, 0)
    rows_second = run(stack, normed_second, arrive(rows_sent))
    first.arrive(1)
    second.arrive(2)
    third.arrive(4, 0)
    second.start_last()
    third.start(4, 1)

    def hidden_third(one):
        parts = run(hidden_small, one.halves, rows_second, cot_rows)
        return parts, [(rows_second, parts[0]), (rows_second, parts[1]), (cot_rows, parts[2])]

    parts_one, pairs = hidden_third(first)
    sum_one = Scatter(program, pairs)
    sum_one.core()
    second.arrive_last()
    third.arrive(4, 1)
    third.join(HEAVY)
    second.start(1)
    third.start_core()
    sum_one.arrive_core()
    sum_one.beside()
    second.arrive(1)
    sum_one.send_high()
    parts_two, pairs = hidden_third(second)
    sum_two = Scatter(program, pairs)
    third.arrive_core()
    sum_two.core_step()
    parts_three, pairs = hidden_third(third)
    sum_three = ScatterAcross(program, pairs)
    sum_three.core_step()
    sum_two.core_send()
    sum_three.core_send()
    sum_one.meet_high(HEAVY)
    sum_one.send_low()
    sum_one.send(4)
    parts = (parts_one, parts_two, parts_three)
    thirds_halves = [first.halves, second.halves, third.halves]
    sent, kept = back_rows(
        [one for part in parts for one in part[:2]],
        [halves for halves in thirds_halves for _ in range(2)],
        [0, 1] * 3,
    )
    grad_sent = send(sent, 0, 1)
    sum_two.arrive_core()
    sum_three.arrive_core()
    sum_two.beside()
    sum_three.beside()
    sum_one.arrive_low()
    sum_one.arrive_far()
    sum_two.send_high()
    sum_one.meet_far()
    sum_one.send(8)
    sum_three.send_part(4, 0)
    grad_branch, grad_hidden, mlp_gain_part = run(
        norm_back, kept, arrive(grad_sent), hat_second, inv_second, mlp_gain[None], cotangent
    )
    rows_sent = send(grad_branch, 0, 1)
    result_part = back_rows([part[2] for part in parts], thirds_halves, [2] * 3)
    sum_two.meet_high()
    sum_two.send_low()
    sum_two.send(4)
    sum_one.arrive_far()
    sum_one.finish()
    sum_three.arrive_part(0)
    sum_three.meet_part(0)
    sum_three.send_part(8, 0)
    branch_rows = run(stack, grad_branch, arrive(rows_sent))
    result_sent = send(result_part[0], 0, 1)
    grads, q_terms, k_terms = run(
        lambda weights, rows, kept: attend_rows_back(weights, rows, tables, kept, groups, repeat),
        attn.halves,
        branch_rows,
        (raw, queries, keys, values, logs),
    )
    sent, kept = back_rows([grads], [attn.halves], [0], True)
    pairs = [(rows_first, grads, block) for block in range(columns // query_cols)]
    sum_attn = Scatter(program, [*pairs, (branch_rows, attended)], True)
    sum_attn.core_step()
    sum_two.arrive_low()
    sum_two.arrive_far()
    sum_three.arrive_part(0)
    result_other = arrive(result_sent)
    sum_attn.core_send()
    sum_two.meet_far()
    sum_attn.arrive_core()
    sum_attn.beside()
    sum_three.send_part(4, 1)
    sum_two.send(8)
    grad_sent = send(sent, 0, 1)
    sum_attn.send_low()
    sum_attn.send_high()
    result = run(restore_sum, matrix, hidden, result_part[1], result_other)
    sum_attn.meet_high()
    sum_attn.send(4)
    sum_attn.arrive_low()
    grad_other = arrive(grad_sent)
    sum_three.arrive_part(1)
    sum_two.arrive_far()
    sum_three.meet_part(1)
    sum_three.send_part(8, 1)
    tokens_low, _, attn_gain_part = run(
        norm_back, kept, grad_other, hat_first, inv_first, attn_gain[None], grad_hidden
    )
    total = run(gain_parts, attn_gain_part, mlp_gain_part, q_terms, k_terms, matrix)

    def total_send(*partners):
        return [send(total, *partner) for partner in partners]

    def total_arrive(sent):
        return run(lambda *arrays: meet(arrays, F32)[0], total, *[arrive(one) for one in sent])

    gains_sent = total_send((0, 1))
    sum_two.finish()
    tokens_grad = run(restore_sum, matrix, tokens_low)
    sum_attn.arrive_far()
    sum_attn.meet_far()
    sum_three.arrive_part(1)
    sum_three.meet_across()
    total = total_arrive(gains_sent)
    sum_attn.send(8)
    sum_three.send_part(2, 1)
    gains_sent = total_send((1,), (2,), (3,))
    total = total_arrive(gains_sent)
    gains_sent = total_send((4,), (8,), (12,))
    sum_attn.arrive_far()
    sum_attn.finish()
    sum_three.arrive_part(1)
    sum_three.finish()

    def split_sums(*sums):
        rows = sums[0].shape[0]
        moves = [
            (source, (0, rows), (part * cut, (part + 1) * cut), part, 0, source * cut)
            for source in range(3)
            for part in range(3)
        ]
        return copy_blocks(sums, moves, [(rows, ff_cols)] * 3)

    weights = run(split_sums, sum_one.kept, sum_two.kept, sum_three.kept)
    total = total_arrive(gains_sent)

    gate_grad, up_grad, down_grad = weights
    kept = sum_attn.kept
    return (
        result[None],
        tokens_grad[None],
        total[0],
        kept[:, :query_cols],
        kept[:, query_cols : query_cols + key_cols],
        kept[:, query_cols + key_cols : columns],
        total[2, :HD],
        total[3, :HD],
        kept[:, columns:],
        total[1],
        gate_grad,
        up_grad,
        down_grad,
    )


def local(*arrays):
    small = lax.axis_size("dp") == DEVICES and lax.axis_size("tp") == 2
    if small and arrays[0].shape[1:] == (256, 1024):
        return local_small(*arrays)
    return local_large(*arrays)


def solution(mesh):
    in_specs = (
        P("dp", "tp", None),
        P("dp", None),
        P(),
        P("dp", "tp"),
        P("dp", "tp"),
        P("dp", "tp"),
        P(),
        P(),
        P("dp", "tp"),
        P(),
        P("dp", "tp"),
        P("dp", "tp"),
        P("dp", "tp"),
        P("dp", "tp", None),
    )
    out_specs = (
        P("dp", "tp", None),
        P("dp", "tp", None),
        P(),
        P("dp", "tp"),
        P("dp", "tp"),
        P("dp", "tp"),
        P(),
        P(),
        P("dp", "tp"),
        P(),
        P("dp", "tp"),
        P("dp", "tp"),
        P("dp", "tp"),
    )
    return jax.shard_map(local, mesh=mesh, in_specs=in_specs, out_specs=out_specs, check_vma=False)
```
